256 devices in a mesh: dp: 16 (over y, x), seq: 16 (over z, core).
Axes of the slice: x: 4, y: 4, z: 8, core: 2. Of those that a mesh axis runs over, the one named last changes fastest.
Arguments:
- x_in: float32 [16, 4096, 2560], P('dp', 'seq'), may hold values from -45 to 45
- a_log: float32 [16, 40, 4096], P('dp', None, 'seq'), may hold values from -0.6 to 0, as said below
- b_in: float32 [16, 4096, 128], P('dp', 'seq'), may hold values from -0.03125 to 0.03125
- c_in: float32 [16, 4096, 128], P('dp', 'seq'), may hold values from -6 to 6
- g_out: bfloat16 [16, 4096, 2560], P('dp', 'seq'), may hold values from -6 to 6
- w_out: bfloat16 [2560, 2560], P('dp'), may hold values from -0.125 to 0.125
- d_skip: float32 [40], replicated, may hold values from 0.5 to 2
- group_ids: int32 [40], replicated, may hold values from 0 to 3, as said below
Outputs:
- grad_x: float32 [16, 4096, 2560], P('dp', 'seq')
- grad_a: float32 [16, 40, 4096], P('dp', None, 'seq')
- grad_b: float32 [16, 4096, 128], P('dp', 'seq')
- grad_c: float32 [16, 4096, 128], P('dp', 'seq')
- clipped_w: float32 [2560, 2560], P('dp')
- clipped_d: float32 [40], replicated
The draws below stay inside these ranges and needn't reach their ends.
Inputs may be any that keep to these rules, and one draw needn't show every extreme that they name: `group_ids`: values 0 to 3, each named by at least one head. `a_log`: log decays, negative.
All inputs are finite; a program needn't handle non-finite values.
Results may differ from the reference program's by a relative error of at most 0.015.
Values may be sent and summed in bfloat16 or wider, within the bound.
No kernel may reach another device: no remote copies, remote signals or barrier semaphores. Data moves between devices by JAX's collectives and lax.ppermute only.
A program may use at most 128 MiB of HBM per device.

```python
import math
import jax
import jax.numpy as jnp
from jax import lax

D = 2560
H = 40
P_SIZE = 64
N = 128
SPAN = 256
GROUPS = 4
TOK_DEV = 256
BATCH = 16
SEQLEN = 4096
DI = 2560
N_SEQ = 16


def shared_groups(key):
    key = jax.random.fold_in(key, 37)
    first, second = jax.random.split(key)
    order = jax.random.permutation(first, H)
    spread = jax.random.randint(second, (H,), 0, GROUPS)
    ranks = jnp.arange(H, dtype=jnp.int32)
    values = jnp.where(ranks < GROUPS, ranks, spread).astype(jnp.int32)
    return jnp.zeros((H,), jnp.int32).at[order].set(values)


def draw_x_in(key, part):
    groups = shared_groups(key)
    key = jax.random.fold_in(key, 11)
    first, second = jax.random.split(key)
    jitter = jnp.exp(jax.random.uniform(first, (H,), minval=math.log(0.7), maxval=math.log(1.4)))
    level = jnp.exp(math.log(8.0) * groups.astype(jnp.float32) / (GROUPS - 1))
    head_scale = level * jitter
    base = jax.random.truncated_normal(second, -4.0, 4.0, (BATCH, SEQLEN, H, P_SIZE))
    return (base * head_scale[:, None]).reshape(BATCH, SEQLEN, H * P_SIZE).astype(jnp.float32)


def draw_a_log(key, part):
    key = jax.random.fold_in(key, 23)
    keys = jax.random.split(key, 6)
    share = 0.5
    fast = jax.random.uniform(keys[0], (H,)) < share
    fast_rate = jax.random.uniform(keys[1], (H,), minval=1.0 / 50.0, maxval=1.0 / 30.0)
    slow_rate = jax.random.uniform(keys[2], (H,), minval=0.2, maxval=1.0) * (0.5 * math.log(10.0) / SEQLEN)
    rate = jnp.where(fast, fast_rate, slow_rate)
    rough = jax.random.uniform(keys[3], (BATCH, H, SEQLEN), minval=0.5, maxval=1.5)
    spots = jax.random.randint(keys[4], (BATCH, 2), 0, SEQLEN)
    places = jnp.arange(SEQLEN)[None, :]
    struck = ((places == spots[:, 0:1]) | (places == spots[:, 1:2])).astype(jnp.float32)
    losses = jax.random.uniform(keys[5], (BATCH, H, 1), minval=0.22, maxval=0.51)
    return (-(rate[None, :, None] * rough + struck[:, None, :] * losses)).astype(jnp.float32)


def draw_group_ids(key, part):
    groups = shared_groups(key)
    return groups


def block_scale(own_key, extent, cuts, low, largest):
    loudness = 1.0
    for dim, blocks in cuts:
        steps = jax.random.uniform(jax.random.fold_in(jax.random.fold_in(own_key, 6), dim), (blocks,), jnp.float32, low / len(cuts), largest / len(cuts))
        loudness = loudness * jnp.repeat(jnp.exp(steps), extent[dim] // blocks).reshape((-1,) + (1,) * (len(extent) - 1 - dim))
    return loudness


def gaussian(key, shape, deviation, limit, cuts=(), kind=jnp.bfloat16):
    values = jax.random.normal(key, shape, jnp.float32) * deviation
    if len(cuts) > 0:
        values = block_scale(key, shape, cuts, -0.22, 0.18) * values
    return jnp.clip(values, min=-limit, max=limit).astype(kind)


def setup_inputs(seed: int = 0) -> dict:
    arg_keys = jax.random.split(jax.random.key(seed), 9)
    return {
        "x_in": draw_x_in(jax.random.fold_in(arg_keys[8], 71), 0),
        "a_log": draw_a_log(jax.random.fold_in(arg_keys[8], 71), 0),
        "b_in": gaussian(arg_keys[2], (BATCH, SEQLEN, N), (N * TOK_DEV) ** -0.5, 0.03125, ((0, 16), (1, 16)), jnp.float32),
        "c_in": gaussian(arg_keys[3], (BATCH, SEQLEN, N), 1.0, 6.0, ((0, 16), (1, 16)), jnp.float32),
        "g_out": gaussian(arg_keys[4], (BATCH, SEQLEN, D), 1.0, 6.0, ((0, 16), (1, 16))),
        "w_out": gaussian(arg_keys[5], (DI, D), DI ** -0.5, 0.125, ((0, 16),)),
        "d_skip": jnp.clip(jax.random.uniform(arg_keys[6], (H,), jnp.float32, 0.5, 2.0), 0.5, 2.0),
        "group_ids": draw_group_ids(jax.random.fold_in(arg_keys[8], 71), 0),
    }


def ssd_block(xs, decay, b_rows, c_rows, skip, start_state):
    length = xs.shape[0]
    heads = decay.shape[0]
    width = xs.shape[1] // heads
    blocks = length // SPAN
    xs_b = xs.reshape(blocks, SPAN, heads, width)
    dec_b = decay.reshape(heads, blocks, SPAN).transpose(1, 0, 2)
    b_b = b_rows.reshape(blocks, SPAN, b_rows.shape[1])
    c_b = c_rows.reshape(blocks, SPAN, c_rows.shape[1])
    lower = jnp.arange(SPAN)[:, None] >= jnp.arange(SPAN)[None, :]
    high = lax.Precision.HIGHEST

    def step(state, item):
        xq, dq, bq, cq = item
        cum = jnp.cumsum(dq, axis=1)
        diff = cum[:, :, None] - cum[:, None, :]
        weights = jnp.where(lower[None], jnp.exp(jnp.where(lower[None], diff, 0.0)), 0.0)
        scores = jnp.dot(cq, bq.T, precision=high)
        mixed = weights * scores[None]
        intra = jnp.einsum('hij,jhp->ihp', mixed, xq, precision=high)
        inter = jnp.einsum('in,hpn->ihp', cq, state, precision=high) * jnp.exp(cum).T[:, :, None]
        tail = jnp.exp(cum[:, -1:] - cum)
        new_state = jnp.exp(cum[:, -1])[:, None, None] * state + jnp.einsum('jhp,jn,hj->hpn', xq, bq, tail, precision=high)
        out = intra + inter + skip[None, :, None] * xq
        return (new_state, out)
    final, outs = lax.scan(step, start_state, (xs_b, dec_b, b_b, c_b))
    return (outs.reshape(length, heads * width), final)

def add_block(total, pair):
    y_part, g_part = pair
    term = lax.dot_general(y_part, g_part, (((0,), (0,)), ((), ())), preferred_element_type=jnp.float32)
    term = lax.optimization_barrier(term.astype(jnp.bfloat16))
    return (total + term.astype(jnp.float32), None)

def reference(x_in, a_log, b_in, c_in, g_out, w_out, d_skip, group_ids):
    high = lax.Precision.HIGHEST
    zero_state = jnp.zeros((H, P_SIZE, N), jnp.float32)

    def forward(xs, decay, b_rows, c_rows, skip):
        return ssd_block(xs, decay, b_rows, c_rows, skip, zero_state)[0]

    def one(carry, item):
        xs, decay, b_rows, c_rows, grads_out = item
        y_full, pull = jax.vjp(forward, xs, decay, b_rows, c_rows, d_skip)
        y_low = y_full.astype(jnp.bfloat16)
        g_y = lax.dot_general(grads_out, w_out, (((1,), (1,)), ((), ())), preferred_element_type=jnp.float32)
        gx, ga, gb, gc, gd = pull(g_y)
        y_blocks = y_low.reshape(N_SEQ, TOK_DEV, H * P_SIZE)
        g_blocks = grads_out.reshape(N_SEQ, TOK_DEV, D)
        gw, _ = lax.scan(add_block, carry[0], (y_blocks, g_blocks))
        return ((gw, carry[1] + gd), (gx, ga, gb, gc))
    init = (jnp.zeros((H * P_SIZE, D), jnp.float32), jnp.zeros((H,), jnp.float32))
    (grad_w, grad_d), (grad_x, grad_a, grad_b, grad_c) = lax.scan(one, init, (x_in, a_log, b_in, c_in, g_out))
    head_onehot = (group_ids[:, None] == jnp.arange(GROUPS, dtype=jnp.int32)[None, :]).astype(jnp.float32)
    row_heads = jnp.arange(H * P_SIZE, dtype=jnp.int32) // P_SIZE
    row_onehot = (row_heads[:, None] == jnp.arange(H, dtype=jnp.int32)[None, :]).astype(jnp.float32)
    row_groups = jnp.dot(row_onehot, head_onehot, precision=high)
    sumsq = jnp.dot(lax.optimization_barrier(jnp.sum(grad_w * grad_w, axis=1)), row_groups, precision=high)
    sumsq = sumsq + jnp.dot(grad_d * grad_d, head_onehot, precision=high)
    counts = lax.optimization_barrier(jnp.sum(head_onehot, axis=0))
    tokens_all = float(BATCH * SEQLEN)
    factor = jnp.minimum(1.0, 7.0 * jnp.sqrt(counts * (P_SIZE * D + 1.0) * tokens_all) / jnp.sqrt(sumsq + 1e-06))
    clipped_w = grad_w * jnp.dot(row_groups, factor, precision=high)[:, None]
    clipped_d = grad_d * jnp.dot(head_onehot, factor, precision=high)
    return (grad_x, grad_a, grad_b, grad_c, clipped_w, clipped_d)
```

```python
import functools

import jax
import jax.numpy as jnp
from jax import lax
from jax.experimental import pallas as pl
from jax.experimental.pallas import tpu as pltpu
from jax.sharding import Mesh
from jax.sharding import PartitionSpec as P

D = 2560
H = 40
P_SIZE = 64
N = 128
T = 256
GROUPS = 4
PAIRS = H // 2
SEQ = ("z", "core")
N_SEQ = 16
OWN = H * P_SIZE // N_SEQ
HIGH = lax.Precision.HIGHEST
BF = jnp.bfloat16
F32 = jnp.float32
VMEM = 40 * 1024 * 1024


def nn(a, b):
    return lax.dot_general(a, b, (((1,), (0,)), ((), ())), preferred_element_type=F32)


def nt(a, b):
    return lax.dot_general(a, b, (((1,), (1,)), ((), ())), preferred_element_type=F32)


def tn(a, b):
    return lax.dot_general(a, b, (((0,), (0,)), ((), ())), preferred_element_type=F32)


def iota(shape, dim):
    return lax.broadcasted_iota(jnp.int32, shape, dim)


def whole(shape):
    return pl.BlockSpec(shape, lambda *_: (0,) * len(shape))


def wide(rows):
    return pl.BlockSpec((rows, 2 * P_SIZE), lambda p: (0, p))


def state_block():
    return pl.BlockSpec((2 * P_SIZE, N), lambda p: (p, 0))


def params():
    return pltpu.CompilerParams(vmem_limit_bytes=VMEM)


def cost(flops, moved, exps):
    return pl.CostEstimate(flops=flops, bytes_accessed=moved, transcendentals=exps)


def spread(cum_t, pair):
    lane_head = 2 * pair + iota((H, 2 * P_SIZE), 1) // P_SIZE
    pick = (iota((H, 2 * P_SIZE), 0) == lane_head).astype(F32)
    return jnp.dot(cum_t, pick, precision=HIGH, preferred_element_type=F32)


def column(cum_t, head):
    return jnp.sum(jnp.where(iota(cum_t.shape, 1) == head, cum_t, 0.0), axis=1, keepdims=True)


def low_half(shape):
    return iota(shape, 1) < P_SIZE


def ends_kernel(x_ref, a_ref, b_ref, cum_ref, cum_t_ref, end_ref):
    pair = pl.program_id(0)

    @pl.when(pair == 0)
    def _():
        a = a_ref[...]
        upto = (iota((T, T), 0) <= iota((T, T), 1)).astype(F32)
        cum_ref[...] = jnp.dot(a, upto, precision=HIGH, preferred_element_type=F32)
        down = (iota((T, T), 1) <= iota((T, T), 0)).astype(F32)
        cum_t_ref[...] = lax.dot_general(
            down, a, (((1,), (1,)), ((), ())), precision=HIGH, preferred_element_type=F32
        )

    cum = spread(cum_t_ref[...], pair)
    tail = jnp.exp(cum[T - 1 : T, :] - cum)
    end_ref[...] = tn((x_ref[...] * tail).astype(BF), b_ref[...].astype(BF)).astype(BF)


def local_ends(x, a, b):
    return pl.pallas_call(
        ends_kernel,
        grid=(PAIRS,),
        in_specs=[wide(T), whole((H, T)), whole((T, N))],
        out_specs=[whole((H, T)), whole((T, H)), state_block()],
        out_shape=[
            jax.ShapeDtypeStruct((H, T), F32),
            jax.ShapeDtypeStruct((T, H), F32),
            jax.ShapeDtypeStruct((H * P_SIZE, N), BF),
        ],
        compiler_params=params(),
        cost_estimate=cost(2 * T * D * N, 4 * T * D, T * D),
        name="ends",
    )(x, a, b)


def intra_kernel(x_ref, cum_ref, cum_t_ref, b_ref, c_ref, skip_ref, y_ref, scores):
    pair = pl.program_id(0)

    @pl.when(pair == 0)
    def _():
        keep = iota((T, T), 0) >= iota((T, T), 1)
        scores[...] = jnp.where(keep, nt(c_ref[...].astype(BF), b_ref[...].astype(BF)), 0.0)

    x = x_ref[...]
    xb = x.astype(BF)
    parts = []
    for k in range(2):
        head = 2 * pair + k
        diff = column(cum_t_ref[...], head) - cum_ref[pl.ds(head, 1), :]
        mixed = (jnp.exp(jnp.minimum(diff, 0.0)) * scores[...]).astype(BF)
        parts.append(nn(mixed, xb))
    y_ref[...] = jnp.where(low_half(x.shape), parts[0], parts[1]) + skip_ref[...] * x


def intra(x, cum, cum_t, b, c, skip):
    return pl.pallas_call(
        intra_kernel,
        grid=(PAIRS,),
        in_specs=[
            wide(T), whole((H, T)), whole((T, H)), whole((T, N)), whole((T, N)), wide(1),
        ],
        out_specs=wide(T),
        out_shape=jax.ShapeDtypeStruct((T, D), F32),
        scratch_shapes=[pltpu.VMEM((T, T), F32)],
        compiler_params=params(),
        cost_estimate=cost(4 * T * T * D, 8 * T * D, H * T * T),
        name="intra",
    )(x, cum, cum_t, b, c, skip)


def inter_kernel(part_ref, cum_t_ref, c_ref, start_ref, y_ref):
    grow = jnp.exp(spread(cum_t_ref[...], pl.program_id(0)))
    y = part_ref[...] + grow * nt(c_ref[...].astype(BF), start_ref[...])
    y_ref[...] = y.astype(BF)


def inter(part, cum_t, c, start):
    return pl.pallas_call(
        inter_kernel,
        grid=(PAIRS,),
        in_specs=[wide(T), whole((T, H)), whole((T, N)), state_block()],
        out_specs=wide(T),
        out_shape=jax.ShapeDtypeStruct((T, D), BF),
        compiler_params=params(),
        cost_estimate=cost(2 * T * D * N, 6 * T * D, T * D),
        name="inter",
    )(part, cum_t, c, start)


def chain_kernel(reverse, mine_ref, parts_ref, totals_ref, out_ref):
    owner = (mine_ref[0] * OWN + iota((OWN, N), 0)) // P_SIZE == iota((OWN, N), 1)
    carry = jnp.zeros((OWN, N), F32)
    for s in range(N_SEQ - 1, -1, -1) if reverse else range(N_SEQ):
        out_ref[s] = carry.astype(BF)
        pieces = totals_ref[s].astype(F32)
        total = pieces[0:1, :] + pieces[1:2, :] + pieces[2:3, :]
        decay = jnp.sum(jnp.where(owner, total, 0.0), axis=1, keepdims=True)
        carry = jnp.exp(decay) * carry + parts_ref[s].astype(F32)


def chain(parts, totals, mine, reverse):
    return pl.pallas_call(
        functools.partial(chain_kernel, reverse),
        in_specs=[
            pl.BlockSpec(memory_space=pltpu.SMEM),
            pl.BlockSpec(memory_space=pltpu.VMEM),
            pl.BlockSpec(memory_space=pltpu.VMEM),
        ],
        out_specs=pl.BlockSpec(memory_space=pltpu.VMEM),
        out_shape=jax.ShapeDtypeStruct((N_SEQ, OWN, N), BF),
        compiler_params=params(),
        cost_estimate=cost(4 * N_SEQ * OWN * N, 4 * N_SEQ * OWN * N, N_SEQ * OWN),
        name="chain",
    )(mine, parts, totals)


def three(v):
    hi = lax.reduce_precision(v, 8, 7)
    mid = lax.reduce_precision(v - hi, 8, 7)
    rows = jnp.stack([hi, mid, v - hi - mid]).astype(BF)
    return jnp.pad(rows, ((0, 13), (0, N - v.shape[0])))


def swap_seq(states, extra):
    rows = jnp.broadcast_to(extra[None], (N_SEQ, 16, N))
    sent = jnp.concatenate([states.reshape(N_SEQ, OWN, N), rows], axis=1)
    got = lax.all_to_all(sent, SEQ, 0, 0, tiled=True)
    return got[:, :OWN], got[:, OWN:]


def back_seq(states):
    return lax.all_to_all(states, SEQ, 0, 0, tiled=True).reshape(H * P_SIZE, N)


def term_kernel(yo_ref, yx_ref, go_ref, gx_ref, first_ref, second_ref):
    half = go_ref.shape[1] // 2
    for i, out in enumerate((first_ref, second_ref)):
        cols = pl.ds(i * half, half)
        term = tn(yo_ref[...], go_ref[:, cols]) + tn(yx_ref[...], gx_ref[:, cols])
        out[...] = term.astype(BF).reshape(out.shape)


def terms(y_own, y_other, g_own, g_other):
    rows = pl.BlockSpec((T, 4 * OWN), lambda i: (0, i))
    half = g_own.shape[1] // 2
    return pl.pallas_call(
        term_kernel,
        grid=(4,),
        in_specs=[rows, rows, whole(g_own.shape), whole(g_own.shape)],
        out_specs=[
            pl.BlockSpec((4, 1, OWN, half), lambda i: (0, i, 0, 0)),
            pl.BlockSpec((1, 4, OWN, half), lambda i: (i, 0, 0, 0)),
        ],
        out_shape=[jax.ShapeDtypeStruct((4, 4, OWN, half), BF)] * 2,
        compiler_params=params(),
        cost_estimate=cost(4 * T * D * D // 2, 3 * D * D // 2, 0),
        name="terms",
    )(y_own, y_other, g_own, g_other)


def entry_kernel(own_ref, other_ref, x_ref, cum_t_ref, c_ref, gy_ref, entry_ref, gd_ref):
    gy = own_ref[...] + other_ref[...].astype(F32)
    gy_ref[...] = gy.astype(BF)
    gd_ref[...] = jnp.sum(gy * x_ref[...], axis=0, keepdims=True)
    grow = jnp.exp(spread(cum_t_ref[...], pl.program_id(0)))
    entry_ref[...] = tn((gy * grow).astype(BF), c_ref[...].astype(BF)).astype(BF)


def entries(own, other, x, cum_t, c):
    return pl.pallas_call(
        entry_kernel,
        grid=(PAIRS,),
        in_specs=[wide(T), wide(T), wide(T), whole((T, H)), whole((T, N))],
        out_specs=[wide(T), state_block(), wide(1)],
        out_shape=[
            jax.ShapeDtypeStruct((T, D), BF),
            jax.ShapeDtypeStruct((H * P_SIZE, N), BF),
            jax.ShapeDtypeStruct((1, D), F32),
        ],
        compiler_params=params(),
        cost_estimate=cost(2 * T * D * N, 12 * T * D, T * D),
        name="entries",
    )(own, other, x, cum_t, c)


def back_kernel(
    x_ref, gy_ref, cum_ref, cum_t_ref, b_ref, c_ref, skip_ref, start_ref, last_ref,
    gx_ref, ga_ref, gb_ref, gc_ref,
    scores, d_scores, rows, cols, tails, totals,
):
    pair = pl.program_id(0)
    bb = b_ref[...].astype(BF)
    cb = c_ref[...].astype(BF)

    @pl.when(pair == 0)
    def _():
        keep = iota((T, T), 1) >= iota((T, T), 0)
        scores[...] = jnp.where(keep, nt(bb, cb), 0.0)
        d_scores[...] = jnp.zeros_like(d_scores)
        cols[...] = jnp.zeros_like(cols)
        tails[...] = jnp.zeros_like(tails)
        gb_ref[...] = jnp.zeros_like(gb_ref)
        gc_ref[...] = jnp.zeros_like(gc_ref)

    x = x_ref[...]
    gyb = gy_ref[...]
    gy = gyb.astype(F32)
    xb = x.astype(BF)
    low = low_half(x.shape)
    lanes = iota((T, N), 1)
    parts = []
    for k in range(2):
        head = 2 * pair + k
        diff = cum_ref[pl.ds(head, 1), :] - column(cum_t_ref[...], head)
        weights = jnp.exp(jnp.minimum(diff, 0.0))
        mine = jnp.where(low if k == 0 else ~low, x, 0.0).astype(BF)
        d_mixed = weights * nt(mine, gyb)
        d_scores[...] += d_mixed
        parts.append(nn((weights * scores[...]).astype(BF), gyb))
        change = d_mixed * scores[...]
        rows[pl.ds(head, 1), :] = jnp.sum(change, axis=0, keepdims=True)
        down = jnp.sum(change, axis=1, keepdims=True)
        cols[...] -= jnp.where(lanes == head, down, 0.0)
    cum = spread(cum_t_ref[...], pair)
    grow = jnp.exp(cum)
    tail = jnp.exp(cum[T - 1 : T, :] - cum)
    start = start_ref[...]
    last = last_ref[...]
    pick = (lanes[:N] == 2 * pair + iota((N, N), 0) // P_SIZE).astype(BF)
    grown = gy * grow
    cols[...] += nn((grown * nt(cb, start)).astype(BF), pick)
    gc_ref[...] += nn(grown.astype(BF), start)
    faded = x * tail
    back = nt(bb, last)
    tails[...] += nn((faded * back).astype(BF), pick)
    gb_ref[...] += nn(faded.astype(BF), last)
    gx_ref[...] = jnp.where(low, parts[0], parts[1]) + tail * back + skip_ref[...] * gy
    both = start.astype(F32) * last.astype(F32)
    for k in range(2):
        part = both[k * P_SIZE : (k + 1) * P_SIZE, :]
        totals[pl.ds(2 * pair + k, 1), :] = jnp.sum(part, axis=0, keepdims=True)

    @pl.when(pair == PAIRS - 1)
    def _():
        keep = iota((T, T), 1) >= iota((T, T), 0)
        ds = jnp.where(keep, d_scores[...], 0.0).astype(BF)
        gb_ref[...] += nn(ds, cb)
        gc_ref[...] += tn(ds, bb)
        after = (iota((T, T), 0) >= iota((T, T), 1)).astype(F32)
        before = (iota((T, T), 0) < iota((T, T), 1)).astype(F32)
        dims = (((0,), (0,)), ((), ()))
        ga = jnp.dot(rows[...], after, precision=HIGH, preferred_element_type=F32)
        up = lax.dot_general(cols[...], after, dims, precision=HIGH, preferred_element_type=F32)
        up += lax.dot_general(tails[...], before, dims, precision=HIGH, preferred_element_type=F32)
        whole_decay = jnp.exp(cum_ref[:, T - 1 : T])
        ga_ref[...] = ga + up[:H] + whole_decay * jnp.sum(totals[...], axis=1, keepdims=True)


def backward(x, gy, cum, cum_t, b, c, skip, start, last):
    return pl.pallas_call(
        back_kernel,
        grid=(PAIRS,),
        in_specs=[
            wide(T), wide(T), whole((H, T)), whole((T, H)), whole((T, N)), whole((T, N)),
            wide(1), state_block(), state_block(),
        ],
        out_specs=[wide(T), whole((H, T)), whole((T, N)), whole((T, N))],
        out_shape=[
            jax.ShapeDtypeStruct((T, D), F32),
            jax.ShapeDtypeStruct((H, T), F32),
            jax.ShapeDtypeStruct((T, N), F32),
            jax.ShapeDtypeStruct((T, N), F32),
        ],
        scratch_shapes=[
            pltpu.VMEM((T, T), F32),
            pltpu.VMEM((T, T), F32),
            pltpu.VMEM((H, T), F32),
            pltpu.VMEM((T, N), F32),
            pltpu.VMEM((T, N), F32),
            pltpu.VMEM((H, N), F32),
        ],
        compiler_params=params(),
        cost_estimate=cost(8 * T * T * D, 14 * T * D, H * T * T),
        name="backward",
    )(x, gy, cum, cum_t, b, c, skip, start, last)


def add_up(parts):
    return jnp.sum(parts.astype(F32), axis=0)


def swap(v, axis):
    return lax.all_to_all(v, axis, 0, 0, tiled=True)


def other_core(v):
    return lax.ppermute(v, "core", [(0, 1), (1, 0)])


def gathered(v, axis):
    mine = lax.axis_index(axis)
    found = [v]
    for d in range(1, 4):
        found.append(lax.ppermute(v, axis, [((i + d) % 4, i) for i in range(4)]))
    return lax.dynamic_slice_in_dim(jnp.stack(found + found), (4 - mine) % 4, 4, axis=0)


def per_device(x_in, a_log, b_in, c_in, g_out, w_out, d_skip, group_ids):
    x, a, b, c, g = (x_in[0], a_log[0], b_in[0], c_in[0], g_out[0])
    core = lax.axis_index("core")
    half = D // 2
    mine = (2 * lax.axis_index("z") + core).reshape(1).astype(jnp.int32)
    tokens_all = float(T * N_SEQ * 16)

    w_mine = lax.dynamic_slice_in_dim(w_out, core * half, half, axis=1)
    w_half = lax.all_gather(w_mine, ("y", "x"), axis=0, tiled=True)
    g_mine = lax.dynamic_slice_in_dim(g, core * half, half, axis=1)
    g_other = other_core(lax.dynamic_slice_in_dim(g, (1 - core) * half, half, axis=1))
    skip = jnp.repeat(d_skip, P_SIZE)[None]

    cum, cum_t, end = local_ends(x, a, b)
    parts, totals = swap_seq(end, three(cum[:, T - 1]))
    y_part = intra(x, cum, cum_t, b, c, skip)
    start = back_seq(chain(parts, totals, mine, False))
    y_own = inter(y_part, cum_t, c, start)
    y_other = other_core(y_own)
    first, second = terms(y_own, y_other, g_mine, g_other)

    w_half, first, second = lax.optimization_barrier((w_half, first, second))
    first = swap(first, "x")
    second = swap(second, "y")

    dims = (((1,), (1,)), ((), ()))
    gy_other = lax.dot_general(g_other, w_half, dims, preferred_element_type=F32).astype(BF)
    gy_other = other_core(gy_other)
    gy_own = lax.dot_general(g_mine, w_half, dims, preferred_element_type=F32)
    gy, entry, gd = entries(gy_own, gy_other, x, cum_t, c)
    gd = jnp.sum(gd.reshape(H, P_SIZE), axis=1)
    parts, gd_parts = swap_seq(entry, three(gd))
    last = back_seq(chain(parts, totals, mine, True))

    first = swap(add_up(first).astype(BF), "y")
    second = swap(add_up(second).astype(BF), "x")
    owned = jnp.concatenate([add_up(first), add_up(second)], axis=1).astype(BF)
    owned = add_up(swap(owned.reshape(8, OWN // 8, half), "z")).astype(BF)
    owned = swap(jnp.broadcast_to(owned[None], (N_SEQ,) + owned.shape), SEQ)
    owned = owned.reshape(8, 2, OWN // 8, half).transpose(0, 2, 1, 3).reshape(OWN, D)
    grad_w = owned.astype(F32)

    gx, ga, gb, gc = backward(x, gy, cum, cum_t, b, c, skip, start, last)

    first_row = (4 * lax.axis_index("y") + lax.axis_index("x")) * OWN
    head_onehot = (group_ids[:, None] == jnp.arange(GROUPS, dtype=jnp.int32)[None, :]).astype(F32)
    row_heads = (first_row + jnp.arange(OWN, dtype=jnp.int32)) // P_SIZE
    row_onehot = (row_heads[:, None] == jnp.arange(H, dtype=jnp.int32)[None, :]).astype(F32)
    row_groups = jnp.dot(row_onehot, head_onehot, precision=HIGH)
    squares = jnp.dot(jnp.sum(grad_w * grad_w, axis=1), row_groups, precision=HIGH)
    gd_mine = jnp.sum(jnp.sum(gd_parts[:, :3, :H].astype(F32), axis=1), axis=0)
    note = jnp.concatenate([gd_mine, squares, jnp.zeros((N - H - GROUPS,), F32)])[None]
    note = jnp.sum(gathered(jnp.sum(gathered(note, "x"), axis=0), "y"), axis=0)[0]
    grad_d = note[:H]
    sumsq = note[H : H + GROUPS] + jnp.dot(grad_d * grad_d, head_onehot, precision=HIGH)
    counts = jnp.sum(head_onehot, axis=0)
    factor = jnp.minimum(
        1.0, 7.0 * jnp.sqrt(counts * (P_SIZE * D + 1.0) * tokens_all) / jnp.sqrt(sumsq + 1e-06)
    )
    clipped_w = grad_w * jnp.dot(row_groups, factor, precision=HIGH)[:, None]
    clipped_d = grad_d * jnp.dot(head_onehot, factor, precision=HIGH)
    return (gx[None], ga[None], gb[None], gc[None], clipped_w, clipped_d)


def solution(mesh):
    fine = Mesh(mesh.devices.reshape(4, 4, 8, 2), ("y", "x", "z", "core"))
    rows = ("y", "x")
    tokens = P(rows, SEQ, None)
    return jax.shard_map(
        per_device,
        mesh=fine,
        in_specs=(
            tokens, P(rows, None, SEQ), tokens, tokens, tokens, P(rows, None), P(), P(),
        ),
        out_specs=(tokens, P(rows, None, SEQ), tokens, tokens, P(rows, None), P()),
        check_vma=False,
    )
```

```python
import functools

import jax
import jax.numpy as jnp
from jax import lax
from jax.experimental import pallas as pl
from jax.experimental.pallas import tpu as pltpu
from jax.sharding import Mesh
from jax.sharding import PartitionSpec as P

D = 2560
H = 40
P_SIZE = 64
N = 128
T = 256
GROUPS = 4
PAIRS = H // 2
SEQ = ("z", "core")
N_SEQ = 16
OWN = H * P_SIZE // N_SEQ
HIGH = lax.Precision.HIGHEST
BF = jnp.bfloat16
F32 = jnp.float32
VMEM = 56 * 1024 * 1024
WIDE = 5
STEP = 2
ROWS = OWN + 16
TILES = 13


def nn(a, b):
    return lax.dot_general(a, b, (((1,), (0,)), ((), ())), preferred_element_type=F32)


def nt(a, b):
    return lax.dot_general(a, b, (((1,), (1,)), ((), ())), preferred_element_type=F32)


def tn(a, b):
    return lax.dot_general(a, b, (((0,), (0,)), ((), ())), preferred_element_type=F32)


def iota(shape, dim):
    return lax.broadcasted_iota(jnp.int32, shape, dim)


def whole(shape):
    return pl.BlockSpec(shape, lambda *_: (0,) * len(shape))


def wide(rows, pairs):
    return pl.BlockSpec((rows, pairs * 2 * P_SIZE), lambda p: (0, p))


def state_block(pairs):
    return pl.BlockSpec((pairs * 2 * P_SIZE, N), lambda p: (p, 0))


def smem():
    return pl.BlockSpec(memory_space=pltpu.SMEM)


def vmem():
    return pl.BlockSpec(memory_space=pltpu.VMEM)


def params():
    return pltpu.CompilerParams(vmem_limit_bytes=VMEM)


def cost(flops, moved, exps):
    return pl.CostEstimate(flops=flops, bytes_accessed=moved, transcendentals=exps)


def column(cum_t, head):
    return jnp.sum(jnp.where(iota(cum_t.shape, 1) == head, cum_t, 0.0), axis=1, keepdims=True)


def low_half(shape):
    return iota(shape, 1) < P_SIZE


def spread(cum_t, pair):
    return jnp.where(
        low_half((T, 2 * P_SIZE)), column(cum_t, 2 * pair), column(cum_t, 2 * pair + 1)
    )


def lanes_of(i):
    return slice(i * 2 * P_SIZE, (i + 1) * 2 * P_SIZE)


def put_states(out_ref, states, first, pairs):
    chunks = pairs * 2 * P_SIZE // OWN
    rows = states.astype(BF).reshape(chunks, OWN, N)
    out_ref[pl.ds(first * 2 * P_SIZE // OWN, chunks), :OWN, :] = rows


def put_note(out_ref, pieces):
    at = iota((16, N), 0)
    note = jnp.zeros((16, N), F32)
    for i, piece in enumerate(pieces):
        note = jnp.where(at == i, piece, note)
    for s in range(N_SEQ):
        out_ref[s, OWN:, :] = note.astype(BF)


def ends_kernel(x_ref, a_ref, b_ref, cum_ref, cum_t_ref, out_ref):
    step = pl.program_id(0)

    @pl.when(step == 0)
    def _():
        a = a_ref[...]
        upto = (iota((T, T), 0) <= iota((T, T), 1)).astype(F32)
        cum_ref[...] = jnp.dot(a, upto, precision=HIGH, preferred_element_type=F32)
        down = (iota((T, T), 1) <= iota((T, T), 0)).astype(F32)
        cum_t = lax.dot_general(
            down, a, (((1,), (1,)), ((), ())), precision=HIGH, preferred_element_type=F32
        )
        cum_t_ref[...] = cum_t
        total = jnp.concatenate([cum_t[T - 1 :, :], jnp.zeros((1, N - H), F32)], axis=1)
        hi = jnp.floor(total)
        mid = jnp.floor((total - hi) * 256.0) / 256.0
        put_note(out_ref, (hi, mid, total - hi - mid))

    cum_t = cum_t_ref[...]
    b = b_ref[...].astype(BF)
    found = []
    for i in range(WIDE):
        cum = spread(cum_t, step * WIDE + i)
        tail = jnp.exp(cum[T - 1 : T, :] - cum)
        found.append(tn((x_ref[:, lanes_of(i)] * tail).astype(BF), b))
    put_states(out_ref, jnp.concatenate(found, axis=0), step * WIDE, WIDE)


def local_ends(x, a, b):
    return pl.pallas_call(
        ends_kernel,
        grid=(PAIRS // WIDE,),
        in_specs=[wide(T, WIDE), whole((H, T)), whole((T, N))],
        out_specs=[whole((H, T)), whole((T, H)), whole((N_SEQ, ROWS, N))],
        out_shape=[
            jax.ShapeDtypeStruct((H, T), F32),
            jax.ShapeDtypeStruct((T, H), F32),
            jax.ShapeDtypeStruct((N_SEQ, ROWS, N), BF),
        ],
        compiler_params=params(),
        cost_estimate=cost(2 * T * D * N, 4 * T * D, T * D),
        name="ends",
    )(x, a, b)


def intra_kernel(x_ref, cum_ref, cum_t_ref, b_ref, c_ref, skip_ref, y_ref, scores):
    step = pl.program_id(0)

    @pl.when(step == 0)
    def _():
        keep = iota((T, T), 0) >= iota((T, T), 1)
        scores[...] = jnp.where(keep, nt(c_ref[...].astype(BF), b_ref[...].astype(BF)), 0.0)

    for i in range(STEP):
        x = x_ref[:, lanes_of(i)]
        xb = x.astype(BF)
        low = low_half(x.shape)
        head = 2 * (step * STEP + i)
        parts = []
        for k in range(2):
            diff = column(cum_t_ref[...], head + k) - cum_ref[pl.ds(head + k, 1), :]
            mixed = (jnp.exp(jnp.minimum(diff, 0.0)) * scores[...]).astype(BF)
            parts.append(nn(mixed, xb))
        skip = jnp.where(low, skip_ref[head], skip_ref[head + 1])
        y_ref[:, lanes_of(i)] = jnp.where(low, parts[0], parts[1]) + skip * x


def intra(x, cum, cum_t, b, c, skip):
    return pl.pallas_call(
        intra_kernel,
        grid=(PAIRS // STEP,),
        in_specs=[
            wide(T, STEP), whole((H, T)), whole((T, H)), whole((T, N)), whole((T, N)), smem(),
        ],
        out_specs=wide(T, STEP),
        out_shape=jax.ShapeDtypeStruct((T, D), F32),
        scratch_shapes=[pltpu.VMEM((T, T), F32)],
        compiler_params=params(),
        cost_estimate=cost(4 * T * T * D, 8 * T * D, H * T * T),
        name="intra",
    )(x, cum, cum_t, b, c, skip)


def inter_kernel(part_ref, cum_t_ref, c_ref, start_ref, y_ref):
    step = pl.program_id(0)
    cum_t = cum_t_ref[...]
    read = nt(c_ref[...].astype(BF), start_ref[...])
    for i in range(WIDE):
        grow = jnp.exp(spread(cum_t, step * WIDE + i))
        at = lanes_of(i)
        y_ref[:, at] = (part_ref[:, at] + grow * read[:, at]).astype(BF)


def inter(part, cum_t, c, start):
    return pl.pallas_call(
        inter_kernel,
        grid=(PAIRS // WIDE,),
        in_specs=[wide(T, WIDE), whole((T, H)), whole((T, N)), state_block(WIDE)],
        out_specs=wide(T, WIDE),
        out_shape=jax.ShapeDtypeStruct((T, D), BF),
        compiler_params=params(),
        cost_estimate=cost(2 * T * D * N, 6 * T * D, T * D),
        name="inter",
    )(part, cum_t, c, start)


def chain_kernel(reverse, mine_ref, parts_ref, totals_ref, out_ref):
    owner = (mine_ref[0] * OWN + iota((OWN, N), 0)) // P_SIZE == iota((OWN, N), 1)
    carry = jnp.zeros((OWN, N), F32)
    for s in range(N_SEQ - 1, -1, -1) if reverse else range(N_SEQ):
        out_ref[s] = carry.astype(BF)
        pieces = totals_ref[s, OWN:, :].astype(F32)
        total = pieces[0:1, :] + pieces[1:2, :] + pieces[2:3, :]
        decay = jnp.sum(jnp.where(owner, total, 0.0), axis=1, keepdims=True)
        carry = jnp.exp(decay) * carry + parts_ref[s, :OWN, :].astype(F32)


def chain(parts, totals, mine, reverse):
    return pl.pallas_call(
        functools.partial(chain_kernel, reverse),
        in_specs=[smem(), vmem(), vmem()],
        out_specs=vmem(),
        out_shape=jax.ShapeDtypeStruct((N_SEQ, OWN, N), BF),
        compiler_params=params(),
        cost_estimate=cost(4 * N_SEQ * OWN * N, 4 * N_SEQ * OWN * N, N_SEQ * OWN),
        name="chain",
    )(mine, parts, totals)


def swap(v, axis):
    return lax.all_to_all(v, axis, 0, 0, tiled=True)


def term_kernel(at_ref, yo_ref, yx_ref, go_ref, gx_ref, first_ref, second_ref):
    step = pl.program_id(0)
    half = go_ref.shape[1] // 2
    for i in range(2):
        cols = slice(i * half, (i + 1) * half)
        term = tn(yo_ref[...], go_ref[:, cols]) + tn(yx_ref[...], gx_ref[:, cols])
        term = term.astype(BF)
        for k in range(4):
            rel = (k + 4 - at_ref[1]) % 4
            rows = term[k * OWN : (k + 1) * OWN, :]
            if i == 0:
                first_ref[rel, step] = rows
            else:
                second_ref[0, rel] = rows


def terms(at, y_own, y_other, g_own, g_other):
    rows = pl.BlockSpec((T, 4 * OWN), lambda i, at: (0, (at[0] + i) % 4))
    half = g_own.shape[1] // 2
    return pl.pallas_call(
        term_kernel,
        grid_spec=pltpu.PrefetchScalarGridSpec(
            num_scalar_prefetch=1,
            grid=(4,),
            in_specs=[rows, rows, whole(g_own.shape), whole(g_own.shape)],
            out_specs=[
                whole((4, 4, OWN, half)),
                pl.BlockSpec((1, 4, OWN, half), lambda i, at: (i, 0, 0, 0)),
            ],
        ),
        out_shape=[jax.ShapeDtypeStruct((4, 4, OWN, half), BF)] * 2,
        compiler_params=params(),
        cost_estimate=cost(4 * T * D * D // 2, 3 * D * D // 2, 0),
        name="terms",
    )(at, y_own, y_other, g_own, g_other)


def entry_kernel(own_ref, other_ref, x_ref, cum_t_ref, c_ref, gy_ref, out_ref, sums):
    step = pl.program_id(0)
    cum_t = cum_t_ref[...]
    c = c_ref[...].astype(BF)
    found = []
    for i in range(WIDE):
        at = lanes_of(i)
        gy = own_ref[:, at] + other_ref[:, at].astype(F32)
        gy_ref[:, at] = gy.astype(BF)
        sums[pl.ds(step * WIDE + i, 1), :] = jnp.sum(gy * x_ref[:, at], axis=0, keepdims=True)
        grow = jnp.exp(spread(cum_t, step * WIDE + i))
        found.append(tn((gy * grow).astype(BF), c))
    put_states(out_ref, jnp.concatenate(found, axis=0), step * WIDE, WIDE)

    @pl.when(step == PAIRS // WIDE - 1)
    def _():
        total = sums[...]
        low = low_half(total.shape)
        head = 2 * iota(total.shape, 0)
        lane = iota(total.shape, 1)
        even = jnp.sum(jnp.where(low, total, 0.0), axis=1, keepdims=True)
        odd = jnp.sum(jnp.where(low, 0.0, total), axis=1, keepdims=True)
        each = jnp.where(lane == head, even, 0.0) + jnp.where(lane == head + 1, odd, 0.0)
        gd = jnp.sum(each, axis=0, keepdims=True)
        hi = gd.astype(BF).astype(F32)
        mid = (gd - hi).astype(BF).astype(F32)
        put_note(out_ref, (hi, mid, gd - hi - mid))


def entries(own, other, x, cum_t, c):
    return pl.pallas_call(
        entry_kernel,
        grid=(PAIRS // WIDE,),
        in_specs=[wide(T, WIDE), wide(T, WIDE), wide(T, WIDE), whole((T, H)), whole((T, N))],
        out_specs=[wide(T, WIDE), whole((N_SEQ, ROWS, N))],
        out_shape=[
            jax.ShapeDtypeStruct((T, D), BF),
            jax.ShapeDtypeStruct((N_SEQ, ROWS, N), BF),
        ],
        scratch_shapes=[pltpu.VMEM((PAIRS, 2 * P_SIZE), F32)],
        compiler_params=params(),
        cost_estimate=cost(2 * T * D * N, 12 * T * D, T * D),
        name="entries",
    )(own, other, x, cum_t, c)


def back_kernel(
    x_ref, gy_ref, cum_ref, cum_t_ref, b_ref, c_ref, skip_ref, start_ref, last_ref,
    gx_ref, ga_ref, gb_ref, gc_ref,
    scores, d_scores, rows, cols, tails, totals,
):
    step = pl.program_id(0)
    bb = b_ref[...].astype(BF)
    cb = c_ref[...].astype(BF)

    @pl.when(step == 0)
    def _():
        keep = iota((T, T), 1) >= iota((T, T), 0)
        scores[...] = jnp.where(keep, nt(bb, cb), 0.0)
        d_scores[...] = jnp.zeros_like(d_scores)
        cols[...] = jnp.zeros_like(cols)
        tails[...] = jnp.zeros_like(tails)
        gb_ref[...] = jnp.zeros_like(gb_ref)
        gc_ref[...] = jnp.zeros_like(gc_ref)

    lanes = iota((T, N), 1)
    low = low_half((T, 2 * P_SIZE))
    for i in range(STEP):
        pair = step * STEP + i
        at = lanes_of(i)
        x = x_ref[:, at]
        gyb = gy_ref[:, at]
        gy = gyb.astype(F32)
        parts = []
        sides = []
        for k in range(2):
            head = 2 * pair + k
            side = column(cum_t_ref[...], head)
            sides.append(side)
            diff = cum_ref[pl.ds(head, 1), :] - side
            weights = jnp.exp(jnp.minimum(diff, 0.0))
            mine = jnp.where(low if k == 0 else ~low, x, 0.0).astype(BF)
            d_mixed = weights * nt(mine, gyb)
            d_scores[...] += d_mixed
            parts.append(nn((weights * scores[...]).astype(BF), gyb))
            change = d_mixed * scores[...]
            rows[pl.ds(head, 1), :] = jnp.sum(change, axis=0, keepdims=True)
            down = jnp.sum(change, axis=1, keepdims=True)
            cols[...] -= jnp.where(lanes == head, down, 0.0)
        cum = jnp.where(low, sides[0], sides[1])
        grow = jnp.exp(cum)
        tail = jnp.exp(cum[T - 1 : T, :] - cum)
        states = slice(i * 2 * P_SIZE, (i + 1) * 2 * P_SIZE)
        start = start_ref[states, :]
        last = last_ref[states, :]
        pick = (lanes[:N] == 2 * pair + iota((N, N), 0) // P_SIZE).astype(BF)
        grown = gy * grow
        cols[...] += nn((grown * nt(cb, start)).astype(BF), pick)
        gc_ref[...] += nn(grown.astype(BF), start)
        faded = x * tail
        back = nt(bb, last)
        tails[...] += nn((faded * back).astype(BF), pick)
        gb_ref[...] += nn(faded.astype(BF), last)
        skip = jnp.where(low, skip_ref[2 * pair], skip_ref[2 * pair + 1])
        gx_ref[:, at] = jnp.where(low, parts[0], parts[1]) + tail * back + skip * gy
        both = start.astype(F32) * last.astype(F32)
        for k in range(2):
            part = both[k * P_SIZE : (k + 1) * P_SIZE, :]
            totals[pl.ds(2 * pair + k, 1), :] = jnp.sum(part, axis=0, keepdims=True)

    @pl.when(step == PAIRS // STEP - 1)
    def _():
        keep = iota((T, T), 1) >= iota((T, T), 0)
        ds = jnp.where(keep, d_scores[...], 0.0).astype(BF)
        gb_ref[...] += nn(ds, cb)
        gc_ref[...] += tn(ds, bb)
        after = (iota((T, T), 0) >= iota((T, T), 1)).astype(F32)
        before = (iota((T, T), 0) < iota((T, T), 1)).astype(F32)
        dims = (((0,), (0,)), ((), ()))
        ga = jnp.dot(rows[...], after, precision=HIGH, preferred_element_type=F32)
        up = lax.dot_general(cols[...], after, dims, precision=HIGH, preferred_element_type=F32)
        up += lax.dot_general(tails[...], before, dims, precision=HIGH, preferred_element_type=F32)
        whole_decay = jnp.exp(cum_ref[:, T - 1 : T])
        ga_ref[...] = ga + up[:H] + whole_decay * jnp.sum(totals[...], axis=1, keepdims=True)


def backward(x, gy, cum, cum_t, b, c, skip, start, last):
    return pl.pallas_call(
        back_kernel,
        grid=(PAIRS // STEP,),
        in_specs=[
            wide(T, STEP), wide(T, STEP), whole((H, T)), whole((T, H)), whole((T, N)),
            whole((T, N)), smem(), state_block(STEP), state_block(STEP),
        ],
        out_specs=[wide(T, STEP), whole((H, T)), whole((T, N)), whole((T, N))],
        out_shape=[
            jax.ShapeDtypeStruct((T, D), F32),
            jax.ShapeDtypeStruct((H, T), F32),
            jax.ShapeDtypeStruct((T, N), F32),
            jax.ShapeDtypeStruct((T, N), F32),
        ],
        scratch_shapes=[
            pltpu.VMEM((T, T), F32),
            pltpu.VMEM((T, T), F32),
            pltpu.VMEM((H, T), F32),
            pltpu.VMEM((T, N), F32),
            pltpu.VMEM((T, N), F32),
            pltpu.VMEM((H, N), F32),
        ],
        compiler_params=params(),
        cost_estimate=cost(8 * T * T * D, 14 * T * D, H * T * T),
        name="backward",
    )(x, gy, cum, cum_t, b, c, skip, start, last)


def fold_kernel(a0, a1, a2, b0, b1, b2, out_ref):
    sums = []
    for parts in ((a0, a1, a2), (b0, b1, b2)):
        total = parts[0][...].astype(F32) + parts[1][...].astype(F32) + parts[2][...].astype(F32)
        sums.append(total.astype(BF))
    for q in range(8 * TILES):
        r, c = divmod(q, 10)
        if r < 10:
            tile = sums[c // 5][16 * r : 16 * r + 16, 128 * (c % 5) : 128 * (c % 5) + 128]
        else:
            tile = jnp.zeros((16, 128), BF)
        out_ref[q // TILES, q % TILES] = tile


def fold(parts):
    return pl.pallas_call(
        fold_kernel,
        in_specs=[vmem()] * 6,
        out_specs=vmem(),
        out_shape=jax.ShapeDtypeStruct((8, TILES, 16, 128), BF),
        compiler_params=params(),
        cost_estimate=cost(4 * OWN * D // 2, 8 * OWN * D // 2, 0),
        name="fold",
    )(*parts)


def zsum_kernel(parts_ref, out_ref):
    total = parts_ref[0].astype(F32)
    for z in range(1, 8):
        total += parts_ref[z].astype(F32)
    for s in range(N_SEQ):
        out_ref[s] = total.astype(BF)


def zsum(parts):
    return pl.pallas_call(
        zsum_kernel,
        in_specs=[vmem()],
        out_specs=vmem(),
        out_shape=jax.ShapeDtypeStruct((N_SEQ, TILES, 16, 128), BF),
        compiler_params=params(),
        cost_estimate=cost(8 * OWN * 160, 6 * OWN * D, 0),
        name="zsum",
    )(parts)


def tile_of(ref, r, c, core):
    z, i = divmod(10 * r + c, TILES)
    return ref[2 * z + core, i].astype(F32)


def row_groups(row0, ids_ref):
    heads = (row0 + iota((OWN, N), 0)) // P_SIZE == iota((OWN, N), 1)
    return jnp.sum(jnp.where(heads, ids_ref[...], 0.0), axis=1, keepdims=True)


def squares_kernel(row0_ref, ids_ref, tiles_ref, got_ref, note_ref):
    found = []
    for r in range(10):
        total = jnp.zeros((16, 128), F32)
        for core in range(2):
            for c in range(10):
                tile = tile_of(tiles_ref, r, c, core)
                total += tile * tile
        found.append(jnp.sum(total, axis=1, keepdims=True))
    squares = jnp.concatenate(found, axis=0)
    place = iota((OWN, N), 1) - H == row_groups(row0_ref[0], ids_ref).astype(jnp.int32)
    note = jnp.sum(jnp.where(place, squares, 0.0), axis=0, keepdims=True)
    for s in range(N_SEQ):
        pieces = got_ref[s, OWN:, :].astype(F32)
        note += pieces[0:1, :] + pieces[1:2, :] + pieces[2:3, :]
    note_ref[...] = note


def squares(row0, ids, tiles, got):
    return pl.pallas_call(
        squares_kernel,
        in_specs=[smem(), vmem(), vmem(), vmem()],
        out_specs=vmem(),
        out_shape=jax.ShapeDtypeStruct((1, N), F32),
        compiler_params=params(),
        cost_estimate=cost(2 * OWN * D, 2 * OWN * D, 0),
        name="squares",
    )(row0, ids, tiles, got)


def clip_kernel(tokens_all, row0_ref, ids_ref, tiles_ref, note_ref, w_ref, d_ref):
    ids = ids_ref[...]
    lane = iota((1, N), 1)
    note = note_ref[...]
    grad_d = jnp.where(lane < H, note, 0.0)
    groups = row_groups(row0_ref[0], ids_ref)
    w_factor = jnp.zeros((OWN, 1), F32)
    d_factor = jnp.zeros((1, N), F32)
    for g in range(GROUPS):
        here = (ids == float(g)) & (lane < H)
        count = jnp.sum(jnp.where(here, 1.0, 0.0), axis=1, keepdims=True)
        sumsq = jnp.sum(jnp.where(lane == H + g, note, 0.0), axis=1, keepdims=True)
        sumsq += jnp.sum(jnp.where(here, grad_d * grad_d, 0.0), axis=1, keepdims=True)
        bound = 7.0 * jnp.sqrt(count * (P_SIZE * D + 1.0) * tokens_all)
        factor = jnp.minimum(1.0, bound / jnp.sqrt(sumsq + 1e-06))
        w_factor += jnp.where(groups == float(g), factor, 0.0)
        d_factor += jnp.where(here, factor, 0.0)
    d_ref[...] = grad_d * d_factor
    for r in range(10):
        scale = w_factor[16 * r : 16 * r + 16, :]
        for core in range(2):
            for c in range(10):
                col = core * (D // 2) + 128 * c
                w_ref[16 * r : 16 * r + 16, col : col + 128] = (
                    tile_of(tiles_ref, r, c, core) * scale
                )


def clip(tokens_all, row0, ids, tiles, note):
    return pl.pallas_call(
        functools.partial(clip_kernel, tokens_all),
        in_specs=[smem(), vmem(), vmem(), vmem()],
        out_specs=[vmem(), vmem()],
        out_shape=[jax.ShapeDtypeStruct((OWN, D), F32), jax.ShapeDtypeStruct((1, N), F32)],
        compiler_params=params(),
        cost_estimate=cost(2 * OWN * D, 6 * OWN * D, 0),
        name="clip",
    )(row0, ids, tiles, note)


def shifted(v, axis, d):
    return lax.ppermute(v, axis, [(i, (i + d) % 4) for i in range(4)])


def plus(a, b):
    return (a.astype(F32) + b.astype(F32)).astype(BF)


def relay(t, axis):
    m = t.shape[1] // 2
    ra = shifted(t[2, :m], axis, 1)
    rb = shifted(t[2, m:], axis, -1)
    up = jnp.concatenate([plus(t[1, :m], ra), t[1, m:]], axis=0)
    down = jnp.concatenate([t[3, :m], plus(t[3, m:], rb)], axis=0)
    return t[0], shifted(up, axis, 1), shifted(down, axis, -1)


def three_sum(parts):
    return (parts[0].astype(F32) + parts[1].astype(F32) + parts[2].astype(F32)).astype(BF)


def other_core(v):
    return lax.ppermute(v, "core", [(0, 1), (1, 0)])


def sum_over(v, axis):
    for bit in (1, 2):
        v = v + lax.ppermute(v, axis, [(i, i ^ bit) for i in range(4)])
    return v


def per_device(x_in, a_log, b_in, c_in, g_out, w_out, d_skip, group_ids):
    x, a, b, c, g = (x_in[0], a_log[0], b_in[0], c_in[0], g_out[0])
    core = lax.axis_index("core")
    half = D // 2
    at = jnp.stack([lax.axis_index("y"), lax.axis_index("x")]).astype(jnp.int32)
    mine = (2 * lax.axis_index("z") + core).reshape(1).astype(jnp.int32)
    row0 = ((4 * at[0] + at[1]) * OWN).reshape(1)
    ids = jnp.pad(group_ids.astype(F32), (0, N - H), constant_values=-1.0)[None]
    tokens_all = float(T * N_SEQ * 16)

    w_mine = lax.dynamic_slice_in_dim(w_out, core * half, half, axis=1)
    w_half = lax.all_gather(w_mine, ("y", "x"), axis=0, tiled=True)
    g_mine = lax.dynamic_slice_in_dim(g, core * half, half, axis=1)
    g_other = other_core(lax.dynamic_slice_in_dim(g, (1 - core) * half, half, axis=1))

    cum, cum_t, sent = local_ends(x, a, b)
    got = swap(sent, SEQ)
    y_part = intra(x, cum, cum_t, b, c, d_skip)
    start = swap(chain(got, got, mine, False), SEQ).reshape(H * P_SIZE, N)
    y_own = inter(y_part, cum_t, c, start)
    y_other = other_core(y_own)
    first, second = terms(at, y_own, y_other, g_mine, g_other)
    w_half, first, second = lax.optimization_barrier((w_half, first, second))

    first = relay(first, "x")
    second = relay(second, "y")
    dims = (((1,), (1,)), ((), ()))
    gy_other = lax.dot_general(g_other, w_half, dims, preferred_element_type=F32).astype(BF)
    gy_other = other_core(gy_other)
    gy_own = lax.dot_general(g_mine, w_half, dims, preferred_element_type=F32)
    gy, sent_back = entries(gy_own, gy_other, x, cum_t, c)
    got_back = swap(sent_back, SEQ)

    first = relay(three_sum(first), "y")
    second = relay(three_sum(second), "x")
    last = swap(chain(got_back, got, mine, True), SEQ).reshape(H * P_SIZE, N)
    tiles = swap(fold(first + second), "z")
    tiles = swap(zsum(tiles), SEQ)

    gx, ga, gb, gc = backward(x, gy, cum, cum_t, b, c, d_skip, start, last)

    note = squares(row0, ids, tiles, got_back)
    note = sum_over(sum_over(note, "x"), "y")
    clipped_w, clipped_d = clip(tokens_all, row0, ids, tiles, note)
    return (gx[None], ga[None], gb[None], gc[None], clipped_w, clipped_d[0, :H])


def solution(mesh):
    fine = Mesh(mesh.devices.reshape(4, 4, 8, 2), ("y", "x", "z", "core"))
    rows = ("y", "x")
    tokens = P(rows, SEQ, None)
    return jax.shard_map(
        per_device,
        mesh=fine,
        in_specs=(
            tokens, P(rows, None, SEQ), tokens, tokens, tokens, P(rows, None), P(), P(),
        ),
        out_specs=(tokens, P(rows, None, SEQ), tokens, tokens, P(rows, None), P()),
        check_vma=False,
    )
```

```python
import functools

import jax
import jax.numpy as jnp
from jax import lax
from jax.experimental import pallas as pl
from jax.experimental.pallas import tpu as pltpu
from jax.sharding import Mesh
from jax.sharding import PartitionSpec as P

D = 2560
H = 40
P_SIZE = 64
N = 128
T = 256
GROUPS = 4
PAIRS = H // 2
SEQ = ("z", "core")
N_SEQ = 16
OWN = H * P_SIZE // N_SEQ
HIGH = lax.Precision.HIGHEST
BF = jnp.bfloat16
F32 = jnp.float32
VMEM = 56 * 1024 * 1024
WIDE = 5
STEP = 2
ROWS = OWN + 16
TILES = 13


def nn(a, b):
    return lax.dot_general(a, b, (((1,), (0,)), ((), ())), preferred_element_type=F32)


def nt(a, b):
    return lax.dot_general(a, b, (((1,), (1,)), ((), ())), preferred_element_type=F32)


def tn(a, b):
    return lax.dot_general(a, b, (((0,), (0,)), ((), ())), preferred_element_type=F32)


def iota(shape, dim):
    return lax.broadcasted_iota(jnp.int32, shape, dim)


def whole(shape):
    return pl.BlockSpec(shape, lambda *_: (0,) * len(shape))


def wide(rows, pairs):
    return pl.BlockSpec((rows, pairs * 2 * P_SIZE), lambda p: (0, p))


def state_block(pairs):
    return pl.BlockSpec((pairs * 2 * P_SIZE, N), lambda p: (p, 0))


def smem():
    return pl.BlockSpec(memory_space=pltpu.SMEM)


def vmem():
    return pl.BlockSpec(memory_space=pltpu.VMEM)


def params():
    return pltpu.CompilerParams(vmem_limit_bytes=VMEM)


def cost(flops, moved, exps):
    return pl.CostEstimate(flops=flops, bytes_accessed=moved, transcendentals=exps)


def column(cum_t, head):
    return jnp.sum(jnp.where(iota(cum_t.shape, 1) == head, cum_t, 0.0), axis=1, keepdims=True)


def low_half(shape):
    return iota(shape, 1) < P_SIZE


def spread(cum_t, pair):
    return jnp.where(
        low_half((T, 2 * P_SIZE)), column(cum_t, 2 * pair), column(cum_t, 2 * pair + 1)
    )


def lanes_of(i):
    return slice(i * 2 * P_SIZE, (i + 1) * 2 * P_SIZE)


def put_states(out_ref, states, first, pairs):
    chunks = pairs * 2 * P_SIZE // OWN
    rows = states.astype(BF).reshape(chunks, OWN, N)
    out_ref[pl.ds(first * 2 * P_SIZE // OWN, chunks), :OWN, :] = rows


def put_note(out_ref, pieces):
    at = iota((16, N), 0)
    note = jnp.zeros((16, N), F32)
    for i, piece in enumerate(pieces):
        note = jnp.where(at == i, piece, note)
    for s in range(N_SEQ):
        out_ref[s, OWN:, :] = note.astype(BF)


def ends_kernel(x_ref, a_ref, b_ref, cum_ref, cum_t_ref, out_ref):
    step = pl.program_id(0)

    @pl.when(step == 0)
    def _():
        a = a_ref[...]
        upto = (iota((T, T), 0) <= iota((T, T), 1)).astype(F32)
        cum_ref[...] = jnp.dot(a, upto, precision=HIGH, preferred_element_type=F32)
        down = (iota((T, T), 1) <= iota((T, T), 0)).astype(F32)
        cum_t = lax.dot_general(
            down, a, (((1,), (1,)), ((), ())), precision=HIGH, preferred_element_type=F32
        )
        cum_t_ref[...] = cum_t
        total = jnp.concatenate([cum_t[T - 1 :, :], jnp.zeros((1, N - H), F32)], axis=1)
        hi = jnp.floor(total)
        mid = jnp.floor((total - hi) * 256.0) / 256.0
        put_note(out_ref, (hi, mid, total - hi - mid))

    cum_t = cum_t_ref[...]
    b = b_ref[...].astype(BF)
    found = []
    for i in range(WIDE):
        cum = spread(cum_t, step * WIDE + i)
        tail = jnp.exp(cum[T - 1 : T, :] - cum)
        found.append(tn((x_ref[:, lanes_of(i)] * tail).astype(BF), b))
    put_states(out_ref, jnp.concatenate(found, axis=0), step * WIDE, WIDE)


def local_ends(x, a, b):
    return pl.pallas_call(
        ends_kernel,
        grid=(PAIRS // WIDE,),
        in_specs=[wide(T, WIDE), whole((H, T)), whole((T, N))],
        out_specs=[whole((H, T)), whole((T, H)), whole((N_SEQ, ROWS, N))],
        out_shape=[
            jax.ShapeDtypeStruct((H, T), F32),
            jax.ShapeDtypeStruct((T, H), F32),
            jax.ShapeDtypeStruct((N_SEQ, ROWS, N), BF),
        ],
        compiler_params=params(),
        cost_estimate=cost(2 * T * D * N, 4 * T * D, T * D),
        name="ends",
    )(x, a, b)


def intra_kernel(x_ref, cum_ref, cum_t_ref, b_ref, c_ref, skip_ref, y_ref, scores):
    step = pl.program_id(0)

    @pl.when(step == 0)
    def _():
        keep = iota((T, T), 0) >= iota((T, T), 1)
        scores[...] = jnp.where(keep, nt(c_ref[...].astype(BF), b_ref[...].astype(BF)), 0.0)

    for i in range(STEP):
        x = x_ref[:, lanes_of(i)]
        xb = x.astype(BF)
        low = low_half(x.shape)
        head = 2 * (step * STEP + i)
        parts = []
        for k in range(2):
            diff = column(cum_t_ref[...], head + k) - cum_ref[pl.ds(head + k, 1), :]
            mixed = (jnp.exp(jnp.minimum(diff, 0.0)) * scores[...]).astype(BF)
            parts.append(nn(mixed, xb))
        skip = jnp.where(low, skip_ref[head], skip_ref[head + 1])
        y_ref[:, lanes_of(i)] = jnp.where(low, parts[0], parts[1]) + skip * x


def intra(x, cum, cum_t, b, c, skip):
    return pl.pallas_call(
        intra_kernel,
        grid=(PAIRS // STEP,),
        in_specs=[
            wide(T, STEP), whole((H, T)), whole((T, H)), whole((T, N)), whole((T, N)), smem(),
        ],
        out_specs=wide(T, STEP),
        out_shape=jax.ShapeDtypeStruct((T, D), F32),
        scratch_shapes=[pltpu.VMEM((T, T), F32)],
        compiler_params=params(),
        cost_estimate=cost(4 * T * T * D, 8 * T * D, H * T * T),
        name="intra",
    )(x, cum, cum_t, b, c, skip)


def inter_kernel(part_ref, cum_t_ref, c_ref, start_ref, y_ref):
    step = pl.program_id(0)
    cum_t = cum_t_ref[...]
    read = nt(c_ref[...].astype(BF), start_ref[...])
    for i in range(WIDE):
        grow = jnp.exp(spread(cum_t, step * WIDE + i))
        at = lanes_of(i)
        y_ref[:, at] = (part_ref[:, at] + grow * read[:, at]).astype(BF)


def inter(part, cum_t, c, start):
    return pl.pallas_call(
        inter_kernel,
        grid=(PAIRS // WIDE,),
        in_specs=[wide(T, WIDE), whole((T, H)), whole((T, N)), state_block(WIDE)],
        out_specs=wide(T, WIDE),
        out_shape=jax.ShapeDtypeStruct((T, D), BF),
        compiler_params=params(),
        cost_estimate=cost(2 * T * D * N, 6 * T * D, T * D),
        name="inter",
    )(part, cum_t, c, start)


def chain_kernel(reverse, mine_ref, parts_ref, totals_ref, out_ref):
    owner = (mine_ref[0] * OWN + iota((OWN, N), 0)) // P_SIZE == iota((OWN, N), 1)
    carry = jnp.zeros((OWN, N), F32)
    for s in range(N_SEQ - 1, -1, -1) if reverse else range(N_SEQ):
        out_ref[s] = carry.astype(BF)
        pieces = totals_ref[s, OWN:, :].astype(F32)
        total = pieces[0:1, :] + pieces[1:2, :] + pieces[2:3, :]
        decay = jnp.sum(jnp.where(owner, total, 0.0), axis=1, keepdims=True)
        carry = jnp.exp(decay) * carry + parts_ref[s, :OWN, :].astype(F32)


def chain(parts, totals, mine, reverse):
    return pl.pallas_call(
        functools.partial(chain_kernel, reverse),
        in_specs=[smem(), vmem(), vmem()],
        out_specs=vmem(),
        out_shape=jax.ShapeDtypeStruct((N_SEQ, OWN, N), BF),
        compiler_params=params(),
        cost_estimate=cost(4 * N_SEQ * OWN * N, 4 * N_SEQ * OWN * N, N_SEQ * OWN),
        name="chain",
    )(mine, parts, totals)


def swap(v, axis):
    return lax.all_to_all(v, axis, 0, 0, tiled=True)


def term_kernel(at_ref, yo_ref, yx_ref, go_ref, gx_ref, first_ref, second_ref):
    step = pl.program_id(0)
    half = go_ref.shape[1] // 2
    for i in range(2):
        cols = slice(i * half, (i + 1) * half)
        term = tn(yo_ref[...], go_ref[:, cols]) + tn(yx_ref[...], gx_ref[:, cols])
        term = term.astype(BF)
        for k in range(4):
            rel = (k + 4 - at_ref[1]) % 4
            rows = term[k * OWN : (k + 1) * OWN, :]
            if i == 0:
                first_ref[rel, 0] = rows
            else:
                second_ref[0, rel] = rows


def terms(at, y_own, y_other, g_own, g_other):
    rows = pl.BlockSpec((T, 4 * OWN), lambda i, at: (0, (at[0] + i) % 4))
    half = g_own.shape[1] // 2
    return pl.pallas_call(
        term_kernel,
        grid_spec=pltpu.PrefetchScalarGridSpec(
            num_scalar_prefetch=1,
            grid=(4,),
            in_specs=[rows, rows, whole(g_own.shape), whole(g_own.shape)],
            out_specs=[
                pl.BlockSpec((4, 1, OWN, half), lambda i, at: (0, i, 0, 0)),
                pl.BlockSpec((1, 4, OWN, half), lambda i, at: (i, 0, 0, 0)),
            ],
        ),
        out_shape=[jax.ShapeDtypeStruct((4, 4, OWN, half), BF)] * 2,
        compiler_params=params(),
        cost_estimate=cost(4 * T * D * D // 2, 3 * D * D // 2, 0),
        name="terms",
    )(at, y_own, y_other, g_own, g_other)


def entry_kernel(own_ref, other_ref, x_ref, cum_t_ref, c_ref, gy_ref, out_ref, sums):
    step = pl.program_id(0)
    cum_t = cum_t_ref[...]
    c = c_ref[...].astype(BF)
    found = []
    for i in range(WIDE):
        at = lanes_of(i)
        gy = own_ref[:, at] + other_ref[:, at].astype(F32)
        gy_ref[:, at] = gy.astype(BF)
        sums[pl.ds(step * WIDE + i, 1), :] = jnp.sum(gy * x_ref[:, at], axis=0, keepdims=True)
        grow = jnp.exp(spread(cum_t, step * WIDE + i))
        found.append(tn((gy * grow).astype(BF), c))
    put_states(out_ref, jnp.concatenate(found, axis=0), step * WIDE, WIDE)

    @pl.when(step == PAIRS // WIDE - 1)
    def _():
        total = sums[...]
        low = low_half(total.shape)
        head = 2 * iota(total.shape, 0)
        lane = iota(total.shape, 1)
        even = jnp.sum(jnp.where(low, total, 0.0), axis=1, keepdims=True)
        odd = jnp.sum(jnp.where(low, 0.0, total), axis=1, keepdims=True)
        each = jnp.where(lane == head, even, 0.0) + jnp.where(lane == head + 1, odd, 0.0)
        gd = jnp.sum(each, axis=0, keepdims=True)
        hi = gd.astype(BF).astype(F32)
        mid = (gd - hi).astype(BF).astype(F32)
        put_note(out_ref, (hi, mid, gd - hi - mid))


def entries(own, other, x, cum_t, c):
    return pl.pallas_call(
        entry_kernel,
        grid=(PAIRS // WIDE,),
        in_specs=[wide(T, WIDE), wide(T, WIDE), wide(T, WIDE), whole((T, H)), whole((T, N))],
        out_specs=[wide(T, WIDE), whole((N_SEQ, ROWS, N))],
        out_shape=[
            jax.ShapeDtypeStruct((T, D), BF),
            jax.ShapeDtypeStruct((N_SEQ, ROWS, N), BF),
        ],
        scratch_shapes=[pltpu.VMEM((PAIRS, 2 * P_SIZE), F32)],
        compiler_params=params(),
        cost_estimate=cost(2 * T * D * N, 12 * T * D, T * D),
        name="entries",
    )(own, other, x, cum_t, c)


def back_kernel(
    x_ref, gy_ref, cum_ref, cum_t_ref, b_ref, c_ref, skip_ref, start_ref, last_ref,
    gx_ref, ga_ref, gb_ref, gc_ref,
    scores, d_scores, rows, cols, tails, totals,
):
    step = pl.program_id(0)
    bb = b_ref[...].astype(BF)
    cb = c_ref[...].astype(BF)

    @pl.when(step == 0)
    def _():
        keep = iota((T, T), 1) >= iota((T, T), 0)
        scores[...] = jnp.where(keep, nt(bb, cb), 0.0)
        d_scores[...] = jnp.zeros_like(d_scores)
        cols[...] = jnp.zeros_like(cols)
        tails[...] = jnp.zeros_like(tails)
        gb_ref[...] = jnp.zeros_like(gb_ref)
        gc_ref[...] = jnp.zeros_like(gc_ref)

    lanes = iota((T, N), 1)
    low = low_half((T, 2 * P_SIZE))
    for i in range(STEP):
        pair = step * STEP + i
        at = lanes_of(i)
        x = x_ref[:, at]
        gyb = gy_ref[:, at]
        gy = gyb.astype(F32)
        parts = []
        sides = []
        for k in range(2):
            head = 2 * pair + k
            side = column(cum_t_ref[...], head)
            sides.append(side)
            diff = cum_ref[pl.ds(head, 1), :] - side
            weights = jnp.exp(jnp.minimum(diff, 0.0))
            mine = jnp.where(low if k == 0 else ~low, x, 0.0).astype(BF)
            d_mixed = weights * nt(mine, gyb)
            d_scores[...] += d_mixed
            parts.append(nn((weights * scores[...]).astype(BF), gyb))
            change = d_mixed * scores[...]
            rows[pl.ds(head, 1), :] = jnp.sum(change, axis=0, keepdims=True)
            down = jnp.sum(change, axis=1, keepdims=True)
            cols[...] -= jnp.where(lanes == head, down, 0.0)
        cum = jnp.where(low, sides[0], sides[1])
        grow = jnp.exp(cum)
        tail = jnp.exp(cum[T - 1 : T, :] - cum)
        states = slice(i * 2 * P_SIZE, (i + 1) * 2 * P_SIZE)
        start = start_ref[states, :]
        last = last_ref[states, :]
        pick = (lanes[:N] == 2 * pair + iota((N, N), 0) // P_SIZE).astype(BF)
        grown = gy * grow
        cols[...] += nn((grown * nt(cb, start)).astype(BF), pick)
        gc_ref[...] += nn(grown.astype(BF), start)
        faded = x * tail
        back = nt(bb, last)
        tails[...] += nn((faded * back).astype(BF), pick)
        gb_ref[...] += nn(faded.astype(BF), last)
        skip = jnp.where(low, skip_ref[2 * pair], skip_ref[2 * pair + 1])
        gx_ref[:, at] = jnp.where(low, parts[0], parts[1]) + tail * back + skip * gy
        both = start.astype(F32) * last.astype(F32)
        for k in range(2):
            part = both[k * P_SIZE : (k + 1) * P_SIZE, :]
            totals[pl.ds(2 * pair + k, 1), :] = jnp.sum(part, axis=0, keepdims=True)

    @pl.when(step == PAIRS // STEP - 1)
    def _():
        keep = iota((T, T), 1) >= iota((T, T), 0)
        ds = jnp.where(keep, d_scores[...], 0.0).astype(BF)
        gb_ref[...] += nn(ds, cb)
        gc_ref[...] += tn(ds, bb)
        after = (iota((T, T), 0) >= iota((T, T), 1)).astype(F32)
        before = (iota((T, T), 0) < iota((T, T), 1)).astype(F32)
        dims = (((0,), (0,)), ((), ()))
        ga = jnp.dot(rows[...], after, precision=HIGH, preferred_element_type=F32)
        up = lax.dot_general(cols[...], after, dims, precision=HIGH, preferred_element_type=F32)
        up += lax.dot_general(tails[...], before, dims, precision=HIGH, preferred_element_type=F32)
        whole_decay = jnp.exp(cum_ref[:, T - 1 : T])
        ga_ref[...] = ga + up[:H] + whole_decay * jnp.sum(totals[...], axis=1, keepdims=True)


def backward(x, gy, cum, cum_t, b, c, skip, start, last):
    return pl.pallas_call(
        back_kernel,
        grid=(PAIRS // STEP,),
        in_specs=[
            wide(T, STEP), wide(T, STEP), whole((H, T)), whole((T, H)), whole((T, N)),
            whole((T, N)), smem(), state_block(STEP), state_block(STEP),
        ],
        out_specs=[wide(T, STEP), whole((H, T)), whole((T, N)), whole((T, N))],
        out_shape=[
            jax.ShapeDtypeStruct((T, D), F32),
            jax.ShapeDtypeStruct((H, T), F32),
            jax.ShapeDtypeStruct((T, N), F32),
            jax.ShapeDtypeStruct((T, N), F32),
        ],
        scratch_shapes=[
            pltpu.VMEM((T, T), F32),
            pltpu.VMEM((T, T), F32),
            pltpu.VMEM((H, T), F32),
            pltpu.VMEM((T, N), F32),
            pltpu.VMEM((T, N), F32),
            pltpu.VMEM((H, N), F32),
        ],
        compiler_params=params(),
        cost_estimate=cost(8 * T * T * D, 14 * T * D, H * T * T),
        name="backward",
    )(x, gy, cum, cum_t, b, c, skip, start, last)


def fold_kernel(a0, a1, a2, a3, b0, b1, b2, b3, out_ref):
    sums = []
    for parts in ((a0, a1, a2, a3), (b0, b1, b2, b3)):
        total = parts[0][...].astype(F32)
        for part in parts[1:]:
            total += part[...].astype(F32)
        sums.append(total.astype(BF))
    for q in range(8 * TILES):
        r, c = divmod(q, 10)
        if r < 10:
            tile = sums[c // 5][16 * r : 16 * r + 16, 128 * (c % 5) : 128 * (c % 5) + 128]
        else:
            tile = jnp.zeros((16, 128), BF)
        out_ref[q // TILES, q % TILES] = tile


def fold(parts):
    return pl.pallas_call(
        fold_kernel,
        in_specs=[vmem()] * 8,
        out_specs=vmem(),
        out_shape=jax.ShapeDtypeStruct((8, TILES, 16, 128), BF),
        compiler_params=params(),
        cost_estimate=cost(4 * OWN * D // 2, 8 * OWN * D // 2, 0),
        name="fold",
    )(*parts)


def groups_of(row0, count, ids_ref):
    heads = (row0 + iota((count, N), 0)) // P_SIZE == iota((count, N), 1)
    return jnp.sum(jnp.where(heads, ids_ref[...], 0.0), axis=1, keepdims=True)


def zsum_kernel(row0_ref, z_ref, ids_ref, parts_ref, got_ref, out_ref, note_ref):
    total = parts_ref[0].astype(F32)
    for z in range(1, 8):
        total += parts_ref[z].astype(F32)
    for s in range(N_SEQ):
        out_ref[s] = total.astype(BF)
    found = jnp.zeros((16, N), F32)
    for i in range(TILES):
        row = row0_ref[0] + 16 * ((z_ref[0] * TILES + i) // 10)
        place = iota((16, N), 1) - H == groups_of(row, 16, ids_ref).astype(jnp.int32)
        tile = total[i]
        found += jnp.where(place, jnp.sum(tile * tile, axis=1, keepdims=True), 0.0)
    d_sum = jnp.zeros((1, N), F32)
    for s in range(N_SEQ):
        pieces = got_ref[s, OWN:, :].astype(F32)
        d_sum += pieces[0:1, :] + pieces[1:2, :] + pieces[2:3, :]
    note_ref[...] = jnp.sum(found, axis=0, keepdims=True) + d_sum / N_SEQ


def zsum(row0, z, ids, parts, got):
    return pl.pallas_call(
        zsum_kernel,
        in_specs=[smem(), smem(), vmem(), vmem(), vmem()],
        out_specs=[vmem(), vmem()],
        out_shape=[
            jax.ShapeDtypeStruct((N_SEQ, TILES, 16, 128), BF),
            jax.ShapeDtypeStruct((1, N), F32),
        ],
        compiler_params=params(),
        cost_estimate=cost(8 * OWN * 160, 6 * OWN * D, 0),
        name="zsum",
    )(row0, z, ids, parts, got)


def tile_of(ref, r, c, core):
    z, i = divmod(10 * r + c, TILES)
    return ref[2 * z + core, i].astype(F32)


def clip_kernel(tokens_all, row0_ref, ids_ref, tiles_ref, note_ref, w_ref, d_ref):
    ids = ids_ref[...]
    lane = iota((1, N), 1)
    note = note_ref[...]
    grad_d = jnp.where(lane < H, note, 0.0)
    groups = groups_of(row0_ref[0], OWN, ids_ref)
    w_factor = jnp.zeros((OWN, 1), F32)
    d_factor = jnp.zeros((1, N), F32)
    for g in range(GROUPS):
        here = (ids == float(g)) & (lane < H)
        count = jnp.sum(jnp.where(here, 1.0, 0.0), axis=1, keepdims=True)
        sumsq = jnp.sum(jnp.where(lane == H + g, note, 0.0), axis=1, keepdims=True)
        sumsq += jnp.sum(jnp.where(here, grad_d * grad_d, 0.0), axis=1, keepdims=True)
        bound = 7.0 * jnp.sqrt(count * (P_SIZE * D + 1.0) * tokens_all)
        factor = jnp.minimum(1.0, bound / jnp.sqrt(sumsq + 1e-06))
        w_factor += jnp.where(groups == float(g), factor, 0.0)
        d_factor += jnp.where(here, factor, 0.0)
    d_ref[...] = grad_d * d_factor
    for r in range(10):
        scale = w_factor[16 * r : 16 * r + 16, :]
        for core in range(2):
            for c in range(10):
                col = core * (D // 2) + 128 * c
                w_ref[16 * r : 16 * r + 16, col : col + 128] = (
                    tile_of(tiles_ref, r, c, core) * scale
                )


def clip(tokens_all, row0, ids, tiles, note):
    return pl.pallas_call(
        functools.partial(clip_kernel, tokens_all),
        in_specs=[smem(), vmem(), vmem(), vmem()],
        out_specs=[vmem(), vmem()],
        out_shape=[jax.ShapeDtypeStruct((OWN, D), F32), jax.ShapeDtypeStruct((1, N), F32)],
        compiler_params=params(),
        cost_estimate=cost(2 * OWN * D, 6 * OWN * D, 0),
        name="clip",
    )(row0, ids, tiles, note)


def shifted(v, axis, d):
    return lax.ppermute(v, axis, [(i, (i + d) % 4) for i in range(4)])


def plus(a, b):
    return (a.astype(F32) + b.astype(F32)).astype(BF)


def far(t, axis):
    m = t.shape[1] // 2
    return shifted(t[2, :m], axis, 1), shifted(t[2, m:], axis, -1)


def near(t, ra, rb, axis):
    m = t.shape[1] // 2
    up = jnp.concatenate([plus(t[1, :m], ra), t[1, m:]], axis=0)
    down = jnp.concatenate([t[3, :m], plus(t[3, m:], rb)], axis=0)
    got = (t[0], shifted(up, axis, 1), shifted(down, axis, -1))
    return (got[0].astype(F32) + got[1].astype(F32) + got[2].astype(F32)).astype(BF)


def direct(t, axis):
    return (t[0],) + tuple(shifted(t[d], axis, d) for d in (1, 3, 2))


def other_core(v):
    return lax.ppermute(v, "core", [(0, 1), (1, 0)])


def sum_over(v, axis):
    n = lax.axis_size(axis)
    bit = 1
    while bit < n:
        v = v + lax.ppermute(v, axis, [(i, i ^ bit) for i in range(n)])
        bit *= 2
    return v


def tie(*values):
    return lax.optimization_barrier(values)


def per_device(x_in, a_log, b_in, c_in, g_out, w_out, d_skip, group_ids):
    x, a, b, c, g = (x_in[0], a_log[0], b_in[0], c_in[0], g_out[0])
    core = lax.axis_index("core")
    half = D // 2
    at = jnp.stack([lax.axis_index("y"), lax.axis_index("x")]).astype(jnp.int32)
    mine = (2 * lax.axis_index("z") + core).reshape(1).astype(jnp.int32)
    at_z = lax.axis_index("z").reshape(1).astype(jnp.int32)
    row0 = ((4 * at[0] + at[1]) * OWN).reshape(1)
    ids = jnp.pad(group_ids.astype(F32), (0, N - H), constant_values=-1.0)[None]
    tokens_all = float(T * N_SEQ * 16)

    w_mine = lax.dynamic_slice_in_dim(w_out, core * half, half, axis=1)
    w_half = lax.all_gather(w_mine, ("y", "x"), axis=0, tiled=True)
    g_mine = lax.dynamic_slice_in_dim(g, core * half, half, axis=1)
    g_other = other_core(lax.dynamic_slice_in_dim(g, (1 - core) * half, half, axis=1))

    cum, cum_t, sent = local_ends(x, a, b)
    got = swap(sent, SEQ)
    y_part = intra(x, cum, cum_t, b, c, d_skip)
    start = swap(chain(got, got, mine, False), SEQ).reshape(H * P_SIZE, N)
    y_own = inter(y_part, cum_t, c, start)
    y_other = other_core(y_own)

    w_half, _ = tie(w_half, y_own)
    dims = (((1,), (1,)), ((), ()))
    gy_other = lax.dot_general(g_other, w_half, dims, preferred_element_type=F32).astype(BF)
    gy_own = lax.dot_general(g_mine, w_half, dims, preferred_element_type=F32)
    y_other, gy_other, gy_own = tie(y_other, gy_other, gy_own)
    gy_other = other_core(gy_other)
    first, second = terms(at, y_own, y_other, g_mine, g_other)
    far_x = far(first, "x")
    far_y = far(second, "y")
    gy_own, gy_other, *_ = tie(gy_own, gy_other, first)
    gy, sent_back = entries(gy_own, gy_other, x, cum_t, c)
    far_x, far_y, sent_back = tie(far_x, far_y, sent_back)
    got_back = swap(sent_back, SEQ)
    first = near(first, *far_x, "x")
    second = near(second, *far_y, "y")
    first, second, got_back = tie(first, second, got_back)
    first = direct(first, "y")
    second = direct(second, "x")
    last = swap(chain(got_back, got, mine, True), SEQ).reshape(H * P_SIZE, N)
    tiles = swap(fold(first + second), "z")

    gx, ga, gb, gc = backward(x, gy, cum, cum_t, b, c, d_skip, start, last)

    tiles, gx = tie(tiles, gx)
    tiles, note = zsum(row0, at_z, ids, tiles, got_back)
    tiles = swap(tiles, SEQ)
    for axis in ("x", "y", "z", "core"):
        note = sum_over(note, axis)
    clipped_w, clipped_d = clip(tokens_all, row0, ids, tiles, note)
    return (gx[None], ga[None], gb[None], gc[None], clipped_w, clipped_d[0, :H])


def solution(mesh):
    fine = Mesh(mesh.devices.reshape(4, 4, 8, 2), ("y", "x", "z", "core"))
    rows = ("y", "x")
    tokens = P(rows, SEQ, None)
    return jax.shard_map(
        per_device,
        mesh=fine,
        in_specs=(
            tokens, P(rows, None, SEQ), tokens, tokens, tokens, P(rows, None), P(), P(),
        ),
        out_specs=(tokens, P(rows, None, SEQ), tokens, tokens, P(rows, None), P()),
        check_vma=False,
    )
```

```python
import functools

import jax
import jax.numpy as jnp
from jax import lax
from jax.experimental import pallas as pl
from jax.experimental.pallas import tpu as pltpu
from jax.sharding import Mesh
from jax.sharding import PartitionSpec as P

D = 2560
H = 40
P_SIZE = 64
N = 128
T = 256
GROUPS = 4
PAIRS = H // 2
SEQ = ("z", "core")
N_SEQ = 16
OWN = H * P_SIZE // N_SEQ
HIGH = lax.Precision.HIGHEST
BF = jnp.bfloat16
F32 = jnp.float32
VMEM = 56 * 1024 * 1024
WIDE = 5
STEP = 2
ROWS = OWN + 16
TILES = 13


def nn(a, b):
    return lax.dot_general(a, b, (((1,), (0,)), ((), ())), preferred_element_type=F32)


def nt(a, b):
    return lax.dot_general(a, b, (((1,), (1,)), ((), ())), preferred_element_type=F32)


def tn(a, b):
    return lax.dot_general(a, b, (((0,), (0,)), ((), ())), preferred_element_type=F32)


def iota(shape, dim):
    return lax.broadcasted_iota(jnp.int32, shape, dim)


def whole(shape):
    return pl.BlockSpec(shape, lambda *_: (0,) * len(shape))


def wide(rows, pairs):
    return pl.BlockSpec((rows, pairs * 2 * P_SIZE), lambda p: (0, p))


def state_block(pairs):
    return pl.BlockSpec((pairs * 2 * P_SIZE, N), lambda p: (p, 0))


def smem():
    return pl.BlockSpec(memory_space=pltpu.SMEM)


def vmem():
    return pl.BlockSpec(memory_space=pltpu.VMEM)


def params():
    return pltpu.CompilerParams(vmem_limit_bytes=VMEM)


def cost(flops, moved, exps):
    return pl.CostEstimate(flops=flops, bytes_accessed=moved, transcendentals=exps)


def column(cum_t, head):
    return jnp.sum(jnp.where(iota(cum_t.shape, 1) == head, cum_t, 0.0), axis=1, keepdims=True)


def low_half(shape):
    return iota(shape, 1) < P_SIZE


def spread(cum_t, pair):
    return jnp.where(
        low_half((T, 2 * P_SIZE)), column(cum_t, 2 * pair), column(cum_t, 2 * pair + 1)
    )


def lanes_of(i):
    return slice(i * 2 * P_SIZE, (i + 1) * 2 * P_SIZE)


def put_states(out_ref, states, first, pairs):
    chunks = pairs * 2 * P_SIZE // OWN
    rows = states.astype(BF).reshape(chunks, OWN, N)
    out_ref[pl.ds(first * 2 * P_SIZE // OWN, chunks), :OWN, :] = rows


def put_note(out_ref, pieces):
    at = iota((16, N), 0)
    note = jnp.zeros((16, N), F32)
    for i, piece in enumerate(pieces):
        note = jnp.where(at == i, piece, note)
    for s in range(N_SEQ):
        out_ref[s, OWN:, :] = note.astype(BF)


def ends_kernel(x_ref, a_ref, b_ref, cum_ref, cum_t_ref, out_ref):
    step = pl.program_id(0)

    @pl.when(step == 0)
    def _():
        a = a_ref[...]
        upto = (iota((T, T), 0) <= iota((T, T), 1)).astype(F32)
        cum_ref[...] = jnp.dot(a, upto, precision=HIGH, preferred_element_type=F32)
        down = (iota((T, T), 1) <= iota((T, T), 0)).astype(F32)
        cum_t = lax.dot_general(
            down, a, (((1,), (1,)), ((), ())), precision=HIGH, preferred_element_type=F32
        )
        cum_t_ref[...] = cum_t
        total = jnp.concatenate([cum_t[T - 1 :, :], jnp.zeros((1, N - H), F32)], axis=1)
        hi = jnp.floor(total)
        mid = jnp.floor((total - hi) * 256.0) / 256.0
        put_note(out_ref, (hi, mid, total - hi - mid))

    cum_t = cum_t_ref[...]
    b = b_ref[...].astype(BF)
    found = []
    for i in range(WIDE):
        cum = spread(cum_t, step * WIDE + i)
        tail = jnp.exp(cum[T - 1 : T, :] - cum)
        found.append(tn((x_ref[:, lanes_of(i)] * tail).astype(BF), b))
    put_states(out_ref, jnp.concatenate(found, axis=0), step * WIDE, WIDE)


def local_ends(x, a, b):
    return pl.pallas_call(
        ends_kernel,
        grid=(PAIRS // WIDE,),
        in_specs=[wide(T, WIDE), whole((H, T)), whole((T, N))],
        out_specs=[whole((H, T)), whole((T, H)), whole((N_SEQ, ROWS, N))],
        out_shape=[
            jax.ShapeDtypeStruct((H, T), F32),
            jax.ShapeDtypeStruct((T, H), F32),
            jax.ShapeDtypeStruct((N_SEQ, ROWS, N), BF),
        ],
        compiler_params=params(),
        cost_estimate=cost(2 * T * D * N, 4 * T * D, T * D),
        name="ends",
    )(x, a, b)


def intra_kernel(x_ref, cum_ref, cum_t_ref, b_ref, c_ref, skip_ref, y_ref, grow_ref, scores):
    step = pl.program_id(0)

    @pl.when(step == 0)
    def _():
        keep = iota((T, T), 0) >= iota((T, T), 1)
        scores[...] = jnp.where(keep, nt(c_ref[...].astype(BF), b_ref[...].astype(BF)), 0.0)

    for i in range(STEP):
        x = x_ref[:, lanes_of(i)]
        xb = x.astype(BF)
        low = low_half(x.shape)
        head = 2 * (step * STEP + i)
        parts = []
        sides = []
        for k in range(2):
            sides.append(column(cum_t_ref[...], head + k))
            diff = sides[k] - cum_ref[pl.ds(head + k, 1), :]
            mixed = (jnp.exp(jnp.minimum(diff, 0.0)) * scores[...]).astype(BF)
            parts.append(nn(mixed, xb))
        skip = jnp.where(low, skip_ref[head], skip_ref[head + 1])
        y_ref[:, lanes_of(i)] = jnp.where(low, parts[0], parts[1]) + skip * x
        grow_ref[:, lanes_of(i)] = jnp.exp(jnp.where(low, sides[0], sides[1]))


def intra(x, cum, cum_t, b, c, skip):
    return pl.pallas_call(
        intra_kernel,
        grid=(PAIRS // STEP,),
        in_specs=[
            wide(T, STEP), whole((H, T)), whole((T, H)), whole((T, N)), whole((T, N)), smem(),
        ],
        out_specs=[wide(T, STEP)] * 2,
        out_shape=[jax.ShapeDtypeStruct((T, D), F32)] * 2,
        scratch_shapes=[pltpu.VMEM((T, T), F32)],
        compiler_params=params(),
        cost_estimate=cost(4 * T * T * D, 8 * T * D, H * T * T),
        name="intra",
    )(x, cum, cum_t, b, c, skip)


def inter_kernel(part_ref, grow_ref, c_ref, start_ref, y_ref):
    read = nt(c_ref[...].astype(BF), start_ref[...])
    y_ref[...] = (part_ref[...] + grow_ref[...] * read).astype(BF)


def inter(part, grow, c, start):
    return pl.pallas_call(
        inter_kernel,
        grid=(PAIRS // WIDE,),
        in_specs=[wide(T, WIDE), wide(T, WIDE), whole((T, N)), state_block(WIDE)],
        out_specs=wide(T, WIDE),
        out_shape=jax.ShapeDtypeStruct((T, D), BF),
        compiler_params=params(),
        cost_estimate=cost(2 * T * D * N, 10 * T * D, 0),
        name="inter",
    )(part, grow, c, start)


def chain_kernel(reverse, mine_ref, parts_ref, totals_ref, out_ref):
    owner = (mine_ref[0] * OWN + iota((OWN, N), 0)) // P_SIZE == iota((OWN, N), 1)
    carry = jnp.zeros((OWN, N), F32)
    for s in range(N_SEQ - 1, -1, -1) if reverse else range(N_SEQ):
        out_ref[s] = carry.astype(BF)
        pieces = totals_ref[s, OWN:, :].astype(F32)
        total = pieces[0:1, :] + pieces[1:2, :] + pieces[2:3, :]
        decay = jnp.sum(jnp.where(owner, total, 0.0), axis=1, keepdims=True)
        carry = jnp.exp(decay) * carry + parts_ref[s, :OWN, :].astype(F32)


def chain(parts, totals, mine, reverse):
    return pl.pallas_call(
        functools.partial(chain_kernel, reverse),
        in_specs=[smem(), vmem(), vmem()],
        out_specs=vmem(),
        out_shape=jax.ShapeDtypeStruct((N_SEQ, OWN, N), BF),
        compiler_params=params(),
        cost_estimate=cost(4 * N_SEQ * OWN * N, 4 * N_SEQ * OWN * N, N_SEQ * OWN),
        name="chain",
    )(mine, parts, totals)


def swap(v, axis):
    return lax.all_to_all(v, axis, 0, 0, tiled=True)


def term_kernel(at_ref, yo_ref, yx_ref, go_ref, gx_ref, first_ref, second_ref):
    half = go_ref.shape[1] // 2
    term = tn(yo_ref[...], go_ref[...]) + tn(yx_ref[...], gx_ref[...])
    term = term.astype(BF)
    for k in range(4):
        rows = slice(k * OWN, (k + 1) * OWN)
        first_ref[k, 0] = term[rows, :half]
        second_ref[0, (k + 4 - at_ref[1]) % 4] = term[rows, half:]


def terms(at, y_own, y_other, g_own, g_other):
    rows = pl.BlockSpec((T, 4 * OWN), lambda i, at: (0, (at[0] + i) % 4))
    half = g_own.shape[1] // 2
    return pl.pallas_call(
        term_kernel,
        grid_spec=pltpu.PrefetchScalarGridSpec(
            num_scalar_prefetch=1,
            grid=(4,),
            in_specs=[rows, rows, whole(g_own.shape), whole(g_own.shape)],
            out_specs=[
                pl.BlockSpec((4, 1, OWN, half), lambda i, at: (0, i, 0, 0)),
                pl.BlockSpec((1, 4, OWN, half), lambda i, at: (i, 0, 0, 0)),
            ],
        ),
        out_shape=[jax.ShapeDtypeStruct((4, 4, OWN, half), BF)] * 2,
        compiler_params=params(),
        cost_estimate=cost(4 * T * D * D // 2, 3 * D * D // 2, 0),
        name="terms",
    )(at, y_own, y_other, g_own, g_other)


def entry_kernel(own_ref, other_ref, x_ref, grow_ref, c_ref, gy_ref, out_ref, sums):
    step = pl.program_id(0)
    c = c_ref[...].astype(BF)
    found = []
    for i in range(WIDE):
        at = lanes_of(i)
        gy = own_ref[:, at] + other_ref[:, at].astype(F32)
        gy_ref[:, at] = gy.astype(BF)
        sums[pl.ds(step * WIDE + i, 1), :] = jnp.sum(gy * x_ref[:, at], axis=0, keepdims=True)
        found.append(tn((gy * grow_ref[:, at]).astype(BF), c))
    put_states(out_ref, jnp.concatenate(found, axis=0), step * WIDE, WIDE)

    @pl.when(step == PAIRS // WIDE - 1)
    def _():
        total = sums[...]
        low = low_half(total.shape)
        head = 2 * iota(total.shape, 0)
        lane = iota(total.shape, 1)
        even = jnp.sum(jnp.where(low, total, 0.0), axis=1, keepdims=True)
        odd = jnp.sum(jnp.where(low, 0.0, total), axis=1, keepdims=True)
        each = jnp.where(lane == head, even, 0.0) + jnp.where(lane == head + 1, odd, 0.0)
        gd = jnp.sum(each, axis=0, keepdims=True)
        hi = gd.astype(BF).astype(F32)
        mid = (gd - hi).astype(BF).astype(F32)
        put_note(out_ref, (hi, mid, gd - hi - mid))


def entries(own, other, x, grow, c):
    return pl.pallas_call(
        entry_kernel,
        grid=(PAIRS // WIDE,),
        in_specs=[wide(T, WIDE)] * 4 + [whole((T, N))],
        out_specs=[wide(T, WIDE), whole((N_SEQ, ROWS, N))],
        out_shape=[
            jax.ShapeDtypeStruct((T, D), BF),
            jax.ShapeDtypeStruct((N_SEQ, ROWS, N), BF),
        ],
        scratch_shapes=[pltpu.VMEM((PAIRS, 2 * P_SIZE), F32)],
        compiler_params=params(),
        cost_estimate=cost(2 * T * D * N, 12 * T * D, T * D),
        name="entries",
    )(own, other, x, grow, c)


def within_kernel(
    x_ref, gy_ref, cum_ref, cum_t_ref, b_ref, c_ref, skip_ref,
    gx_ref, ga_ref, gb_ref, gc_ref,
    scores, d_scores, rows, cols,
):
    step = pl.program_id(0)

    @pl.when(step == 0)
    def _():
        keep = iota((T, T), 1) >= iota((T, T), 0)
        scores[...] = jnp.where(keep, nt(b_ref[...].astype(BF), c_ref[...].astype(BF)), 0.0)
        d_scores[...] = jnp.zeros_like(d_scores)
        cols[...] = jnp.zeros_like(cols)

    lanes = iota((T, N), 1)
    low = low_half((T, 2 * P_SIZE))
    for i in range(STEP):
        pair = step * STEP + i
        at = lanes_of(i)
        x = x_ref[:, at]
        gyb = gy_ref[:, at]
        parts = []
        for k in range(2):
            head = 2 * pair + k
            diff = cum_ref[pl.ds(head, 1), :] - column(cum_t_ref[...], head)
            weights = jnp.exp(jnp.minimum(diff, 0.0))
            mine = jnp.where(low if k == 0 else ~low, x, 0.0).astype(BF)
            d_mixed = weights * nt(mine, gyb)
            d_scores[...] += d_mixed
            parts.append(nn((weights * scores[...]).astype(BF), gyb))
            change = d_mixed * scores[...]
            rows[pl.ds(head, 1), :] = jnp.sum(change, axis=0, keepdims=True)
            down = jnp.sum(change, axis=1, keepdims=True)
            cols[...] -= jnp.where(lanes == head, down, 0.0)
        skip = jnp.where(low, skip_ref[2 * pair], skip_ref[2 * pair + 1])
        gx_ref[:, at] = jnp.where(low, parts[0], parts[1]) + skip * gyb.astype(F32)

    @pl.when(step == PAIRS // STEP - 1)
    def _():
        keep = iota((T, T), 1) >= iota((T, T), 0)
        ds = jnp.where(keep, d_scores[...], 0.0).astype(BF)
        gb_ref[...] = nn(ds, c_ref[...].astype(BF))
        gc_ref[...] = tn(ds, b_ref[...].astype(BF))
        after = (iota((T, T), 0) >= iota((T, T), 1)).astype(F32)
        dims = (((0,), (0,)), ((), ()))
        ga = jnp.dot(rows[...], after, precision=HIGH, preferred_element_type=F32)
        up = lax.dot_general(cols[...], after, dims, precision=HIGH, preferred_element_type=F32)
        ga_ref[...] = ga + up[:H]


def within(x, gy, cum, cum_t, b, c, skip):
    return pl.pallas_call(
        within_kernel,
        grid=(PAIRS // STEP,),
        in_specs=[
            wide(T, STEP), wide(T, STEP), whole((H, T)), whole((T, H)), whole((T, N)),
            whole((T, N)), smem(),
        ],
        out_specs=[wide(T, STEP), whole((H, T)), whole((T, N)), whole((T, N))],
        out_shape=[
            jax.ShapeDtypeStruct((T, D), F32),
            jax.ShapeDtypeStruct((H, T), F32),
            jax.ShapeDtypeStruct((T, N), F32),
            jax.ShapeDtypeStruct((T, N), F32),
        ],
        scratch_shapes=[
            pltpu.VMEM((T, T), F32),
            pltpu.VMEM((T, T), F32),
            pltpu.VMEM((H, T), F32),
            pltpu.VMEM((T, N), F32),
        ],
        compiler_params=params(),
        cost_estimate=cost(6 * T * T * D, 10 * T * D, H * T * T),
        name="within",
    )(x, gy, cum, cum_t, b, c, skip)


def across_kernel(
    x_ref, gy_ref, grow_ref, part_ref, cum_ref, cum_t_ref, b_ref, c_ref, start_ref, last_ref,
    ga_in, gb_in, gc_in,
    gx_ref, ga_ref, gb_ref, gc_ref,
    cols, tails, totals,
):
    step = pl.program_id(0)
    bb = b_ref[...].astype(BF)
    cb = c_ref[...].astype(BF)

    @pl.when(step == 0)
    def _():
        cols[...] = jnp.zeros_like(cols)
        tails[...] = jnp.zeros_like(tails)
        gb_ref[...] = gb_in[...]
        gc_ref[...] = gc_in[...]

    width = WIDE * 2 * P_SIZE
    start = start_ref[...]
    last = last_ref[...]
    cum_t = cum_t_ref[...]
    sides = [spread(cum_t, step * WIDE + i) for i in range(WIDE)]
    cum = jnp.concatenate(sides, axis=1)
    tail = jnp.exp(cum[T - 1 : T, :] - cum)
    pick = iota((width, N), 1) == step * 2 * WIDE + iota((width, N), 0) // P_SIZE
    grown = gy_ref[...].astype(F32) * grow_ref[...]
    cols[...] += nn((grown * nt(cb, start)).astype(BF), pick.astype(BF))
    gc_ref[...] += nn(grown.astype(BF), start)
    faded = x_ref[...] * tail
    back = nt(bb, last)
    tails[...] += nn((faded * back).astype(BF), pick.astype(BF))
    gb_ref[...] += nn(faded.astype(BF), last)
    gx_ref[...] = part_ref[...] + tail * back
    both = jnp.sum(start.astype(F32) * last.astype(F32), axis=1, keepdims=True)
    totals[pl.ds(step, 1), :] = jnp.sum(jnp.where(pick, both, 0.0), axis=0, keepdims=True)

    @pl.when(step == PAIRS // WIDE - 1)
    def _():
        after = (iota((T, T), 0) >= iota((T, T), 1)).astype(F32)
        before = (iota((T, T), 0) < iota((T, T), 1)).astype(F32)
        dims = (((0,), (0,)), ((), ()))
        up = lax.dot_general(cols[...], after, dims, precision=HIGH, preferred_element_type=F32)
        up += lax.dot_general(tails[...], before, dims, precision=HIGH, preferred_element_type=F32)
        total = jnp.sum(totals[...], axis=0, keepdims=True)
        total = jnp.sum(jnp.where(iota((H, N), 0) == iota((H, N), 1), total, 0.0), axis=1, keepdims=True)
        ga_ref[...] = ga_in[...] + up[:H] + jnp.exp(cum_ref[:, T - 1 : T]) * total


def across(x, gy, grow, part, cum, cum_t, b, c, start, last, ga, gb, gc):
    return pl.pallas_call(
        across_kernel,
        grid=(PAIRS // WIDE,),
        in_specs=[wide(T, WIDE)] * 4
        + [whole((H, T)), whole((T, H)), whole((T, N)), whole((T, N))]
        + [state_block(WIDE), state_block(WIDE), whole((H, T)), whole((T, N)), whole((T, N))],
        out_specs=[wide(T, WIDE), whole((H, T)), whole((T, N)), whole((T, N))],
        out_shape=[
            jax.ShapeDtypeStruct((T, D), F32),
            jax.ShapeDtypeStruct((H, T), F32),
            jax.ShapeDtypeStruct((T, N), F32),
            jax.ShapeDtypeStruct((T, N), F32),
        ],
        scratch_shapes=[
            pltpu.VMEM((T, N), F32),
            pltpu.VMEM((T, N), F32),
            pltpu.VMEM((PAIRS // WIDE, N), F32),
        ],
        compiler_params=params(),
        cost_estimate=cost(8 * T * D * N, 20 * T * D, T * D),
        name="across",
    )(x, gy, grow, part, cum, cum_t, b, c, start, last, ga, gb, gc)


def fold_kernel(z_ref, a0, a1, a2, a3, b0, b1, b2, b3, *rest):
    outs, sums = rest[:8], rest[8]
    half = a0.shape[1]
    for i, parts in enumerate(((a0, a1, a2, a3), (b0, b1, b2, b3))):
        total = parts[0][...].astype(F32)
        for part in parts[1:]:
            total += part[...].astype(F32)
        sums[:, i * half : (i + 1) * half] = total
    for d in range(8):
        for i in range(TILES):
            q = TILES * ((z_ref[0] + d) % 8) + i
            r = jnp.minimum(q // 10, 9)
            row = pl.multiple_of(16 * r, 16)
            col = pl.multiple_of(128 * (q % 10), 128)
            tile = sums[pl.ds(row, 16), pl.ds(col, 128)]
            outs[d][i] = jnp.where(q < 100, tile, 0.0).astype(BF)


def fold(z, parts):
    return pl.pallas_call(
        fold_kernel,
        in_specs=[smem()] + [vmem()] * 8,
        out_specs=[vmem()] * 8,
        out_shape=[jax.ShapeDtypeStruct((TILES, 16, 128), BF)] * 8,
        scratch_shapes=[pltpu.VMEM((OWN, D // 2), F32)],
        compiler_params=params(),
        cost_estimate=cost(4 * OWN * D // 2, 8 * OWN * D // 2, 0),
        name="fold",
    )(z, *parts)


def groups_of(row0, count, ids_ref):
    heads = (row0 + iota((count, N), 0)) // P_SIZE == iota((count, N), 1)
    return jnp.sum(jnp.where(heads, ids_ref[...], 0.0), axis=1, keepdims=True)


def zsum_kernel(row0_ref, z_ref, ids_ref, got_ref, *rest):
    parts, out_ref, note_ref = rest[:8], rest[8], rest[9]
    total = parts[0][...].astype(F32)
    for part in parts[1:]:
        total += part[...].astype(F32)
    for s in range(8):
        out_ref[s] = total.astype(BF)
    found = jnp.zeros((16, N), F32)
    for i in range(TILES):
        row = row0_ref[0] + 16 * ((z_ref[0] * TILES + i) // 10)
        place = iota((16, N), 1) - H == groups_of(row, 16, ids_ref).astype(jnp.int32)
        tile = total[i]
        found += jnp.where(place, jnp.sum(tile * tile, axis=1, keepdims=True), 0.0)
    d_sum = jnp.zeros((1, N), F32)
    for s in range(N_SEQ):
        pieces = got_ref[s, OWN:, :].astype(F32)
        d_sum += pieces[0:1, :] + pieces[1:2, :] + pieces[2:3, :]
    note_ref[...] = jnp.sum(found, axis=0, keepdims=True) + d_sum / N_SEQ


def zsum(row0, z, ids, parts, got):
    return pl.pallas_call(
        zsum_kernel,
        in_specs=[smem(), smem()] + [vmem()] * 10,
        out_specs=[vmem(), vmem()],
        out_shape=[
            jax.ShapeDtypeStruct((8, TILES, 16, 128), BF),
            jax.ShapeDtypeStruct((1, N), F32),
        ],
        compiler_params=params(),
        cost_estimate=cost(8 * OWN * 160, 6 * OWN * D, 0),
        name="zsum",
    )(row0, z, ids, got, *parts)


def tile_of(ref, r, c):
    z, i = divmod(10 * r + c, TILES)
    return ref[z, i].astype(F32)


def clip_kernel(tokens_all, row0_ref, core_ref, ids_ref, own_ref, other_ref, note_ref, w_ref, d_ref):
    ids = ids_ref[...]
    lane = iota((1, N), 1)
    note = note_ref[0]
    for s in range(1, N_SEQ):
        note = note + note_ref[s]
    grad_d = jnp.where(lane < H, note, 0.0)
    groups = groups_of(row0_ref[0], OWN, ids_ref)
    w_factor = jnp.zeros((OWN, 1), F32)
    d_factor = jnp.zeros((1, N), F32)
    for g in range(GROUPS):
        here = (ids == float(g)) & (lane < H)
        count = jnp.sum(jnp.where(here, 1.0, 0.0), axis=1, keepdims=True)
        sumsq = jnp.sum(jnp.where(lane == H + g, note, 0.0), axis=1, keepdims=True)
        sumsq += jnp.sum(jnp.where(here, grad_d * grad_d, 0.0), axis=1, keepdims=True)
        bound = 7.0 * jnp.sqrt(count * (P_SIZE * D + 1.0) * tokens_all)
        factor = jnp.minimum(1.0, bound / jnp.sqrt(sumsq + 1e-06))
        w_factor += jnp.where(groups == float(g), factor, 0.0)
        d_factor += jnp.where(here, factor, 0.0)
    d_ref[...] = grad_d * d_factor
    for r in range(10):
        scale = w_factor[16 * r : 16 * r + 16, :]
        for ref, core in ((own_ref, core_ref[0]), (other_ref, 1 - core_ref[0])):
            for c in range(10):
                col = pl.multiple_of(core * (D // 2) + 128 * c, 128)
                w_ref[16 * r : 16 * r + 16, pl.ds(col, 128)] = tile_of(ref, r, c) * scale


def clip(tokens_all, row0, core, ids, own, other, note):
    return pl.pallas_call(
        functools.partial(clip_kernel, tokens_all),
        in_specs=[smem(), smem()] + [vmem()] * 4,
        out_specs=[vmem(), vmem()],
        out_shape=[jax.ShapeDtypeStruct((OWN, D), F32), jax.ShapeDtypeStruct((1, N), F32)],
        compiler_params=params(),
        cost_estimate=cost(2 * OWN * D, 6 * OWN * D, 0),
        name="clip",
    )(row0, core, ids, own, other, note)


def shifted(v, axis, d):
    return lax.ppermute(v, axis, [(i, (i + d) % 4) for i in range(4)])


def plus(a, b):
    return (a.astype(F32) + b.astype(F32)).astype(BF)


def far(t, axis):
    m = t.shape[1] // 2
    return shifted(t[2, :m], axis, 1), shifted(t[2, m:], axis, -1)


def passed(t, ra, rb):
    m = t.shape[1] // 2
    up = jnp.concatenate([plus(t[1, :m], ra), t[1, m:]], axis=0)
    down = jnp.concatenate([t[3, :m], plus(t[3, m:], rb)], axis=0)
    return up, down


def near(t, up, down, axis):
    total = t[0].astype(F32) + shifted(up, axis, 1).astype(F32)
    return (total + shifted(down, axis, -1).astype(F32)).astype(BF)


def direct(t, axis):
    return (t[0],) + tuple(shifted(t[d], axis, d) for d in (1, 3, 2))


def other_core(v):
    return lax.ppermute(v, "core", [(0, 1), (1, 0)])


def sum_over(v, axis):
    got = [lax.ppermute(v, axis, [(i, i ^ k) for i in range(4)]) for k in (1, 2, 3)]
    return (v + got[0]) + (got[1] + got[2])


def along_z(parts):
    got = [lax.ppermute(parts[d], "z", [(i, (i + d) % 8) for i in range(8)]) for d in range(1, 8)]
    return [parts[0]] + got


def tie(*values):
    return lax.optimization_barrier(values)


def per_device(x_in, a_log, b_in, c_in, g_out, w_out, d_skip, group_ids):
    x, a, b, c, g = (x_in[0], a_log[0], b_in[0], c_in[0], g_out[0])
    core = lax.axis_index("core")
    half = D // 2
    at = jnp.stack([lax.axis_index("y"), lax.axis_index("x")]).astype(jnp.int32)
    mine = (2 * lax.axis_index("z") + core).reshape(1).astype(jnp.int32)
    at_z = lax.axis_index("z").reshape(1).astype(jnp.int32)
    row0 = ((4 * at[0] + at[1]) * OWN).reshape(1)
    ids = jnp.pad(group_ids.astype(F32), (0, N - H), constant_values=-1.0)[None]
    tokens_all = float(T * N_SEQ * 16)

    w_mine = lax.dynamic_slice_in_dim(w_out, core * half, half, axis=1)
    w_half = lax.all_gather(w_mine, ("y", "x"), axis=0, tiled=True)
    g_mine = lax.dynamic_slice_in_dim(g, core * half, half, axis=1)
    g_other = other_core(lax.dynamic_slice_in_dim(g, (1 - core) * half, half, axis=1))

    cum, cum_t, sent = local_ends(x, a, b)
    got = swap(sent, SEQ)
    y_part, grow = intra(x, cum, cum_t, b, c, d_skip)
    start = swap(chain(got, got, mine, False), SEQ).reshape(H * P_SIZE, N)
    y_own = inter(y_part, grow, c, start)
    y_other = other_core(y_own)
    first, second = terms(at, y_own, y_other, g_mine, g_other)

    first = lax.psum_scatter(first.reshape(-1, half // 2), "x", scatter_dimension=0, tiled=True)
    far_y = far(second, "y")
    w_half, _ = tie(w_half, second)
    dims = (((1,), (1,)), ((), ()))
    gy_other = lax.dot_general(g_other, w_half, dims, preferred_element_type=F32).astype(BF)
    gy_own = lax.dot_general(g_mine, w_half, dims, preferred_element_type=F32)
    gy_other = other_core(gy_other)
    far_y = tie(*far_y, gy_own)[:2]
    up, down = passed(second, *far_y)
    up, down, gy_own, gy_other = tie(up, down, gy_own, gy_other)
    second = near(second, up, down, "y")
    gy, sent_back = entries(gy_own, gy_other, x, grow, c)
    got_back = swap(sent_back, SEQ)
    gx, ga, gb, gc = within(x, gy, cum, cum_t, b, c, d_skip)
    first, second, gx = tie(first, second, gx)
    first = direct(first.reshape(4, OWN, half // 2), "y")
    second = direct(second, "x")
    mine, _ = tie(mine, second[0])
    last = swap(chain(got_back, got, mine, True), SEQ).reshape(H * P_SIZE, N)

    tiles = along_z(fold(at_z, first + second))
    tiles, note = zsum(row0, at_z, ids, tiles, got_back)
    tiles = swap(tiles, "z")
    note = sum_over(sum_over(note, "x"), "y")
    tiles_other = other_core(tiles)
    gx, ga, gb, gc = across(x, gy, grow, gx, cum, cum_t, b, c, start, last, ga, gb, gc)
    note = swap(jnp.broadcast_to(note[None], (N_SEQ, 1, N)), SEQ)
    core = core.reshape(1).astype(jnp.int32)
    clipped_w, clipped_d = clip(tokens_all, row0, core, ids, tiles, tiles_other, note)
    return (gx[None], ga[None], gb[None], gc[None], clipped_w, clipped_d[0, :H])


def solution(mesh):
    fine = Mesh(mesh.devices.reshape(4, 4, 8, 2), ("y", "x", "z", "core"))
    rows = ("y", "x")
    tokens = P(rows, SEQ, None)
    return jax.shard_map(
        per_device,
        mesh=fine,
        in_specs=(
            tokens, P(rows, None, SEQ), tokens, tokens, tokens, P(rows, None), P(), P(),
        ),
        out_specs=(tokens, P(rows, None, SEQ), tokens, tokens, P(rows, None), P()),
        check_vma=False,
    )
```

```python
import functools

import jax
import jax.numpy as jnp
from jax import lax
from jax.experimental import pallas as pl
from jax.experimental.pallas import tpu as pltpu
from jax.sharding import Mesh
from jax.sharding import PartitionSpec as P

D = 2560
H = 40
P_SIZE = 64
N = 128
T = 256
GROUPS = 4
PAIRS = H // 2
SEQ = ("z", "core")
N_SEQ = 16
OWN = H * P_SIZE // N_SEQ
HIGH = lax.Precision.HIGHEST
BF = jnp.bfloat16
F32 = jnp.float32
VMEM = 56 * 1024 * 1024
WIDE = 5
STEP = 2
ROWS = OWN + 16
TILES = 13


def nn(a, b):
    return lax.dot_general(a, b, (((1,), (0,)), ((), ())), preferred_element_type=F32)


def nt(a, b):
    return lax.dot_general(a, b, (((1,), (1,)), ((), ())), preferred_element_type=F32)


def tn(a, b):
    return lax.dot_general(a, b, (((0,), (0,)), ((), ())), preferred_element_type=F32)


def iota(shape, dim):
    return lax.broadcasted_iota(jnp.int32, shape, dim)


def whole(shape):
    return pl.BlockSpec(shape, lambda *_: (0,) * len(shape))


def wide(rows, pairs):
    return pl.BlockSpec((rows, pairs * 2 * P_SIZE), lambda p: (0, p))


def state_block(pairs):
    return pl.BlockSpec((pairs * 2 * P_SIZE, N), lambda p: (p, 0))


def smem():
    return pl.BlockSpec(memory_space=pltpu.SMEM)


def vmem():
    return pl.BlockSpec(memory_space=pltpu.VMEM)


def params():
    return pltpu.CompilerParams(vmem_limit_bytes=VMEM)


def cost():
    return pl.CostEstimate(flops=1, bytes_accessed=1, transcendentals=0)


def column(cum_t, head):
    return jnp.sum(jnp.where(iota(cum_t.shape, 1) == head, cum_t, 0.0), axis=1, keepdims=True)


def low_half(shape):
    return iota(shape, 1) < P_SIZE


def lanes_of(i):
    return slice(i * 2 * P_SIZE, (i + 1) * 2 * P_SIZE)


def put_states(out_ref, states, first, pairs):
    chunks = pairs * 2 * P_SIZE // OWN
    rows = states.astype(BF).reshape(chunks, OWN, N)
    out_ref[pl.ds(first * 2 * P_SIZE // OWN, chunks), :OWN, :] = rows


def put_note(out_ref, pieces):
    at = iota((16, N), 0)
    note = jnp.zeros((16, N), F32)
    for i, piece in enumerate(pieces):
        note = jnp.where(at == i, piece, note)
    for s in range(N_SEQ):
        out_ref[s, OWN:, :] = note.astype(BF)


def ends_kernel(x_ref, a_ref, b_ref, cum_ref, cum_t_ref, tail_ref, out_ref, pieces):
    step = pl.program_id(0)

    @pl.when(step == 0)
    def _():
        a = a_ref[...]
        upto = (iota((T, T), 0) <= iota((T, T), 1)).astype(F32)
        cum_ref[...] = jnp.dot(a, upto, precision=HIGH, preferred_element_type=F32)
        down = (iota((T, T), 1) <= iota((T, T), 0)).astype(F32)
        cum_t = lax.dot_general(
            down, a, (((1,), (1,)), ((), ())), precision=HIGH, preferred_element_type=F32
        )
        cum_t_ref[...] = cum_t
        total = jnp.concatenate([cum_t[T - 1 :, :], jnp.zeros((1, N - H), F32)], axis=1)
        hi = jnp.floor(total)
        mid = jnp.floor((total - hi) * 256.0) / 256.0
        put_note(out_ref, (hi, mid, total - hi - mid))
        tail = jnp.exp(cum_t[T - 1 :, :] - cum_t)
        high = tail.astype(BF)
        pieces[0] = high
        pieces[1] = (tail - high.astype(F32)).astype(BF)

    width = WIDE * 2 * P_SIZE
    pick = iota((H, width), 0) == step * 2 * WIDE + iota((H, width), 1) // P_SIZE
    pick = pick.astype(BF)
    tail = nn(pieces[0], pick) + nn(pieces[1], pick)
    tail_ref[...] = tail
    states = tn((x_ref[...] * tail).astype(BF), b_ref[...].astype(BF))
    put_states(out_ref, states, step * WIDE, WIDE)


def local_ends(x, a, b):
    return pl.pallas_call(
        ends_kernel,
        grid=(PAIRS // WIDE,),
        in_specs=[wide(T, WIDE), whole((H, T)), whole((T, N))],
        out_specs=[whole((H, T)), whole((T, H)), wide(T, WIDE), whole((N_SEQ, ROWS, N))],
        out_shape=[
            jax.ShapeDtypeStruct((H, T), F32),
            jax.ShapeDtypeStruct((T, H), F32),
            jax.ShapeDtypeStruct((T, D), F32),
            jax.ShapeDtypeStruct((N_SEQ, ROWS, N), BF),
        ],
        scratch_shapes=[pltpu.VMEM((2, T, H), BF)],
        compiler_params=params(),
        cost_estimate=cost(),
        name="ends",
    )(x, a, b)


def intra_kernel(x_ref, cum_ref, cum_t_ref, b_ref, c_ref, skip_ref, y_ref, grow_ref, scores):
    step = pl.program_id(0)

    @pl.when(step == 0)
    def _():
        keep = iota((T, T), 0) >= iota((T, T), 1)
        scores[...] = jnp.where(keep, nt(c_ref[...].astype(BF), b_ref[...].astype(BF)), 0.0)

    for i in range(STEP):
        x = x_ref[:, lanes_of(i)]
        xb = x.astype(BF)
        low = low_half(x.shape)
        head = 2 * (step * STEP + i)
        parts = []
        sides = []
        for k in range(2):
            sides.append(column(cum_t_ref[...], head + k))
            diff = sides[k] - cum_ref[pl.ds(head + k, 1), :]
            mixed = (jnp.exp(jnp.minimum(diff, 0.0)) * scores[...]).astype(BF)
            parts.append(nn(mixed, xb))
        skip = jnp.where(low, skip_ref[head], skip_ref[head + 1])
        y_ref[:, lanes_of(i)] = jnp.where(low, parts[0], parts[1]) + skip * x
        grow_ref[:, lanes_of(i)] = jnp.exp(jnp.where(low, sides[0], sides[1]))


def intra(x, cum, cum_t, b, c, skip):
    return pl.pallas_call(
        intra_kernel,
        grid=(PAIRS // STEP,),
        in_specs=[
            wide(T, STEP), whole((H, T)), whole((T, H)), whole((T, N)), whole((T, N)), smem(),
        ],
        out_specs=[wide(T, STEP)] * 2,
        out_shape=[jax.ShapeDtypeStruct((T, D), F32)] * 2,
        scratch_shapes=[pltpu.VMEM((T, T), F32)],
        compiler_params=params(),
        cost_estimate=cost(),
        name="intra",
    )(x, cum, cum_t, b, c, skip)


def inter_kernel(part_ref, grow_ref, c_ref, start_ref, y_ref):
    read = nt(c_ref[...].astype(BF), start_ref[...])
    y_ref[...] = (part_ref[...] + grow_ref[...] * read).astype(BF)


def inter(part, grow, c, start):
    return pl.pallas_call(
        inter_kernel,
        grid=(PAIRS // WIDE,),
        in_specs=[wide(T, WIDE), wide(T, WIDE), whole((T, N)), state_block(WIDE)],
        out_specs=wide(T, WIDE),
        out_shape=jax.ShapeDtypeStruct((T, D), BF),
        compiler_params=params(),
        cost_estimate=cost(),
        name="inter",
    )(part, grow, c, start)


def chain_kernel(reverse, mine_ref, parts_ref, totals_ref, out_ref):
    owner = (mine_ref[0] * OWN + iota((OWN, N), 0)) // P_SIZE == iota((OWN, N), 1)
    carry = jnp.zeros((OWN, N), F32)
    for s in range(N_SEQ - 1, -1, -1) if reverse else range(N_SEQ):
        out_ref[s] = carry.astype(BF)
        pieces = totals_ref[s, OWN:, :].astype(F32)
        total = pieces[0:1, :] + pieces[1:2, :] + pieces[2:3, :]
        decay = jnp.sum(jnp.where(owner, total, 0.0), axis=1, keepdims=True)
        carry = jnp.exp(decay) * carry + parts_ref[s, :OWN, :].astype(F32)


def chain(parts, totals, mine, reverse):
    return pl.pallas_call(
        functools.partial(chain_kernel, reverse),
        in_specs=[smem(), vmem(), vmem()],
        out_specs=vmem(),
        out_shape=jax.ShapeDtypeStruct((N_SEQ, OWN, N), BF),
        compiler_params=params(),
        cost_estimate=cost(),
        name="chain",
    )(mine, parts, totals)


def swap(v, axis):
    return lax.all_to_all(v, axis, 0, 0, tiled=True)


def term_kernel(at_ref, yo_ref, yx_ref, g_ref, first_ref, second_ref):
    half = g_ref.shape[1] // 2
    term = tn(jnp.concatenate([yo_ref[...], yx_ref[...]], axis=0), g_ref[...]).astype(BF)
    for k in range(4):
        rows = slice(k * OWN, (k + 1) * OWN)
        first_ref[k, 0] = term[rows, :half]
        second_ref[0, (k + 4 - at_ref[1]) % 4] = term[rows, half:]


def terms(at, y_own, y_other, g):
    rows = pl.BlockSpec((T, 4 * OWN), lambda i, at: (0, (at[0] + i) % 4))
    half = g.shape[1] // 2
    return pl.pallas_call(
        term_kernel,
        grid_spec=pltpu.PrefetchScalarGridSpec(
            num_scalar_prefetch=1,
            grid=(4,),
            in_specs=[rows, rows, whole(g.shape)],
            out_specs=[
                pl.BlockSpec((4, 1, OWN, half), lambda i, at: (0, i, 0, 0)),
                pl.BlockSpec((1, 4, OWN, half), lambda i, at: (i, 0, 0, 0)),
            ],
        ),
        out_shape=[jax.ShapeDtypeStruct((4, 4, OWN, half), BF)] * 2,
        compiler_params=params(),
        cost_estimate=cost(),
        name="terms",
    )(at, y_own, y_other, g)


def gy_kernel(g_ref, w_ref, own_ref, other_ref):
    got = nt(g_ref[...], w_ref[...])
    own_ref[...] = got[:T]
    other_ref[...] = got[T:].astype(BF)


def gy_parts(g, w):
    rows = 4 * OWN
    return pl.pallas_call(
        gy_kernel,
        grid=(4,),
        in_specs=[whole(g.shape), pl.BlockSpec((rows, w.shape[1]), lambda i: (i, 0))],
        out_specs=[pl.BlockSpec((T, rows), lambda i: (0, i))] * 2,
        out_shape=[jax.ShapeDtypeStruct((T, D), F32), jax.ShapeDtypeStruct((T, D), BF)],
        compiler_params=params(),
        cost_estimate=cost(),
        name="gy_parts",
    )(g, w)


def entry_kernel(own_ref, other_ref, x_ref, grow_ref, c_ref, gy_ref, out_ref, sums):
    step = pl.program_id(0)
    c = c_ref[...].astype(BF)
    found = []
    for i in range(WIDE):
        at = lanes_of(i)
        gy = own_ref[:, at] + other_ref[:, at].astype(F32)
        gy_ref[:, at] = gy.astype(BF)
        sums[pl.ds(step * WIDE + i, 1), :] = jnp.sum(gy * x_ref[:, at], axis=0, keepdims=True)
        found.append(tn((gy * grow_ref[:, at]).astype(BF), c))
    put_states(out_ref, jnp.concatenate(found, axis=0), step * WIDE, WIDE)

    @pl.when(step == PAIRS // WIDE - 1)
    def _():
        total = sums[...]
        low = low_half(total.shape)
        head = 2 * iota(total.shape, 0)
        lane = iota(total.shape, 1)
        even = jnp.sum(jnp.where(low, total, 0.0), axis=1, keepdims=True)
        odd = jnp.sum(jnp.where(low, 0.0, total), axis=1, keepdims=True)
        each = jnp.where(lane == head, even, 0.0) + jnp.where(lane == head + 1, odd, 0.0)
        gd = jnp.sum(each, axis=0, keepdims=True)
        hi = gd.astype(BF).astype(F32)
        mid = (gd - hi).astype(BF).astype(F32)
        put_note(out_ref, (hi, mid, gd - hi - mid))


def entries(own, other, x, grow, c):
    return pl.pallas_call(
        entry_kernel,
        grid=(PAIRS // WIDE,),
        in_specs=[wide(T, WIDE)] * 4 + [whole((T, N))],
        out_specs=[wide(T, WIDE), whole((N_SEQ, ROWS, N))],
        out_shape=[
            jax.ShapeDtypeStruct((T, D), BF),
            jax.ShapeDtypeStruct((N_SEQ, ROWS, N), BF),
        ],
        scratch_shapes=[pltpu.VMEM((PAIRS, 2 * P_SIZE), F32)],
        compiler_params=params(),
        cost_estimate=cost(),
        name="entries",
    )(own, other, x, grow, c)


def within_kernel(
    first, steps, x_ref, gy_ref, cum_ref, cum_t_ref, b_ref, c_ref, skip_ref, *rest
):
    before = rest[:-8]
    gx_ref, ga_ref, gb_ref, gc_ref, scores, d_scores, rows, cols = rest[-8:]
    step = pl.program_id(0)

    @pl.when(step == 0)
    def _():
        keep = iota((T, T), 1) >= iota((T, T), 0)
        scores[...] = jnp.where(keep, nt(b_ref[...].astype(BF), c_ref[...].astype(BF)), 0.0)
        d_scores[...] = jnp.zeros_like(d_scores)
        rows[...] = jnp.zeros_like(rows)
        cols[...] = jnp.zeros_like(cols)

    lanes = iota((T, N), 1)
    low = low_half((T, 2 * P_SIZE))
    for i in range(STEP):
        pair = (first + step) * STEP + i
        at = lanes_of(i)
        x = x_ref[:, at]
        gyb = gy_ref[:, at]
        parts = []
        for k in range(2):
            head = 2 * pair + k
            diff = cum_ref[pl.ds(head, 1), :] - column(cum_t_ref[...], head)
            weights = jnp.exp(jnp.minimum(diff, 0.0))
            mine = jnp.where(low if k == 0 else ~low, x, 0.0).astype(BF)
            d_mixed = weights * nt(mine, gyb)
            d_scores[...] += d_mixed
            parts.append(nn((weights * scores[...]).astype(BF), gyb))
            change = d_mixed * scores[...]
            rows[pl.ds(head, 1), :] = jnp.sum(change, axis=0, keepdims=True)
            down = jnp.sum(change, axis=1, keepdims=True)
            cols[...] -= jnp.where(lanes == head, down, 0.0)
        skip = jnp.where(low, skip_ref[2 * pair], skip_ref[2 * pair + 1])
        gx_ref[:, at] = jnp.where(low, parts[0], parts[1]) + skip * gyb.astype(F32)

    @pl.when(step == steps - 1)
    def _():
        keep = iota((T, T), 1) >= iota((T, T), 0)
        ds = jnp.where(keep, d_scores[...], 0.0).astype(BF)
        gb = nn(ds, c_ref[...].astype(BF))
        gc = tn(ds, b_ref[...].astype(BF))
        after = (iota((T, T), 0) >= iota((T, T), 1)).astype(F32)
        dims = (((0,), (0,)), ((), ()))
        ga = jnp.dot(rows[...], after, precision=HIGH, preferred_element_type=F32)
        up = lax.dot_general(cols[...], after, dims, precision=HIGH, preferred_element_type=F32)
        for out, add, ref in zip((ga_ref, gb_ref, gc_ref), (ga + up[:H], gb, gc), before or (None,) * 3):
            out[...] = add if ref is None else add + ref[...]


def within(first, steps, x, gy, cum, cum_t, b, c, skip, before=()):
    here = pl.BlockSpec((T, STEP * 2 * P_SIZE), lambda p: (0, first + p))
    return pl.pallas_call(
        functools.partial(within_kernel, first, steps),
        grid=(steps,),
        in_specs=[
            here, here, whole((H, T)), whole((T, H)), whole((T, N)), whole((T, N)), smem(),
        ]
        + [whole(v.shape) for v in before],
        out_specs=[wide(T, STEP), whole((H, T)), whole((T, N)), whole((T, N))],
        out_shape=[
            jax.ShapeDtypeStruct((T, steps * STEP * 2 * P_SIZE), F32),
            jax.ShapeDtypeStruct((H, T), F32),
            jax.ShapeDtypeStruct((T, N), F32),
            jax.ShapeDtypeStruct((T, N), F32),
        ],
        scratch_shapes=[
            pltpu.VMEM((T, T), F32),
            pltpu.VMEM((T, T), F32),
            pltpu.VMEM((H, T), F32),
            pltpu.VMEM((T, N), F32),
        ],
        compiler_params=params(),
        cost_estimate=cost(),
        name="within",
    )(x, gy, cum, cum_t, b, c, skip, *before)


def across_kernel(
    x_ref, gy_ref, grow_ref, tail_ref, part_ref, part2_ref, cum_ref, b_ref, c_ref, start_ref, last_ref,
    ga_in, gb_in, gc_in,
    gx_ref, ga_ref, gb_ref, gc_ref,
    cols, tails, totals,
):
    step = pl.program_id(0)
    bb = b_ref[...].astype(BF)
    cb = c_ref[...].astype(BF)

    @pl.when(step == 0)
    def _():
        cols[...] = jnp.zeros_like(cols)
        tails[...] = jnp.zeros_like(tails)
        gb_ref[...] = gb_in[...]
        gc_ref[...] = gc_in[...]

    width = WIDE * 2 * P_SIZE
    start = start_ref[...]
    last = last_ref[...]
    tail = tail_ref[...]
    pick = iota((width, N), 1) == step * 2 * WIDE + iota((width, N), 0) // P_SIZE
    grown = gy_ref[...].astype(F32) * grow_ref[...]
    cols[...] += nn((grown * nt(cb, start)).astype(BF), pick.astype(BF))
    gc_ref[...] += nn(grown.astype(BF), start)
    faded = x_ref[...] * tail
    back = nt(bb, last)
    tails[...] += nn((faded * back).astype(BF), pick.astype(BF))
    gb_ref[...] += nn(faded.astype(BF), last)
    part = jnp.where(step < PAIRS // WIDE // 2, part_ref[...], part2_ref[...])
    gx_ref[...] = part + tail * back
    both = jnp.sum(start.astype(F32) * last.astype(F32), axis=1, keepdims=True)
    totals[pl.ds(step, 1), :] = jnp.sum(jnp.where(pick, both, 0.0), axis=0, keepdims=True)

    @pl.when(step == PAIRS // WIDE - 1)
    def _():
        after = (iota((T, T), 0) >= iota((T, T), 1)).astype(F32)
        before = (iota((T, T), 0) < iota((T, T), 1)).astype(F32)
        dims = (((0,), (0,)), ((), ()))
        up = lax.dot_general(cols[...], after, dims, precision=HIGH, preferred_element_type=F32)
        up += lax.dot_general(tails[...], before, dims, precision=HIGH, preferred_element_type=F32)
        total = jnp.sum(totals[...], axis=0, keepdims=True)
        total = jnp.sum(jnp.where(iota((H, N), 0) == iota((H, N), 1), total, 0.0), axis=1, keepdims=True)
        ga_ref[...] = ga_in[...] + up[:H] + jnp.exp(cum_ref[:, T - 1 : T]) * total


def across(x, gy, grow, tail, part, part2, cum, b, c, start, last, ga, gb, gc):
    width = WIDE * 2 * P_SIZE
    last_part = PAIRS // WIDE // 2 - 1
    return pl.pallas_call(
        across_kernel,
        grid=(PAIRS // WIDE,),
        in_specs=[wide(T, WIDE)] * 4
        + [
            pl.BlockSpec((T, width), lambda p: (0, jnp.minimum(p, last_part))),
            pl.BlockSpec((T, width), lambda p: (0, jnp.maximum(p - last_part - 1, 0))),
        ]
        + [whole((H, T)), whole((T, N)), whole((T, N))]
        + [state_block(WIDE), state_block(WIDE), whole((H, T)), whole((T, N)), whole((T, N))],
        out_specs=[wide(T, WIDE), whole((H, T)), whole((T, N)), whole((T, N))],
        out_shape=[
            jax.ShapeDtypeStruct((T, D), F32),
            jax.ShapeDtypeStruct((H, T), F32),
            jax.ShapeDtypeStruct((T, N), F32),
            jax.ShapeDtypeStruct((T, N), F32),
        ],
        scratch_shapes=[
            pltpu.VMEM((T, N), F32),
            pltpu.VMEM((T, N), F32),
            pltpu.VMEM((PAIRS // WIDE, N), F32),
        ],
        compiler_params=params(),
        cost_estimate=cost(),
        name="across",
    )(x, gy, grow, tail, part, part2, cum, b, c, start, last, ga, gb, gc)


def fold_kernel(z_ref, a0, a1, a2, a3, b0, b1, b2, b3, *rest):
    outs, sums = rest[:8], rest[8]
    half = a0.shape[1]
    for i, parts in enumerate(((a0, a1, a2, a3), (b0, b1, b2, b3))):
        total = parts[0][...].astype(F32)
        for part in parts[1:]:
            total += part[...].astype(F32)
        sums[:, i * half : (i + 1) * half] = total
    for d in range(8):
        for i in range(TILES):
            q = TILES * ((z_ref[0] + d) % 8) + i
            r = jnp.minimum(q // 10, 9)
            row = pl.multiple_of(16 * r, 16)
            col = pl.multiple_of(128 * (q % 10), 128)
            tile = sums[pl.ds(row, 16), pl.ds(col, 128)]
            outs[d][i] = jnp.where(q < 100, tile, 0.0).astype(BF)


def fold(z, parts):
    return pl.pallas_call(
        fold_kernel,
        in_specs=[smem()] + [vmem()] * 8,
        out_specs=[vmem()] * 8,
        out_shape=[jax.ShapeDtypeStruct((TILES, 16, 128), BF)] * 8,
        scratch_shapes=[pltpu.VMEM((OWN, D // 2), F32)],
        compiler_params=params(),
        cost_estimate=cost(),
        name="fold",
    )(z, *parts)


def groups_of(row0, count, ids_ref):
    heads = (row0 + iota((count, N), 0)) // P_SIZE == iota((count, N), 1)
    return jnp.sum(jnp.where(heads, ids_ref[...], 0.0), axis=1, keepdims=True)


def zsum_kernel(row0_ref, z_ref, ids_ref, got_ref, *rest):
    parts, out_ref, note_ref = rest[:8], rest[8], rest[9]
    total = parts[0][...].astype(F32)
    for part in parts[1:]:
        total += part[...].astype(F32)
    for s in range(8):
        out_ref[s] = total.astype(BF)
    found = jnp.zeros((16, N), F32)
    for i in range(TILES):
        row = row0_ref[0] + 16 * ((z_ref[0] * TILES + i) // 10)
        place = iota((16, N), 1) - H == groups_of(row, 16, ids_ref).astype(jnp.int32)
        tile = total[i]
        found += jnp.where(place, jnp.sum(tile * tile, axis=1, keepdims=True), 0.0)
    d_sum = jnp.zeros((1, N), F32)
    for s in range(N_SEQ):
        pieces = got_ref[s, OWN:, :].astype(F32)
        d_sum += pieces[0:1, :] + pieces[1:2, :] + pieces[2:3, :]
    note_ref[...] = jnp.sum(found, axis=0, keepdims=True) + d_sum / N_SEQ


def zsum(row0, z, ids, parts, got):
    return pl.pallas_call(
        zsum_kernel,
        in_specs=[smem(), smem()] + [vmem()] * 10,
        out_specs=[vmem(), vmem()],
        out_shape=[
            jax.ShapeDtypeStruct((8, TILES, 16, 128), BF),
            jax.ShapeDtypeStruct((1, N), F32),
        ],
        compiler_params=params(),
        cost_estimate=cost(),
        name="zsum",
    )(row0, z, ids, got, *parts)


def tile_of(ref, r, c):
    z, i = divmod(10 * r + c, TILES)
    return ref[z, i].astype(F32)


def clip_kernel(tokens_all, row0_ref, core_ref, ids_ref, own_ref, other_ref, note_ref, w_ref, d_ref):
    ids = ids_ref[...]
    lane = iota((1, N), 1)
    note = note_ref[0]
    for s in range(1, N_SEQ):
        note = note + note_ref[s]
    grad_d = jnp.where(lane < H, note, 0.0)
    groups = groups_of(row0_ref[0], OWN, ids_ref)
    w_factor = jnp.zeros((OWN, 1), F32)
    d_factor = jnp.zeros((1, N), F32)
    for g in range(GROUPS):
        here = (ids == float(g)) & (lane < H)
        count = jnp.sum(jnp.where(here, 1.0, 0.0), axis=1, keepdims=True)
        sumsq = jnp.sum(jnp.where(lane == H + g, note, 0.0), axis=1, keepdims=True)
        sumsq += jnp.sum(jnp.where(here, grad_d * grad_d, 0.0), axis=1, keepdims=True)
        bound = 7.0 * jnp.sqrt(count * (P_SIZE * D + 1.0) * tokens_all)
        factor = jnp.minimum(1.0, bound / jnp.sqrt(sumsq + 1e-06))
        w_factor += jnp.where(groups == float(g), factor, 0.0)
        d_factor += jnp.where(here, factor, 0.0)
    d_ref[...] = grad_d * d_factor
    for r in range(10):
        scale = w_factor[16 * r : 16 * r + 16, :]
        for ref, core in ((own_ref, core_ref[0]), (other_ref, 1 - core_ref[0])):
            for c in range(10):
                col = pl.multiple_of(core * (D // 2) + 128 * c, 128)
                w_ref[16 * r : 16 * r + 16, pl.ds(col, 128)] = tile_of(ref, r, c) * scale


def clip(tokens_all, row0, core, ids, own, other, note):
    return pl.pallas_call(
        functools.partial(clip_kernel, tokens_all),
        in_specs=[smem(), smem()] + [vmem()] * 4,
        out_specs=[vmem(), vmem()],
        out_shape=[jax.ShapeDtypeStruct((OWN, D), F32), jax.ShapeDtypeStruct((1, N), F32)],
        compiler_params=params(),
        cost_estimate=cost(),
        name="clip",
    )(row0, core, ids, own, other, note)


def shifted(v, axis, d):
    return lax.ppermute(v, axis, [(i, (i + d) % 4) for i in range(4)])


def plus(a, b):
    return (a.astype(F32) + b.astype(F32)).astype(BF)


def far(t, axis):
    m = t.shape[1] // 2
    return shifted(t[2, :m], axis, 1), shifted(t[2, m:], axis, -1)


def passed(t, ra, rb):
    m = t.shape[1] // 2
    up = jnp.concatenate([plus(t[1, :m], ra), t[1, m:]], axis=0)
    down = jnp.concatenate([t[3, :m], plus(t[3, m:], rb)], axis=0)
    return up, down


def near(t, up, down, axis):
    total = t[0].astype(F32) + shifted(up, axis, 1).astype(F32)
    return (total + shifted(down, axis, -1).astype(F32)).astype(BF)


def direct(t, axis):
    return (t[0],) + tuple(shifted(t[d], axis, d) for d in (1, 3, 2))


def other_core(v):
    return lax.ppermute(v, "core", [(0, 1), (1, 0)])


def sum_over(v, axis):
    got = [lax.ppermute(v, axis, [(i, i ^ k) for i in range(4)]) for k in (1, 2, 3)]
    return (v + got[0]) + (got[1] + got[2])


def along_z(parts):
    got = [lax.ppermute(parts[d], "z", [(i, (i + d) % 8) for i in range(8)]) for d in range(1, 8)]
    return [parts[0]] + got


def tie(*values):
    return lax.optimization_barrier(values)


def per_device(x_in, a_log, b_in, c_in, g_out, w_out, d_skip, group_ids):
    x, a, b, c, g = (x_in[0], a_log[0], b_in[0], c_in[0], g_out[0])
    core = lax.axis_index("core")
    half = D // 2
    at = jnp.stack([lax.axis_index("y"), lax.axis_index("x")]).astype(jnp.int32)
    mine = (2 * lax.axis_index("z") + core).reshape(1).astype(jnp.int32)
    at_z = lax.axis_index("z").reshape(1).astype(jnp.int32)
    row0 = ((4 * at[0] + at[1]) * OWN).reshape(1)
    ids = jnp.pad(group_ids.astype(F32), (0, N - H), constant_values=-1.0)[None]
    tokens_all = float(T * N_SEQ * 16)

    w_mine = lax.dynamic_slice_in_dim(w_out, core * half, half, axis=1)
    w_half = lax.all_gather(w_mine, ("y", "x"), axis=0, tiled=True)
    g_mine = lax.dynamic_slice_in_dim(g, core * half, half, axis=1)
    g_other = other_core(lax.dynamic_slice_in_dim(g, (1 - core) * half, half, axis=1))

    g_both = jnp.concatenate([g_mine, g_other], axis=0)

    cum, cum_t, tail, sent = local_ends(x, a, b)
    got = swap(sent, SEQ)
    y_part, grow = intra(x, cum, cum_t, b, c, d_skip)
    start = swap(chain(got, got, mine, False), SEQ).reshape(H * P_SIZE, N)
    y_own = inter(y_part, grow, c, start)
    y_other = other_core(y_own)
    first, second = terms(at, y_own, y_other, g_both)

    first = lax.psum_scatter(first.reshape(-1, half // 2), "x", scatter_dimension=0, tiled=True)
    far_y = far(second, "y")
    w_half, _ = tie(w_half, second)
    gy_own, gy_other = gy_parts(g_both, w_half)
    far_y = tie(*far_y, gy_own)[:2]
    gy_other = other_core(gy_other)
    up, down = passed(second, *far_y)
    up, down, gy_own, gy_other = tie(up, down, gy_own, gy_other)
    second = near(second, up, down, "y")
    gy, sent_back = entries(gy_own, gy_other, x, grow, c)
    got_back = swap(sent_back, SEQ)
    steps = PAIRS // STEP // 2
    gx1, *sums = within(0, steps, x, gy, cum, cum_t, b, c, d_skip)
    first, second, gx1 = tie(first, second, gx1)
    first = direct(first.reshape(4, OWN, half // 2), "y")
    second = direct(second, "x")
    mine, _ = tie(mine, second[0])
    states = chain(got_back, got, mine, True)
    states, parts = tie(states, first + second)
    last = swap(states, SEQ).reshape(H * P_SIZE, N)

    tiles = along_z(fold(at_z, parts))
    tiles, note = zsum(row0, at_z, ids, tiles, got_back)
    tiles, last = tie(tiles, last)
    tiles = swap(tiles, "z")
    gy, note = tie(gy, note)
    gx2, *sums = within(steps, steps, x, gy, cum, cum_t, b, c, d_skip, sums)
    note = sum_over(sum_over(note, "x"), "y")
    tiles, note, gx2, last = tie(tiles, note, gx2, last)
    note = swap(jnp.broadcast_to(note[None], (N_SEQ, 1, N)), SEQ)
    tiles_other = other_core(tiles)
    gx, ga, gb, gc = across(x, gy, grow, tail, gx1, gx2, cum, b, c, start, last, *sums)
    note, ga = tie(note, ga)
    core = core.reshape(1).astype(jnp.int32)
    clipped_w, clipped_d = clip(tokens_all, row0, core, ids, tiles, tiles_other, note)
    return (gx[None], ga[None], gb[None], gc[None], clipped_w, clipped_d[0, :H])


def solution(mesh):
    fine = Mesh(mesh.devices.reshape(4, 4, 8, 2), ("y", "x", "z", "core"))
    rows = ("y", "x")
    tokens = P(rows, SEQ, None)
    return jax.shard_map(
        per_device,
        mesh=fine,
        in_specs=(
            tokens, P(rows, None, SEQ), tokens, tokens, tokens, P(rows, None), P(), P(),
        ),
        out_specs=(tokens, P(rows, None, SEQ), tokens, tokens, P(rows, None), P()),
        check_vma=False,
    )
```

```python
import functools

import jax
import jax.numpy as jnp
from jax import lax
from jax.experimental import pallas as pl
from jax.experimental.pallas import tpu as pltpu
from jax.sharding import Mesh
from jax.sharding import PartitionSpec as P

D = 2560
H = 40
P_SIZE = 64
N = 128
T = 256
GROUPS = 4
PAIRS = H // 2
SEQ = ("z", "core")
N_SEQ = 16
OWN = H * P_SIZE // N_SEQ
HIGH = lax.Precision.HIGHEST
BF = jnp.bfloat16
F32 = jnp.float32
VMEM = 56 * 1024 * 1024
WIDE = 5
STEP = 2
ROWS = OWN + 16
TILES = 13


def nn(a, b):
    return lax.dot_general(a, b, (((1,), (0,)), ((), ())), preferred_element_type=F32)


def nt(a, b):
    return lax.dot_general(a, b, (((1,), (1,)), ((), ())), preferred_element_type=F32)


def tn(a, b):
    return lax.dot_general(a, b, (((0,), (0,)), ((), ())), preferred_element_type=F32)


def iota(shape, dim):
    return lax.broadcasted_iota(jnp.int32, shape, dim)


def whole(shape):
    return pl.BlockSpec(shape, lambda *_: (0,) * len(shape))


def wide(rows, pairs):
    return pl.BlockSpec((rows, pairs * 2 * P_SIZE), lambda p: (0, p))


def state_block(pairs):
    return pl.BlockSpec((pairs * 2 * P_SIZE, N), lambda p: (p, 0))


def smem():
    return pl.BlockSpec(memory_space=pltpu.SMEM)


def vmem():
    return pl.BlockSpec(memory_space=pltpu.VMEM)


def params():
    return pltpu.CompilerParams(vmem_limit_bytes=VMEM)


def cost(micros):
    return pl.CostEstimate(flops=0, bytes_accessed=int(micros * 3e6), transcendentals=0)


def column(cum_t, head):
    return jnp.sum(jnp.where(iota(cum_t.shape, 1) == head, cum_t, 0.0), axis=1, keepdims=True)


def low_half(shape):
    return iota(shape, 1) < P_SIZE


def lanes_of(i):
    return slice(i * 2 * P_SIZE, (i + 1) * 2 * P_SIZE)


def put_states(out_ref, states, first, pairs):
    chunks = pairs * 2 * P_SIZE // OWN
    rows = states.astype(BF).reshape(chunks, OWN, N)
    out_ref[pl.ds(first * 2 * P_SIZE // OWN, chunks), :OWN, :] = rows


def put_note(out_ref, pieces):
    at = iota((16, N), 0)
    note = jnp.zeros((16, N), F32)
    for i, piece in enumerate(pieces):
        note = jnp.where(at == i, piece, note)
    for s in range(N_SEQ):
        out_ref[s, OWN:, :] = note.astype(BF)


def ends_kernel(x_ref, a_ref, b_ref, cum_ref, cum_t_ref, tail_ref, out_ref, pieces):
    step = pl.program_id(0)

    @pl.when(step == 0)
    def _():
        a = a_ref[...]
        upto = (iota((T, T), 0) <= iota((T, T), 1)).astype(F32)
        cum_ref[...] = jnp.dot(a, upto, precision=HIGH, preferred_element_type=F32)
        down = (iota((T, T), 1) <= iota((T, T), 0)).astype(F32)
        cum_t = lax.dot_general(
            down, a, (((1,), (1,)), ((), ())), precision=HIGH, preferred_element_type=F32
        )
        cum_t_ref[...] = cum_t
        total = jnp.concatenate([cum_t[T - 1 :, :], jnp.zeros((1, N - H), F32)], axis=1)
        hi = jnp.floor(total)
        mid = jnp.floor((total - hi) * 256.0) / 256.0
        put_note(out_ref, (hi, mid, total - hi - mid))
        tail = jnp.exp(cum_t[T - 1 :, :] - cum_t)
        high = tail.astype(BF)
        pieces[0] = high
        pieces[1] = (tail - high.astype(F32)).astype(BF)

    width = WIDE * 2 * P_SIZE
    pick = iota((H, width), 0) == step * 2 * WIDE + iota((H, width), 1) // P_SIZE
    pick = pick.astype(BF)
    tail = nn(pieces[0], pick) + nn(pieces[1], pick)
    tail_ref[...] = tail
    states = tn((x_ref[...] * tail).astype(BF), b_ref[...].astype(BF))
    put_states(out_ref, states, step * WIDE, WIDE)


def local_ends(x, a, b):
    return pl.pallas_call(
        ends_kernel,
        grid=(PAIRS // WIDE,),
        in_specs=[wide(T, WIDE), whole((H, T)), whole((T, N))],
        out_specs=[whole((H, T)), whole((T, H)), wide(T, WIDE), whole((N_SEQ, ROWS, N))],
        out_shape=[
            jax.ShapeDtypeStruct((H, T), F32),
            jax.ShapeDtypeStruct((T, H), F32),
            jax.ShapeDtypeStruct((T, D), F32),
            jax.ShapeDtypeStruct((N_SEQ, ROWS, N), BF),
        ],
        scratch_shapes=[pltpu.VMEM((2, T, H), BF)],
        compiler_params=params(),
        cost_estimate=cost(6),
        name="ends",
    )(x, a, b)


def intra_kernel(x_ref, cum_ref, cum_t_ref, b_ref, c_ref, skip_ref, y_ref, grow_ref, scores):
    step = pl.program_id(0)

    @pl.when(step == 0)
    def _():
        keep = iota((T, T), 0) >= iota((T, T), 1)
        scores[...] = jnp.where(keep, nt(c_ref[...].astype(BF), b_ref[...].astype(BF)), 0.0)

    for i in range(STEP):
        x = x_ref[:, lanes_of(i)]
        xb = x.astype(BF)
        low = low_half(x.shape)
        head = 2 * (step * STEP + i)
        parts = []
        sides = []
        for k in range(2):
            sides.append(column(cum_t_ref[...], head + k))
            diff = sides[k] - cum_ref[pl.ds(head + k, 1), :]
            mixed = (jnp.exp(jnp.minimum(diff, 0.0)) * scores[...]).astype(BF)
            parts.append(nn(mixed, xb))
        skip = jnp.where(low, skip_ref[head], skip_ref[head + 1])
        y_ref[:, lanes_of(i)] = jnp.where(low, parts[0], parts[1]) + skip * x
        grow_ref[:, lanes_of(i)] = jnp.exp(jnp.where(low, sides[0], sides[1]))


def intra(x, cum, cum_t, b, c, skip):
    return pl.pallas_call(
        intra_kernel,
        grid=(PAIRS // STEP,),
        in_specs=[
            wide(T, STEP), whole((H, T)), whole((T, H)), whole((T, N)), whole((T, N)), smem(),
        ],
        out_specs=[wide(T, STEP)] * 2,
        out_shape=[jax.ShapeDtypeStruct((T, D), F32)] * 2,
        scratch_shapes=[pltpu.VMEM((T, T), F32)],
        compiler_params=params(),
        cost_estimate=cost(9),
        name="intra",
    )(x, cum, cum_t, b, c, skip)


def inter_kernel(part_ref, grow_ref, c_ref, start_ref, y_ref):
    read = nt(c_ref[...].astype(BF), start_ref[...])
    y_ref[...] = (part_ref[...] + grow_ref[...] * read).astype(BF)


def inter(part, grow, c, start):
    return pl.pallas_call(
        inter_kernel,
        grid=(PAIRS // WIDE,),
        in_specs=[wide(T, WIDE), wide(T, WIDE), whole((T, N)), state_block(WIDE)],
        out_specs=wide(T, WIDE),
        out_shape=jax.ShapeDtypeStruct((T, D), BF),
        compiler_params=params(),
        cost_estimate=cost(5),
        name="inter",
    )(part, grow, c, start)


def chain_kernel(reverse, mine_ref, parts_ref, totals_ref, out_ref):
    owner = (mine_ref[0] * OWN + iota((OWN, N), 0)) // P_SIZE == iota((OWN, N), 1)
    carry = jnp.zeros((OWN, N), F32)
    for s in range(N_SEQ - 1, -1, -1) if reverse else range(N_SEQ):
        out_ref[s] = carry.astype(BF)
        pieces = totals_ref[s, OWN:, :].astype(F32)
        total = pieces[0:1, :] + pieces[1:2, :] + pieces[2:3, :]
        decay = jnp.sum(jnp.where(owner, total, 0.0), axis=1, keepdims=True)
        carry = jnp.exp(decay) * carry + parts_ref[s, :OWN, :].astype(F32)


def chain(parts, totals, mine, reverse):
    return pl.pallas_call(
        functools.partial(chain_kernel, reverse),
        in_specs=[smem(), vmem(), vmem()],
        out_specs=vmem(),
        out_shape=jax.ShapeDtypeStruct((N_SEQ, OWN, N), BF),
        compiler_params=params(),
        cost_estimate=cost(3),
        name="chain",
    )(mine, parts, totals)


def swap(v, axis):
    return lax.all_to_all(v, axis, 0, 0, tiled=True)


def term_kernel(at_ref, yo_ref, yx_ref, g_ref, first_ref, second_ref):
    half = g_ref.shape[1] // 2
    term = tn(jnp.concatenate([yo_ref[...], yx_ref[...]], axis=0), g_ref[...]).astype(BF)
    for k in range(4):
        rows = slice(k * OWN, (k + 1) * OWN)
        first_ref[k, 0] = term[rows, :half]
        second_ref[0, (k + 4 - at_ref[1]) % 4] = term[rows, half:]


def terms(at, y_own, y_other, g):
    rows = pl.BlockSpec((T, 4 * OWN), lambda i, at: (0, (at[0] + i) % 4))
    half = g.shape[1] // 2
    return pl.pallas_call(
        term_kernel,
        grid_spec=pltpu.PrefetchScalarGridSpec(
            num_scalar_prefetch=1,
            grid=(4,),
            in_specs=[rows, rows, whole(g.shape)],
            out_specs=[
                pl.BlockSpec((4, 1, OWN, half), lambda i, at: (0, i, 0, 0)),
                pl.BlockSpec((1, 4, OWN, half), lambda i, at: (i, 0, 0, 0)),
            ],
        ),
        out_shape=[jax.ShapeDtypeStruct((4, 4, OWN, half), BF)] * 2,
        compiler_params=params(),
        cost_estimate=cost(8),
        name="terms",
    )(at, y_own, y_other, g)


def gy_kernel(g_ref, w_ref, own_ref, other_ref):
    got = nt(g_ref[...], w_ref[...])
    own_ref[...] = got[:T]
    other_ref[...] = got[T:].astype(BF)


def gy_parts(g, w):
    rows = 4 * OWN
    return pl.pallas_call(
        gy_kernel,
        grid=(4,),
        in_specs=[whole(g.shape), pl.BlockSpec((rows, w.shape[1]), lambda i: (i, 0))],
        out_specs=[pl.BlockSpec((T, rows), lambda i: (0, i))] * 2,
        out_shape=[jax.ShapeDtypeStruct((T, D), F32), jax.ShapeDtypeStruct((T, D), BF)],
        compiler_params=params(),
        cost_estimate=cost(8),
        name="gy_parts",
    )(g, w)


def entry_kernel(own_ref, other_ref, x_ref, grow_ref, c_ref, gy_ref, out_ref, sums):
    step = pl.program_id(0)
    c = c_ref[...].astype(BF)
    found = []
    for i in range(WIDE):
        at = lanes_of(i)
        gy = own_ref[:, at] + other_ref[:, at].astype(F32)
        gy_ref[:, at] = gy.astype(BF)
        sums[pl.ds(step * WIDE + i, 1), :] = jnp.sum(gy * x_ref[:, at], axis=0, keepdims=True)
        found.append(tn((gy * grow_ref[:, at]).astype(BF), c))
    put_states(out_ref, jnp.concatenate(found, axis=0), step * WIDE, WIDE)

    @pl.when(step == PAIRS // WIDE - 1)
    def _():
        total = sums[...]
        low = low_half(total.shape)
        head = 2 * iota(total.shape, 0)
        lane = iota(total.shape, 1)
        even = jnp.sum(jnp.where(low, total, 0.0), axis=1, keepdims=True)
        odd = jnp.sum(jnp.where(low, 0.0, total), axis=1, keepdims=True)
        each = jnp.where(lane == head, even, 0.0) + jnp.where(lane == head + 1, odd, 0.0)
        gd = jnp.sum(each, axis=0, keepdims=True)
        hi = gd.astype(BF).astype(F32)
        mid = (gd - hi).astype(BF).astype(F32)
        put_note(out_ref, (hi, mid, gd - hi - mid))


def entries(own, other, x, grow, c):
    return pl.pallas_call(
        entry_kernel,
        grid=(PAIRS // WIDE,),
        in_specs=[wide(T, WIDE)] * 4 + [whole((T, N))],
        out_specs=[wide(T, WIDE), whole((N_SEQ, ROWS, N))],
        out_shape=[
            jax.ShapeDtypeStruct((T, D), BF),
            jax.ShapeDtypeStruct((N_SEQ, ROWS, N), BF),
        ],
        scratch_shapes=[pltpu.VMEM((PAIRS, 2 * P_SIZE), F32)],
        compiler_params=params(),
        cost_estimate=cost(6),
        name="entries",
    )(own, other, x, grow, c)


def within_kernel(
    first, steps, x_ref, gy_ref, cum_ref, cum_t_ref, b_ref, c_ref, skip_ref, *rest
):
    before = rest[:-8]
    gx_ref, ga_ref, gb_ref, gc_ref, scores, d_scores, rows, cols = rest[-8:]
    step = pl.program_id(0)

    @pl.when(step == 0)
    def _():
        keep = iota((T, T), 1) >= iota((T, T), 0)
        scores[...] = jnp.where(keep, nt(b_ref[...].astype(BF), c_ref[...].astype(BF)), 0.0)
        d_scores[...] = jnp.zeros_like(d_scores)
        rows[...] = jnp.zeros_like(rows)
        cols[...] = jnp.zeros_like(cols)

    lanes = iota((T, N), 1)
    low = low_half((T, 2 * P_SIZE))
    for i in range(STEP):
        pair = (first + step) * STEP + i
        at = lanes_of(i)
        x = x_ref[:, at]
        gyb = gy_ref[:, at]
        parts = []
        for k in range(2):
            head = 2 * pair + k
            diff = cum_ref[pl.ds(head, 1), :] - column(cum_t_ref[...], head)
            weights = jnp.exp(jnp.minimum(diff, 0.0))
            mine = jnp.where(low if k == 0 else ~low, x, 0.0).astype(BF)
            d_mixed = weights * nt(mine, gyb)
            d_scores[...] += d_mixed
            parts.append(nn((weights * scores[...]).astype(BF), gyb))
            change = d_mixed * scores[...]
            rows[pl.ds(head, 1), :] = jnp.sum(change, axis=0, keepdims=True)
            down = jnp.sum(change, axis=1, keepdims=True)
            cols[...] -= jnp.where(lanes == head, down, 0.0)
        skip = jnp.where(low, skip_ref[2 * pair], skip_ref[2 * pair + 1])
        gx_ref[:, at] = jnp.where(low, parts[0], parts[1]) + skip * gyb.astype(F32)

    @pl.when(step == steps - 1)
    def _():
        keep = iota((T, T), 1) >= iota((T, T), 0)
        ds = jnp.where(keep, d_scores[...], 0.0).astype(BF)
        gb = nn(ds, c_ref[...].astype(BF))
        gc = tn(ds, b_ref[...].astype(BF))
        after = (iota((T, T), 0) >= iota((T, T), 1)).astype(F32)
        dims = (((0,), (0,)), ((), ()))
        ga = jnp.dot(rows[...], after, precision=HIGH, preferred_element_type=F32)
        up = lax.dot_general(cols[...], after, dims, precision=HIGH, preferred_element_type=F32)
        for out, add, ref in zip((ga_ref, gb_ref, gc_ref), (ga + up[:H], gb, gc), before or (None,) * 3):
            out[...] = add if ref is None else add + ref[...]


def within(first, steps, x, gy, cum, cum_t, b, c, skip, before=()):
    here = pl.BlockSpec((T, STEP * 2 * P_SIZE), lambda p: (0, first + p))
    return pl.pallas_call(
        functools.partial(within_kernel, first, steps),
        grid=(steps,),
        in_specs=[
            here, here, whole((H, T)), whole((T, H)), whole((T, N)), whole((T, N)), smem(),
        ]
        + [whole(v.shape) for v in before],
        out_specs=[wide(T, STEP), whole((H, T)), whole((T, N)), whole((T, N))],
        out_shape=[
            jax.ShapeDtypeStruct((T, steps * STEP * 2 * P_SIZE), F32),
            jax.ShapeDtypeStruct((H, T), F32),
            jax.ShapeDtypeStruct((T, N), F32),
            jax.ShapeDtypeStruct((T, N), F32),
        ],
        scratch_shapes=[
            pltpu.VMEM((T, T), F32),
            pltpu.VMEM((T, T), F32),
            pltpu.VMEM((H, T), F32),
            pltpu.VMEM((T, N), F32),
        ],
        compiler_params=params(),
        cost_estimate=cost(7),
        name="within",
    )(x, gy, cum, cum_t, b, c, skip, *before)


def across_kernel(
    x_ref, gy_ref, grow_ref, tail_ref, part_ref, part2_ref, cum_ref, b_ref, c_ref, start_ref, last_ref,
    ga_in, gb_in, gc_in,
    gx_ref, ga_ref, gb_ref, gc_ref,
    cols, tails, totals,
):
    step = pl.program_id(0)
    bb = b_ref[...].astype(BF)
    cb = c_ref[...].astype(BF)

    @pl.when(step == 0)
    def _():
        cols[...] = jnp.zeros_like(cols)
        tails[...] = jnp.zeros_like(tails)
        gb_ref[...] = gb_in[...]
        gc_ref[...] = gc_in[...]

    width = WIDE * 2 * P_SIZE
    start = start_ref[...]
    last = last_ref[...]
    tail = tail_ref[...]
    pick = iota((width, N), 1) == step * 2 * WIDE + iota((width, N), 0) // P_SIZE
    grown = gy_ref[...].astype(F32) * grow_ref[...]
    cols[...] += nn((grown * nt(cb, start)).astype(BF), pick.astype(BF))
    gc_ref[...] += nn(grown.astype(BF), start)
    faded = x_ref[...] * tail
    back = nt(bb, last)
    tails[...] += nn((faded * back).astype(BF), pick.astype(BF))
    gb_ref[...] += nn(faded.astype(BF), last)
    part = jnp.where(step < PAIRS // WIDE // 2, part_ref[...], part2_ref[...])
    gx_ref[...] = part + tail * back
    both = jnp.sum(start.astype(F32) * last.astype(F32), axis=1, keepdims=True)
    totals[pl.ds(step, 1), :] = jnp.sum(jnp.where(pick, both, 0.0), axis=0, keepdims=True)

    @pl.when(step == PAIRS // WIDE - 1)
    def _():
        after = (iota((T, T), 0) >= iota((T, T), 1)).astype(F32)
        before = (iota((T, T), 0) < iota((T, T), 1)).astype(F32)
        dims = (((0,), (0,)), ((), ()))
        up = lax.dot_general(cols[...], after, dims, precision=HIGH, preferred_element_type=F32)
        up += lax.dot_general(tails[...], before, dims, precision=HIGH, preferred_element_type=F32)
        total = jnp.sum(totals[...], axis=0, keepdims=True)
        total = jnp.sum(jnp.where(iota((H, N), 0) == iota((H, N), 1), total, 0.0), axis=1, keepdims=True)
        ga_ref[...] = ga_in[...] + up[:H] + jnp.exp(cum_ref[:, T - 1 : T]) * total


def across(x, gy, grow, tail, part, part2, cum, b, c, start, last, ga, gb, gc):
    width = WIDE * 2 * P_SIZE
    last_part = PAIRS // WIDE // 2 - 1
    return pl.pallas_call(
        across_kernel,
        grid=(PAIRS // WIDE,),
        in_specs=[wide(T, WIDE)] * 4
        + [
            pl.BlockSpec((T, width), lambda p: (0, jnp.minimum(p, last_part))),
            pl.BlockSpec((T, width), lambda p: (0, jnp.maximum(p - last_part - 1, 0))),
        ]
        + [whole((H, T)), whole((T, N)), whole((T, N))]
        + [state_block(WIDE), state_block(WIDE), whole((H, T)), whole((T, N)), whole((T, N))],
        out_specs=[wide(T, WIDE), whole((H, T)), whole((T, N)), whole((T, N))],
        out_shape=[
            jax.ShapeDtypeStruct((T, D), F32),
            jax.ShapeDtypeStruct((H, T), F32),
            jax.ShapeDtypeStruct((T, N), F32),
            jax.ShapeDtypeStruct((T, N), F32),
        ],
        scratch_shapes=[
            pltpu.VMEM((T, N), F32),
            pltpu.VMEM((T, N), F32),
            pltpu.VMEM((PAIRS // WIDE, N), F32),
        ],
        compiler_params=params(),
        cost_estimate=cost(8),
        name="across",
    )(x, gy, grow, tail, part, part2, cum, b, c, start, last, ga, gb, gc)


def fold_kernel(a0, a1, a2, a3, b0, b1, b2, b3, out_ref):
    sums = []
    for parts in ((a0, a1, a2, a3), (b0, b1, b2, b3)):
        total = parts[0][...].astype(F32)
        for part in parts[1:]:
            total += part[...].astype(F32)
        sums.append(total.astype(BF))
    for q in range(8 * TILES):
        r, c = divmod(q, 10)
        if r < 10:
            tile = sums[c // 5][16 * r : 16 * r + 16, 128 * (c % 5) : 128 * (c % 5) + 128]
        else:
            tile = jnp.zeros((16, 128), BF)
        out_ref[q // TILES, q % TILES] = tile


def fold(parts):
    return pl.pallas_call(
        fold_kernel,
        in_specs=[vmem()] * 8,
        out_specs=vmem(),
        out_shape=jax.ShapeDtypeStruct((8, TILES, 16, 128), BF),
        compiler_params=params(),
        cost_estimate=cost(3),
        name="fold",
    )(*parts)


def groups_of(row0, count, ids_ref):
    heads = (row0 + iota((count, N), 0)) // P_SIZE == iota((count, N), 1)
    return jnp.sum(jnp.where(heads, ids_ref[...], 0.0), axis=1, keepdims=True)


def zsum_kernel(row0_ref, z_ref, ids_ref, got_ref, parts_ref, out_ref, note_ref):
    total = parts_ref[0].astype(F32)
    for z in range(1, 8):
        total += parts_ref[z].astype(F32)
    for s in range(8):
        out_ref[s] = total.astype(BF)
    found = jnp.zeros((16, N), F32)
    for i in range(TILES):
        row = row0_ref[0] + 16 * ((z_ref[0] * TILES + i) // 10)
        place = iota((16, N), 1) - H == groups_of(row, 16, ids_ref).astype(jnp.int32)
        tile = total[i]
        found += jnp.where(place, jnp.sum(tile * tile, axis=1, keepdims=True), 0.0)
    d_sum = jnp.zeros((1, N), F32)
    for s in range(N_SEQ):
        pieces = got_ref[s, OWN:, :].astype(F32)
        d_sum += pieces[0:1, :] + pieces[1:2, :] + pieces[2:3, :]
    note_ref[...] = jnp.sum(found, axis=0, keepdims=True) + d_sum / N_SEQ


def zsum(row0, z, ids, parts, got):
    return pl.pallas_call(
        zsum_kernel,
        in_specs=[smem(), smem()] + [vmem()] * 3,
        out_specs=[vmem(), vmem()],
        out_shape=[
            jax.ShapeDtypeStruct((8, TILES, 16, 128), BF),
            jax.ShapeDtypeStruct((1, N), F32),
        ],
        compiler_params=params(),
        cost_estimate=cost(2),
        name="zsum",
    )(row0, z, ids, got, parts)


def tile_of(ref, r, c):
    z, i = divmod(10 * r + c, TILES)
    return ref[z, i].astype(F32)


def clip_kernel(tokens_all, row0_ref, core_ref, ids_ref, own_ref, other_ref, note_ref, w_ref, d_ref):
    ids = ids_ref[...]
    lane = iota((1, N), 1)
    note = note_ref[...]
    grad_d = jnp.where(lane < H, note, 0.0)
    groups = groups_of(row0_ref[0], OWN, ids_ref)
    w_factor = jnp.zeros((OWN, 1), F32)
    d_factor = jnp.zeros((1, N), F32)
    for g in range(GROUPS):
        here = (ids == float(g)) & (lane < H)
        count = jnp.sum(jnp.where(here, 1.0, 0.0), axis=1, keepdims=True)
        sumsq = jnp.sum(jnp.where(lane == H + g, note, 0.0), axis=1, keepdims=True)
        sumsq += jnp.sum(jnp.where(here, grad_d * grad_d, 0.0), axis=1, keepdims=True)
        bound = 7.0 * jnp.sqrt(count * (P_SIZE * D + 1.0) * tokens_all)
        factor = jnp.minimum(1.0, bound / jnp.sqrt(sumsq + 1e-06))
        w_factor += jnp.where(groups == float(g), factor, 0.0)
        d_factor += jnp.where(here, factor, 0.0)
    d_ref[...] = grad_d * d_factor
    for r in range(10):
        scale = w_factor[16 * r : 16 * r + 16, :]
        for ref, core in ((own_ref, core_ref[0]), (other_ref, 1 - core_ref[0])):
            for c in range(10):
                col = pl.multiple_of(core * (D // 2) + 128 * c, 128)
                w_ref[16 * r : 16 * r + 16, pl.ds(col, 128)] = tile_of(ref, r, c) * scale


def clip(tokens_all, row0, core, ids, own, other, note):
    return pl.pallas_call(
        functools.partial(clip_kernel, tokens_all),
        in_specs=[smem(), smem()] + [vmem()] * 4,
        out_specs=[vmem(), vmem()],
        out_shape=[jax.ShapeDtypeStruct((OWN, D), F32), jax.ShapeDtypeStruct((1, N), F32)],
        compiler_params=params(),
        cost_estimate=cost(3),
        name="clip",
    )(row0, core, ids, own, other, note)


def shifted(v, axis, d):
    return lax.ppermute(v, axis, [(i, (i + d) % 4) for i in range(4)])


def plus(a, b):
    return (a.astype(F32) + b.astype(F32)).astype(BF)


def far(t, axis):
    m = t.shape[1] // 2
    return shifted(t[2, :m], axis, 1), shifted(t[2, m:], axis, -1)


def passed(t, ra, rb):
    m = t.shape[1] // 2
    up = jnp.concatenate([plus(t[1, :m], ra), t[1, m:]], axis=0)
    down = jnp.concatenate([t[3, :m], plus(t[3, m:], rb)], axis=0)
    return up, down


def near(t, up, down, axis):
    total = t[0].astype(F32) + shifted(up, axis, 1).astype(F32)
    return (total + shifted(down, axis, -1).astype(F32)).astype(BF)


def direct(t, axis):
    return (t[0],) + tuple(shifted(t[d], axis, d) for d in (1, 3, 2))


def other_core(v):
    return lax.ppermute(v, "core", [(0, 1), (1, 0)])


def sum_over(v, axes):
    for unit in (1, 4):
        got = [
            lax.ppermute(v, axes, [(i, i ^ (unit * k)) for i in range(16)]) for k in (1, 2, 3)
        ]
        v = (v + got[0]) + (got[1] + got[2])
    return v


def tie(*values):
    return lax.optimization_barrier(values)


def per_device(x_in, a_log, b_in, c_in, g_out, w_out, d_skip, group_ids):
    x, a, b, c, g = (x_in[0], a_log[0], b_in[0], c_in[0], g_out[0])
    core = lax.axis_index("core")
    half = D // 2
    at = jnp.stack([lax.axis_index("y"), lax.axis_index("x")]).astype(jnp.int32)
    mine = (2 * lax.axis_index("z") + core).reshape(1).astype(jnp.int32)
    at_z = lax.axis_index("z").reshape(1).astype(jnp.int32)
    row0 = ((4 * at[0] + at[1]) * OWN).reshape(1)
    ids = jnp.pad(group_ids.astype(F32), (0, N - H), constant_values=-1.0)[None]
    tokens_all = float(T * N_SEQ * 16)

    w_mine = lax.dynamic_slice_in_dim(w_out, core * half, half, axis=1)
    w_half = lax.all_gather(w_mine, ("y", "x"), axis=0, tiled=True)
    g_mine = lax.dynamic_slice_in_dim(g, core * half, half, axis=1)
    g_other = other_core(lax.dynamic_slice_in_dim(g, (1 - core) * half, half, axis=1))

    g_both = jnp.concatenate([g_mine, g_other], axis=0)

    cum, cum_t, tail, sent = local_ends(x, a, b)
    got = swap(sent, SEQ)
    y_part, grow = intra(x, cum, cum_t, b, c, d_skip)
    start = swap(chain(got, got, mine, False), SEQ).reshape(H * P_SIZE, N)
    y_own = inter(y_part, grow, c, start)
    y_other = other_core(y_own)
    w_half, _ = tie(w_half, y_own)
    gy_own, gy_other = gy_parts(g_both, w_half)
    y_other, gy_own, gy_other = tie(y_other, gy_own, gy_other)
    gy_other = other_core(gy_other)
    first, second = terms(at, y_own, y_other, g_both)

    first = lax.psum_scatter(first.reshape(-1, half // 2), "x", scatter_dimension=0, tiled=True)
    far_y = far(second, "y")
    gy_own, gy_other, _ = tie(gy_own, gy_other, second)
    gy, sent_back = entries(gy_own, gy_other, x, grow, c)
    *far_y, sent_back = tie(*far_y, sent_back)
    got_back = swap(sent_back, SEQ)
    up, down = passed(second, *far_y)
    up, down, gy = tie(up, down, gy)
    second = near(second, up, down, "y")
    steps = PAIRS // STEP // 2
    gx1, *sums = within(0, steps, x, gy, cum, cum_t, b, c, d_skip)
    states = chain(got_back, got, mine, True)
    first, second, gx1, states = tie(first, second, gx1, states)
    last = swap(states, SEQ).reshape(H * P_SIZE, N)
    first = direct(first.reshape(4, OWN, half // 2), "y")
    second = direct(second, "x")
    parts, last = tie(first + second, last)
    tiles = fold(parts)
    gy, tiles = tie(gy, tiles)
    tiles = swap(tiles, "z")
    gx2, *sums = within(steps, steps, x, gy, cum, cum_t, b, c, d_skip, sums)
    gx, ga, gb, gc = across(x, gy, grow, tail, gx1, gx2, cum, b, c, start, last, *sums)
    tiles, ga = tie(tiles, ga)
    tiles, note = zsum(row0, at_z, ids, tiles, got_back)
    tiles = swap(tiles, "z")
    note = sum_over(sum_over(note, ("y", "x")), SEQ)
    tiles_other = other_core(tiles)
    core = core.reshape(1).astype(jnp.int32)
    clipped_w, clipped_d = clip(tokens_all, row0, core, ids, tiles, tiles_other, note)
    return (gx[None], ga[None], gb[None], gc[None], clipped_w, clipped_d[0, :H])


def solution(mesh):
    fine = Mesh(mesh.devices.reshape(4, 4, 8, 2), ("y", "x", "z", "core"))
    rows = ("y", "x")
    tokens = P(rows, SEQ, None)
    return jax.shard_map(
        per_device,
        mesh=fine,
        in_specs=(
            tokens, P(rows, None, SEQ), tokens, tokens, tokens, P(rows, None), P(), P(),
        ),
        out_specs=(tokens, P(rows, None, SEQ), tokens, tokens, P(rows, None), P()),
        check_vma=False,
    )
```

```python
import functools

import jax
import jax.numpy as jnp
from jax import lax
from jax.experimental import pallas as pl
from jax.experimental.pallas import tpu as pltpu
from jax.sharding import Mesh
from jax.sharding import PartitionSpec as P

D = 2560
H = 40
P_SIZE = 64
N = 128
T = 256
GROUPS = 4
PAIRS = H // 2
SEQ = ("z", "core")
N_SEQ = 16
OWN = H * P_SIZE // N_SEQ
HIGH = lax.Precision.HIGHEST
BF = jnp.bfloat16
F32 = jnp.float32
VMEM = 56 * 1024 * 1024
WIDE = 5
STEP = 2
ROWS = OWN + 16
TILES = 13


def nn(a, b):
    return lax.dot_general(a, b, (((1,), (0,)), ((), ())), preferred_element_type=F32)


def nt(a, b):
    return lax.dot_general(a, b, (((1,), (1,)), ((), ())), preferred_element_type=F32)


def tn(a, b):
    return lax.dot_general(a, b, (((0,), (0,)), ((), ())), preferred_element_type=F32)


def iota(shape, dim):
    return lax.broadcasted_iota(jnp.int32, shape, dim)


def whole(shape):
    return pl.BlockSpec(shape, lambda *_: (0,) * len(shape))


def wide(rows, pairs):
    return pl.BlockSpec((rows, pairs * 2 * P_SIZE), lambda p: (0, p))


def state_block(pairs):
    return pl.BlockSpec((pairs * 2 * P_SIZE, N), lambda p: (p, 0))


def smem():
    return pl.BlockSpec(memory_space=pltpu.SMEM)


def vmem():
    return pl.BlockSpec(memory_space=pltpu.VMEM)


def params():
    return pltpu.CompilerParams(vmem_limit_bytes=VMEM)


def cost(micros):
    return pl.CostEstimate(flops=0, bytes_accessed=int(micros * 3e6), transcendentals=0)


def column(cum_t, head):
    return jnp.sum(jnp.where(iota(cum_t.shape, 1) == head, cum_t, 0.0), axis=1, keepdims=True)


def low_half(shape):
    return iota(shape, 1) < P_SIZE


def lanes_of(i):
    return slice(i * 2 * P_SIZE, (i + 1) * 2 * P_SIZE)


def put_states(out_ref, states, first, pairs):
    chunks = pairs * 2 * P_SIZE // OWN
    rows = states.astype(BF).reshape(chunks, OWN, N)
    out_ref[pl.ds(first * 2 * P_SIZE // OWN, chunks), :OWN, :] = rows


def put_note(out_ref, pieces):
    at = iota((16, N), 0)
    note = jnp.zeros((16, N), F32)
    for i, piece in enumerate(pieces):
        note = jnp.where(at == i, piece, note)
    for s in range(N_SEQ):
        out_ref[s, OWN:, :] = note.astype(BF)


def ends_kernel(x_ref, a_ref, b_ref, cum_ref, cum_t_ref, tail_ref, out_ref, pieces):
    step = pl.program_id(0)

    @pl.when(step == 0)
    def _():
        a = a_ref[...]
        upto = (iota((T, T), 0) <= iota((T, T), 1)).astype(F32)
        cum_ref[...] = jnp.dot(a, upto, precision=HIGH, preferred_element_type=F32)
        down = (iota((T, T), 1) <= iota((T, T), 0)).astype(F32)
        cum_t = lax.dot_general(
            down, a, (((1,), (1,)), ((), ())), precision=HIGH, preferred_element_type=F32
        )
        cum_t_ref[...] = cum_t
        total = jnp.concatenate([cum_t[T - 1 :, :], jnp.zeros((1, N - H), F32)], axis=1)
        hi = jnp.floor(total)
        mid = jnp.floor((total - hi) * 256.0) / 256.0
        put_note(out_ref, (hi, mid, total - hi - mid))
        tail = jnp.exp(cum_t[T - 1 :, :] - cum_t)
        high = tail.astype(BF)
        pieces[0] = high
        pieces[1] = (tail - high.astype(F32)).astype(BF)

    width = WIDE * 2 * P_SIZE
    pick = iota((H, width), 0) == step * 2 * WIDE + iota((H, width), 1) // P_SIZE
    pick = pick.astype(BF)
    tail = nn(pieces[0], pick) + nn(pieces[1], pick)
    tail_ref[...] = tail.astype(BF)
    states = tn((x_ref[...] * tail).astype(BF), b_ref[...].astype(BF))
    put_states(out_ref, states, step * WIDE, WIDE)


def local_ends(x, a, b):
    return pl.pallas_call(
        ends_kernel,
        grid=(PAIRS // WIDE,),
        in_specs=[wide(T, WIDE), whole((H, T)), whole((T, N))],
        out_specs=[whole((H, T)), whole((T, H)), wide(T, WIDE), whole((N_SEQ, ROWS, N))],
        out_shape=[
            jax.ShapeDtypeStruct((H, T), F32),
            jax.ShapeDtypeStruct((T, H), F32),
            jax.ShapeDtypeStruct((T, D), BF),
            jax.ShapeDtypeStruct((N_SEQ, ROWS, N), BF),
        ],
        scratch_shapes=[pltpu.VMEM((2, T, H), BF)],
        compiler_params=params(),
        cost_estimate=cost(6),
        name="ends",
    )(x, a, b)


def intra_kernel(x_ref, cum_ref, cum_t_ref, b_ref, c_ref, skip_ref, y_ref, grow_ref, scores):
    step = pl.program_id(0)

    @pl.when(step == 0)
    def _():
        keep = iota((T, T), 0) >= iota((T, T), 1)
        scores[...] = jnp.where(keep, nt(c_ref[...].astype(BF), b_ref[...].astype(BF)), 0.0)

    for i in range(STEP):
        x = x_ref[:, lanes_of(i)]
        xb = x.astype(BF)
        low = low_half(x.shape)
        head = 2 * (step * STEP + i)
        parts = []
        sides = []
        for k in range(2):
            sides.append(column(cum_t_ref[...], head + k))
            diff = sides[k] - cum_ref[pl.ds(head + k, 1), :]
            mixed = (jnp.exp(jnp.minimum(diff, 0.0)) * scores[...]).astype(BF)
            parts.append(nn(mixed, xb))
        skip = jnp.where(low, skip_ref[head], skip_ref[head + 1])
        y_ref[:, lanes_of(i)] = jnp.where(low, parts[0], parts[1]) + skip * x
        grow = jnp.exp(jnp.where(low, sides[0], sides[1]))
        grow_ref[:, lanes_of(i)] = grow.astype(BF)


def intra(x, cum, cum_t, b, c, skip):
    return pl.pallas_call(
        intra_kernel,
        grid=(PAIRS // STEP,),
        in_specs=[
            wide(T, STEP), whole((H, T)), whole((T, H)), whole((T, N)), whole((T, N)), smem(),
        ],
        out_specs=[wide(T, STEP)] * 2,
        out_shape=[jax.ShapeDtypeStruct((T, D), F32), jax.ShapeDtypeStruct((T, D), BF)],
        scratch_shapes=[pltpu.VMEM((T, T), F32)],
        compiler_params=params(),
        cost_estimate=cost(9),
        name="intra",
    )(x, cum, cum_t, b, c, skip)


def inter_kernel(part_ref, grow_ref, c_ref, start_ref, y_ref):
    read = nt(c_ref[...].astype(BF), start_ref[...])
    y_ref[...] = (part_ref[...] + grow_ref[...].astype(F32) * read).astype(BF)


def inter(part, grow, c, start):
    return pl.pallas_call(
        inter_kernel,
        grid=(PAIRS // WIDE,),
        in_specs=[wide(T, WIDE), wide(T, WIDE), whole((T, N)), state_block(WIDE)],
        out_specs=wide(T, WIDE),
        out_shape=jax.ShapeDtypeStruct((T, D), BF),
        compiler_params=params(),
        cost_estimate=cost(5),
        name="inter",
    )(part, grow, c, start)


def chain_kernel(reverse, mine_ref, parts_ref, totals_ref, out_ref):
    owner = (mine_ref[0] * OWN + iota((OWN, N), 0)) // P_SIZE == iota((OWN, N), 1)
    carry = jnp.zeros((OWN, N), F32)
    for s in range(N_SEQ - 1, -1, -1) if reverse else range(N_SEQ):
        out_ref[s] = carry.astype(BF)
        pieces = totals_ref[s, OWN:, :].astype(F32)
        total = pieces[0:1, :] + pieces[1:2, :] + pieces[2:3, :]
        decay = jnp.sum(jnp.where(owner, total, 0.0), axis=1, keepdims=True)
        carry = jnp.exp(decay) * carry + parts_ref[s, :OWN, :].astype(F32)


def chain(parts, totals, mine, reverse):
    return pl.pallas_call(
        functools.partial(chain_kernel, reverse),
        in_specs=[smem(), vmem(), vmem()],
        out_specs=vmem(),
        out_shape=jax.ShapeDtypeStruct((N_SEQ, OWN, N), BF),
        compiler_params=params(),
        cost_estimate=cost(3),
        name="chain",
    )(mine, parts, totals)


def swap(v, axis):
    return lax.all_to_all(v, axis, 0, 0, tiled=True)


def term_kernel(at_ref, yo_ref, yx_ref, g_ref, first_ref, second_ref):
    half = g_ref.shape[1] // 2
    term = tn(jnp.concatenate([yo_ref[...], yx_ref[...]], axis=0), g_ref[...]).astype(BF)
    for k in range(4):
        rows = slice(k * OWN, (k + 1) * OWN)
        first_ref[k, 0] = term[rows, :half]
        second_ref[0, (k + 4 - at_ref[1]) % 4] = term[rows, half:]


def terms(at, y_own, y_other, g):
    rows = pl.BlockSpec((T, 4 * OWN), lambda i, at: (0, (at[0] + i) % 4))
    half = g.shape[1] // 2
    return pl.pallas_call(
        term_kernel,
        grid_spec=pltpu.PrefetchScalarGridSpec(
            num_scalar_prefetch=1,
            grid=(4,),
            in_specs=[rows, rows, whole(g.shape)],
            out_specs=[
                pl.BlockSpec((4, 1, OWN, half), lambda i, at: (0, i, 0, 0)),
                pl.BlockSpec((1, 4, OWN, half), lambda i, at: (i, 0, 0, 0)),
            ],
        ),
        out_shape=[jax.ShapeDtypeStruct((4, 4, OWN, half), BF)] * 2,
        compiler_params=params(),
        cost_estimate=cost(8),
        name="terms",
    )(at, y_own, y_other, g)


def gy_kernel(g_ref, w_ref, own_ref, other_ref):
    got = nt(g_ref[...], w_ref[...])
    own_ref[...] = got[:T]
    other_ref[...] = got[T:].astype(BF)


def gy_parts(g, w):
    rows = 4 * OWN
    return pl.pallas_call(
        gy_kernel,
        grid=(4,),
        in_specs=[whole(g.shape), pl.BlockSpec((rows, w.shape[1]), lambda i: (i, 0))],
        out_specs=[pl.BlockSpec((T, rows), lambda i: (0, i))] * 2,
        out_shape=[jax.ShapeDtypeStruct((T, D), F32), jax.ShapeDtypeStruct((T, D), BF)],
        compiler_params=params(),
        cost_estimate=cost(8),
        name="gy_parts",
    )(g, w)


def entry_kernel(own_ref, other_ref, x_ref, grow_ref, c_ref, gy_ref, out_ref, sums):
    step = pl.program_id(0)
    c = c_ref[...].astype(BF)
    found = []
    for i in range(WIDE):
        at = lanes_of(i)
        gy = own_ref[:, at] + other_ref[:, at].astype(F32)
        gy_ref[:, at] = gy.astype(BF)
        sums[pl.ds(step * WIDE + i, 1), :] = jnp.sum(gy * x_ref[:, at], axis=0, keepdims=True)
        found.append(tn((gy * grow_ref[:, at].astype(F32)).astype(BF), c))
    put_states(out_ref, jnp.concatenate(found, axis=0), step * WIDE, WIDE)

    @pl.when(step == PAIRS // WIDE - 1)
    def _():
        total = sums[...]
        low = low_half(total.shape)
        head = 2 * iota(total.shape, 0)
        lane = iota(total.shape, 1)
        even = jnp.sum(jnp.where(low, total, 0.0), axis=1, keepdims=True)
        odd = jnp.sum(jnp.where(low, 0.0, total), axis=1, keepdims=True)
        each = jnp.where(lane == head, even, 0.0) + jnp.where(lane == head + 1, odd, 0.0)
        gd = jnp.sum(each, axis=0, keepdims=True)
        hi = gd.astype(BF).astype(F32)
        mid = (gd - hi).astype(BF).astype(F32)
        put_note(out_ref, (hi, mid, gd - hi - mid))


def entries(own, other, x, grow, c):
    return pl.pallas_call(
        entry_kernel,
        grid=(PAIRS // WIDE,),
        in_specs=[wide(T, WIDE)] * 4 + [whole((T, N))],
        out_specs=[wide(T, WIDE), whole((N_SEQ, ROWS, N))],
        out_shape=[
            jax.ShapeDtypeStruct((T, D), BF),
            jax.ShapeDtypeStruct((N_SEQ, ROWS, N), BF),
        ],
        scratch_shapes=[pltpu.VMEM((PAIRS, 2 * P_SIZE), F32)],
        compiler_params=params(),
        cost_estimate=cost(6),
        name="entries",
    )(own, other, x, grow, c)


def within_kernel(
    first, steps, x_ref, gy_ref, cum_ref, cum_t_ref, b_ref, c_ref, skip_ref, *rest
):
    before = rest[:-8]
    gx_ref, ga_ref, gb_ref, gc_ref, scores, d_scores, rows, cols = rest[-8:]
    step = pl.program_id(0)

    @pl.when(step == 0)
    def _():
        keep = iota((T, T), 1) >= iota((T, T), 0)
        scores[...] = jnp.where(keep, nt(b_ref[...].astype(BF), c_ref[...].astype(BF)), 0.0)
        d_scores[...] = jnp.zeros_like(d_scores)
        rows[...] = jnp.zeros_like(rows)
        cols[...] = jnp.zeros_like(cols)

    lanes = iota((T, N), 1)
    low = low_half((T, 2 * P_SIZE))
    for i in range(STEP):
        pair = (first + step) * STEP + i
        at = lanes_of(i)
        x = x_ref[:, at]
        gyb = gy_ref[:, at]
        parts = []
        for k in range(2):
            head = 2 * pair + k
            diff = cum_ref[pl.ds(head, 1), :] - column(cum_t_ref[...], head)
            weights = jnp.exp(jnp.minimum(diff, 0.0))
            mine = jnp.where(low if k == 0 else ~low, x, 0.0).astype(BF)
            d_mixed = weights * nt(mine, gyb)
            d_scores[...] += d_mixed
            parts.append(nn((weights * scores[...]).astype(BF), gyb))
            change = d_mixed * scores[...]
            rows[pl.ds(head, 1), :] = jnp.sum(change, axis=0, keepdims=True)
            down = jnp.sum(change, axis=1, keepdims=True)
            cols[...] -= jnp.where(lanes == head, down, 0.0)
        skip = jnp.where(low, skip_ref[2 * pair], skip_ref[2 * pair + 1])
        gx_ref[:, at] = jnp.where(low, parts[0], parts[1]) + skip * gyb.astype(F32)

    @pl.when(step == steps - 1)
    def _():
        keep = iota((T, T), 1) >= iota((T, T), 0)
        ds = jnp.where(keep, d_scores[...], 0.0).astype(BF)
        gb = nn(ds, c_ref[...].astype(BF))
        gc = tn(ds, b_ref[...].astype(BF))
        after = (iota((T, T), 0) >= iota((T, T), 1)).astype(F32)
        dims = (((0,), (0,)), ((), ()))
        ga = jnp.dot(rows[...], after, precision=HIGH, preferred_element_type=F32)
        up = lax.dot_general(cols[...], after, dims, precision=HIGH, preferred_element_type=F32)
        for out, add, ref in zip((ga_ref, gb_ref, gc_ref), (ga + up[:H], gb, gc), before or (None,) * 3):
            out[...] = add if ref is None else add + ref[...]


def within(first, steps, x, gy, cum, cum_t, b, c, skip, before=()):
    here = pl.BlockSpec((T, STEP * 2 * P_SIZE), lambda p: (0, first + p))
    return pl.pallas_call(
        functools.partial(within_kernel, first, steps),
        grid=(steps,),
        in_specs=[
            here, here, whole((H, T)), whole((T, H)), whole((T, N)), whole((T, N)), smem(),
        ]
        + [whole(v.shape) for v in before],
        out_specs=[wide(T, STEP), whole((H, T)), whole((T, N)), whole((T, N))],
        out_shape=[
            jax.ShapeDtypeStruct((T, steps * STEP * 2 * P_SIZE), F32),
            jax.ShapeDtypeStruct((H, T), F32),
            jax.ShapeDtypeStruct((T, N), F32),
            jax.ShapeDtypeStruct((T, N), F32),
        ],
        scratch_shapes=[
            pltpu.VMEM((T, T), F32),
            pltpu.VMEM((T, T), F32),
            pltpu.VMEM((H, T), F32),
            pltpu.VMEM((T, N), F32),
        ],
        compiler_params=params(),
        cost_estimate=cost(7),
        name="within",
    )(x, gy, cum, cum_t, b, c, skip, *before)


def across_kernel(
    x_ref, gy_ref, grow_ref, tail_ref, part_ref, part2_ref, cum_ref, b_ref, c_ref, start_ref, last_ref,
    ga_in, gb_in, gc_in,
    gx_ref, ga_ref, gb_ref, gc_ref,
    cols, tails, totals,
):
    step = pl.program_id(0)
    bb = b_ref[...].astype(BF)
    cb = c_ref[...].astype(BF)

    @pl.when(step == 0)
    def _():
        cols[...] = jnp.zeros_like(cols)
        tails[...] = jnp.zeros_like(tails)
        gb_ref[...] = gb_in[...]
        gc_ref[...] = gc_in[...]

    width = WIDE * 2 * P_SIZE
    start = start_ref[...]
    last = last_ref[...]
    tail = tail_ref[...].astype(F32)
    pick = iota((width, N), 1) == step * 2 * WIDE + iota((width, N), 0) // P_SIZE
    grown = gy_ref[...].astype(F32) * grow_ref[...].astype(F32)
    cols[...] += nn((grown * nt(cb, start)).astype(BF), pick.astype(BF))
    gc_ref[...] += nn(grown.astype(BF), start)
    faded = x_ref[...] * tail
    back = nt(bb, last)
    tails[...] += nn((faded * back).astype(BF), pick.astype(BF))
    gb_ref[...] += nn(faded.astype(BF), last)
    part = jnp.where(step < PAIRS // WIDE // 2, part_ref[...], part2_ref[...])
    gx_ref[...] = part + tail * back
    both = jnp.sum(start.astype(F32) * last.astype(F32), axis=1, keepdims=True)
    totals[pl.ds(step, 1), :] = jnp.sum(jnp.where(pick, both, 0.0), axis=0, keepdims=True)

    @pl.when(step == PAIRS // WIDE - 1)
    def _():
        after = (iota((T, T), 0) >= iota((T, T), 1)).astype(F32)
        before = (iota((T, T), 0) < iota((T, T), 1)).astype(F32)
        dims = (((0,), (0,)), ((), ()))
        up = lax.dot_general(cols[...], after, dims, precision=HIGH, preferred_element_type=F32)
        up += lax.dot_general(tails[...], before, dims, precision=HIGH, preferred_element_type=F32)
        total = jnp.sum(totals[...], axis=0, keepdims=True)
        total = jnp.sum(jnp.where(iota((H, N), 0) == iota((H, N), 1), total, 0.0), axis=1, keepdims=True)
        ga_ref[...] = ga_in[...] + up[:H] + jnp.exp(cum_ref[:, T - 1 : T]) * total


def across(x, gy, grow, tail, part, part2, cum, b, c, start, last, ga, gb, gc):
    width = WIDE * 2 * P_SIZE
    last_part = PAIRS // WIDE // 2 - 1
    return pl.pallas_call(
        across_kernel,
        grid=(PAIRS // WIDE,),
        in_specs=[wide(T, WIDE)] * 4
        + [
            pl.BlockSpec((T, width), lambda p: (0, jnp.minimum(p, last_part))),
            pl.BlockSpec((T, width), lambda p: (0, jnp.maximum(p - last_part - 1, 0))),
        ]
        + [whole((H, T)), whole((T, N)), whole((T, N))]
        + [state_block(WIDE), state_block(WIDE), whole((H, T)), whole((T, N)), whole((T, N))],
        out_specs=[wide(T, WIDE), whole((H, T)), whole((T, N)), whole((T, N))],
        out_shape=[
            jax.ShapeDtypeStruct((T, D), F32),
            jax.ShapeDtypeStruct((H, T), F32),
            jax.ShapeDtypeStruct((T, N), F32),
            jax.ShapeDtypeStruct((T, N), F32),
        ],
        scratch_shapes=[
            pltpu.VMEM((T, N), F32),
            pltpu.VMEM((T, N), F32),
            pltpu.VMEM((PAIRS // WIDE, N), F32),
        ],
        compiler_params=params(),
        cost_estimate=cost(8),
        name="across",
    )(x, gy, grow, tail, part, part2, cum, b, c, start, last, ga, gb, gc)


def fold_kernel(a0, a1, a2, a3, b0, b1, b2, b3, out_ref):
    sums = []
    for parts in ((a0, a1, a2, a3), (b0, b1, b2, b3)):
        total = parts[0][...].astype(F32)
        for part in parts[1:]:
            total += part[...].astype(F32)
        sums.append(total.astype(BF))
    for q in range(8 * TILES):
        r, c = divmod(q, 10)
        if r < 10:
            tile = sums[c // 5][16 * r : 16 * r + 16, 128 * (c % 5) : 128 * (c % 5) + 128]
        else:
            tile = jnp.zeros((16, 128), BF)
        out_ref[q // TILES, q % TILES] = tile


def fold(parts):
    return pl.pallas_call(
        fold_kernel,
        in_specs=[vmem()] * 8,
        out_specs=vmem(),
        out_shape=jax.ShapeDtypeStruct((8, TILES, 16, 128), BF),
        compiler_params=params(),
        cost_estimate=cost(3),
        name="fold",
    )(*parts)


def groups_of(row0, count, ids_ref):
    heads = (row0 + iota((count, N), 0)) // P_SIZE == iota((count, N), 1)
    return jnp.sum(jnp.where(heads, ids_ref[...], 0.0), axis=1, keepdims=True)


def zsum_kernel(row0_ref, z_ref, ids_ref, got_ref, parts_ref, out_ref, note_ref):
    total = parts_ref[0].astype(F32)
    for z in range(1, 8):
        total += parts_ref[z].astype(F32)
    for s in range(8):
        out_ref[s] = total.astype(BF)
    found = jnp.zeros((16, N), F32)
    for i in range(TILES):
        row = row0_ref[0] + 16 * ((z_ref[0] * TILES + i) // 10)
        place = iota((16, N), 1) - H == groups_of(row, 16, ids_ref).astype(jnp.int32)
        tile = total[i]
        found += jnp.where(place, jnp.sum(tile * tile, axis=1, keepdims=True), 0.0)
    d_sum = jnp.zeros((1, N), F32)
    for s in range(N_SEQ):
        pieces = got_ref[s, OWN:, :].astype(F32)
        d_sum += pieces[0:1, :] + pieces[1:2, :] + pieces[2:3, :]
    note_ref[...] = jnp.sum(found, axis=0, keepdims=True) + d_sum / N_SEQ


def zsum(row0, z, ids, parts, got):
    return pl.pallas_call(
        zsum_kernel,
        in_specs=[smem(), smem()] + [vmem()] * 3,
        out_specs=[vmem(), vmem()],
        out_shape=[
            jax.ShapeDtypeStruct((8, TILES, 16, 128), BF),
            jax.ShapeDtypeStruct((1, N), F32),
        ],
        compiler_params=params(),
        cost_estimate=cost(2),
        name="zsum",
    )(row0, z, ids, got, parts)


def tile_of(ref, r, c):
    z, i = divmod(10 * r + c, TILES)
    return ref[z, i].astype(F32)


def clip_kernel(tokens_all, row0_ref, core_ref, ids_ref, own_ref, other_ref, note_ref, w_ref, d_ref):
    ids = ids_ref[...]
    lane = iota((1, N), 1)
    note = note_ref[...]
    grad_d = jnp.where(lane < H, note, 0.0)
    groups = groups_of(row0_ref[0], OWN, ids_ref)
    w_factor = jnp.zeros((OWN, 1), F32)
    d_factor = jnp.zeros((1, N), F32)
    for g in range(GROUPS):
        here = (ids == float(g)) & (lane < H)
        count = jnp.sum(jnp.where(here, 1.0, 0.0), axis=1, keepdims=True)
        sumsq = jnp.sum(jnp.where(lane == H + g, note, 0.0), axis=1, keepdims=True)
        sumsq += jnp.sum(jnp.where(here, grad_d * grad_d, 0.0), axis=1, keepdims=True)
        bound = 7.0 * jnp.sqrt(count * (P_SIZE * D + 1.0) * tokens_all)
        factor = jnp.minimum(1.0, bound / jnp.sqrt(sumsq + 1e-06))
        w_factor += jnp.where(groups == float(g), factor, 0.0)
        d_factor += jnp.where(here, factor, 0.0)
    d_ref[...] = grad_d * d_factor
    for r in range(10):
        scale = w_factor[16 * r : 16 * r + 16, :]
        for ref, core in ((own_ref, core_ref[0]), (other_ref, 1 - core_ref[0])):
            for c in range(10):
                col = pl.multiple_of(core * (D // 2) + 128 * c, 128)
                w_ref[16 * r : 16 * r + 16, pl.ds(col, 128)] = tile_of(ref, r, c) * scale


def clip(tokens_all, row0, core, ids, own, other, note):
    return pl.pallas_call(
        functools.partial(clip_kernel, tokens_all),
        in_specs=[smem(), smem()] + [vmem()] * 4,
        out_specs=[vmem(), vmem()],
        out_shape=[jax.ShapeDtypeStruct((OWN, D), F32), jax.ShapeDtypeStruct((1, N), F32)],
        compiler_params=params(),
        cost_estimate=cost(3),
        name="clip",
    )(row0, core, ids, own, other, note)


def shifted(v, axis, d):
    return lax.ppermute(v, axis, [(i, (i + d) % 4) for i in range(4)])


def plus(a, b):
    return (a.astype(F32) + b.astype(F32)).astype(BF)


def far(t, axis):
    m = t.shape[1] // 2
    return shifted(t[2, :m], axis, 1), shifted(t[2, m:], axis, -1)


def passed(t, ra, rb):
    m = t.shape[1] // 2
    up = jnp.concatenate([plus(t[1, :m], ra), t[1, m:]], axis=0)
    down = jnp.concatenate([t[3, :m], plus(t[3, m:], rb)], axis=0)
    return up, down


def near(t, up, down, axis):
    total = t[0].astype(F32) + shifted(up, axis, 1).astype(F32)
    return (total + shifted(down, axis, -1).astype(F32)).astype(BF)


def direct(t, axis):
    return (t[0],) + tuple(shifted(t[d], axis, d) for d in (1, 3, 2))


def other_core(v):
    return lax.ppermute(v, "core", [(0, 1), (1, 0)])


def sum_over(v, axes):
    for unit in (1, 4):
        got = [
            lax.ppermute(v, axes, [(i, i ^ (unit * k)) for i in range(16)]) for k in (1, 2, 3)
        ]
        v = (v + got[0]) + (got[1] + got[2])
    return v


def tie(*values):
    return lax.optimization_barrier(values)


def per_device(x_in, a_log, b_in, c_in, g_out, w_out, d_skip, group_ids):
    x, a, b, c, g = (x_in[0], a_log[0], b_in[0], c_in[0], g_out[0])
    core = lax.axis_index("core")
    half = D // 2
    at = jnp.stack([lax.axis_index("y"), lax.axis_index("x")]).astype(jnp.int32)
    mine = (2 * lax.axis_index("z") + core).reshape(1).astype(jnp.int32)
    at_z = lax.axis_index("z").reshape(1).astype(jnp.int32)
    row0 = ((4 * at[0] + at[1]) * OWN).reshape(1)
    ids = jnp.pad(group_ids.astype(F32), (0, N - H), constant_values=-1.0)[None]
    tokens_all = float(T * N_SEQ * 16)

    g_mine = lax.dynamic_slice_in_dim(g, core * half, half, axis=1)
    g_other = other_core(lax.dynamic_slice_in_dim(g, (1 - core) * half, half, axis=1))

    g_both = jnp.concatenate([g_mine, g_other], axis=0)

    cum, cum_t, tail, sent = local_ends(x, a, b)
    w_out, sent = tie(w_out, sent)
    w_mine = lax.dynamic_slice_in_dim(w_out, core * half, half, axis=1)
    w_half = lax.all_gather(w_mine, ("y", "x"), axis=0, tiled=True)
    got = swap(sent, SEQ)
    y_part, grow = intra(x, cum, cum_t, b, c, d_skip)
    start = swap(chain(got, got, mine, False), SEQ).reshape(H * P_SIZE, N)
    y_own = inter(y_part, grow, c, start)
    y_other = other_core(y_own)
    first, second = terms(at, y_own, y_other, g_both)

    first = lax.psum_scatter(first.reshape(-1, half // 2), "x", scatter_dimension=0, tiled=True)
    far_y = far(second, "y")
    w_half, _ = tie(w_half, second)
    gy_own, gy_other = gy_parts(g_both, w_half)
    *far_y, gy_own, gy_other = tie(*far_y, gy_own, gy_other)
    gy_other = other_core(gy_other)
    up, down = passed(second, *far_y)
    up, down, gy_own, gy_other = tie(up, down, gy_own, gy_other)
    second = near(second, up, down, "y")
    gy, sent_back = entries(gy_own, gy_other, x, grow, c)
    got_back = swap(sent_back, SEQ)
    steps = PAIRS // STEP // 2
    gx1, *sums = within(0, steps, x, gy, cum, cum_t, b, c, d_skip)
    first, second, gx1 = tie(first, second, gx1)
    first = direct(first.reshape(4, OWN, half // 2), "y")
    second = direct(second, "x")
    tiles = fold(first + second)
    gy, mine, tiles = tie(gy, mine, tiles)
    tiles = swap(tiles, "z")
    states = chain(got_back, got, mine, True)
    gx2, *sums = within(steps, steps, x, gy, cum, cum_t, b, c, d_skip, sums)
    tiles, gx2, states = tie(tiles, gx2, states)
    tiles, note = zsum(row0, at_z, ids, tiles, got_back)
    note, states = tie(note, states)
    last = swap(states, SEQ).reshape(H * P_SIZE, N)
    tiles, last = tie(tiles, last)
    tiles = swap(tiles, "z")
    note = sum_over(sum_over(note, ("y", "x")), SEQ)
    last, note = tie(last, note)
    gx, ga, gb, gc = across(x, gy, grow, tail, gx1, gx2, cum, b, c, start, last, *sums)
    tiles, ga = tie(tiles, ga)
    tiles_other = other_core(tiles)
    core = core.reshape(1).astype(jnp.int32)
    clipped_w, clipped_d = clip(tokens_all, row0, core, ids, tiles, tiles_other, note)
    return (gx[None], ga[None], gb[None], gc[None], clipped_w, clipped_d[0, :H])


def solution(mesh):
    fine = Mesh(mesh.devices.reshape(4, 4, 8, 2), ("y", "x", "z", "core"))
    rows = ("y", "x")
    tokens = P(rows, SEQ, None)
    return jax.shard_map(
        per_device,
        mesh=fine,
        in_specs=(
            tokens, P(rows, None, SEQ), tokens, tokens, tokens, P(rows, None), P(), P(),
        ),
        out_specs=(tokens, P(rows, None, SEQ), tokens, tokens, P(rows, None), P()),
        check_vma=False,
    )
```

```python
import functools

import jax
import jax.numpy as jnp
from jax import lax
from jax.experimental import pallas as pl
from jax.experimental.pallas import tpu as pltpu
from jax.sharding import Mesh
from jax.sharding import PartitionSpec as P

D = 2560
H = 40
P_SIZE = 64
N = 128
T = 256
GROUPS = 4
PAIRS = H // 2
SEQ = ("z", "core")
N_SEQ = 16
OWN = H * P_SIZE // N_SEQ
HIGH = lax.Precision.HIGHEST
BF = jnp.bfloat16
F32 = jnp.float32
VMEM = 56 * 1024 * 1024
WIDE = 5
STEP = 2
ROWS = OWN + 16
TILES = 13


def nn(a, b):
    return lax.dot_general(a, b, (((1,), (0,)), ((), ())), preferred_element_type=F32)


def nt(a, b):
    return lax.dot_general(a, b, (((1,), (1,)), ((), ())), preferred_element_type=F32)


def tn(a, b):
    return lax.dot_general(a, b, (((0,), (0,)), ((), ())), preferred_element_type=F32)


def iota(shape, dim):
    return lax.broadcasted_iota(jnp.int32, shape, dim)


def whole(shape):
    return pl.BlockSpec(shape, lambda *_: (0,) * len(shape))


def wide(rows, pairs):
    return pl.BlockSpec((rows, pairs * 2 * P_SIZE), lambda p: (0, p))


def state_block(pairs):
    return pl.BlockSpec((pairs * 2 * P_SIZE, N), lambda p: (p, 0))


def smem():
    return pl.BlockSpec(memory_space=pltpu.SMEM)


def vmem():
    return pl.BlockSpec(memory_space=pltpu.VMEM)


def params():
    return pltpu.CompilerParams(vmem_limit_bytes=VMEM)


def cost(micros):
    return pl.CostEstimate(flops=0, bytes_accessed=int(micros * 3e6), transcendentals=0)


def column(cum_t, head):
    return jnp.sum(jnp.where(iota(cum_t.shape, 1) == head, cum_t, 0.0), axis=1, keepdims=True)


def low_half(shape):
    return iota(shape, 1) < P_SIZE


def lanes_of(i):
    return slice(i * 2 * P_SIZE, (i + 1) * 2 * P_SIZE)


def put_states(out_ref, states, first, pairs):
    chunks = pairs * 2 * P_SIZE // OWN
    rows = states.astype(BF).reshape(chunks, OWN, N)
    out_ref[pl.ds(first * 2 * P_SIZE // OWN, chunks), :OWN, :] = rows


def put_note(out_ref, pieces):
    at = iota((16, N), 0)
    note = jnp.zeros((16, N), F32)
    for i, piece in enumerate(pieces):
        note = jnp.where(at == i, piece, note)
    for s in range(N_SEQ):
        out_ref[s, OWN:, :] = note.astype(BF)


def ends_kernel(x_ref, a_ref, b_ref, cum_ref, cum_t_ref, tail_ref, out_ref, pieces):
    step = pl.program_id(0)

    @pl.when(step == 0)
    def _():
        a = a_ref[...]
        upto = (iota((T, T), 0) <= iota((T, T), 1)).astype(F32)
        cum_ref[...] = jnp.dot(a, upto, precision=HIGH, preferred_element_type=F32)
        down = (iota((T, T), 1) <= iota((T, T), 0)).astype(F32)
        cum_t = lax.dot_general(
            down, a, (((1,), (1,)), ((), ())), precision=HIGH, preferred_element_type=F32
        )
        cum_t_ref[...] = cum_t
        total = jnp.concatenate([cum_t[T - 1 :, :], jnp.zeros((1, N - H), F32)], axis=1)
        hi = jnp.floor(total)
        mid = jnp.floor((total - hi) * 256.0) / 256.0
        put_note(out_ref, (hi, mid, total - hi - mid))
        tail = jnp.exp(cum_t[T - 1 :, :] - cum_t)
        high = tail.astype(BF)
        pieces[0] = high
        pieces[1] = (tail - high.astype(F32)).astype(BF)

    width = WIDE * 2 * P_SIZE
    pick = iota((H, width), 0) == step * 2 * WIDE + iota((H, width), 1) // P_SIZE
    pick = pick.astype(BF)
    tail = nn(pieces[0], pick) + nn(pieces[1], pick)
    tail_ref[...] = tail.astype(BF)
    states = tn((x_ref[...] * tail).astype(BF), b_ref[...].astype(BF))
    put_states(out_ref, states, step * WIDE, WIDE)


def local_ends(x, a, b):
    return pl.pallas_call(
        ends_kernel,
        grid=(PAIRS // WIDE,),
        in_specs=[wide(T, WIDE), whole((H, T)), whole((T, N))],
        out_specs=[whole((H, T)), whole((T, H)), wide(T, WIDE), whole((N_SEQ, ROWS, N))],
        out_shape=[
            jax.ShapeDtypeStruct((H, T), F32),
            jax.ShapeDtypeStruct((T, H), F32),
            jax.ShapeDtypeStruct((T, D), BF),
            jax.ShapeDtypeStruct((N_SEQ, ROWS, N), BF),
        ],
        scratch_shapes=[pltpu.VMEM((2, T, H), BF)],
        compiler_params=params(),
        cost_estimate=cost(6),
        name="ends",
    )(x, a, b)


def intra_kernel(x_ref, cum_ref, cum_t_ref, b_ref, c_ref, skip_ref, y_ref, grow_ref, scores):
    step = pl.program_id(0)

    @pl.when(step == 0)
    def _():
        keep = iota((T, T), 0) >= iota((T, T), 1)
        scores[...] = jnp.where(keep, nt(c_ref[...].astype(BF), b_ref[...].astype(BF)), 0.0)

    for i in range(STEP):
        x = x_ref[:, lanes_of(i)]
        xb = x.astype(BF)
        low = low_half(x.shape)
        head = 2 * (step * STEP + i)
        parts = []
        sides = []
        for k in range(2):
            sides.append(column(cum_t_ref[...], head + k))
            diff = sides[k] - cum_ref[pl.ds(head + k, 1), :]
            mixed = (jnp.exp(jnp.minimum(diff, 0.0)) * scores[...]).astype(BF)
            parts.append(nn(mixed, xb))
        skip = jnp.where(low, skip_ref[head], skip_ref[head + 1])
        y_ref[:, lanes_of(i)] = jnp.where(low, parts[0], parts[1]) + skip * x
        grow = jnp.exp(jnp.where(low, sides[0], sides[1]))
        grow_ref[:, lanes_of(i)] = grow.astype(BF)


def intra(x, cum, cum_t, b, c, skip):
    return pl.pallas_call(
        intra_kernel,
        grid=(PAIRS // STEP,),
        in_specs=[
            wide(T, STEP), whole((H, T)), whole((T, H)), whole((T, N)), whole((T, N)), smem(),
        ],
        out_specs=[wide(T, STEP)] * 2,
        out_shape=[jax.ShapeDtypeStruct((T, D), F32), jax.ShapeDtypeStruct((T, D), BF)],
        scratch_shapes=[pltpu.VMEM((T, T), F32)],
        compiler_params=params(),
        cost_estimate=cost(9),
        name="intra",
    )(x, cum, cum_t, b, c, skip)


def inter_kernel(part_ref, grow_ref, c_ref, start_ref, y_ref):
    read = nt(c_ref[...].astype(BF), start_ref[...])
    y_ref[...] = (part_ref[...] + grow_ref[...].astype(F32) * read).astype(BF)


def inter(part, grow, c, start):
    return pl.pallas_call(
        inter_kernel,
        grid=(PAIRS // WIDE,),
        in_specs=[wide(T, WIDE), wide(T, WIDE), whole((T, N)), state_block(WIDE)],
        out_specs=wide(T, WIDE),
        out_shape=jax.ShapeDtypeStruct((T, D), BF),
        compiler_params=params(),
        cost_estimate=cost(5),
        name="inter",
    )(part, grow, c, start)


def chain_kernel(reverse, mine_ref, parts_ref, totals_ref, out_ref):
    owner = (mine_ref[0] * OWN + iota((OWN, N), 0)) // P_SIZE == iota((OWN, N), 1)
    carry = jnp.zeros((OWN, N), F32)
    for s in range(N_SEQ - 1, -1, -1) if reverse else range(N_SEQ):
        out_ref[s] = carry.astype(BF)
        pieces = totals_ref[s, OWN:, :].astype(F32)
        total = pieces[0:1, :] + pieces[1:2, :] + pieces[2:3, :]
        decay = jnp.sum(jnp.where(owner, total, 0.0), axis=1, keepdims=True)
        carry = jnp.exp(decay) * carry + parts_ref[s, :OWN, :].astype(F32)


def chain(parts, totals, mine, reverse):
    return pl.pallas_call(
        functools.partial(chain_kernel, reverse),
        in_specs=[smem(), vmem(), vmem()],
        out_specs=vmem(),
        out_shape=jax.ShapeDtypeStruct((N_SEQ, OWN, N), BF),
        compiler_params=params(),
        cost_estimate=cost(3),
        name="chain",
    )(mine, parts, totals)


def swap(v, axis):
    return lax.all_to_all(v, axis, 0, 0, tiled=True)


def term_kernel(at_ref, yo_ref, yx_ref, g_ref, first_ref, second_ref):
    half = g_ref.shape[1] // 2
    term = tn(jnp.concatenate([yo_ref[...], yx_ref[...]], axis=0), g_ref[...]).astype(BF)
    for k in range(4):
        rows = slice(k * OWN, (k + 1) * OWN)
        first_ref[k, 0] = term[rows, :half]
        second_ref[0, (k + 4 - at_ref[1]) % 4] = term[rows, half:]


def terms(at, y_own, y_other, g):
    rows = pl.BlockSpec((T, 4 * OWN), lambda i, at: (0, (at[0] + i) % 4))
    half = g.shape[1] // 2
    return pl.pallas_call(
        term_kernel,
        grid_spec=pltpu.PrefetchScalarGridSpec(
            num_scalar_prefetch=1,
            grid=(4,),
            in_specs=[rows, rows, whole(g.shape)],
            out_specs=[
                pl.BlockSpec((4, 1, OWN, half), lambda i, at: (0, i, 0, 0)),
                pl.BlockSpec((1, 4, OWN, half), lambda i, at: (i, 0, 0, 0)),
            ],
        ),
        out_shape=[jax.ShapeDtypeStruct((4, 4, OWN, half), BF)] * 2,
        compiler_params=params(),
        cost_estimate=cost(8),
        name="terms",
    )(at, y_own, y_other, g)


def gy_kernel(g_ref, w_ref, own_ref, other_ref):
    got = nt(g_ref[...], w_ref[...])
    own_ref[...] = got[:T]
    other_ref[...] = got[T:].astype(BF)


def gy_parts(g, w):
    rows = 4 * OWN
    return pl.pallas_call(
        gy_kernel,
        grid=(4,),
        in_specs=[whole(g.shape), pl.BlockSpec((rows, w.shape[1]), lambda i: (i, 0))],
        out_specs=[pl.BlockSpec((T, rows), lambda i: (0, i))] * 2,
        out_shape=[jax.ShapeDtypeStruct((T, D), F32), jax.ShapeDtypeStruct((T, D), BF)],
        compiler_params=params(),
        cost_estimate=cost(8),
        name="gy_parts",
    )(g, w)


def entry_kernel(own_ref, other_ref, x_ref, grow_ref, c_ref, gy_ref, out_ref, sums):
    step = pl.program_id(0)
    c = c_ref[...].astype(BF)
    found = []
    for i in range(WIDE):
        at = lanes_of(i)
        gy = own_ref[:, at] + other_ref[:, at].astype(F32)
        gy_ref[:, at] = gy.astype(BF)
        sums[pl.ds(step * WIDE + i, 1), :] = jnp.sum(gy * x_ref[:, at], axis=0, keepdims=True)
        found.append(tn((gy * grow_ref[:, at].astype(F32)).astype(BF), c))
    put_states(out_ref, jnp.concatenate(found, axis=0), step * WIDE, WIDE)

    @pl.when(step == PAIRS // WIDE - 1)
    def _():
        total = sums[...]
        low = low_half(total.shape)
        head = 2 * iota(total.shape, 0)
        lane = iota(total.shape, 1)
        even = jnp.sum(jnp.where(low, total, 0.0), axis=1, keepdims=True)
        odd = jnp.sum(jnp.where(low, 0.0, total), axis=1, keepdims=True)
        each = jnp.where(lane == head, even, 0.0) + jnp.where(lane == head + 1, odd, 0.0)
        gd = jnp.sum(each, axis=0, keepdims=True)
        hi = gd.astype(BF).astype(F32)
        mid = (gd - hi).astype(BF).astype(F32)
        put_note(out_ref, (hi, mid, gd - hi - mid))


def entries(own, other, x, grow, c):
    return pl.pallas_call(
        entry_kernel,
        grid=(PAIRS // WIDE,),
        in_specs=[wide(T, WIDE)] * 4 + [whole((T, N))],
        out_specs=[wide(T, WIDE), whole((N_SEQ, ROWS, N))],
        out_shape=[
            jax.ShapeDtypeStruct((T, D), BF),
            jax.ShapeDtypeStruct((N_SEQ, ROWS, N), BF),
        ],
        scratch_shapes=[pltpu.VMEM((PAIRS, 2 * P_SIZE), F32)],
        compiler_params=params(),
        cost_estimate=cost(6),
        name="entries",
    )(own, other, x, grow, c)


def within_kernel(
    first, steps, x_ref, gy_ref, cum_ref, cum_t_ref, b_ref, c_ref, skip_ref, *rest
):
    before = rest[:-8]
    gx_ref, ga_ref, gb_ref, gc_ref, scores, d_scores, rows, cols = rest[-8:]
    step = pl.program_id(0)

    @pl.when(step == 0)
    def _():
        keep = iota((T, T), 1) >= iota((T, T), 0)
        scores[...] = jnp.where(keep, nt(b_ref[...].astype(BF), c_ref[...].astype(BF)), 0.0)
        d_scores[...] = jnp.zeros_like(d_scores)
        rows[...] = jnp.zeros_like(rows)
        cols[...] = jnp.zeros_like(cols)

    lanes = iota((T, N), 1)
    low = low_half((T, 2 * P_SIZE))
    for i in range(STEP):
        pair = (first + step) * STEP + i
        at = lanes_of(i)
        x = x_ref[:, at]
        gyb = gy_ref[:, at]
        parts = []
        for k in range(2):
            head = 2 * pair + k
            diff = cum_ref[pl.ds(head, 1), :] - column(cum_t_ref[...], head)
            weights = jnp.exp(jnp.minimum(diff, 0.0))
            mine = jnp.where(low if k == 0 else ~low, x, 0.0).astype(BF)
            d_mixed = weights * nt(mine, gyb)
            d_scores[...] += d_mixed
            parts.append(nn((weights * scores[...]).astype(BF), gyb))
            change = d_mixed * scores[...]
            rows[pl.ds(head, 1), :] = jnp.sum(change, axis=0, keepdims=True)
            down = jnp.sum(change, axis=1, keepdims=True)
            cols[...] -= jnp.where(lanes == head, down, 0.0)
        skip = jnp.where(low, skip_ref[2 * pair], skip_ref[2 * pair + 1])
        gx_ref[:, at] = jnp.where(low, parts[0], parts[1]) + skip * gyb.astype(F32)

    @pl.when(step == steps - 1)
    def _():
        keep = iota((T, T), 1) >= iota((T, T), 0)
        ds = jnp.where(keep, d_scores[...], 0.0).astype(BF)
        gb = nn(ds, c_ref[...].astype(BF))
        gc = tn(ds, b_ref[...].astype(BF))
        after = (iota((T, T), 0) >= iota((T, T), 1)).astype(F32)
        dims = (((0,), (0,)), ((), ()))
        ga = jnp.dot(rows[...], after, precision=HIGH, preferred_element_type=F32)
        up = lax.dot_general(cols[...], after, dims, precision=HIGH, preferred_element_type=F32)
        for out, add, ref in zip((ga_ref, gb_ref, gc_ref), (ga + up[:H], gb, gc), before or (None,) * 3):
            out[...] = add if ref is None else add + ref[...]


def within(first, steps, x, gy, cum, cum_t, b, c, skip, before=()):
    here = pl.BlockSpec((T, STEP * 2 * P_SIZE), lambda p: (0, first + p))
    return pl.pallas_call(
        functools.partial(within_kernel, first, steps),
        grid=(steps,),
        in_specs=[
            here, here, whole((H, T)), whole((T, H)), whole((T, N)), whole((T, N)), smem(),
        ]
        + [whole(v.shape) for v in before],
        out_specs=[wide(T, STEP), whole((H, T)), whole((T, N)), whole((T, N))],
        out_shape=[
            jax.ShapeDtypeStruct((T, steps * STEP * 2 * P_SIZE), F32),
            jax.ShapeDtypeStruct((H, T), F32),
            jax.ShapeDtypeStruct((T, N), F32),
            jax.ShapeDtypeStruct((T, N), F32),
        ],
        scratch_shapes=[
            pltpu.VMEM((T, T), F32),
            pltpu.VMEM((T, T), F32),
            pltpu.VMEM((H, T), F32),
            pltpu.VMEM((T, N), F32),
        ],
        compiler_params=params(),
        cost_estimate=cost(7),
        name="within",
    )(x, gy, cum, cum_t, b, c, skip, *before)


def across_kernel(
    x_ref, gy_ref, grow_ref, tail_ref, part_ref, part2_ref, cum_ref, b_ref, c_ref, start_ref, last_ref,
    ga_in, gb_in, gc_in,
    gx_ref, ga_ref, gb_ref, gc_ref,
    cols, tails, totals,
):
    step = pl.program_id(0)
    bb = b_ref[...].astype(BF)
    cb = c_ref[...].astype(BF)

    @pl.when(step == 0)
    def _():
        cols[...] = jnp.zeros_like(cols)
        tails[...] = jnp.zeros_like(tails)
        gb_ref[...] = gb_in[...]
        gc_ref[...] = gc_in[...]

    width = WIDE * 2 * P_SIZE
    start = start_ref[...]
    last = last_ref[...]
    tail = tail_ref[...].astype(F32)
    pick = iota((width, N), 1) == step * 2 * WIDE + iota((width, N), 0) // P_SIZE
    grown = gy_ref[...].astype(F32) * grow_ref[...].astype(F32)
    cols[...] += nn((grown * nt(cb, start)).astype(BF), pick.astype(BF))
    gc_ref[...] += nn(grown.astype(BF), start)
    faded = x_ref[...] * tail
    back = nt(bb, last)
    tails[...] += nn((faded * back).astype(BF), pick.astype(BF))
    gb_ref[...] += nn(faded.astype(BF), last)
    part = jnp.where(step < PAIRS // WIDE // 2, part_ref[...], part2_ref[...])
    gx_ref[...] = part + tail * back
    both = jnp.sum(start.astype(F32) * last.astype(F32), axis=1, keepdims=True)
    totals[pl.ds(step, 1), :] = jnp.sum(jnp.where(pick, both, 0.0), axis=0, keepdims=True)

    @pl.when(step == PAIRS // WIDE - 1)
    def _():
        after = (iota((T, T), 0) >= iota((T, T), 1)).astype(F32)
        before = (iota((T, T), 0) < iota((T, T), 1)).astype(F32)
        dims = (((0,), (0,)), ((), ()))
        up = lax.dot_general(cols[...], after, dims, precision=HIGH, preferred_element_type=F32)
        up += lax.dot_general(tails[...], before, dims, precision=HIGH, preferred_element_type=F32)
        total = jnp.sum(totals[...], axis=0, keepdims=True)
        total = jnp.sum(jnp.where(iota((H, N), 0) == iota((H, N), 1), total, 0.0), axis=1, keepdims=True)
        ga_ref[...] = ga_in[...] + up[:H] + jnp.exp(cum_ref[:, T - 1 : T]) * total


def across(x, gy, grow, tail, part, part2, cum, b, c, start, last, ga, gb, gc):
    width = WIDE * 2 * P_SIZE
    last_part = PAIRS // WIDE // 2 - 1
    return pl.pallas_call(
        across_kernel,
        grid=(PAIRS // WIDE,),
        in_specs=[wide(T, WIDE)] * 4
        + [
            pl.BlockSpec((T, width), lambda p: (0, jnp.minimum(p, last_part))),
            pl.BlockSpec((T, width), lambda p: (0, jnp.maximum(p - last_part - 1, 0))),
        ]
        + [whole((H, T)), whole((T, N)), whole((T, N))]
        + [state_block(WIDE), state_block(WIDE), whole((H, T)), whole((T, N)), whole((T, N))],
        out_specs=[wide(T, WIDE), whole((H, T)), whole((T, N)), whole((T, N))],
        out_shape=[
            jax.ShapeDtypeStruct((T, D), F32),
            jax.ShapeDtypeStruct((H, T), F32),
            jax.ShapeDtypeStruct((T, N), F32),
            jax.ShapeDtypeStruct((T, N), F32),
        ],
        scratch_shapes=[
            pltpu.VMEM((T, N), F32),
            pltpu.VMEM((T, N), F32),
            pltpu.VMEM((PAIRS // WIDE, N), F32),
        ],
        compiler_params=params(),
        cost_estimate=cost(8),
        name="across",
    )(x, gy, grow, tail, part, part2, cum, b, c, start, last, ga, gb, gc)


def fold_kernel(a0, a1, a2, a3, b0, b1, b2, b3, out_ref):
    sums = []
    for parts in ((a0, a1, a2, a3), (b0, b1, b2, b3)):
        total = parts[0][...].astype(F32)
        for part in parts[1:]:
            total += part[...].astype(F32)
        sums.append(total.astype(BF))
    for q in range(8 * TILES):
        r, c = divmod(q, 10)
        if r < 10:
            tile = sums[c // 5][16 * r : 16 * r + 16, 128 * (c % 5) : 128 * (c % 5) + 128]
        else:
            tile = jnp.zeros((16, 128), BF)
        out_ref[q // TILES, q % TILES] = tile


def fold(parts):
    return pl.pallas_call(
        fold_kernel,
        in_specs=[vmem()] * 8,
        out_specs=vmem(),
        out_shape=jax.ShapeDtypeStruct((8, TILES, 16, 128), BF),
        compiler_params=params(),
        cost_estimate=cost(3),
        name="fold",
    )(*parts)


def groups_of(row0, count, ids_ref):
    heads = (row0 + iota((count, N), 0)) // P_SIZE == iota((count, N), 1)
    return jnp.sum(jnp.where(heads, ids_ref[...], 0.0), axis=1, keepdims=True)


def zsum_kernel(row0_ref, z_ref, ids_ref, got_ref, parts_ref, out_ref, note_ref):
    total = parts_ref[0].astype(F32)
    for z in range(1, 8):
        total += parts_ref[z].astype(F32)
    for s in range(8):
        out_ref[s] = total.astype(BF)
    found = jnp.zeros((16, N), F32)
    for i in range(TILES):
        row = row0_ref[0] + 16 * ((z_ref[0] * TILES + i) // 10)
        place = iota((16, N), 1) - H == groups_of(row, 16, ids_ref).astype(jnp.int32)
        tile = total[i]
        found += jnp.where(place, jnp.sum(tile * tile, axis=1, keepdims=True), 0.0)
    d_sum = jnp.zeros((1, N), F32)
    for s in range(N_SEQ):
        pieces = got_ref[s, OWN:, :].astype(F32)
        d_sum += pieces[0:1, :] + pieces[1:2, :] + pieces[2:3, :]
    note_ref[...] = jnp.sum(found, axis=0, keepdims=True) + d_sum / N_SEQ


def zsum(row0, z, ids, parts, got):
    return pl.pallas_call(
        zsum_kernel,
        in_specs=[smem(), smem()] + [vmem()] * 3,
        out_specs=[vmem(), vmem()],
        out_shape=[
            jax.ShapeDtypeStruct((8, TILES, 16, 128), BF),
            jax.ShapeDtypeStruct((1, N), F32),
        ],
        compiler_params=params(),
        cost_estimate=cost(2),
        name="zsum",
    )(row0, z, ids, got, parts)


def tile_of(ref, r, c):
    z, i = divmod(10 * r + c, TILES)
    return ref[z, i].astype(F32)


def clip_kernel(tokens_all, row0_ref, core_ref, ids_ref, own_ref, other_ref, note_ref, w_ref, d_ref):
    ids = ids_ref[...]
    lane = iota((1, N), 1)
    note = note_ref[...]
    grad_d = jnp.where(lane < H, note, 0.0)
    groups = groups_of(row0_ref[0], OWN, ids_ref)
    w_factor = jnp.zeros((OWN, 1), F32)
    d_factor = jnp.zeros((1, N), F32)
    for g in range(GROUPS):
        here = (ids == float(g)) & (lane < H)
        count = jnp.sum(jnp.where(here, 1.0, 0.0), axis=1, keepdims=True)
        sumsq = jnp.sum(jnp.where(lane == H + g, note, 0.0), axis=1, keepdims=True)
        sumsq += jnp.sum(jnp.where(here, grad_d * grad_d, 0.0), axis=1, keepdims=True)
        bound = 7.0 * jnp.sqrt(count * (P_SIZE * D + 1.0) * tokens_all)
        factor = jnp.minimum(1.0, bound / jnp.sqrt(sumsq + 1e-06))
        w_factor += jnp.where(groups == float(g), factor, 0.0)
        d_factor += jnp.where(here, factor, 0.0)
    d_ref[...] = grad_d * d_factor
    for r in range(10):
        scale = w_factor[16 * r : 16 * r + 16, :]
        for ref, core in ((own_ref, core_ref[0]), (other_ref, 1 - core_ref[0])):
            for c in range(10):
                col = pl.multiple_of(core * (D // 2) + 128 * c, 128)
                w_ref[16 * r : 16 * r + 16, pl.ds(col, 128)] = tile_of(ref, r, c) * scale


def clip(tokens_all, row0, core, ids, own, other, note):
    return pl.pallas_call(
        functools.partial(clip_kernel, tokens_all),
        in_specs=[smem(), smem()] + [vmem()] * 4,
        out_specs=[vmem(), vmem()],
        out_shape=[jax.ShapeDtypeStruct((OWN, D), F32), jax.ShapeDtypeStruct((1, N), F32)],
        compiler_params=params(),
        cost_estimate=cost(3),
        name="clip",
    )(row0, core, ids, own, other, note)


def shifted(v, axis, d):
    return lax.ppermute(v, axis, [(i, (i + d) % 4) for i in range(4)])


def plus(a, b):
    return (a.astype(F32) + b.astype(F32)).astype(BF)


def far(t, axis):
    m = t.shape[1] // 2
    return shifted(t[2, :m], axis, 1), shifted(t[2, m:], axis, -1)


def passed(t, ra, rb):
    m = t.shape[1] // 2
    up = jnp.concatenate([plus(t[1, :m], ra), t[1, m:]], axis=0)
    down = jnp.concatenate([t[3, :m], plus(t[3, m:], rb)], axis=0)
    return up, down


def near(t, up, down, axis):
    total = t[0].astype(F32) + shifted(up, axis, 1).astype(F32)
    return (total + shifted(down, axis, -1).astype(F32)).astype(BF)


def direct(t, axis):
    return (t[0],) + tuple(shifted(t[d], axis, d) for d in (1, 3, 2))


def other_core(v):
    return lax.ppermute(v, "core", [(0, 1), (1, 0)])


def sum_over(v, axes):
    for unit in (1, 4):
        got = [
            lax.ppermute(v, axes, [(i, i ^ (unit * k)) for i in range(16)]) for k in (1, 2, 3)
        ]
        v = (v + got[0]) + (got[1] + got[2])
    return v


def tie(*values):
    return lax.optimization_barrier(values)


def per_device(x_in, a_log, b_in, c_in, g_out, w_out, d_skip, group_ids):
    x, a, b, c, g = (x_in[0], a_log[0], b_in[0], c_in[0], g_out[0])
    core = lax.axis_index("core")
    half = D // 2
    at = jnp.stack([lax.axis_index("y"), lax.axis_index("x")]).astype(jnp.int32)
    mine = (2 * lax.axis_index("z") + core).reshape(1).astype(jnp.int32)
    at_z = lax.axis_index("z").reshape(1).astype(jnp.int32)
    row0 = ((4 * at[0] + at[1]) * OWN).reshape(1)
    ids = jnp.pad(group_ids.astype(F32), (0, N - H), constant_values=-1.0)[None]
    tokens_all = float(T * N_SEQ * 16)

    g_mine = lax.dynamic_slice_in_dim(g, core * half, half, axis=1)
    g_other = other_core(lax.dynamic_slice_in_dim(g, (1 - core) * half, half, axis=1))

    g_both = jnp.concatenate([g_mine, g_other], axis=0)

    cum, cum_t, tail, sent = local_ends(x, a, b)
    w_out, sent = tie(w_out, sent)
    w_mine = lax.dynamic_slice_in_dim(w_out, core * half, half, axis=1)
    w_half = lax.all_gather(w_mine, ("y", "x"), axis=0, tiled=True)
    got = swap(sent, SEQ)
    y_part, grow = intra(x, cum, cum_t, b, c, d_skip)
    start = swap(chain(got, got, mine, False), SEQ).reshape(H * P_SIZE, N)
    y_own = inter(y_part, grow, c, start)
    y_other = other_core(y_own)
    first, second = terms(at, y_own, y_other, g_both)

    first = lax.psum_scatter(first.reshape(-1, half // 2), "x", scatter_dimension=0, tiled=True)
    far_y = far(second, "y")
    w_half, _ = tie(w_half, second)
    gy_own, gy_other = gy_parts(g_both, w_half)
    *far_y, gy_own, gy_other = tie(*far_y, gy_own, gy_other)
    gy_other = other_core(gy_other)
    up, down = passed(second, *far_y)
    up, down, gy_own, gy_other = tie(up, down, gy_own, gy_other)
    second = near(second, up, down, "y")
    gy, sent_back = entries(gy_own, gy_other, x, grow, c)
    got_back = swap(sent_back, SEQ)
    steps = PAIRS // STEP // 2
    gx1, *sums = within(0, steps, x, gy, cum, cum_t, b, c, d_skip)
    first, second, gx1 = tie(first, second, gx1)
    first = direct(first.reshape(4, OWN, half // 2), "y")
    second = direct(second, "x")
    tiles = fold(first + second)
    gy, mine, tiles = tie(gy, mine, tiles)
    tiles = swap(tiles, "z")
    states = chain(got_back, got, mine, True)
    gx2, *sums = within(steps, steps, x, gy, cum, cum_t, b, c, d_skip, sums)
    tiles, gx2, states = tie(tiles, gx2, states)
    tiles, note = zsum(row0, at_z, ids, tiles, got_back)
    tiles = swap(tiles, "z")
    note = sum_over(note, ("y", "x"))
    tiles, note, states = tie(tiles, note, states)
    last = swap(states, SEQ).reshape(H * P_SIZE, N)
    tiles_other = other_core(tiles)
    note = sum_over(note, SEQ)
    core = core.reshape(1).astype(jnp.int32)
    clipped_w, clipped_d = clip(tokens_all, row0, core, ids, tiles, tiles_other, note)
    clipped_w, last = tie(clipped_w, last)
    gx, ga, gb, gc = across(x, gy, grow, tail, gx1, gx2, cum, b, c, start, last, *sums)
    return (gx[None], ga[None], gb[None], gc[None], clipped_w, clipped_d[0, :H])


def solution(mesh):
    fine = Mesh(mesh.devices.reshape(4, 4, 8, 2), ("y", "x", "z", "core"))
    rows = ("y", "x")
    tokens = P(rows, SEQ, None)
    return jax.shard_map(
        per_device,
        mesh=fine,
        in_specs=(
            tokens, P(rows, None, SEQ), tokens, tokens, tokens, P(rows, None), P(), P(),
        ),
        out_specs=(tokens, P(rows, None, SEQ), tokens, tokens, P(rows, None), P()),
        check_vma=False,
    )
```

```python
import functools

import jax
import jax.numpy as jnp
from jax import lax
from jax.experimental import pallas as pl
from jax.experimental.pallas import tpu as pltpu
from jax.sharding import Mesh
from jax.sharding import PartitionSpec as P

D = 2560
H = 40
P_SIZE = 64
N = 128
T = 256
GROUPS = 4
PAIRS = H // 2
SEQ = ("z", "core")
N_SEQ = 16
OWN = H * P_SIZE // N_SEQ
HIGH = lax.Precision.HIGHEST
BF = jnp.bfloat16
F32 = jnp.float32
VMEM = 56 * 1024 * 1024
WIDE = 5
STEP = 2
ROWS = OWN + 16
TILES = 13


def nn(a, b):
    return lax.dot_general(a, b, (((1,), (0,)), ((), ())), preferred_element_type=F32)


def nt(a, b):
    return lax.dot_general(a, b, (((1,), (1,)), ((), ())), preferred_element_type=F32)


def tn(a, b):
    return lax.dot_general(a, b, (((0,), (0,)), ((), ())), preferred_element_type=F32)


def iota(shape, dim):
    return lax.broadcasted_iota(jnp.int32, shape, dim)


def whole(shape):
    return pl.BlockSpec(shape, lambda *_: (0,) * len(shape))


def wide(rows, pairs):
    return pl.BlockSpec((rows, pairs * 2 * P_SIZE), lambda p: (0, p))


def state_block(pairs):
    return pl.BlockSpec((pairs * 2 * P_SIZE, N), lambda p: (p, 0))


def smem():
    return pl.BlockSpec(memory_space=pltpu.SMEM)


def vmem():
    return pl.BlockSpec(memory_space=pltpu.VMEM)


def params():
    return pltpu.CompilerParams(vmem_limit_bytes=VMEM)


def cost(micros):
    return pl.CostEstimate(flops=0, bytes_accessed=int(micros * 3e6), transcendentals=0)


def column(cum_t, head):
    return jnp.sum(jnp.where(iota(cum_t.shape, 1) == head, cum_t, 0.0), axis=1, keepdims=True)


def low_half(shape):
    return iota(shape, 1) < P_SIZE


def lanes_of(i):
    return slice(i * 2 * P_SIZE, (i + 1) * 2 * P_SIZE)


def put_states(out_ref, states, first, pairs):
    chunks = pairs * 2 * P_SIZE // OWN
    rows = states.astype(BF).reshape(chunks, OWN, N)
    out_ref[pl.ds(first * 2 * P_SIZE // OWN, chunks), :OWN, :] = rows


def put_note(out_ref, pieces):
    at = iota((16, N), 0)
    note = jnp.zeros((16, N), F32)
    for i, piece in enumerate(pieces):
        note = jnp.where(at == i, piece, note)
    for s in range(N_SEQ):
        out_ref[s, OWN:, :] = note.astype(BF)


def ends_kernel(x_ref, a_ref, b_ref, cum_ref, cum_t_ref, tail_ref, out_ref, pieces):
    step = pl.program_id(0)

    @pl.when(step == 0)
    def _():
        a = a_ref[...]
        upto = (iota((T, T), 0) <= iota((T, T), 1)).astype(F32)
        cum_ref[...] = jnp.dot(a, upto, precision=HIGH, preferred_element_type=F32)
        down = (iota((T, T), 1) <= iota((T, T), 0)).astype(F32)
        cum_t = lax.dot_general(
            down, a, (((1,), (1,)), ((), ())), precision=HIGH, preferred_element_type=F32
        )
        cum_t_ref[...] = cum_t
        total = jnp.concatenate([cum_t[T - 1 :, :], jnp.zeros((1, N - H), F32)], axis=1)
        hi = jnp.floor(total)
        mid = jnp.floor((total - hi) * 256.0) / 256.0
        put_note(out_ref, (hi, mid, total - hi - mid))
        tail = jnp.exp(cum_t[T - 1 :, :] - cum_t)
        high = tail.astype(BF)
        pieces[0] = high
        pieces[1] = (tail - high.astype(F32)).astype(BF)

    width = WIDE * 2 * P_SIZE
    pick = iota((H, width), 0) == step * 2 * WIDE + iota((H, width), 1) // P_SIZE
    pick = pick.astype(BF)
    tail = nn(pieces[0], pick) + nn(pieces[1], pick)
    tail_ref[...] = tail.astype(BF)
    states = tn((x_ref[...] * tail).astype(BF), b_ref[...].astype(BF))
    put_states(out_ref, states, step * WIDE, WIDE)


def local_ends(x, a, b):
    return pl.pallas_call(
        ends_kernel,
        grid=(PAIRS // WIDE,),
        in_specs=[wide(T, WIDE), whole((H, T)), whole((T, N))],
        out_specs=[whole((H, T)), whole((T, H)), wide(T, WIDE), whole((N_SEQ, ROWS, N))],
        out_shape=[
            jax.ShapeDtypeStruct((H, T), F32),
            jax.ShapeDtypeStruct((T, H), F32),
            jax.ShapeDtypeStruct((T, D), BF),
            jax.ShapeDtypeStruct((N_SEQ, ROWS, N), BF),
        ],
        scratch_shapes=[pltpu.VMEM((2, T, H), BF)],
        compiler_params=params(),
        cost_estimate=cost(6),
        name="ends",
    )(x, a, b)


def intra_kernel(x_ref, cum_ref, cum_t_ref, b_ref, c_ref, skip_ref, y_ref, grow_ref, scores):
    step = pl.program_id(0)

    @pl.when(step == 0)
    def _():
        keep = iota((T, T), 0) >= iota((T, T), 1)
        scores[...] = jnp.where(keep, nt(c_ref[...].astype(BF), b_ref[...].astype(BF)), 0.0)

    for i in range(STEP):
        x = x_ref[:, lanes_of(i)]
        xb = x.astype(BF)
        low = low_half(x.shape)
        head = 2 * (step * STEP + i)
        parts = []
        sides = []
        for k in range(2):
            sides.append(column(cum_t_ref[...], head + k))
            diff = sides[k] - cum_ref[pl.ds(head + k, 1), :]
            mixed = (jnp.exp(jnp.minimum(diff, 0.0)) * scores[...]).astype(BF)
            parts.append(nn(mixed, xb))
        skip = jnp.where(low, skip_ref[head], skip_ref[head + 1])
        y_ref[:, lanes_of(i)] = jnp.where(low, parts[0], parts[1]) + skip * x
        grow = jnp.exp(jnp.where(low, sides[0], sides[1]))
        grow_ref[:, lanes_of(i)] = grow.astype(BF)


def intra(x, cum, cum_t, b, c, skip):
    return pl.pallas_call(
        intra_kernel,
        grid=(PAIRS // STEP,),
        in_specs=[
            wide(T, STEP), whole((H, T)), whole((T, H)), whole((T, N)), whole((T, N)), smem(),
        ],
        out_specs=[wide(T, STEP)] * 2,
        out_shape=[jax.ShapeDtypeStruct((T, D), F32), jax.ShapeDtypeStruct((T, D), BF)],
        scratch_shapes=[pltpu.VMEM((T, T), F32)],
        compiler_params=params(),
        cost_estimate=cost(9),
        name="intra",
    )(x, cum, cum_t, b, c, skip)


def inter_kernel(part_ref, grow_ref, c_ref, start_ref, y_ref):
    read = nt(c_ref[...].astype(BF), start_ref[...])
    y_ref[...] = (part_ref[...] + grow_ref[...].astype(F32) * read).astype(BF)


def inter(part, grow, c, start):
    return pl.pallas_call(
        inter_kernel,
        grid=(PAIRS // WIDE,),
        in_specs=[wide(T, WIDE), wide(T, WIDE), whole((T, N)), state_block(WIDE)],
        out_specs=wide(T, WIDE),
        out_shape=jax.ShapeDtypeStruct((T, D), BF),
        compiler_params=params(),
        cost_estimate=cost(5),
        name="inter",
    )(part, grow, c, start)


def chain_kernel(reverse, mine_ref, parts_ref, totals_ref, out_ref):
    owner = (mine_ref[0] * OWN + iota((OWN, N), 0)) // P_SIZE == iota((OWN, N), 1)
    carry = jnp.zeros((OWN, N), F32)
    for s in range(N_SEQ - 1, -1, -1) if reverse else range(N_SEQ):
        out_ref[s] = carry.astype(BF)
        pieces = totals_ref[s, OWN:, :].astype(F32)
        total = pieces[0:1, :] + pieces[1:2, :] + pieces[2:3, :]
        decay = jnp.sum(jnp.where(owner, total, 0.0), axis=1, keepdims=True)
        carry = jnp.exp(decay) * carry + parts_ref[s, :OWN, :].astype(F32)


def chain(parts, totals, mine, reverse):
    return pl.pallas_call(
        functools.partial(chain_kernel, reverse),
        in_specs=[smem(), vmem(), vmem()],
        out_specs=vmem(),
        out_shape=jax.ShapeDtypeStruct((N_SEQ, OWN, N), BF),
        compiler_params=params(),
        cost_estimate=cost(3),
        name="chain",
    )(mine, parts, totals)


def swap(v, axis):
    return lax.all_to_all(v, axis, 0, 0, tiled=True)


def term_kernel(at_ref, yo_ref, yx_ref, g_ref, first_ref, second_ref):
    half = g_ref.shape[1] // 2
    term = tn(jnp.concatenate([yo_ref[...], yx_ref[...]], axis=0), g_ref[...]).astype(BF)
    for k in range(4):
        rows = slice(k * OWN, (k + 1) * OWN)
        first_ref[k, 0] = term[rows, :half]
        second_ref[0, (k + 4 - at_ref[1]) % 4] = term[rows, half:]


def terms(at, y_own, y_other, g):
    rows = pl.BlockSpec((T, 4 * OWN), lambda i, at: (0, (at[0] + i) % 4))
    half = g.shape[1] // 2
    return pl.pallas_call(
        term_kernel,
        grid_spec=pltpu.PrefetchScalarGridSpec(
            num_scalar_prefetch=1,
            grid=(4,),
            in_specs=[rows, rows, whole(g.shape)],
            out_specs=[
                pl.BlockSpec((4, 1, OWN, half), lambda i, at: (0, i, 0, 0)),
                pl.BlockSpec((1, 4, OWN, half), lambda i, at: (i, 0, 0, 0)),
            ],
        ),
        out_shape=[jax.ShapeDtypeStruct((4, 4, OWN, half), BF)] * 2,
        compiler_params=params(),
        cost_estimate=cost(8),
        name="terms",
    )(at, y_own, y_other, g)


def gy_kernel(g_ref, w_ref, own_ref, other_ref):
    got = nt(g_ref[...], w_ref[...])
    own_ref[...] = got[:T]
    other_ref[...] = got[T:].astype(BF)


def gy_parts(g, w):
    rows = 4 * OWN
    return pl.pallas_call(
        gy_kernel,
        grid=(4,),
        in_specs=[whole(g.shape), pl.BlockSpec((rows, w.shape[1]), lambda i: (i, 0))],
        out_specs=[pl.BlockSpec((T, rows), lambda i: (0, i))] * 2,
        out_shape=[jax.ShapeDtypeStruct((T, D), F32), jax.ShapeDtypeStruct((T, D), BF)],
        compiler_params=params(),
        cost_estimate=cost(8),
        name="gy_parts",
    )(g, w)


def entry_kernel(own_ref, other_ref, x_ref, grow_ref, c_ref, gy_ref, out_ref, sums):
    step = pl.program_id(0)
    c = c_ref[...].astype(BF)
    found = []
    for i in range(WIDE):
        at = lanes_of(i)
        gy = own_ref[:, at] + other_ref[:, at].astype(F32)
        gy_ref[:, at] = gy.astype(BF)
        sums[pl.ds(step * WIDE + i, 1), :] = jnp.sum(gy * x_ref[:, at], axis=0, keepdims=True)
        found.append(tn((gy * grow_ref[:, at].astype(F32)).astype(BF), c))
    put_states(out_ref, jnp.concatenate(found, axis=0), step * WIDE, WIDE)

    @pl.when(step == PAIRS // WIDE - 1)
    def _():
        total = sums[...]
        low = low_half(total.shape)
        head = 2 * iota(total.shape, 0)
        lane = iota(total.shape, 1)
        even = jnp.sum(jnp.where(low, total, 0.0), axis=1, keepdims=True)
        odd = jnp.sum(jnp.where(low, 0.0, total), axis=1, keepdims=True)
        each = jnp.where(lane == head, even, 0.0) + jnp.where(lane == head + 1, odd, 0.0)
        gd = jnp.sum(each, axis=0, keepdims=True)
        hi = gd.astype(BF).astype(F32)
        mid = (gd - hi).astype(BF).astype(F32)
        put_note(out_ref, (hi, mid, gd - hi - mid))


def entries(own, other, x, grow, c):
    return pl.pallas_call(
        entry_kernel,
        grid=(PAIRS // WIDE,),
        in_specs=[wide(T, WIDE)] * 4 + [whole((T, N))],
        out_specs=[wide(T, WIDE), whole((N_SEQ, ROWS, N))],
        out_shape=[
            jax.ShapeDtypeStruct((T, D), BF),
            jax.ShapeDtypeStruct((N_SEQ, ROWS, N), BF),
        ],
        scratch_shapes=[pltpu.VMEM((PAIRS, 2 * P_SIZE), F32)],
        compiler_params=params(),
        cost_estimate=cost(6),
        name="entries",
    )(own, other, x, grow, c)


def within_kernel(
    first, steps, x_ref, gy_ref, cum_ref, cum_t_ref, b_ref, c_ref, skip_ref, *rest
):
    before = rest[:-8]
    gx_ref, ga_ref, gb_ref, gc_ref, scores, d_scores, rows, cols = rest[-8:]
    step = pl.program_id(0)

    @pl.when(step == 0)
    def _():
        keep = iota((T, T), 1) >= iota((T, T), 0)
        scores[...] = jnp.where(keep, nt(b_ref[...].astype(BF), c_ref[...].astype(BF)), 0.0)
        d_scores[...] = jnp.zeros_like(d_scores)
        rows[...] = jnp.zeros_like(rows)
        cols[...] = jnp.zeros_like(cols)

    lanes = iota((T, N), 1)
    low = low_half((T, 2 * P_SIZE))
    for i in range(STEP):
        pair = (first + step) * STEP + i
        at = lanes_of(i)
        x = x_ref[:, at]
        gyb = gy_ref[:, at]
        parts = []
        for k in range(2):
            head = 2 * pair + k
            diff = cum_ref[pl.ds(head, 1), :] - column(cum_t_ref[...], head)
            weights = jnp.exp(jnp.minimum(diff, 0.0))
            mine = jnp.where(low if k == 0 else ~low, x, 0.0).astype(BF)
            d_mixed = weights * nt(mine, gyb)
            d_scores[...] += d_mixed
            parts.append(nn((weights * scores[...]).astype(BF), gyb))
            change = d_mixed * scores[...]
            rows[pl.ds(head, 1), :] = jnp.sum(change, axis=0, keepdims=True)
            down = jnp.sum(change, axis=1, keepdims=True)
            cols[...] -= jnp.where(lanes == head, down, 0.0)
        skip = jnp.where(low, skip_ref[2 * pair], skip_ref[2 * pair + 1])
        gx_ref[:, at] = jnp.where(low, parts[0], parts[1]) + skip * gyb.astype(F32)

    @pl.when(step == steps - 1)
    def _():
        keep = iota((T, T), 1) >= iota((T, T), 0)
        ds = jnp.where(keep, d_scores[...], 0.0).astype(BF)
        gb = nn(ds, c_ref[...].astype(BF))
        gc = tn(ds, b_ref[...].astype(BF))
        after = (iota((T, T), 0) >= iota((T, T), 1)).astype(F32)
        dims = (((0,), (0,)), ((), ()))
        ga = jnp.dot(rows[...], after, precision=HIGH, preferred_element_type=F32)
        up = lax.dot_general(cols[...], after, dims, precision=HIGH, preferred_element_type=F32)
        for out, add, ref in zip((ga_ref, gb_ref, gc_ref), (ga + up[:H], gb, gc), before or (None,) * 3):
            out[...] = add if ref is None else add + ref[...]


def within(first, steps, x, gy, cum, cum_t, b, c, skip, before=()):
    here = pl.BlockSpec((T, STEP * 2 * P_SIZE), lambda p: (0, first + p))
    return pl.pallas_call(
        functools.partial(within_kernel, first, steps),
        grid=(steps,),
        in_specs=[
            here, here, whole((H, T)), whole((T, H)), whole((T, N)), whole((T, N)), smem(),
        ]
        + [whole(v.shape) for v in before],
        out_specs=[wide(T, STEP), whole((H, T)), whole((T, N)), whole((T, N))],
        out_shape=[
            jax.ShapeDtypeStruct((T, steps * STEP * 2 * P_SIZE), F32),
            jax.ShapeDtypeStruct((H, T), F32),
            jax.ShapeDtypeStruct((T, N), F32),
            jax.ShapeDtypeStruct((T, N), F32),
        ],
        scratch_shapes=[
            pltpu.VMEM((T, T), F32),
            pltpu.VMEM((T, T), F32),
            pltpu.VMEM((H, T), F32),
            pltpu.VMEM((T, N), F32),
        ],
        compiler_params=params(),
        cost_estimate=cost(7),
        name="within",
    )(x, gy, cum, cum_t, b, c, skip, *before)


def across_kernel(
    x_ref, gy_ref, grow_ref, tail_ref, part_ref, part2_ref, cum_ref, b_ref, c_ref, start_ref, last_ref,
    ga_in, gb_in, gc_in,
    gx_ref, ga_ref, gb_ref, gc_ref,
    cols, tails, totals,
):
    step = pl.program_id(0)
    bb = b_ref[...].astype(BF)
    cb = c_ref[...].astype(BF)

    @pl.when(step == 0)
    def _():
        cols[...] = jnp.zeros_like(cols)
        tails[...] = jnp.zeros_like(tails)
        gb_ref[...] = gb_in[...]
        gc_ref[...] = gc_in[...]

    width = WIDE * 2 * P_SIZE
    start = start_ref[...]
    last = last_ref[...]
    tail = tail_ref[...].astype(F32)
    pick = iota((width, N), 1) == step * 2 * WIDE + iota((width, N), 0) // P_SIZE
    grown = gy_ref[...].astype(F32) * grow_ref[...].astype(F32)
    cols[...] += nn((grown * nt(cb, start)).astype(BF), pick.astype(BF))
    gc_ref[...] += nn(grown.astype(BF), start)
    faded = x_ref[...] * tail
    back = nt(bb, last)
    tails[...] += nn((faded * back).astype(BF), pick.astype(BF))
    gb_ref[...] += nn(faded.astype(BF), last)
    part = jnp.where(step < PAIRS // WIDE // 2, part_ref[...], part2_ref[...])
    gx_ref[...] = part + tail * back
    both = jnp.sum(start.astype(F32) * last.astype(F32), axis=1, keepdims=True)
    totals[pl.ds(step, 1), :] = jnp.sum(jnp.where(pick, both, 0.0), axis=0, keepdims=True)

    @pl.when(step == PAIRS // WIDE - 1)
    def _():
        after = (iota((T, T), 0) >= iota((T, T), 1)).astype(F32)
        before = (iota((T, T), 0) < iota((T, T), 1)).astype(F32)
        dims = (((0,), (0,)), ((), ()))
        up = lax.dot_general(cols[...], after, dims, precision=HIGH, preferred_element_type=F32)
        up += lax.dot_general(tails[...], before, dims, precision=HIGH, preferred_element_type=F32)
        total = jnp.sum(totals[...], axis=0, keepdims=True)
        total = jnp.sum(jnp.where(iota((H, N), 0) == iota((H, N), 1), total, 0.0), axis=1, keepdims=True)
        ga_ref[...] = ga_in[...] + up[:H] + jnp.exp(cum_ref[:, T - 1 : T]) * total


def across(x, gy, grow, tail, part, part2, cum, b, c, start, last, ga, gb, gc):
    width = WIDE * 2 * P_SIZE
    last_part = PAIRS // WIDE // 2 - 1
    return pl.pallas_call(
        across_kernel,
        grid=(PAIRS // WIDE,),
        in_specs=[wide(T, WIDE)] * 4
        + [
            pl.BlockSpec((T, width), lambda p: (0, jnp.minimum(p, last_part))),
            pl.BlockSpec((T, width), lambda p: (0, jnp.maximum(p - last_part - 1, 0))),
        ]
        + [whole((H, T)), whole((T, N)), whole((T, N))]
        + [state_block(WIDE), state_block(WIDE), whole((H, T)), whole((T, N)), whole((T, N))],
        out_specs=[wide(T, WIDE), whole((H, T)), whole((T, N)), whole((T, N))],
        out_shape=[
            jax.ShapeDtypeStruct((T, D), F32),
            jax.ShapeDtypeStruct((H, T), F32),
            jax.ShapeDtypeStruct((T, N), F32),
            jax.ShapeDtypeStruct((T, N), F32),
        ],
        scratch_shapes=[
            pltpu.VMEM((T, N), F32),
            pltpu.VMEM((T, N), F32),
            pltpu.VMEM((PAIRS // WIDE, N), F32),
        ],
        compiler_params=params(),
        cost_estimate=cost(8),
        name="across",
    )(x, gy, grow, tail, part, part2, cum, b, c, start, last, ga, gb, gc)


def fold_kernel(a0, a1, a2, a3, b0, b1, b2, b3, out_ref):
    sums = []
    for parts in ((a0, a1, a2, a3), (b0, b1, b2, b3)):
        total = parts[0][...].astype(F32)
        for part in parts[1:]:
            total += part[...].astype(F32)
        sums.append(total.astype(BF))
    for q in range(8 * TILES):
        r, c = divmod(q, 10)
        if r < 10:
            tile = sums[c // 5][16 * r : 16 * r + 16, 128 * (c % 5) : 128 * (c % 5) + 128]
        else:
            tile = jnp.zeros((16, 128), BF)
        out_ref[q // TILES, q % TILES] = tile


def fold(parts):
    return pl.pallas_call(
        fold_kernel,
        in_specs=[vmem()] * 8,
        out_specs=vmem(),
        out_shape=jax.ShapeDtypeStruct((8, TILES, 16, 128), BF),
        compiler_params=params(),
        cost_estimate=cost(3),
        name="fold",
    )(*parts)


def groups_of(row0, count, ids_ref):
    heads = (row0 + iota((count, N), 0)) // P_SIZE == iota((count, N), 1)
    return jnp.sum(jnp.where(heads, ids_ref[...], 0.0), axis=1, keepdims=True)


def zsum_kernel(row0_ref, z_ref, ids_ref, got_ref, parts_ref, out_ref, note_ref):
    total = parts_ref[0].astype(F32)
    for z in range(1, 8):
        total += parts_ref[z].astype(F32)
    for s in range(8):
        out_ref[s] = total.astype(BF)
    found = jnp.zeros((16, N), F32)
    for i in range(TILES):
        row = row0_ref[0] + 16 * ((z_ref[0] * TILES + i) // 10)
        place = iota((16, N), 1) - H == groups_of(row, 16, ids_ref).astype(jnp.int32)
        tile = total[i]
        found += jnp.where(place, jnp.sum(tile * tile, axis=1, keepdims=True), 0.0)
    d_sum = jnp.zeros((1, N), F32)
    for s in range(N_SEQ):
        pieces = got_ref[s, OWN:, :].astype(F32)
        d_sum += pieces[0:1, :] + pieces[1:2, :] + pieces[2:3, :]
    note_ref[...] = jnp.sum(found, axis=0, keepdims=True) + d_sum / N_SEQ


def zsum(row0, z, ids, parts, got):
    return pl.pallas_call(
        zsum_kernel,
        in_specs=[smem(), smem()] + [vmem()] * 3,
        out_specs=[vmem(), vmem()],
        out_shape=[
            jax.ShapeDtypeStruct((8, TILES, 16, 128), BF),
            jax.ShapeDtypeStruct((1, N), F32),
        ],
        compiler_params=params(),
        cost_estimate=cost(2),
        name="zsum",
    )(row0, z, ids, got, parts)


def tile_of(ref, r, c):
    z, i = divmod(10 * r + c, TILES)
    return ref[z, i].astype(F32)


def clip_kernel(tokens_all, row0_ref, core_ref, ids_ref, own_ref, other_ref, note_ref, w_ref, d_ref):
    ids = ids_ref[...]
    lane = iota((1, N), 1)
    note = note_ref[...]
    grad_d = jnp.where(lane < H, note, 0.0)
    groups = groups_of(row0_ref[0], OWN, ids_ref)
    w_factor = jnp.zeros((OWN, 1), F32)
    d_factor = jnp.zeros((1, N), F32)
    for g in range(GROUPS):
        here = (ids == float(g)) & (lane < H)
        count = jnp.sum(jnp.where(here, 1.0, 0.0), axis=1, keepdims=True)
        sumsq = jnp.sum(jnp.where(lane == H + g, note, 0.0), axis=1, keepdims=True)
        sumsq += jnp.sum(jnp.where(here, grad_d * grad_d, 0.0), axis=1, keepdims=True)
        bound = 7.0 * jnp.sqrt(count * (P_SIZE * D + 1.0) * tokens_all)
        factor = jnp.minimum(1.0, bound / jnp.sqrt(sumsq + 1e-06))
        w_factor += jnp.where(groups == float(g), factor, 0.0)
        d_factor += jnp.where(here, factor, 0.0)
    d_ref[...] = (grad_d * d_factor)[:, :H]
    for r in range(10):
        scale = w_factor[16 * r : 16 * r + 16, :]
        for ref, core in ((own_ref, core_ref[0]), (other_ref, 1 - core_ref[0])):
            for c in range(10):
                col = pl.multiple_of(core * (D // 2) + 128 * c, 128)
                w_ref[16 * r : 16 * r + 16, pl.ds(col, 128)] = tile_of(ref, r, c) * scale


def clip(tokens_all, row0, core, ids, own, other, note):
    return pl.pallas_call(
        functools.partial(clip_kernel, tokens_all),
        in_specs=[smem(), smem()] + [vmem()] * 4,
        out_specs=[vmem(), vmem()],
        out_shape=[jax.ShapeDtypeStruct((OWN, D), F32), jax.ShapeDtypeStruct((1, H), F32)],
        compiler_params=params(),
        cost_estimate=cost(3),
        name="clip",
    )(row0, core, ids, own, other, note)


def shifted(v, axis, d):
    return lax.ppermute(v, axis, [(i, (i + d) % 4) for i in range(4)])


def plus(a, b):
    return (a.astype(F32) + b.astype(F32)).astype(BF)


def far(t, axis):
    m = t.shape[1] // 2
    return shifted(t[2, :m], axis, 1), shifted(t[2, m:], axis, -1)


def passed(t, ra, rb):
    m = t.shape[1] // 2
    up = jnp.concatenate([plus(t[1, :m], ra), t[1, m:]], axis=0)
    down = jnp.concatenate([t[3, :m], plus(t[3, m:], rb)], axis=0)
    return up, down


def near(t, up, down, axis):
    total = t[0].astype(F32) + shifted(up, axis, 1).astype(F32)
    return (total + shifted(down, axis, -1).astype(F32)).astype(BF)


def direct(t, axis):
    return (t[0],) + tuple(shifted(t[d], axis, d) for d in (1, 3, 2))


def other_core(v):
    return lax.ppermute(v, "core", [(0, 1), (1, 0)])


def sum_over(v, axes):
    for unit in (1, 4):
        got = [
            lax.ppermute(v, axes, [(i, i ^ (unit * k)) for i in range(16)]) for k in (1, 2, 3)
        ]
        v = (v + got[0]) + (got[1] + got[2])
    return v


def tie(*values):
    return lax.optimization_barrier(values)


def per_device(x_in, a_log, b_in, c_in, g_out, w_out, d_skip, group_ids):
    x, a, b, c, g = (x_in[0], a_log[0], b_in[0], c_in[0], g_out[0])
    core = lax.axis_index("core")
    half = D // 2
    at = jnp.stack([lax.axis_index("y"), lax.axis_index("x")]).astype(jnp.int32)
    mine = (2 * lax.axis_index("z") + core).reshape(1).astype(jnp.int32)
    at_z = lax.axis_index("z").reshape(1).astype(jnp.int32)
    row0 = ((4 * at[0] + at[1]) * OWN).reshape(1)
    ids = jnp.pad(group_ids.astype(F32), (0, N - H), constant_values=-1.0)[None]
    tokens_all = float(T * N_SEQ * 16)

    g_mine = lax.dynamic_slice_in_dim(g, core * half, half, axis=1)
    g_other = other_core(lax.dynamic_slice_in_dim(g, (1 - core) * half, half, axis=1))

    g_both = jnp.concatenate([g_mine, g_other], axis=0)

    cum, cum_t, tail, sent = local_ends(x, a, b)
    w_out, sent = tie(w_out, sent)
    w_mine = lax.dynamic_slice_in_dim(w_out, core * half, half, axis=1)
    w_half = lax.all_gather(w_mine, ("y", "x"), axis=0, tiled=True)
    got = swap(sent, SEQ)
    y_part, grow = intra(x, cum, cum_t, b, c, d_skip)
    y_part, g_both, at = tie(y_part, g_both, at)
    start = swap(chain(got, got, mine, False), SEQ).reshape(H * P_SIZE, N)
    y_own = inter(y_part, grow, c, start)
    y_other = other_core(y_own)
    first, second = terms(at, y_own, y_other, g_both)

    first = lax.psum_scatter(first.reshape(-1, half // 2), "x", scatter_dimension=0, tiled=True)
    far_y = far(second, "y")
    w_half, _ = tie(w_half, second)
    gy_own, gy_other = gy_parts(g_both, w_half)
    *far_y, gy_own, gy_other = tie(*far_y, gy_own, gy_other)
    gy_other = other_core(gy_other)
    up, down = passed(second, *far_y)
    up, down, gy_own, gy_other = tie(up, down, gy_own, gy_other)
    second = near(second, up, down, "y")
    gy, sent_back = entries(gy_own, gy_other, x, grow, c)
    got_back = swap(sent_back, SEQ)
    steps = PAIRS // STEP // 2
    gx1, *sums = within(0, steps, x, gy, cum, cum_t, b, c, d_skip)
    first, second, gx1 = tie(first, second, gx1)
    first = direct(first.reshape(4, OWN, half // 2), "y")
    second = direct(second, "x")
    states = chain(got_back, got, mine, True)
    last = swap(states, SEQ).reshape(H * P_SIZE, N)
    parts, states = tie(first + second, states)
    tiles = fold(parts)
    gy, last, tiles = tie(gy, last, tiles)
    tiles = swap(tiles, "z")
    gx2, *sums = within(steps, steps, x, gy, cum, cum_t, b, c, d_skip, sums)
    gx, ga, gb, gc = across(x, gy, grow, tail, gx1, gx2, cum, b, c, start, last, *sums)
    tiles, ga = tie(tiles, ga)
    tiles, note = zsum(row0, at_z, ids, tiles, got_back)
    tiles = swap(tiles, "z")
    note = sum_over(note, ("y", "x"))
    tiles, note = tie(tiles, note)
    note = sum_over(note, SEQ)
    tiles_other = other_core(tiles)
    core = core.reshape(1).astype(jnp.int32)
    clipped_w, clipped_d = clip(tokens_all, row0, core, ids, tiles, tiles_other, note)
    return (gx[None], ga[None], gb[None], gc[None], clipped_w, clipped_d[0])


def solution(mesh):
    fine = Mesh(mesh.devices.reshape(4, 4, 8, 2), ("y", "x", "z", "core"))
    rows = ("y", "x")
    tokens = P(rows, SEQ, None)
    return jax.shard_map(
        per_device,
        mesh=fine,
        in_specs=(
            tokens, P(rows, None, SEQ), tokens, tokens, tokens, P(rows, None), P(), P(),
        ),
        out_specs=(tokens, P(rows, None, SEQ), tokens, tokens, P(rows, None), P()),
        check_vma=False,
    )
```

```python
import functools

import jax
import jax.numpy as jnp
from jax import lax
from jax.experimental import pallas as pl
from jax.experimental.pallas import tpu as pltpu
from jax.sharding import Mesh
from jax.sharding import PartitionSpec as P

D = 2560
H = 40
P_SIZE = 64
N = 128
T = 256
GROUPS = 4
PAIRS = H // 2
SEQ = ("z", "core")
N_SEQ = 16
OWN = H * P_SIZE // N_SEQ
HIGH = lax.Precision.HIGHEST
BF = jnp.bfloat16
F32 = jnp.float32
VMEM = 56 * 1024 * 1024
WIDE = 5
STEP = 2
ROWS = OWN + 16
TILES = 13


def nn(a, b):
    return lax.dot_general(a, b, (((1,), (0,)), ((), ())), preferred_element_type=F32)


def nt(a, b):
    return lax.dot_general(a, b, (((1,), (1,)), ((), ())), preferred_element_type=F32)


def tn(a, b):
    return lax.dot_general(a, b, (((0,), (0,)), ((), ())), preferred_element_type=F32)


def iota(shape, dim):
    return lax.broadcasted_iota(jnp.int32, shape, dim)


def whole(shape):
    return pl.BlockSpec(shape, lambda *_: (0,) * len(shape))


def wide(rows, pairs):
    return pl.BlockSpec((rows, pairs * 2 * P_SIZE), lambda p: (0, p))


def state_block(pairs):
    return pl.BlockSpec((pairs * 2 * P_SIZE, N), lambda p: (p, 0))


def smem():
    return pl.BlockSpec(memory_space=pltpu.SMEM)


def vmem():
    return pl.BlockSpec(memory_space=pltpu.VMEM)


def params():
    return pltpu.CompilerParams(vmem_limit_bytes=VMEM)


def cost(micros):
    return pl.CostEstimate(flops=0, bytes_accessed=int(micros * 3e6), transcendentals=0)


def column(cum_t, head):
    return jnp.sum(jnp.where(iota(cum_t.shape, 1) == head, cum_t, 0.0), axis=1, keepdims=True)


def low_half(shape):
    return iota(shape, 1) < P_SIZE


def lanes_of(i):
    return slice(i * 2 * P_SIZE, (i + 1) * 2 * P_SIZE)


def put_states(out_ref, states, first, pairs):
    chunks = pairs * 2 * P_SIZE // OWN
    rows = states.astype(BF).reshape(chunks, OWN, N)
    out_ref[pl.ds(first * 2 * P_SIZE // OWN, chunks), :OWN, :] = rows


def put_note(out_ref, pieces):
    at = iota((16, N), 0)
    note = jnp.zeros((16, N), F32)
    for i, piece in enumerate(pieces):
        note = jnp.where(at == i, piece, note)
    for s in range(N_SEQ):
        out_ref[s, OWN:, :] = note.astype(BF)


def ends_kernel(x_ref, a_ref, b_ref, cum_ref, cum_t_ref, tail_ref, out_ref, pieces):
    step = pl.program_id(0)

    @pl.when(step == 0)
    def _():
        a = a_ref[...]
        upto = (iota((T, T), 0) <= iota((T, T), 1)).astype(F32)
        cum_ref[...] = jnp.dot(a, upto, precision=HIGH, preferred_element_type=F32)
        down = (iota((T, T), 1) <= iota((T, T), 0)).astype(F32)
        cum_t = lax.dot_general(
            down, a, (((1,), (1,)), ((), ())), precision=HIGH, preferred_element_type=F32
        )
        cum_t_ref[...] = cum_t
        total = jnp.concatenate([cum_t[T - 1 :, :], jnp.zeros((1, N - H), F32)], axis=1)
        hi = jnp.floor(total)
        mid = jnp.floor((total - hi) * 256.0) / 256.0
        put_note(out_ref, (hi, mid, total - hi - mid))
        tail = jnp.exp(cum_t[T - 1 :, :] - cum_t)
        high = tail.astype(BF)
        pieces[0] = high
        pieces[1] = (tail - high.astype(F32)).astype(BF)

    width = WIDE * 2 * P_SIZE
    pick = iota((H, width), 0) == step * 2 * WIDE + iota((H, width), 1) // P_SIZE
    pick = pick.astype(BF)
    tail = nn(pieces[0], pick) + nn(pieces[1], pick)
    tail_ref[...] = tail.astype(BF)
    states = tn((x_ref[...] * tail).astype(BF), b_ref[...].astype(BF))
    put_states(out_ref, states, step * WIDE, WIDE)


def local_ends(x, a, b):
    return pl.pallas_call(
        ends_kernel,
        grid=(PAIRS // WIDE,),
        in_specs=[wide(T, WIDE), whole((H, T)), whole((T, N))],
        out_specs=[whole((H, T)), whole((T, H)), wide(T, WIDE), whole((N_SEQ, ROWS, N))],
        out_shape=[
            jax.ShapeDtypeStruct((H, T), F32),
            jax.ShapeDtypeStruct((T, H), F32),
            jax.ShapeDtypeStruct((T, D), BF),
            jax.ShapeDtypeStruct((N_SEQ, ROWS, N), BF),
        ],
        scratch_shapes=[pltpu.VMEM((2, T, H), BF)],
        compiler_params=params(),
        cost_estimate=cost(6),
        name="ends",
    )(x, a, b)


def intra_kernel(x_ref, cum_ref, cum_t_ref, b_ref, c_ref, skip_ref, y_ref, grow_ref, scores):
    step = pl.program_id(0)

    @pl.when(step == 0)
    def _():
        keep = iota((T, T), 0) >= iota((T, T), 1)
        scores[...] = jnp.where(keep, nt(c_ref[...].astype(BF), b_ref[...].astype(BF)), 0.0)

    for i in range(STEP):
        x = x_ref[:, lanes_of(i)]
        xb = x.astype(BF)
        low = low_half(x.shape)
        head = 2 * (step * STEP + i)
        parts = []
        sides = []
        for k in range(2):
            sides.append(column(cum_t_ref[...], head + k))
            diff = sides[k] - cum_ref[pl.ds(head + k, 1), :]
            mixed = (jnp.exp(jnp.minimum(diff, 0.0)) * scores[...]).astype(BF)
            parts.append(nn(mixed, xb))
        skip = jnp.where(low, skip_ref[head], skip_ref[head + 1])
        y_ref[:, lanes_of(i)] = jnp.where(low, parts[0], parts[1]) + skip * x
        grow = jnp.exp(jnp.where(low, sides[0], sides[1]))
        grow_ref[:, lanes_of(i)] = grow.astype(BF)


def intra(x, cum, cum_t, b, c, skip):
    return pl.pallas_call(
        intra_kernel,
        grid=(PAIRS // STEP,),
        in_specs=[
            wide(T, STEP), whole((H, T)), whole((T, H)), whole((T, N)), whole((T, N)), smem(),
        ],
        out_specs=[wide(T, STEP)] * 2,
        out_shape=[jax.ShapeDtypeStruct((T, D), F32), jax.ShapeDtypeStruct((T, D), BF)],
        scratch_shapes=[pltpu.VMEM((T, T), F32)],
        compiler_params=params(),
        cost_estimate=cost(9),
        name="intra",
    )(x, cum, cum_t, b, c, skip)


def inter_kernel(part_ref, grow_ref, c_ref, start_ref, y_ref):
    read = nt(c_ref[...].astype(BF), start_ref[...])
    y_ref[...] = (part_ref[...] + grow_ref[...].astype(F32) * read).astype(BF)


def inter(part, grow, c, start):
    return pl.pallas_call(
        inter_kernel,
        grid=(PAIRS // WIDE,),
        in_specs=[wide(T, WIDE), wide(T, WIDE), whole((T, N)), state_block(WIDE)],
        out_specs=wide(T, WIDE),
        out_shape=jax.ShapeDtypeStruct((T, D), BF),
        compiler_params=params(),
        cost_estimate=cost(5),
        name="inter",
    )(part, grow, c, start)


def chain_kernel(reverse, mine_ref, parts_ref, totals_ref, out_ref):
    owner = (mine_ref[0] * OWN + iota((OWN, N), 0)) // P_SIZE == iota((OWN, N), 1)
    carry = jnp.zeros((OWN, N), F32)
    for s in range(N_SEQ - 1, -1, -1) if reverse else range(N_SEQ):
        out_ref[s] = carry.astype(BF)
        pieces = totals_ref[s, OWN:, :].astype(F32)
        total = pieces[0:1, :] + pieces[1:2, :] + pieces[2:3, :]
        decay = jnp.sum(jnp.where(owner, total, 0.0), axis=1, keepdims=True)
        carry = jnp.exp(decay) * carry + parts_ref[s, :OWN, :].astype(F32)


def chain(parts, totals, mine, reverse):
    return pl.pallas_call(
        functools.partial(chain_kernel, reverse),
        in_specs=[smem(), vmem(), vmem()],
        out_specs=vmem(),
        out_shape=jax.ShapeDtypeStruct((N_SEQ, OWN, N), BF),
        compiler_params=params(),
        cost_estimate=cost(3),
        name="chain",
    )(mine, parts, totals)


def swap(v, axis):
    return lax.all_to_all(v, axis, 0, 0, tiled=True)


def term_kernel(at_ref, yo_ref, yx_ref, g_ref, first_ref, second_ref):
    half = g_ref.shape[1] // 2
    term = tn(jnp.concatenate([yo_ref[...], yx_ref[...]], axis=0), g_ref[...]).astype(BF)
    for k in range(4):
        rows = slice(k * OWN, (k + 1) * OWN)
        first_ref[k, 0] = term[rows, :half]
        second_ref[0, (k + 4 - at_ref[1]) % 4] = term[rows, half:]


def terms(at, y_own, y_other, g):
    rows = pl.BlockSpec((T, 4 * OWN), lambda i, at: (0, (at[0] + i) % 4))
    half = g.shape[1] // 2
    return pl.pallas_call(
        term_kernel,
        grid_spec=pltpu.PrefetchScalarGridSpec(
            num_scalar_prefetch=1,
            grid=(4,),
            in_specs=[rows, rows, whole(g.shape)],
            out_specs=[
                pl.BlockSpec((4, 1, OWN, half), lambda i, at: (0, i, 0, 0)),
                pl.BlockSpec((1, 4, OWN, half), lambda i, at: (i, 0, 0, 0)),
            ],
        ),
        out_shape=[jax.ShapeDtypeStruct((4, 4, OWN, half), BF)] * 2,
        compiler_params=params(),
        cost_estimate=cost(8),
        name="terms",
    )(at, y_own, y_other, g)


def gy_kernel(g_ref, w_ref, own_ref, other_ref):
    got = nt(g_ref[...], w_ref[...])
    own_ref[...] = got[:T]
    other_ref[...] = got[T:].astype(BF)


def gy_parts(g, w):
    rows = 4 * OWN
    return pl.pallas_call(
        gy_kernel,
        grid=(4,),
        in_specs=[whole(g.shape), pl.BlockSpec((rows, w.shape[1]), lambda i: (i, 0))],
        out_specs=[pl.BlockSpec((T, rows), lambda i: (0, i))] * 2,
        out_shape=[jax.ShapeDtypeStruct((T, D), F32), jax.ShapeDtypeStruct((T, D), BF)],
        compiler_params=params(),
        cost_estimate=cost(8),
        name="gy_parts",
    )(g, w)


def entry_kernel(own_ref, other_ref, x_ref, grow_ref, c_ref, gy_ref, out_ref, sums):
    step = pl.program_id(0)
    c = c_ref[...].astype(BF)
    found = []
    for i in range(WIDE):
        at = lanes_of(i)
        gy = own_ref[:, at] + other_ref[:, at].astype(F32)
        gy_ref[:, at] = gy.astype(BF)
        sums[pl.ds(step * WIDE + i, 1), :] = jnp.sum(gy * x_ref[:, at], axis=0, keepdims=True)
        found.append(tn((gy * grow_ref[:, at].astype(F32)).astype(BF), c))
    put_states(out_ref, jnp.concatenate(found, axis=0), step * WIDE, WIDE)

    @pl.when(step == PAIRS // WIDE - 1)
    def _():
        total = sums[...]
        low = low_half(total.shape)
        head = 2 * iota(total.shape, 0)
        lane = iota(total.shape, 1)
        even = jnp.sum(jnp.where(low, total, 0.0), axis=1, keepdims=True)
        odd = jnp.sum(jnp.where(low, 0.0, total), axis=1, keepdims=True)
        each = jnp.where(lane == head, even, 0.0) + jnp.where(lane == head + 1, odd, 0.0)
        gd = jnp.sum(each, axis=0, keepdims=True)
        hi = gd.astype(BF).astype(F32)
        mid = (gd - hi).astype(BF).astype(F32)
        put_note(out_ref, (hi, mid, gd - hi - mid))


def entries(own, other, x, grow, c):
    return pl.pallas_call(
        entry_kernel,
        grid=(PAIRS // WIDE,),
        in_specs=[wide(T, WIDE)] * 4 + [whole((T, N))],
        out_specs=[wide(T, WIDE), whole((N_SEQ, ROWS, N))],
        out_shape=[
            jax.ShapeDtypeStruct((T, D), BF),
            jax.ShapeDtypeStruct((N_SEQ, ROWS, N), BF),
        ],
        scratch_shapes=[pltpu.VMEM((PAIRS, 2 * P_SIZE), F32)],
        compiler_params=params(),
        cost_estimate=cost(6),
        name="entries",
    )(own, other, x, grow, c)


def within_kernel(
    first, steps, x_ref, gy_ref, cum_ref, cum_t_ref, b_ref, c_ref, skip_ref, *rest
):
    before = rest[:-8]
    gx_ref, ga_ref, gb_ref, gc_ref, scores, d_scores, rows, cols = rest[-8:]
    step = pl.program_id(0)

    @pl.when(step == 0)
    def _():
        keep = iota((T, T), 1) >= iota((T, T), 0)
        scores[...] = jnp.where(keep, nt(b_ref[...].astype(BF), c_ref[...].astype(BF)), 0.0)
        d_scores[...] = jnp.zeros_like(d_scores)
        rows[...] = jnp.zeros_like(rows)
        cols[...] = jnp.zeros_like(cols)

    lanes = iota((T, N), 1)
    low = low_half((T, 2 * P_SIZE))
    for i in range(STEP):
        pair = (first + step) * STEP + i
        at = lanes_of(i)
        x = x_ref[:, at]
        gyb = gy_ref[:, at]
        parts = []
        for k in range(2):
            head = 2 * pair + k
            diff = cum_ref[pl.ds(head, 1), :] - column(cum_t_ref[...], head)
            weights = jnp.exp(jnp.minimum(diff, 0.0))
            mine = jnp.where(low if k == 0 else ~low, x, 0.0).astype(BF)
            d_mixed = weights * nt(mine, gyb)
            d_scores[...] += d_mixed
            parts.append(nn((weights * scores[...]).astype(BF), gyb))
            change = d_mixed * scores[...]
            rows[pl.ds(head, 1), :] = jnp.sum(change, axis=0, keepdims=True)
            down = jnp.sum(change, axis=1, keepdims=True)
            cols[...] -= jnp.where(lanes == head, down, 0.0)
        skip = jnp.where(low, skip_ref[2 * pair], skip_ref[2 * pair + 1])
        gx_ref[:, at] = jnp.where(low, parts[0], parts[1]) + skip * gyb.astype(F32)

    @pl.when(step == steps - 1)
    def _():
        keep = iota((T, T), 1) >= iota((T, T), 0)
        ds = jnp.where(keep, d_scores[...], 0.0).astype(BF)
        gb = nn(ds, c_ref[...].astype(BF))
        gc = tn(ds, b_ref[...].astype(BF))
        after = (iota((T, T), 0) >= iota((T, T), 1)).astype(F32)
        dims = (((0,), (0,)), ((), ()))
        ga = jnp.dot(rows[...], after, precision=HIGH, preferred_element_type=F32)
        up = lax.dot_general(cols[...], after, dims, precision=HIGH, preferred_element_type=F32)
        for out, add, ref in zip((ga_ref, gb_ref, gc_ref), (ga + up[:H], gb, gc), before or (None,) * 3):
            out[...] = add if ref is None else add + ref[...]


def within(first, steps, x, gy, cum, cum_t, b, c, skip, before=()):
    here = pl.BlockSpec((T, STEP * 2 * P_SIZE), lambda p: (0, first + p))
    return pl.pallas_call(
        functools.partial(within_kernel, first, steps),
        grid=(steps,),
        in_specs=[
            here, here, whole((H, T)), whole((T, H)), whole((T, N)), whole((T, N)), smem(),
        ]
        + [whole(v.shape) for v in before],
        out_specs=[wide(T, STEP), whole((H, T)), whole((T, N)), whole((T, N))],
        out_shape=[
            jax.ShapeDtypeStruct((T, steps * STEP * 2 * P_SIZE), F32),
            jax.ShapeDtypeStruct((H, T), F32),
            jax.ShapeDtypeStruct((T, N), F32),
            jax.ShapeDtypeStruct((T, N), F32),
        ],
        scratch_shapes=[
            pltpu.VMEM((T, T), F32),
            pltpu.VMEM((T, T), F32),
            pltpu.VMEM((H, T), F32),
            pltpu.VMEM((T, N), F32),
        ],
        compiler_params=params(),
        cost_estimate=cost(7),
        name="within",
    )(x, gy, cum, cum_t, b, c, skip, *before)


def across_kernel(
    x_ref, gy_ref, grow_ref, tail_ref, part_ref, part2_ref, cum_ref, b_ref, c_ref, start_ref, last_ref,
    ga_in, gb_in, gc_in,
    gx_ref, ga_ref, gb_ref, gc_ref,
    cols, tails, totals,
):
    step = pl.program_id(0)
    bb = b_ref[...].astype(BF)
    cb = c_ref[...].astype(BF)

    @pl.when(step == 0)
    def _():
        cols[...] = jnp.zeros_like(cols)
        tails[...] = jnp.zeros_like(tails)
        gb_ref[...] = gb_in[...]
        gc_ref[...] = gc_in[...]

    width = WIDE * 2 * P_SIZE
    start = start_ref[...]
    last = last_ref[...]
    tail = tail_ref[...].astype(F32)
    pick = iota((width, N), 1) == step * 2 * WIDE + iota((width, N), 0) // P_SIZE
    grown = gy_ref[...].astype(F32) * grow_ref[...].astype(F32)
    cols[...] += nn((grown * nt(cb, start)).astype(BF), pick.astype(BF))
    gc_ref[...] += nn(grown.astype(BF), start)
    faded = x_ref[...] * tail
    back = nt(bb, last)
    tails[...] += nn((faded * back).astype(BF), pick.astype(BF))
    gb_ref[...] += nn(faded.astype(BF), last)
    part = jnp.where(step < PAIRS // WIDE // 2, part_ref[...], part2_ref[...])
    gx_ref[...] = part + tail * back
    both = jnp.sum(start.astype(F32) * last.astype(F32), axis=1, keepdims=True)
    totals[pl.ds(step, 1), :] = jnp.sum(jnp.where(pick, both, 0.0), axis=0, keepdims=True)

    @pl.when(step == PAIRS // WIDE - 1)
    def _():
        after = (iota((T, T), 0) >= iota((T, T), 1)).astype(F32)
        before = (iota((T, T), 0) < iota((T, T), 1)).astype(F32)
        dims = (((0,), (0,)), ((), ()))
        up = lax.dot_general(cols[...], after, dims, precision=HIGH, preferred_element_type=F32)
        up += lax.dot_general(tails[...], before, dims, precision=HIGH, preferred_element_type=F32)
        total = jnp.sum(totals[...], axis=0, keepdims=True)
        total = jnp.sum(jnp.where(iota((H, N), 0) == iota((H, N), 1), total, 0.0), axis=1, keepdims=True)
        ga_ref[...] = ga_in[...] + up[:H] + jnp.exp(cum_ref[:, T - 1 : T]) * total


def across(x, gy, grow, tail, part, part2, cum, b, c, start, last, ga, gb, gc):
    width = WIDE * 2 * P_SIZE
    last_part = PAIRS // WIDE // 2 - 1
    return pl.pallas_call(
        across_kernel,
        grid=(PAIRS // WIDE,),
        in_specs=[wide(T, WIDE)] * 4
        + [
            pl.BlockSpec((T, width), lambda p: (0, jnp.minimum(p, last_part))),
            pl.BlockSpec((T, width), lambda p: (0, jnp.maximum(p - last_part - 1, 0))),
        ]
        + [whole((H, T)), whole((T, N)), whole((T, N))]
        + [state_block(WIDE), state_block(WIDE), whole((H, T)), whole((T, N)), whole((T, N))],
        out_specs=[wide(T, WIDE), whole((H, T)), whole((T, N)), whole((T, N))],
        out_shape=[
            jax.ShapeDtypeStruct((T, D), F32),
            jax.ShapeDtypeStruct((H, T), F32),
            jax.ShapeDtypeStruct((T, N), F32),
            jax.ShapeDtypeStruct((T, N), F32),
        ],
        scratch_shapes=[
            pltpu.VMEM((T, N), F32),
            pltpu.VMEM((T, N), F32),
            pltpu.VMEM((PAIRS // WIDE, N), F32),
        ],
        compiler_params=params(),
        cost_estimate=cost(8),
        name="across",
    )(x, gy, grow, tail, part, part2, cum, b, c, start, last, ga, gb, gc)


def fold_kernel(a0, a1, a2, a3, b0, b1, b2, b3, out_ref):
    sums = []
    for parts in ((a0, a1, a2, a3), (b0, b1, b2, b3)):
        total = parts[0][...].astype(F32)
        for part in parts[1:]:
            total += part[...].astype(F32)
        sums.append(total.astype(BF))
    for q in range(8 * TILES):
        r, c = divmod(q, 10)
        if r < 10:
            tile = sums[c // 5][16 * r : 16 * r + 16, 128 * (c % 5) : 128 * (c % 5) + 128]
        else:
            tile = jnp.zeros((16, 128), BF)
        out_ref[q // TILES, q % TILES] = tile


def fold(parts):
    return pl.pallas_call(
        fold_kernel,
        in_specs=[vmem()] * 8,
        out_specs=vmem(),
        out_shape=jax.ShapeDtypeStruct((8, TILES, 16, 128), BF),
        compiler_params=params(),
        cost_estimate=cost(3),
        name="fold",
    )(*parts)


def groups_of(row0, count, ids_ref):
    heads = (row0 + iota((count, N), 0)) // P_SIZE == iota((count, N), 1)
    return jnp.sum(jnp.where(heads, ids_ref[...], 0.0), axis=1, keepdims=True)


def zsum_kernel(row0_ref, z_ref, ids_ref, got_ref, parts_ref, out_ref, note_ref):
    total = parts_ref[0].astype(F32)
    for z in range(1, 8):
        total += parts_ref[z].astype(F32)
    out_ref[...] = total.astype(BF)
    found = jnp.zeros((16, N), F32)
    for i in range(TILES):
        row = row0_ref[0] + 16 * ((z_ref[0] * TILES + i) // 10)
        place = iota((16, N), 1) - H == groups_of(row, 16, ids_ref).astype(jnp.int32)
        tile = total[i]
        found += jnp.where(place, jnp.sum(tile * tile, axis=1, keepdims=True), 0.0)
    d_sum = jnp.zeros((1, N), F32)
    for s in range(N_SEQ):
        pieces = got_ref[s, OWN:, :].astype(F32)
        d_sum += pieces[0:1, :] + pieces[1:2, :] + pieces[2:3, :]
    note_ref[...] = jnp.sum(found, axis=0, keepdims=True) + d_sum / N_SEQ


def zsum(row0, z, ids, parts, got):
    return pl.pallas_call(
        zsum_kernel,
        in_specs=[smem(), smem()] + [vmem()] * 3,
        out_specs=[vmem(), vmem()],
        out_shape=[
            jax.ShapeDtypeStruct((TILES, 16, 128), BF),
            jax.ShapeDtypeStruct((1, N), F32),
        ],
        compiler_params=params(),
        cost_estimate=cost(2),
        name="zsum",
    )(row0, z, ids, got, parts)


def pack_kernel(tiles_ref, note_ref, out_ref):
    note = note_ref[...]
    hi = note.astype(BF).astype(F32)
    mid = (note - hi).astype(BF).astype(F32)
    at = iota((16, N), 0)
    rows = jnp.where(at == 0, hi, jnp.where(at == 1, mid, jnp.where(at == 2, note - hi - mid, 0.0)))
    for z in range(8):
        out_ref[z, :TILES] = tiles_ref[...]
        out_ref[z, TILES] = rows.astype(BF)


def pack(tiles, note):
    return pl.pallas_call(
        pack_kernel,
        in_specs=[vmem(), vmem()],
        out_specs=vmem(),
        out_shape=jax.ShapeDtypeStruct((8, TILES + 1, 16, 128), BF),
        compiler_params=params(),
        cost_estimate=cost(2),
        name="pack",
    )(tiles, note)


def note_of(ref):
    total = jnp.zeros((1, N), F32)
    for z in range(8):
        rows = ref[z, TILES].astype(F32)
        total += rows[0:1, :] + rows[1:2, :] + rows[2:3, :]
    return total


def tile_of(ref, r, c):
    z, i = divmod(10 * r + c, TILES)
    return ref[z, i].astype(F32)


def clip_kernel(tokens_all, row0_ref, core_ref, ids_ref, own_ref, other_ref, w_ref, d_ref):
    ids = ids_ref[...]
    lane = iota((1, N), 1)
    note = note_of(own_ref) + note_of(other_ref)
    grad_d = jnp.where(lane < H, note, 0.0)
    groups = groups_of(row0_ref[0], OWN, ids_ref)
    w_factor = jnp.zeros((OWN, 1), F32)
    d_factor = jnp.zeros((1, N), F32)
    for g in range(GROUPS):
        here = (ids == float(g)) & (lane < H)
        count = jnp.sum(jnp.where(here, 1.0, 0.0), axis=1, keepdims=True)
        sumsq = jnp.sum(jnp.where(lane == H + g, note, 0.0), axis=1, keepdims=True)
        sumsq += jnp.sum(jnp.where(here, grad_d * grad_d, 0.0), axis=1, keepdims=True)
        bound = 7.0 * jnp.sqrt(count * (P_SIZE * D + 1.0) * tokens_all)
        factor = jnp.minimum(1.0, bound / jnp.sqrt(sumsq + 1e-06))
        w_factor += jnp.where(groups == float(g), factor, 0.0)
        d_factor += jnp.where(here, factor, 0.0)
    d_ref[...] = (grad_d * d_factor)[:, :H]
    for r in range(10):
        scale = w_factor[16 * r : 16 * r + 16, :]
        for ref, core in ((own_ref, core_ref[0]), (other_ref, 1 - core_ref[0])):
            for c in range(10):
                col = pl.multiple_of(core * (D // 2) + 128 * c, 128)
                w_ref[16 * r : 16 * r + 16, pl.ds(col, 128)] = tile_of(ref, r, c) * scale


def clip(tokens_all, row0, core, ids, own, other):
    return pl.pallas_call(
        functools.partial(clip_kernel, tokens_all),
        in_specs=[smem(), smem()] + [vmem()] * 3,
        out_specs=[vmem(), vmem()],
        out_shape=[jax.ShapeDtypeStruct((OWN, D), F32), jax.ShapeDtypeStruct((1, H), F32)],
        compiler_params=params(),
        cost_estimate=cost(3),
        name="clip",
    )(row0, core, ids, own, other)


def shifted(v, axis, d):
    return lax.ppermute(v, axis, [(i, (i + d) % 4) for i in range(4)])


def plus(a, b):
    return (a.astype(F32) + b.astype(F32)).astype(BF)


def far(t, axis):
    m = t.shape[1] // 2
    return shifted(t[2, :m], axis, 1), shifted(t[2, m:], axis, -1)


def passed(t, ra, rb):
    m = t.shape[1] // 2
    up = jnp.concatenate([plus(t[1, :m], ra), t[1, m:]], axis=0)
    down = jnp.concatenate([t[3, :m], plus(t[3, m:], rb)], axis=0)
    return up, down


def near(t, up, down, axis):
    total = t[0].astype(F32) + shifted(up, axis, 1).astype(F32)
    return (total + shifted(down, axis, -1).astype(F32)).astype(BF)


def direct(t, axis):
    return (t[0],) + tuple(shifted(t[d], axis, d) for d in (1, 3, 2))


def other_core(v):
    return lax.ppermute(v, "core", [(0, 1), (1, 0)])


def sum_over(v, axes):
    for unit in (1, 4):
        got = [
            lax.ppermute(v, axes, [(i, i ^ (unit * k)) for i in range(16)]) for k in (1, 2, 3)
        ]
        v = (v + got[0]) + (got[1] + got[2])
    return v


def tie(*values):
    return lax.optimization_barrier(values)


def per_device(x_in, a_log, b_in, c_in, g_out, w_out, d_skip, group_ids):
    x, a, b, c, g = (x_in[0], a_log[0], b_in[0], c_in[0], g_out[0])
    core = lax.axis_index("core")
    half = D // 2
    at = jnp.stack([lax.axis_index("y"), lax.axis_index("x")]).astype(jnp.int32)
    mine = (2 * lax.axis_index("z") + core).reshape(1).astype(jnp.int32)
    at_z = lax.axis_index("z").reshape(1).astype(jnp.int32)
    row0 = ((4 * at[0] + at[1]) * OWN).reshape(1)
    ids = jnp.pad(group_ids.astype(F32), (0, N - H), constant_values=-1.0)[None]
    tokens_all = float(T * N_SEQ * 16)

    g_mine = lax.dynamic_slice_in_dim(g, core * half, half, axis=1)
    g_other = other_core(lax.dynamic_slice_in_dim(g, (1 - core) * half, half, axis=1))

    g_both = jnp.concatenate([g_mine, g_other], axis=0)

    cum, cum_t, tail, sent = local_ends(x, a, b)
    w_out, sent = tie(w_out, sent)
    w_mine = lax.dynamic_slice_in_dim(w_out, core * half, half, axis=1)
    w_half = lax.all_gather(w_mine, ("y", "x"), axis=0, tiled=True)
    got = swap(sent, SEQ)
    y_part, grow = intra(x, cum, cum_t, b, c, d_skip)
    y_part, g_both, at = tie(y_part, g_both, at)
    start = swap(chain(got, got, mine, False), SEQ).reshape(H * P_SIZE, N)
    y_own = inter(y_part, grow, c, start)
    y_other = other_core(y_own)
    first, second = terms(at, y_own, y_other, g_both)

    first = lax.psum_scatter(first.reshape(-1, half // 2), "x", scatter_dimension=0, tiled=True)
    far_y = far(second, "y")
    w_half, _ = tie(w_half, second)
    gy_own, gy_other = gy_parts(g_both, w_half)
    *far_y, gy_own, gy_other = tie(*far_y, gy_own, gy_other)
    gy_other = other_core(gy_other)
    up, down = passed(second, *far_y)
    up, down, gy_own, gy_other = tie(up, down, gy_own, gy_other)
    second = near(second, up, down, "y")
    gy, sent_back = entries(gy_own, gy_other, x, grow, c)
    got_back = swap(sent_back, SEQ)
    steps = PAIRS // STEP // 2
    gx1, *sums = within(0, steps, x, gy, cum, cum_t, b, c, d_skip)
    first, second, gx1 = tie(first, second, gx1)
    first = direct(first.reshape(4, OWN, half // 2), "y")
    second = direct(second, "x")
    tiles = fold(first + second)
    gy, mine, tiles = tie(gy, mine, tiles)
    tiles = swap(tiles, "z")
    states = chain(got_back, got, mine, True)
    gx2, *sums = within(steps, steps, x, gy, cum, cum_t, b, c, d_skip, sums)
    tiles, gx2, states = tie(tiles, gx2, states)
    tiles, note = zsum(row0, at_z, ids, tiles, got_back)
    note, states = tie(note, states)
    last = swap(states, SEQ).reshape(H * P_SIZE, N)
    note = sum_over(note, ("y", "x"))
    tiles, note, last = tie(tiles, note, last)
    tiles = pack(tiles, note)
    tiles, last = tie(tiles, last)
    tiles = swap(tiles, "z")
    gx, ga, gb, gc = across(x, gy, grow, tail, gx1, gx2, cum, b, c, start, last, *sums)
    tiles, ga = tie(tiles, ga)
    tiles_other = other_core(tiles)
    core = core.reshape(1).astype(jnp.int32)
    clipped_w, clipped_d = clip(tokens_all, row0, core, ids, tiles, tiles_other)
    return (gx[None], ga[None], gb[None], gc[None], clipped_w, clipped_d[0])


def solution(mesh):
    fine = Mesh(mesh.devices.reshape(4, 4, 8, 2), ("y", "x", "z", "core"))
    rows = ("y", "x")
    tokens = P(rows, SEQ, None)
    return jax.shard_map(
        per_device,
        mesh=fine,
        in_specs=(
            tokens, P(rows, None, SEQ), tokens, tokens, tokens, P(rows, None), P(), P(),
        ),
        out_specs=(tokens, P(rows, None, SEQ), tokens, tokens, P(rows, None), P()),
        check_vma=False,
    )
```

```python
import functools

import jax
import jax.numpy as jnp
from jax import lax
from jax.experimental import pallas as pl
from jax.experimental.pallas import tpu as pltpu
from jax.sharding import Mesh
from jax.sharding import PartitionSpec as P

D = 2560
H = 40
P_SIZE = 64
N = 128
T = 256
GROUPS = 4
PAIRS = H // 2
SEQ = ("z", "core")
N_SEQ = 16
OWN = H * P_SIZE // N_SEQ
HIGH = lax.Precision.HIGHEST
BF = jnp.bfloat16
F32 = jnp.float32
VMEM = 56 * 1024 * 1024
WIDE = 5
STEP = 2
ROWS = OWN + 16
TILES = 13


def nn(a, b):
    return lax.dot_general(a, b, (((1,), (0,)), ((), ())), preferred_element_type=F32)


def nt(a, b):
    return lax.dot_general(a, b, (((1,), (1,)), ((), ())), preferred_element_type=F32)


def tn(a, b):
    return lax.dot_general(a, b, (((0,), (0,)), ((), ())), preferred_element_type=F32)


def iota(shape, dim):
    return lax.broadcasted_iota(jnp.int32, shape, dim)


def whole(shape):
    return pl.BlockSpec(shape, lambda *_: (0,) * len(shape))


def wide(rows, pairs):
    return pl.BlockSpec((rows, pairs * 2 * P_SIZE), lambda p: (0, p))


def state_block(pairs):
    return pl.BlockSpec((pairs * 2 * P_SIZE, N), lambda p: (p, 0))


def smem():
    return pl.BlockSpec(memory_space=pltpu.SMEM)


def vmem():
    return pl.BlockSpec(memory_space=pltpu.VMEM)


def params():
    return pltpu.CompilerParams(vmem_limit_bytes=VMEM)


def cost(micros):
    return pl.CostEstimate(flops=0, bytes_accessed=int(micros * 3e6), transcendentals=0)


def column(cum_t, head):
    return jnp.sum(jnp.where(iota(cum_t.shape, 1) == head, cum_t, 0.0), axis=1, keepdims=True)


def low_half(shape):
    return iota(shape, 1) < P_SIZE


def lanes_of(i):
    return slice(i * 2 * P_SIZE, (i + 1) * 2 * P_SIZE)


def put_states(out_ref, states, first, pairs):
    chunks = pairs * 2 * P_SIZE // OWN
    rows = states.astype(BF).reshape(chunks, OWN, N)
    out_ref[pl.ds(first * 2 * P_SIZE // OWN, chunks), :OWN, :] = rows


def put_note(out_ref, pieces):
    at = iota((16, N), 0)
    note = jnp.zeros((16, N), F32)
    for i, piece in enumerate(pieces):
        note = jnp.where(at == i, piece, note)
    for s in range(N_SEQ):
        out_ref[s, OWN:, :] = note.astype(BF)


def ends_kernel(x_ref, a_ref, b_ref, cum_ref, cum_t_ref, tail_ref, out_ref, pieces):
    step = pl.program_id(0)

    @pl.when(step == 0)
    def _():
        a = a_ref[...]
        upto = (iota((T, T), 0) <= iota((T, T), 1)).astype(F32)
        cum_ref[...] = jnp.dot(a, upto, precision=HIGH, preferred_element_type=F32)
        down = (iota((T, T), 1) <= iota((T, T), 0)).astype(F32)
        cum_t = lax.dot_general(
            down, a, (((1,), (1,)), ((), ())), precision=HIGH, preferred_element_type=F32
        )
        cum_t_ref[...] = cum_t
        total = jnp.concatenate([cum_t[T - 1 :, :], jnp.zeros((1, N - H), F32)], axis=1)
        hi = jnp.floor(total)
        mid = jnp.floor((total - hi) * 256.0) / 256.0
        put_note(out_ref, (hi, mid, total - hi - mid))
        tail = jnp.exp(cum_t[T - 1 :, :] - cum_t)
        high = tail.astype(BF)
        pieces[0] = high
        pieces[1] = (tail - high.astype(F32)).astype(BF)

    width = WIDE * 2 * P_SIZE
    pick = iota((H, width), 0) == step * 2 * WIDE + iota((H, width), 1) // P_SIZE
    pick = pick.astype(BF)
    tail = nn(pieces[0], pick) + nn(pieces[1], pick)
    tail_ref[...] = tail.astype(BF)
    states = tn((x_ref[...] * tail).astype(BF), b_ref[...].astype(BF))
    put_states(out_ref, states, step * WIDE, WIDE)


def local_ends(x, a, b):
    return pl.pallas_call(
        ends_kernel,
        grid=(PAIRS // WIDE,),
        in_specs=[wide(T, WIDE), whole((H, T)), whole((T, N))],
        out_specs=[whole((H, T)), whole((T, H)), wide(T, WIDE), whole((N_SEQ, ROWS, N))],
        out_shape=[
            jax.ShapeDtypeStruct((H, T), F32),
            jax.ShapeDtypeStruct((T, H), F32),
            jax.ShapeDtypeStruct((T, D), BF),
            jax.ShapeDtypeStruct((N_SEQ, ROWS, N), BF),
        ],
        scratch_shapes=[pltpu.VMEM((2, T, H), BF)],
        compiler_params=params(),
        cost_estimate=cost(6),
        name="ends",
    )(x, a, b)


def intra_kernel(x_ref, cum_ref, cum_t_ref, b_ref, c_ref, skip_ref, y_ref, grow_ref, scores):
    step = pl.program_id(0)

    @pl.when(step == 0)
    def _():
        keep = iota((T, T), 0) >= iota((T, T), 1)
        scores[...] = jnp.where(keep, nt(c_ref[...].astype(BF), b_ref[...].astype(BF)), 0.0)

    for i in range(STEP):
        x = x_ref[:, lanes_of(i)]
        xb = x.astype(BF)
        low = low_half(x.shape)
        head = 2 * (step * STEP + i)
        parts = []
        sides = []
        for k in range(2):
            sides.append(column(cum_t_ref[...], head + k))
            diff = sides[k] - cum_ref[pl.ds(head + k, 1), :]
            mixed = (jnp.exp(jnp.minimum(diff, 0.0)) * scores[...]).astype(BF)
            parts.append(nn(mixed, xb))
        skip = jnp.where(low, skip_ref[head], skip_ref[head + 1])
        y_ref[:, lanes_of(i)] = jnp.where(low, parts[0], parts[1]) + skip * x
        grow = jnp.exp(jnp.where(low, sides[0], sides[1]))
        grow_ref[:, lanes_of(i)] = grow.astype(BF)


def intra(x, cum, cum_t, b, c, skip):
    return pl.pallas_call(
        intra_kernel,
        grid=(PAIRS // STEP,),
        in_specs=[
            wide(T, STEP), whole((H, T)), whole((T, H)), whole((T, N)), whole((T, N)), smem(),
        ],
        out_specs=[wide(T, STEP)] * 2,
        out_shape=[jax.ShapeDtypeStruct((T, D), F32), jax.ShapeDtypeStruct((T, D), BF)],
        scratch_shapes=[pltpu.VMEM((T, T), F32)],
        compiler_params=params(),
        cost_estimate=cost(9),
        name="intra",
    )(x, cum, cum_t, b, c, skip)


def inter_kernel(part_ref, grow_ref, c_ref, start_ref, y_ref):
    read = nt(c_ref[...].astype(BF), start_ref[...])
    y_ref[...] = (part_ref[...] + grow_ref[...].astype(F32) * read).T.astype(BF)


def inter(part, grow, c, start):
    return pl.pallas_call(
        inter_kernel,
        grid=(PAIRS // WIDE,),
        in_specs=[wide(T, WIDE), wide(T, WIDE), whole((T, N)), state_block(WIDE)],
        out_specs=pl.BlockSpec((WIDE * 2 * P_SIZE, T), lambda p: (p, 0)),
        out_shape=jax.ShapeDtypeStruct((D, T), BF),
        compiler_params=params(),
        cost_estimate=cost(5),
        name="inter",
    )(part, grow, c, start)


def chain_kernel(reverse, mine_ref, parts_ref, totals_ref, out_ref):
    owner = (mine_ref[0] * OWN + iota((OWN, N), 0)) // P_SIZE == iota((OWN, N), 1)
    carry = jnp.zeros((OWN, N), F32)
    for s in range(N_SEQ - 1, -1, -1) if reverse else range(N_SEQ):
        out_ref[s] = carry.astype(BF)
        pieces = totals_ref[s, OWN:, :].astype(F32)
        total = pieces[0:1, :] + pieces[1:2, :] + pieces[2:3, :]
        decay = jnp.sum(jnp.where(owner, total, 0.0), axis=1, keepdims=True)
        carry = jnp.exp(decay) * carry + parts_ref[s, :OWN, :].astype(F32)


def chain(parts, totals, mine, reverse):
    return pl.pallas_call(
        functools.partial(chain_kernel, reverse),
        in_specs=[smem(), vmem(), vmem()],
        out_specs=vmem(),
        out_shape=jax.ShapeDtypeStruct((N_SEQ, OWN, N), BF),
        compiler_params=params(),
        cost_estimate=cost(3),
        name="chain",
    )(mine, parts, totals)


def swap(v, axis):
    return lax.all_to_all(v, axis, 0, 0, tiled=True)


def term_kernel(at_ref, yo_ref, yx_ref, g_ref, first_ref, near_ref, far_up_ref, far_down_ref):
    step = pl.program_id(0)
    half = g_ref.shape[1] // 2
    term = nn(jnp.concatenate([yo_ref[...], yx_ref[...]], axis=1), g_ref[...]).astype(BF)
    for k in range(4):
        rows = slice(k * OWN, (k + 1) * OWN)
        first_ref[k, 0] = term[rows, :half]
        rel = (k + 4 - at_ref[1]) % 4

        @pl.when(step != 2)
        def _():
            near_ref[0, rel] = term[rows, half:]

        @pl.when((step == 2) & (rel < 2))
        def _():
            far_up_ref[rel] = term[rows, half:]

        @pl.when((step == 2) & (rel >= 2))
        def _():
            far_down_ref[rel - 2] = term[rows, half:]


def terms(at, y_own, y_other, g):
    rows = pl.BlockSpec((4 * OWN, T), lambda i, at: ((at[0] + i) % 4, 0))
    half = g.shape[1] // 2
    part = jax.ShapeDtypeStruct((2, OWN, half), BF)
    return pl.pallas_call(
        term_kernel,
        grid_spec=pltpu.PrefetchScalarGridSpec(
            num_scalar_prefetch=1,
            grid=(4,),
            in_specs=[rows, rows, whole(g.shape)],
            out_specs=[
                pl.BlockSpec((4, 1, OWN, half), lambda i, at: (0, i, 0, 0)),
                pl.BlockSpec((1, 4, OWN, half), lambda i, at: (i - i // 2, 0, 0, 0)),
                whole(part.shape),
                whole(part.shape),
            ],
        ),
        out_shape=[
            jax.ShapeDtypeStruct((4, 4, OWN, half), BF),
            jax.ShapeDtypeStruct((3, 4, OWN, half), BF),
            part,
            part,
        ],
        compiler_params=params(),
        cost_estimate=cost(8),
        name="terms",
    )(at, y_own, y_other, g)


def gy_kernel(g_ref, w_ref, own_ref, other_ref):
    got = nt(g_ref[...], w_ref[...])
    own_ref[...] = got[:T]
    other_ref[...] = got[T:].astype(BF)


def gy_parts(g, w):
    rows = 4 * OWN
    return pl.pallas_call(
        gy_kernel,
        grid=(4,),
        in_specs=[whole(g.shape), pl.BlockSpec((rows, w.shape[1]), lambda i: (i, 0))],
        out_specs=[pl.BlockSpec((T, rows), lambda i: (0, i))] * 2,
        out_shape=[jax.ShapeDtypeStruct((T, D), F32), jax.ShapeDtypeStruct((T, D), BF)],
        compiler_params=params(),
        cost_estimate=cost(8),
        name="gy_parts",
    )(g, w)


def entry_kernel(own_ref, other_ref, x_ref, grow_ref, c_ref, gy_ref, out_ref, sums):
    step = pl.program_id(0)
    c = c_ref[...].astype(BF)
    found = []
    for i in range(WIDE):
        at = lanes_of(i)
        gy = own_ref[:, at] + other_ref[:, at].astype(F32)
        gy_ref[:, at] = gy.astype(BF)
        sums[pl.ds(step * WIDE + i, 1), :] = jnp.sum(gy * x_ref[:, at], axis=0, keepdims=True)
        found.append(tn((gy * grow_ref[:, at].astype(F32)).astype(BF), c))
    put_states(out_ref, jnp.concatenate(found, axis=0), step * WIDE, WIDE)

    @pl.when(step == PAIRS // WIDE - 1)
    def _():
        total = sums[...]
        low = low_half(total.shape)
        head = 2 * iota(total.shape, 0)
        lane = iota(total.shape, 1)
        even = jnp.sum(jnp.where(low, total, 0.0), axis=1, keepdims=True)
        odd = jnp.sum(jnp.where(low, 0.0, total), axis=1, keepdims=True)
        each = jnp.where(lane == head, even, 0.0) + jnp.where(lane == head + 1, odd, 0.0)
        gd = jnp.sum(each, axis=0, keepdims=True)
        hi = gd.astype(BF).astype(F32)
        mid = (gd - hi).astype(BF).astype(F32)
        put_note(out_ref, (hi, mid, gd - hi - mid))


def entries(own, other, x, grow, c):
    return pl.pallas_call(
        entry_kernel,
        grid=(PAIRS // WIDE,),
        in_specs=[wide(T, WIDE)] * 4 + [whole((T, N))],
        out_specs=[wide(T, WIDE), whole((N_SEQ, ROWS, N))],
        out_shape=[
            jax.ShapeDtypeStruct((T, D), BF),
            jax.ShapeDtypeStruct((N_SEQ, ROWS, N), BF),
        ],
        scratch_shapes=[pltpu.VMEM((PAIRS, 2 * P_SIZE), F32)],
        compiler_params=params(),
        cost_estimate=cost(6),
        name="entries",
    )(own, other, x, grow, c)


def within_kernel(
    first, steps, x_ref, gy_ref, cum_ref, cum_t_ref, b_ref, c_ref, skip_ref, *rest
):
    before = rest[:-8]
    gx_ref, ga_ref, gb_ref, gc_ref, scores, d_scores, rows, cols = rest[-8:]
    step = pl.program_id(0)

    @pl.when(step == 0)
    def _():
        keep = iota((T, T), 1) >= iota((T, T), 0)
        scores[...] = jnp.where(keep, nt(b_ref[...].astype(BF), c_ref[...].astype(BF)), 0.0)
        d_scores[...] = jnp.zeros_like(d_scores)
        rows[...] = jnp.zeros_like(rows)
        cols[...] = jnp.zeros_like(cols)

    lanes = iota((T, N), 1)
    low = low_half((T, 2 * P_SIZE))
    for i in range(STEP):
        pair = (first + step) * STEP + i
        at = lanes_of(i)
        x = x_ref[:, at]
        gyb = gy_ref[:, at]
        parts = []
        for k in range(2):
            head = 2 * pair + k
            diff = cum_ref[pl.ds(head, 1), :] - column(cum_t_ref[...], head)
            weights = jnp.exp(jnp.minimum(diff, 0.0))
            mine = jnp.where(low if k == 0 else ~low, x, 0.0).astype(BF)
            d_mixed = weights * nt(mine, gyb)
            d_scores[...] += d_mixed
            parts.append(nn((weights * scores[...]).astype(BF), gyb))
            change = d_mixed * scores[...]
            rows[pl.ds(head, 1), :] = jnp.sum(change, axis=0, keepdims=True)
            down = jnp.sum(change, axis=1, keepdims=True)
            cols[...] -= jnp.where(lanes == head, down, 0.0)
        skip = jnp.where(low, skip_ref[2 * pair], skip_ref[2 * pair + 1])
        gx_ref[:, at] = jnp.where(low, parts[0], parts[1]) + skip * gyb.astype(F32)

    @pl.when(step == steps - 1)
    def _():
        keep = iota((T, T), 1) >= iota((T, T), 0)
        ds = jnp.where(keep, d_scores[...], 0.0).astype(BF)
        gb = nn(ds, c_ref[...].astype(BF))
        gc = tn(ds, b_ref[...].astype(BF))
        after = (iota((T, T), 0) >= iota((T, T), 1)).astype(F32)
        dims = (((0,), (0,)), ((), ()))
        ga = jnp.dot(rows[...], after, precision=HIGH, preferred_element_type=F32)
        up = lax.dot_general(cols[...], after, dims, precision=HIGH, preferred_element_type=F32)
        for out, add, ref in zip((ga_ref, gb_ref, gc_ref), (ga + up[:H], gb, gc), before or (None,) * 3):
            out[...] = add if ref is None else add + ref[...]


def within(first, steps, x, gy, cum, cum_t, b, c, skip, before=()):
    here = pl.BlockSpec((T, STEP * 2 * P_SIZE), lambda p: (0, first + p))
    return pl.pallas_call(
        functools.partial(within_kernel, first, steps),
        grid=(steps,),
        in_specs=[
            here, here, whole((H, T)), whole((T, H)), whole((T, N)), whole((T, N)), smem(),
        ]
        + [whole(v.shape) for v in before],
        out_specs=[wide(T, STEP), whole((H, T)), whole((T, N)), whole((T, N))],
        out_shape=[
            jax.ShapeDtypeStruct((T, steps * STEP * 2 * P_SIZE), F32),
            jax.ShapeDtypeStruct((H, T), F32),
            jax.ShapeDtypeStruct((T, N), F32),
            jax.ShapeDtypeStruct((T, N), F32),
        ],
        scratch_shapes=[
            pltpu.VMEM((T, T), F32),
            pltpu.VMEM((T, T), F32),
            pltpu.VMEM((H, T), F32),
            pltpu.VMEM((T, N), F32),
        ],
        compiler_params=params(),
        cost_estimate=cost(7),
        name="within",
    )(x, gy, cum, cum_t, b, c, skip, *before)


def across_kernel(
    x_ref, gy_ref, grow_ref, tail_ref, part_ref, part2_ref, cum_ref, b_ref, c_ref, start_ref, last_ref,
    ga_in, gb_in, gc_in,
    gx_ref, ga_ref, gb_ref, gc_ref,
    cols, tails, totals,
):
    step = pl.program_id(0)
    bb = b_ref[...].astype(BF)
    cb = c_ref[...].astype(BF)

    @pl.when(step == 0)
    def _():
        cols[...] = jnp.zeros_like(cols)
        tails[...] = jnp.zeros_like(tails)
        gb_ref[...] = gb_in[...]
        gc_ref[...] = gc_in[...]

    width = WIDE * 2 * P_SIZE
    start = start_ref[...]
    last = last_ref[...]
    tail = tail_ref[...].astype(F32)
    pick = iota((width, N), 1) == step * 2 * WIDE + iota((width, N), 0) // P_SIZE
    grown = gy_ref[...].astype(F32) * grow_ref[...].astype(F32)
    cols[...] += nn((grown * nt(cb, start)).astype(BF), pick.astype(BF))
    gc_ref[...] += nn(grown.astype(BF), start)
    faded = x_ref[...] * tail
    back = nt(bb, last)
    tails[...] += nn((faded * back).astype(BF), pick.astype(BF))
    gb_ref[...] += nn(faded.astype(BF), last)
    part = jnp.where(step < PAIRS // WIDE // 2, part_ref[...], part2_ref[...])
    gx_ref[...] = part + tail * back
    both = jnp.sum(start.astype(F32) * last.astype(F32), axis=1, keepdims=True)
    totals[pl.ds(step, 1), :] = jnp.sum(jnp.where(pick, both, 0.0), axis=0, keepdims=True)

    @pl.when(step == PAIRS // WIDE - 1)
    def _():
        after = (iota((T, T), 0) >= iota((T, T), 1)).astype(F32)
        before = (iota((T, T), 0) < iota((T, T), 1)).astype(F32)
        dims = (((0,), (0,)), ((), ()))
        up = lax.dot_general(cols[...], after, dims, precision=HIGH, preferred_element_type=F32)
        up += lax.dot_general(tails[...], before, dims, precision=HIGH, preferred_element_type=F32)
        total = jnp.sum(totals[...], axis=0, keepdims=True)
        total = jnp.sum(jnp.where(iota((H, N), 0) == iota((H, N), 1), total, 0.0), axis=1, keepdims=True)
        ga_ref[...] = ga_in[...] + up[:H] + jnp.exp(cum_ref[:, T - 1 : T]) * total


def across(x, gy, grow, tail, part, part2, cum, b, c, start, last, ga, gb, gc):
    width = WIDE * 2 * P_SIZE
    last_part = PAIRS // WIDE // 2 - 1
    return pl.pallas_call(
        across_kernel,
        grid=(PAIRS // WIDE,),
        in_specs=[wide(T, WIDE)] * 4
        + [
            pl.BlockSpec((T, width), lambda p: (0, jnp.minimum(p, last_part))),
            pl.BlockSpec((T, width), lambda p: (0, jnp.maximum(p - last_part - 1, 0))),
        ]
        + [whole((H, T)), whole((T, N)), whole((T, N))]
        + [state_block(WIDE), state_block(WIDE), whole((H, T)), whole((T, N)), whole((T, N))],
        out_specs=[wide(T, WIDE), whole((H, T)), whole((T, N)), whole((T, N))],
        out_shape=[
            jax.ShapeDtypeStruct((T, D), F32),
            jax.ShapeDtypeStruct((H, T), F32),
            jax.ShapeDtypeStruct((T, N), F32),
            jax.ShapeDtypeStruct((T, N), F32),
        ],
        scratch_shapes=[
            pltpu.VMEM((T, N), F32),
            pltpu.VMEM((T, N), F32),
            pltpu.VMEM((PAIRS // WIDE, N), F32),
        ],
        compiler_params=params(),
        cost_estimate=cost(8),
        name="across",
    )(x, gy, grow, tail, part, part2, cum, b, c, start, last, ga, gb, gc)


def fold_kernel(a0, a1, a2, a3, b0, b1, b2, b3, out_ref):
    sums = []
    for parts in ((a0, a1, a2, a3), (b0, b1, b2, b3)):
        total = parts[0][...].astype(F32)
        for part in parts[1:]:
            total += part[...].astype(F32)
        sums.append(total.astype(BF))
    for q in range(8 * TILES):
        r, c = divmod(q, 10)
        if r < 10:
            tile = sums[c // 5][16 * r : 16 * r + 16, 128 * (c % 5) : 128 * (c % 5) + 128]
        else:
            tile = jnp.zeros((16, 128), BF)
        out_ref[q // TILES, q % TILES] = tile


def fold(parts):
    return pl.pallas_call(
        fold_kernel,
        in_specs=[vmem()] * 8,
        out_specs=vmem(),
        out_shape=jax.ShapeDtypeStruct((8, TILES, 16, 128), BF),
        compiler_params=params(),
        cost_estimate=cost(3),
        name="fold",
    )(*parts)


def groups_of(row0, count, ids_ref):
    heads = (row0 + iota((count, N), 0)) // P_SIZE == iota((count, N), 1)
    return jnp.sum(jnp.where(heads, ids_ref[...], 0.0), axis=1, keepdims=True)


def zsum_kernel(row0_ref, z_ref, ids_ref, got_ref, parts_ref, out_ref, note_ref):
    total = parts_ref[0].astype(F32)
    for z in range(1, 8):
        total += parts_ref[z].astype(F32)
    out_ref[...] = total.astype(BF)
    found = jnp.zeros((16, N), F32)
    for i in range(TILES):
        row = row0_ref[0] + 16 * ((z_ref[0] * TILES + i) // 10)
        place = iota((16, N), 1) - H == groups_of(row, 16, ids_ref).astype(jnp.int32)
        tile = total[i]
        found += jnp.where(place, jnp.sum(tile * tile, axis=1, keepdims=True), 0.0)
    d_sum = jnp.zeros((1, N), F32)
    for s in range(N_SEQ):
        pieces = got_ref[s, OWN:, :].astype(F32)
        d_sum += pieces[0:1, :] + pieces[1:2, :] + pieces[2:3, :]
    note_ref[...] = jnp.sum(found, axis=0, keepdims=True) + d_sum / N_SEQ


def zsum(row0, z, ids, parts, got):
    return pl.pallas_call(
        zsum_kernel,
        in_specs=[smem(), smem()] + [vmem()] * 3,
        out_specs=[vmem(), vmem()],
        out_shape=[
            jax.ShapeDtypeStruct((TILES, 16, 128), BF),
            jax.ShapeDtypeStruct((1, N), F32),
        ],
        compiler_params=params(),
        cost_estimate=cost(2),
        name="zsum",
    )(row0, z, ids, got, parts)


def pack_kernel(tiles_ref, note_ref, out_ref):
    note = note_ref[...]
    hi = note.astype(BF).astype(F32)
    mid = (note - hi).astype(BF).astype(F32)
    at = iota((16, N), 0)
    rows = jnp.where(at == 0, hi, jnp.where(at == 1, mid, jnp.where(at == 2, note - hi - mid, 0.0)))
    for z in range(8):
        out_ref[z, :TILES] = tiles_ref[...]
        out_ref[z, TILES] = rows.astype(BF)


def pack(tiles, note):
    return pl.pallas_call(
        pack_kernel,
        in_specs=[vmem(), vmem()],
        out_specs=vmem(),
        out_shape=jax.ShapeDtypeStruct((8, TILES + 1, 16, 128), BF),
        compiler_params=params(),
        cost_estimate=cost(2),
        name="pack",
    )(tiles, note)


def note_of(ref):
    total = jnp.zeros((1, N), F32)
    for z in range(8):
        rows = ref[z, TILES].astype(F32)
        total += rows[0:1, :] + rows[1:2, :] + rows[2:3, :]
    return total


def tile_of(ref, r, c):
    z, i = divmod(10 * r + c, TILES)
    return ref[z, i].astype(F32)


def clip_kernel(tokens_all, row0_ref, core_ref, ids_ref, own_ref, other_ref, w_ref, d_ref):
    ids = ids_ref[...]
    lane = iota((1, N), 1)
    note = note_of(own_ref) + note_of(other_ref)
    grad_d = jnp.where(lane < H, note, 0.0)
    groups = groups_of(row0_ref[0], OWN, ids_ref)
    w_factor = jnp.zeros((OWN, 1), F32)
    d_factor = jnp.zeros((1, N), F32)
    for g in range(GROUPS):
        here = (ids == float(g)) & (lane < H)
        count = jnp.sum(jnp.where(here, 1.0, 0.0), axis=1, keepdims=True)
        sumsq = jnp.sum(jnp.where(lane == H + g, note, 0.0), axis=1, keepdims=True)
        sumsq += jnp.sum(jnp.where(here, grad_d * grad_d, 0.0), axis=1, keepdims=True)
        bound = 7.0 * jnp.sqrt(count * (P_SIZE * D + 1.0) * tokens_all)
        factor = jnp.minimum(1.0, bound / jnp.sqrt(sumsq + 1e-06))
        w_factor += jnp.where(groups == float(g), factor, 0.0)
        d_factor += jnp.where(here, factor, 0.0)
    d_ref[...] = (grad_d * d_factor)[:, :H]
    for r in range(10):
        scale = w_factor[16 * r : 16 * r + 16, :]
        for ref, core in ((own_ref, core_ref[0]), (other_ref, 1 - core_ref[0])):
            for c in range(10):
                col = pl.multiple_of(core * (D // 2) + 128 * c, 128)
                w_ref[16 * r : 16 * r + 16, pl.ds(col, 128)] = tile_of(ref, r, c) * scale


def clip(tokens_all, row0, core, ids, own, other):
    return pl.pallas_call(
        functools.partial(clip_kernel, tokens_all),
        in_specs=[smem(), smem()] + [vmem()] * 3,
        out_specs=[vmem(), vmem()],
        out_shape=[jax.ShapeDtypeStruct((OWN, D), F32), jax.ShapeDtypeStruct((1, H), F32)],
        compiler_params=params(),
        cost_estimate=cost(3),
        name="clip",
    )(row0, core, ids, own, other)


def shifted(v, axis, d):
    return lax.ppermute(v, axis, [(i, (i + d) % 4) for i in range(4)])


def plus(a, b):
    return (a.astype(F32) + b.astype(F32)).astype(BF)


def passed(t, ra, rb):
    m = t.shape[1] // 2
    up = jnp.concatenate([plus(t[1, :m], ra), t[1, m:]], axis=0)
    down = jnp.concatenate([t[2, :m], plus(t[2, m:], rb)], axis=0)
    return up, down


def near(t, up, down, axis):
    total = t[0].astype(F32) + shifted(up, axis, 1).astype(F32)
    return (total + shifted(down, axis, -1).astype(F32)).astype(BF)


def direct(t, axis):
    return (t[0],) + tuple(shifted(t[d], axis, d) for d in (1, 3, 2))


def other_core(v):
    return lax.ppermute(v, "core", [(0, 1), (1, 0)])


def sum_over(v, axes):
    for unit in (1, 4):
        got = [
            lax.ppermute(v, axes, [(i, i ^ (unit * k)) for i in range(16)]) for k in (1, 2, 3)
        ]
        v = (v + got[0]) + (got[1] + got[2])
    return v


def tie(*values):
    return lax.optimization_barrier(values)


def per_device(x_in, a_log, b_in, c_in, g_out, w_out, d_skip, group_ids):
    x, a, b, c, g = (x_in[0], a_log[0], b_in[0], c_in[0], g_out[0])
    core = lax.axis_index("core")
    half = D // 2
    at = jnp.stack([lax.axis_index("y"), lax.axis_index("x")]).astype(jnp.int32)
    mine = (2 * lax.axis_index("z") + core).reshape(1).astype(jnp.int32)
    at_z = lax.axis_index("z").reshape(1).astype(jnp.int32)
    row0 = ((4 * at[0] + at[1]) * OWN).reshape(1)
    ids = jnp.pad(group_ids.astype(F32), (0, N - H), constant_values=-1.0)[None]
    tokens_all = float(T * N_SEQ * 16)

    g_mine = lax.dynamic_slice_in_dim(g, core * half, half, axis=1)
    g_other = other_core(lax.dynamic_slice_in_dim(g, (1 - core) * half, half, axis=1))

    g_both = jnp.concatenate([g_mine, g_other], axis=0)

    cum, cum_t, tail, sent = local_ends(x, a, b)
    w_out, sent = tie(w_out, sent)
    w_mine = lax.dynamic_slice_in_dim(w_out, core * half, half, axis=1)
    w_half = lax.all_gather(w_mine, ("y", "x"), axis=0, tiled=True)
    got = swap(sent, SEQ)
    y_part, grow = intra(x, cum, cum_t, b, c, d_skip)
    y_part, g_both, at = tie(y_part, g_both, at)
    start = swap(chain(got, got, mine, False), SEQ).reshape(H * P_SIZE, N)
    y_own = inter(y_part, grow, c, start)
    y_other = other_core(y_own)
    first, second, far_up, far_down = terms(at, y_own, y_other, g_both)

    first = lax.psum_scatter(first.reshape(-1, half // 2), "x", scatter_dimension=0, tiled=True)
    far_y = (shifted(far_up, "y", 1), shifted(far_down, "y", -1))
    w_half, _ = tie(w_half, second)
    gy_own, gy_other = gy_parts(g_both, w_half)
    *far_y, gy_own, gy_other = tie(*far_y, gy_own, gy_other)
    gy_other = other_core(gy_other)
    up, down = passed(second, *far_y)
    up, down, gy_own, gy_other = tie(up, down, gy_own, gy_other)
    second = near(second, up, down, "y")
    gy, sent_back = entries(gy_own, gy_other, x, grow, c)
    got_back = swap(sent_back, SEQ)
    steps = PAIRS // STEP // 2
    gx1, *sums = within(0, steps, x, gy, cum, cum_t, b, c, d_skip)
    first, gx1 = tie(first, gx1)
    first = direct(first.reshape(4, OWN, half // 2), "y")
    second = direct(second, "x")
    tiles = fold(first + second)
    gy, mine, tiles = tie(gy, mine, tiles)
    tiles = swap(tiles, "z")
    states = chain(got_back, got, mine, True)
    gx2, *sums = within(steps, steps, x, gy, cum, cum_t, b, c, d_skip, sums)
    tiles, gx2, states = tie(tiles, gx2, states)
    tiles, note = zsum(row0, at_z, ids, tiles, got_back)
    note, states = tie(note, states)
    last = swap(states, SEQ).reshape(H * P_SIZE, N)
    note = sum_over(note, ("y", "x"))
    tiles, note, last = tie(tiles, note, last)
    tiles = pack(tiles, note)
    tiles, last = tie(tiles, last)
    tiles = swap(tiles, "z")
    gx, ga, gb, gc = across(x, gy, grow, tail, gx1, gx2, cum, b, c, start, last, *sums)
    tiles, ga = tie(tiles, ga)
    tiles_other = other_core(tiles)
    core = core.reshape(1).astype(jnp.int32)
    clipped_w, clipped_d = clip(tokens_all, row0, core, ids, tiles, tiles_other)
    return (gx[None], ga[None], gb[None], gc[None], clipped_w, clipped_d[0])


def solution(mesh):
    fine = Mesh(mesh.devices.reshape(4, 4, 8, 2), ("y", "x", "z", "core"))
    rows = ("y", "x")
    tokens = P(rows, SEQ, None)
    return jax.shard_map(
        per_device,
        mesh=fine,
        in_specs=(
            tokens, P(rows, None, SEQ), tokens, tokens, tokens, P(rows, None), P(), P(),
        ),
        out_specs=(tokens, P(rows, None, SEQ), tokens, tokens, P(rows, None), P()),
        check_vma=False,
    )
```

```python
import functools

import jax
import jax.numpy as jnp
from jax import lax
from jax.experimental import pallas as pl
from jax.experimental.pallas import tpu as pltpu
from jax.sharding import Mesh
from jax.sharding import PartitionSpec as P

D = 2560
H = 40
P_SIZE = 64
N = 128
T = 256
GROUPS = 4
PAIRS = H // 2
SEQ = ("z", "core")
N_SEQ = 16
OWN = H * P_SIZE // N_SEQ
HIGH = lax.Precision.HIGHEST
BF = jnp.bfloat16
F32 = jnp.float32
VMEM = 62 * 1024 * 1024
WIDE = 5
STEP = 2
ROWS = OWN + 16
TILES = 13


def nn(a, b):
    return lax.dot_general(a, b, (((1,), (0,)), ((), ())), preferred_element_type=F32)


def nt(a, b):
    return lax.dot_general(a, b, (((1,), (1,)), ((), ())), preferred_element_type=F32)


def tn(a, b):
    return lax.dot_general(a, b, (((0,), (0,)), ((), ())), preferred_element_type=F32)


def iota(shape, dim):
    return lax.broadcasted_iota(jnp.int32, shape, dim)


def whole(shape):
    return pl.BlockSpec(shape, lambda *_: (0,) * len(shape))


def wide(rows, pairs):
    return pl.BlockSpec((rows, pairs * 2 * P_SIZE), lambda p: (0, p))


def state_block(pairs):
    return pl.BlockSpec((pairs * 2 * P_SIZE, N), lambda p: (p, 0))


def smem():
    return pl.BlockSpec(memory_space=pltpu.SMEM)


def vmem():
    return pl.BlockSpec(memory_space=pltpu.VMEM)


def params():
    return pltpu.CompilerParams(vmem_limit_bytes=VMEM)


def cost(micros):
    return pl.CostEstimate(flops=0, bytes_accessed=int(micros * 3e6), transcendentals=0)


def column(cum_t, head):
    return jnp.sum(jnp.where(iota(cum_t.shape, 1) == head, cum_t, 0.0), axis=1, keepdims=True)


def low_half(shape):
    return iota(shape, 1) < P_SIZE


def lanes_of(i):
    return slice(i * 2 * P_SIZE, (i + 1) * 2 * P_SIZE)


def put_states(out_ref, states, first, pairs):
    chunks = pairs * 2 * P_SIZE // OWN
    rows = states.astype(BF).reshape(chunks, OWN, N)
    out_ref[pl.ds(first * 2 * P_SIZE // OWN, chunks), :OWN, :] = rows


def put_note(out_ref, pieces):
    at = iota((16, N), 0)
    note = jnp.zeros((16, N), F32)
    for i, piece in enumerate(pieces):
        note = jnp.where(at == i, piece, note)
    for s in range(N_SEQ):
        out_ref[s, OWN:, :] = note.astype(BF)


def ends_kernel(x_ref, a_ref, b_ref, cum_ref, cum_t_ref, tail_ref, out_ref, pieces):
    step = pl.program_id(0)

    @pl.when(step == 0)
    def _():
        a = a_ref[...]
        upto = (iota((T, T), 0) <= iota((T, T), 1)).astype(F32)
        cum_ref[...] = jnp.dot(a, upto, precision=HIGH, preferred_element_type=F32)
        down = (iota((T, T), 1) <= iota((T, T), 0)).astype(F32)
        cum_t = lax.dot_general(
            down, a, (((1,), (1,)), ((), ())), precision=HIGH, preferred_element_type=F32
        )
        cum_t_ref[...] = cum_t
        total = jnp.concatenate([cum_t[T - 1 :, :], jnp.zeros((1, N - H), F32)], axis=1)
        hi = jnp.floor(total)
        mid = jnp.floor((total - hi) * 256.0) / 256.0
        put_note(out_ref, (hi, mid, total - hi - mid))
        tail = jnp.exp(cum_t[T - 1 :, :] - cum_t)
        high = tail.astype(BF)
        pieces[0] = high
        pieces[1] = (tail - high.astype(F32)).astype(BF)

    width = WIDE * 2 * P_SIZE
    pick = iota((H, width), 0) == step * 2 * WIDE + iota((H, width), 1) // P_SIZE
    pick = pick.astype(BF)
    tail = nn(pieces[0], pick) + nn(pieces[1], pick)
    tail_ref[...] = tail.astype(BF)
    states = tn((x_ref[...] * tail).astype(BF), b_ref[...].astype(BF))
    put_states(out_ref, states, step * WIDE, WIDE)


def local_ends(x, a, b):
    return pl.pallas_call(
        ends_kernel,
        grid=(PAIRS // WIDE,),
        in_specs=[wide(T, WIDE), whole((H, T)), whole((T, N))],
        out_specs=[whole((H, T)), whole((T, H)), wide(T, WIDE), whole((N_SEQ, ROWS, N))],
        out_shape=[
            jax.ShapeDtypeStruct((H, T), F32),
            jax.ShapeDtypeStruct((T, H), F32),
            jax.ShapeDtypeStruct((T, D), BF),
            jax.ShapeDtypeStruct((N_SEQ, ROWS, N), BF),
        ],
        scratch_shapes=[pltpu.VMEM((2, T, H), BF)],
        compiler_params=params(),
        cost_estimate=cost(6),
        name="ends",
    )(x, a, b)


def intra_kernel(x_ref, cum_ref, cum_t_ref, b_ref, c_ref, skip_ref, y_ref, grow_ref, scores):
    step = pl.program_id(0)

    @pl.when(step == 0)
    def _():
        keep = iota((T, T), 0) >= iota((T, T), 1)
        scores[...] = jnp.where(keep, nt(c_ref[...].astype(BF), b_ref[...].astype(BF)), 0.0)

    for i in range(STEP):
        x = x_ref[:, lanes_of(i)]
        xb = x.astype(BF)
        low = low_half(x.shape)
        head = 2 * (step * STEP + i)
        parts = []
        sides = []
        for k in range(2):
            sides.append(column(cum_t_ref[...], head + k))
            diff = sides[k] - cum_ref[pl.ds(head + k, 1), :]
            mixed = (jnp.exp(jnp.minimum(diff, 0.0)) * scores[...]).astype(BF)
            parts.append(nn(mixed, xb))
        skip = jnp.where(low, skip_ref[head], skip_ref[head + 1])
        y_ref[:, lanes_of(i)] = jnp.where(low, parts[0], parts[1]) + skip * x
        grow = jnp.exp(jnp.where(low, sides[0], sides[1]))
        grow_ref[:, lanes_of(i)] = grow.astype(BF)


def intra(x, cum, cum_t, b, c, skip):
    return pl.pallas_call(
        intra_kernel,
        grid=(PAIRS // STEP,),
        in_specs=[
            wide(T, STEP), whole((H, T)), whole((T, H)), whole((T, N)), whole((T, N)), smem(),
        ],
        out_specs=[wide(T, STEP)] * 2,
        out_shape=[jax.ShapeDtypeStruct((T, D), F32), jax.ShapeDtypeStruct((T, D), BF)],
        scratch_shapes=[pltpu.VMEM((T, T), F32)],
        compiler_params=params(),
        cost_estimate=cost(9),
        name="intra",
    )(x, cum, cum_t, b, c, skip)


def inter_kernel(part_ref, grow_ref, c_ref, start_ref, y_ref):
    read = nt(c_ref[...].astype(BF), start_ref[...])
    y_ref[...] = (part_ref[...] + grow_ref[...].astype(F32) * read).T.astype(BF)


def inter(part, grow, c, start):
    return pl.pallas_call(
        inter_kernel,
        grid=(PAIRS // WIDE,),
        in_specs=[wide(T, WIDE), wide(T, WIDE), whole((T, N)), state_block(WIDE)],
        out_specs=pl.BlockSpec((WIDE * 2 * P_SIZE, T), lambda p: (p, 0)),
        out_shape=jax.ShapeDtypeStruct((D, T), BF),
        compiler_params=params(),
        cost_estimate=cost(5),
        name="inter",
    )(part, grow, c, start)


def chain_kernel(reverse, mine_ref, parts_ref, totals_ref, out_ref):
    owner = (mine_ref[0] * OWN + iota((OWN, N), 0)) // P_SIZE == iota((OWN, N), 1)
    carry = jnp.zeros((OWN, N), F32)
    for s in range(N_SEQ - 1, -1, -1) if reverse else range(N_SEQ):
        out_ref[s] = carry.astype(BF)
        pieces = totals_ref[s, OWN:, :].astype(F32)
        total = pieces[0:1, :] + pieces[1:2, :] + pieces[2:3, :]
        decay = jnp.sum(jnp.where(owner, total, 0.0), axis=1, keepdims=True)
        carry = jnp.exp(decay) * carry + parts_ref[s, :OWN, :].astype(F32)


def chain(parts, totals, mine, reverse):
    return pl.pallas_call(
        functools.partial(chain_kernel, reverse),
        in_specs=[smem(), vmem(), vmem()],
        out_specs=vmem(),
        out_shape=jax.ShapeDtypeStruct((N_SEQ, OWN, N), BF),
        compiler_params=params(),
        cost_estimate=cost(3),
        name="chain",
    )(mine, parts, totals)


def swap(v, axis):
    return lax.all_to_all(v, axis, 0, 0, tiled=True)


def term_kernel(at_ref, yo_ref, yx_ref, g_ref, first_ref, near_ref, far_up_ref, far_down_ref):
    step = pl.program_id(0)
    half = g_ref.shape[1] // 2
    term = nn(jnp.concatenate([yo_ref[...], yx_ref[...]], axis=1), g_ref[...]).astype(BF)
    for k in range(4):
        rows = slice(k * OWN, (k + 1) * OWN)
        first_ref[k, 0] = term[rows, :half]
        rel = (k + 4 - at_ref[1]) % 4

        @pl.when(step != 2)
        def _():
            near_ref[0, rel] = term[rows, half:]

        @pl.when((step == 2) & (rel < 2))
        def _():
            far_up_ref[rel] = term[rows, half:]

        @pl.when((step == 2) & (rel >= 2))
        def _():
            far_down_ref[rel - 2] = term[rows, half:]


def terms(at, y_own, y_other, g):
    rows = pl.BlockSpec((4 * OWN, T), lambda i, at: ((at[0] + i) % 4, 0))
    half = g.shape[1] // 2
    part = jax.ShapeDtypeStruct((2, OWN, half), BF)
    return pl.pallas_call(
        term_kernel,
        grid_spec=pltpu.PrefetchScalarGridSpec(
            num_scalar_prefetch=1,
            grid=(4,),
            in_specs=[rows, rows, whole(g.shape)],
            out_specs=[
                pl.BlockSpec((4, 1, OWN, half), lambda i, at: (0, i, 0, 0)),
                pl.BlockSpec((1, 4, OWN, half), lambda i, at: (i - i // 2, 0, 0, 0)),
                whole(part.shape),
                whole(part.shape),
            ],
        ),
        out_shape=[
            jax.ShapeDtypeStruct((4, 4, OWN, half), BF),
            jax.ShapeDtypeStruct((3, 4, OWN, half), BF),
            part,
            part,
        ],
        compiler_params=params(),
        cost_estimate=cost(8),
        name="terms",
    )(at, y_own, y_other, g)


def gy_kernel(g_ref, w_ref, own_ref, other_ref):
    got = nt(g_ref[...], w_ref[...])
    own_ref[...] = got[:T]
    other_ref[...] = got[T:].astype(BF)


def gy_parts(g, w):
    rows = 4 * OWN
    return pl.pallas_call(
        gy_kernel,
        grid=(4,),
        in_specs=[whole(g.shape), pl.BlockSpec((rows, w.shape[1]), lambda i: (i, 0))],
        out_specs=[pl.BlockSpec((T, rows), lambda i: (0, i))] * 2,
        out_shape=[jax.ShapeDtypeStruct((T, D), F32), jax.ShapeDtypeStruct((T, D), BF)],
        compiler_params=params(),
        cost_estimate=cost(8),
        name="gy_parts",
    )(g, w)


def entry_kernel(own_ref, other_ref, x_ref, grow_ref, c_ref, gy_ref, out_ref, sums):
    step = pl.program_id(0)
    c = c_ref[...].astype(BF)
    found = []
    for i in range(WIDE):
        at = lanes_of(i)
        gy = own_ref[:, at] + other_ref[:, at].astype(F32)
        gy_ref[:, at] = gy.astype(BF)
        sums[pl.ds(step * WIDE + i, 1), :] = jnp.sum(gy * x_ref[:, at], axis=0, keepdims=True)
        found.append(tn((gy * grow_ref[:, at].astype(F32)).astype(BF), c))
    put_states(out_ref, jnp.concatenate(found, axis=0), step * WIDE, WIDE)

    @pl.when(step == PAIRS // WIDE - 1)
    def _():
        total = sums[...]
        low = low_half(total.shape)
        head = 2 * iota(total.shape, 0)
        lane = iota(total.shape, 1)
        even = jnp.sum(jnp.where(low, total, 0.0), axis=1, keepdims=True)
        odd = jnp.sum(jnp.where(low, 0.0, total), axis=1, keepdims=True)
        each = jnp.where(lane == head, even, 0.0) + jnp.where(lane == head + 1, odd, 0.0)
        gd = jnp.sum(each, axis=0, keepdims=True)
        hi = gd.astype(BF).astype(F32)
        mid = (gd - hi).astype(BF).astype(F32)
        put_note(out_ref, (hi, mid, gd - hi - mid))


def entries(own, other, x, grow, c):
    return pl.pallas_call(
        entry_kernel,
        grid=(PAIRS // WIDE,),
        in_specs=[wide(T, WIDE)] * 4 + [whole((T, N))],
        out_specs=[wide(T, WIDE), whole((N_SEQ, ROWS, N))],
        out_shape=[
            jax.ShapeDtypeStruct((T, D), BF),
            jax.ShapeDtypeStruct((N_SEQ, ROWS, N), BF),
        ],
        scratch_shapes=[pltpu.VMEM((PAIRS, 2 * P_SIZE), F32)],
        compiler_params=params(),
        cost_estimate=cost(6),
        name="entries",
    )(own, other, x, grow, c)


def within_kernel(
    first, steps, x_ref, gy_ref, cum_ref, cum_t_ref, b_ref, c_ref, skip_ref, *rest
):
    before = rest[:-8]
    gx_ref, ga_ref, gb_ref, gc_ref, scores, d_scores, rows, cols = rest[-8:]
    step = pl.program_id(0)

    @pl.when(step == 0)
    def _():
        keep = iota((T, T), 1) >= iota((T, T), 0)
        scores[...] = jnp.where(keep, nt(b_ref[...].astype(BF), c_ref[...].astype(BF)), 0.0)
        d_scores[...] = jnp.zeros_like(d_scores)
        rows[...] = jnp.zeros_like(rows)
        cols[...] = jnp.zeros_like(cols)

    lanes = iota((T, N), 1)
    low = low_half((T, 2 * P_SIZE))
    for i in range(STEP):
        pair = (first + step) * STEP + i
        at = lanes_of(i)
        x = x_ref[:, at]
        gyb = gy_ref[:, at]
        parts = []
        for k in range(2):
            head = 2 * pair + k
            diff = cum_ref[pl.ds(head, 1), :] - column(cum_t_ref[...], head)
            weights = jnp.exp(jnp.minimum(diff, 0.0))
            mine = jnp.where(low if k == 0 else ~low, x, 0.0).astype(BF)
            d_mixed = weights * nt(mine, gyb)
            d_scores[...] += d_mixed
            parts.append(nn((weights * scores[...]).astype(BF), gyb))
            change = d_mixed * scores[...]
            rows[pl.ds(head, 1), :] = jnp.sum(change, axis=0, keepdims=True)
            down = jnp.sum(change, axis=1, keepdims=True)
            cols[...] -= jnp.where(lanes == head, down, 0.0)
        skip = jnp.where(low, skip_ref[2 * pair], skip_ref[2 * pair + 1])
        gx_ref[:, at] = jnp.where(low, parts[0], parts[1]) + skip * gyb.astype(F32)

    @pl.when(step == steps - 1)
    def _():
        keep = iota((T, T), 1) >= iota((T, T), 0)
        ds = jnp.where(keep, d_scores[...], 0.0).astype(BF)
        gb = nn(ds, c_ref[...].astype(BF))
        gc = tn(ds, b_ref[...].astype(BF))
        after = (iota((T, T), 0) >= iota((T, T), 1)).astype(F32)
        dims = (((0,), (0,)), ((), ()))
        ga = jnp.dot(rows[...], after, precision=HIGH, preferred_element_type=F32)
        up = lax.dot_general(cols[...], after, dims, precision=HIGH, preferred_element_type=F32)
        for out, add, ref in zip((ga_ref, gb_ref, gc_ref), (ga + up[:H], gb, gc), before or (None,) * 3):
            out[...] = add if ref is None else add + ref[...]


def within(first, steps, x, gy, cum, cum_t, b, c, skip, before=()):
    here = pl.BlockSpec((T, STEP * 2 * P_SIZE), lambda p: (0, first + p))
    return pl.pallas_call(
        functools.partial(within_kernel, first, steps),
        grid=(steps,),
        in_specs=[
            here, here, whole((H, T)), whole((T, H)), whole((T, N)), whole((T, N)), smem(),
        ]
        + [whole(v.shape) for v in before],
        out_specs=[wide(T, STEP), whole((H, T)), whole((T, N)), whole((T, N))],
        out_shape=[
            jax.ShapeDtypeStruct((T, steps * STEP * 2 * P_SIZE), F32),
            jax.ShapeDtypeStruct((H, T), F32),
            jax.ShapeDtypeStruct((T, N), F32),
            jax.ShapeDtypeStruct((T, N), F32),
        ],
        scratch_shapes=[
            pltpu.VMEM((T, T), F32),
            pltpu.VMEM((T, T), F32),
            pltpu.VMEM((H, T), F32),
            pltpu.VMEM((T, N), F32),
        ],
        compiler_params=params(),
        cost_estimate=cost(7),
        name="within",
    )(x, gy, cum, cum_t, b, c, skip, *before)


def across_kernel(
    x_ref, gy_ref, grow_ref, tail_ref, part_ref, part2_ref, cum_ref, b_ref, c_ref, start_ref, last_ref,
    ga_in, gb_in, gc_in,
    gx_ref, ga_ref, gb_ref, gc_ref,
    cols, tails, totals,
):
    step = pl.program_id(0)
    bb = b_ref[...].astype(BF)
    cb = c_ref[...].astype(BF)

    @pl.when(step == 0)
    def _():
        cols[...] = jnp.zeros_like(cols)
        tails[...] = jnp.zeros_like(tails)
        gb_ref[...] = gb_in[...]
        gc_ref[...] = gc_in[...]

    width = WIDE * 2 * P_SIZE
    start = start_ref[...]
    last = last_ref[...]
    tail = tail_ref[...].astype(F32)
    pick = iota((width, N), 1) == step * 2 * WIDE + iota((width, N), 0) // P_SIZE
    grown = gy_ref[...].astype(F32) * grow_ref[...].astype(F32)
    cols[...] += nn((grown * nt(cb, start)).astype(BF), pick.astype(BF))
    gc_ref[...] += nn(grown.astype(BF), start)
    faded = x_ref[...] * tail
    back = nt(bb, last)
    tails[...] += nn((faded * back).astype(BF), pick.astype(BF))
    gb_ref[...] += nn(faded.astype(BF), last)
    part = jnp.where(step < PAIRS // WIDE // 2, part_ref[...], part2_ref[...])
    gx_ref[...] = part + tail * back
    both = jnp.sum(start.astype(F32) * last.astype(F32), axis=1, keepdims=True)
    totals[pl.ds(step, 1), :] = jnp.sum(jnp.where(pick, both, 0.0), axis=0, keepdims=True)

    @pl.when(step == PAIRS // WIDE - 1)
    def _():
        after = (iota((T, T), 0) >= iota((T, T), 1)).astype(F32)
        before = (iota((T, T), 0) < iota((T, T), 1)).astype(F32)
        dims = (((0,), (0,)), ((), ()))
        up = lax.dot_general(cols[...], after, dims, precision=HIGH, preferred_element_type=F32)
        up += lax.dot_general(tails[...], before, dims, precision=HIGH, preferred_element_type=F32)
        total = jnp.sum(totals[...], axis=0, keepdims=True)
        total = jnp.sum(jnp.where(iota((H, N), 0) == iota((H, N), 1), total, 0.0), axis=1, keepdims=True)
        ga_ref[...] = ga_in[...] + up[:H] + jnp.exp(cum_ref[:, T - 1 : T]) * total


def across(x, gy, grow, tail, part, part2, cum, b, c, start, last, ga, gb, gc):
    width = WIDE * 2 * P_SIZE
    last_part = PAIRS // WIDE // 2 - 1
    return pl.pallas_call(
        across_kernel,
        grid=(PAIRS // WIDE,),
        in_specs=[wide(T, WIDE)] * 4
        + [
            pl.BlockSpec((T, width), lambda p: (0, jnp.minimum(p, last_part))),
            pl.BlockSpec((T, width), lambda p: (0, jnp.maximum(p - last_part - 1, 0))),
        ]
        + [whole((H, T)), whole((T, N)), whole((T, N))]
        + [state_block(WIDE), state_block(WIDE), whole((H, T)), whole((T, N)), whole((T, N))],
        out_specs=[wide(T, WIDE), whole((H, T)), whole((T, N)), whole((T, N))],
        out_shape=[
            jax.ShapeDtypeStruct((T, D), F32),
            jax.ShapeDtypeStruct((H, T), F32),
            jax.ShapeDtypeStruct((T, N), F32),
            jax.ShapeDtypeStruct((T, N), F32),
        ],
        scratch_shapes=[
            pltpu.VMEM((T, N), F32),
            pltpu.VMEM((T, N), F32),
            pltpu.VMEM((PAIRS // WIDE, N), F32),
        ],
        compiler_params=params(),
        cost_estimate=cost(8),
        name="across",
    )(x, gy, grow, tail, part, part2, cum, b, c, start, last, ga, gb, gc)


def fold_kernel(a0, a1, a2, a3, b0, b1, b2, b3, out_ref):
    sums = []
    for parts in ((a0, a1, a2, a3), (b0, b1, b2, b3)):
        total = parts[0][...].astype(F32)
        for part in parts[1:]:
            total += part[...].astype(F32)
        sums.append(total.astype(BF))
    for q in range(8 * TILES):
        r, c = divmod(q, 10)
        if r < 10:
            tile = sums[c // 5][16 * r : 16 * r + 16, 128 * (c % 5) : 128 * (c % 5) + 128]
        else:
            tile = jnp.zeros((16, 128), BF)
        out_ref[q // TILES, q % TILES] = tile


def fold(parts):
    return pl.pallas_call(
        fold_kernel,
        in_specs=[vmem()] * 8,
        out_specs=vmem(),
        out_shape=jax.ShapeDtypeStruct((8, TILES, 16, 128), BF),
        compiler_params=params(),
        cost_estimate=cost(3),
        name="fold",
    )(*parts)


def groups_of(row0, count, ids_ref):
    heads = (row0 + iota((count, N), 0)) // P_SIZE == iota((count, N), 1)
    return jnp.sum(jnp.where(heads, ids_ref[...], 0.0), axis=1, keepdims=True)


def zsum_kernel(row0_ref, z_ref, ids_ref, got_ref, parts_ref, out_ref, note_ref):
    total = parts_ref[0].astype(F32)
    for z in range(1, 8):
        total += parts_ref[z].astype(F32)
    out_ref[...] = total.astype(BF)
    found = jnp.zeros((16, N), F32)
    for i in range(TILES):
        row = row0_ref[0] + 16 * ((z_ref[0] * TILES + i) // 10)
        place = iota((16, N), 1) - H == groups_of(row, 16, ids_ref).astype(jnp.int32)
        tile = total[i]
        found += jnp.where(place, jnp.sum(tile * tile, axis=1, keepdims=True), 0.0)
    d_sum = jnp.zeros((1, N), F32)
    for s in range(N_SEQ):
        pieces = got_ref[s, OWN:, :].astype(F32)
        d_sum += pieces[0:1, :] + pieces[1:2, :] + pieces[2:3, :]
    note_ref[...] = jnp.sum(found, axis=0, keepdims=True) + d_sum / N_SEQ


def zsum(row0, z, ids, parts, got):
    return pl.pallas_call(
        zsum_kernel,
        in_specs=[smem(), smem()] + [vmem()] * 3,
        out_specs=[vmem(), vmem()],
        out_shape=[
            jax.ShapeDtypeStruct((TILES, 16, 128), BF),
            jax.ShapeDtypeStruct((1, N), F32),
        ],
        compiler_params=params(),
        cost_estimate=cost(2),
        name="zsum",
    )(row0, z, ids, got, parts)


def pack_kernel(tiles_ref, note_ref, out_ref):
    note = note_ref[...]
    hi = note.astype(BF).astype(F32)
    mid = (note - hi).astype(BF).astype(F32)
    at = iota((16, N), 0)
    rows = jnp.where(at == 0, hi, jnp.where(at == 1, mid, jnp.where(at == 2, note - hi - mid, 0.0)))
    for z in range(8):
        out_ref[z, :TILES] = tiles_ref[...]
        out_ref[z, TILES] = rows.astype(BF)


def pack(tiles, note):
    return pl.pallas_call(
        pack_kernel,
        in_specs=[vmem(), vmem()],
        out_specs=vmem(),
        out_shape=jax.ShapeDtypeStruct((8, TILES + 1, 16, 128), BF),
        compiler_params=params(),
        cost_estimate=cost(2),
        name="pack",
    )(tiles, note)


def note_of(ref):
    total = jnp.zeros((1, N), F32)
    for z in range(8):
        rows = ref[z, TILES].astype(F32)
        total += rows[0:1, :] + rows[1:2, :] + rows[2:3, :]
    return total


def tile_of(ref, r, c):
    z, i = divmod(10 * r + c, TILES)
    return ref[z, i].astype(F32)


def clip_kernel(tokens_all, row0_ref, core_ref, ids_ref, own_ref, other_ref, w_ref, d_ref):
    ids = ids_ref[...]
    lane = iota((1, N), 1)
    note = note_of(own_ref) + note_of(other_ref)
    grad_d = jnp.where(lane < H, note, 0.0)
    groups = groups_of(row0_ref[0], OWN, ids_ref)
    w_factor = jnp.zeros((OWN, 1), F32)
    d_factor = jnp.zeros((1, N), F32)
    for g in range(GROUPS):
        here = (ids == float(g)) & (lane < H)
        count = jnp.sum(jnp.where(here, 1.0, 0.0), axis=1, keepdims=True)
        sumsq = jnp.sum(jnp.where(lane == H + g, note, 0.0), axis=1, keepdims=True)
        sumsq += jnp.sum(jnp.where(here, grad_d * grad_d, 0.0), axis=1, keepdims=True)
        bound = 7.0 * jnp.sqrt(count * (P_SIZE * D + 1.0) * tokens_all)
        factor = jnp.minimum(1.0, bound / jnp.sqrt(sumsq + 1e-06))
        w_factor += jnp.where(groups == float(g), factor, 0.0)
        d_factor += jnp.where(here, factor, 0.0)
    d_ref[...] = (grad_d * d_factor)[:, :H]
    for r in range(10):
        scale = w_factor[16 * r : 16 * r + 16, :]
        for ref, core in ((own_ref, core_ref[0]), (other_ref, 1 - core_ref[0])):
            for c in range(10):
                col = pl.multiple_of(core * (D // 2) + 128 * c, 128)
                w_ref[16 * r : 16 * r + 16, pl.ds(col, 128)] = tile_of(ref, r, c) * scale


def clip(tokens_all, row0, core, ids, own, other):
    return pl.pallas_call(
        functools.partial(clip_kernel, tokens_all),
        in_specs=[smem(), smem()] + [vmem()] * 3,
        out_specs=[vmem(), vmem()],
        out_shape=[jax.ShapeDtypeStruct((OWN, D), F32), jax.ShapeDtypeStruct((1, H), F32)],
        compiler_params=params(),
        cost_estimate=cost(3),
        name="clip",
    )(row0, core, ids, own, other)


def shifted(v, axis, d):
    return lax.ppermute(v, axis, [(i, (i + d) % 4) for i in range(4)])


def plus(a, b):
    return (a.astype(F32) + b.astype(F32)).astype(BF)


def passed(t, ra, rb):
    m = t.shape[1] // 2
    up = jnp.concatenate([plus(t[1, :m], ra), t[1, m:]], axis=0)
    down = jnp.concatenate([t[2, :m], plus(t[2, m:], rb)], axis=0)
    return up, down


def near(t, up, down, axis):
    total = t[0].astype(F32) + shifted(up, axis, 1).astype(F32)
    return (total + shifted(down, axis, -1).astype(F32)).astype(BF)


def direct(t, axis):
    return (t[0],) + tuple(shifted(t[d], axis, d) for d in (1, 3, 2))


def other_core(v):
    return lax.ppermute(v, "core", [(0, 1), (1, 0)])


def sum_over(v, axes):
    for unit in (1, 4):
        got = [
            lax.ppermute(v, axes, [(i, i ^ (unit * k)) for i in range(16)]) for k in (1, 2, 3)
        ]
        v = (v + got[0]) + (got[1] + got[2])
    return v


def tie(*values):
    return lax.optimization_barrier(values)


def per_device(x_in, a_log, b_in, c_in, g_out, w_out, d_skip, group_ids):
    x, a, b, c, g = (x_in[0], a_log[0], b_in[0], c_in[0], g_out[0])
    core = lax.axis_index("core")
    half = D // 2
    at = jnp.stack([lax.axis_index("y"), lax.axis_index("x")]).astype(jnp.int32)
    mine = (2 * lax.axis_index("z") + core).reshape(1).astype(jnp.int32)
    at_z = lax.axis_index("z").reshape(1).astype(jnp.int32)
    row0 = ((4 * at[0] + at[1]) * OWN).reshape(1)
    ids = jnp.pad(group_ids.astype(F32), (0, N - H), constant_values=-1.0)[None]
    tokens_all = float(T * N_SEQ * 16)

    g_mine = lax.dynamic_slice_in_dim(g, core * half, half, axis=1)
    g_other = other_core(lax.dynamic_slice_in_dim(g, (1 - core) * half, half, axis=1))

    g_both = jnp.concatenate([g_mine, g_other], axis=0)

    cum, cum_t, tail, sent = local_ends(x, a, b)
    w_out, sent = tie(w_out, sent)
    w_mine = lax.dynamic_slice_in_dim(w_out, core * half, half, axis=1)
    w_half = lax.all_gather(w_mine, ("y", "x"), axis=0, tiled=True)
    got = swap(sent, SEQ)
    y_part, grow = intra(x, cum, cum_t, b, c, d_skip)
    y_part, g_both, at = tie(y_part, g_both, at)
    start = swap(chain(got, got, mine, False), SEQ).reshape(H * P_SIZE, N)
    y_own = inter(y_part, grow, c, start)
    y_other = other_core(y_own)
    first, second, far_up, far_down = terms(at, y_own, y_other, g_both)

    first = lax.psum_scatter(first.reshape(-1, half // 2), "x", scatter_dimension=0, tiled=True)
    far_y = (shifted(far_up, "y", 1), shifted(far_down, "y", -1))
    w_half, _ = tie(w_half, second)
    gy_own, gy_other = gy_parts(g_both, w_half)
    *far_y, gy_own, gy_other = tie(*far_y, gy_own, gy_other)
    gy_other = other_core(gy_other)
    up, down = passed(second, *far_y)
    up, down, gy_own, gy_other = tie(up, down, gy_own, gy_other)
    second = near(second, up, down, "y")
    gy, sent_back = entries(gy_own, gy_other, x, grow, c)
    got_back = swap(sent_back, SEQ)
    steps = PAIRS // STEP // 2
    gx1, *sums = within(0, steps, x, gy, cum, cum_t, b, c, d_skip)
    first, gx1 = tie(first, gx1)
    first = direct(first.reshape(4, OWN, half // 2), "y")
    second = direct(second, "x")
    tiles = fold(first + second)
    gy, mine, tiles = tie(gy, mine, tiles)
    tiles = swap(tiles, "z")
    states = chain(got_back, got, mine, True)
    gx2, *sums = within(steps, steps, x, gy, cum, cum_t, b, c, d_skip, sums)
    tiles, gx2, states = tie(tiles, gx2, states)
    tiles, note = zsum(row0, at_z, ids, tiles, got_back)
    note, states = tie(note, states)
    last = swap(states, SEQ).reshape(H * P_SIZE, N)
    note = sum_over(note, ("y", "x"))
    tiles, note, last = tie(tiles, note, last)
    tiles = pack(tiles, note)
    tiles, last = tie(tiles, last)
    tiles = swap(tiles, "z")
    gx, ga, gb, gc = across(x, gy, grow, tail, gx1, gx2, cum, b, c, start, last, *sums)
    tiles, ga = tie(tiles, ga)
    tiles_other = other_core(tiles)
    core = core.reshape(1).astype(jnp.int32)
    clipped_w, clipped_d = clip(tokens_all, row0, core, ids, tiles, tiles_other)
    return (gx[None], ga[None], gb[None], gc[None], clipped_w, clipped_d[0])


def solution(mesh):
    fine = Mesh(mesh.devices.reshape(4, 4, 8, 2), ("y", "x", "z", "core"))
    rows = ("y", "x")
    tokens = P(rows, SEQ, None)
    return jax.shard_map(
        per_device,
        mesh=fine,
        in_specs=(
            tokens, P(rows, None, SEQ), tokens, tokens, tokens, P(rows, None), P(), P(),
        ),
        out_specs=(tokens, P(rows, None, SEQ), tokens, tokens, P(rows, None), P()),
        check_vma=False,
    )
```

```python
import functools

import jax
import jax.numpy as jnp
from jax import lax
from jax.experimental import pallas as pl
from jax.experimental.pallas import tpu as pltpu
from jax.sharding import Mesh
from jax.sharding import PartitionSpec as P

D = 2560
H = 40
P_SIZE = 64
N = 128
T = 256
GROUPS = 4
PAIRS = H // 2
SEQ = ("z", "core")
N_SEQ = 16
OWN = H * P_SIZE // N_SEQ
HIGH = lax.Precision.HIGHEST
BF = jnp.bfloat16
F32 = jnp.float32
VMEM = 62 * 1024 * 1024
WIDE = 5
STEP = 2
ROWS = OWN + 16
TILES = 13


def nn(a, b):
    return lax.dot_general(a, b, (((1,), (0,)), ((), ())), preferred_element_type=F32)


def nt(a, b):
    return lax.dot_general(a, b, (((1,), (1,)), ((), ())), preferred_element_type=F32)


def tn(a, b):
    return lax.dot_general(a, b, (((0,), (0,)), ((), ())), preferred_element_type=F32)


def iota(shape, dim):
    return lax.broadcasted_iota(jnp.int32, shape, dim)


def whole(shape):
    return pl.BlockSpec(shape, lambda *_: (0,) * len(shape))


def wide(rows, pairs):
    return pl.BlockSpec((rows, pairs * 2 * P_SIZE), lambda p: (0, p))


def state_block(pairs):
    return pl.BlockSpec((pairs * 2 * P_SIZE, N), lambda p: (p, 0))


def smem():
    return pl.BlockSpec(memory_space=pltpu.SMEM)


def vmem():
    return pl.BlockSpec(memory_space=pltpu.VMEM)


def params():
    return pltpu.CompilerParams(vmem_limit_bytes=VMEM)


def cost(micros):
    return pl.CostEstimate(flops=0, bytes_accessed=int(micros * 3e6), transcendentals=0)


def column(cum_t, head):
    return jnp.sum(jnp.where(iota(cum_t.shape, 1) == head, cum_t, 0.0), axis=1, keepdims=True)


def low_half(shape):
    return iota(shape, 1) < P_SIZE


def lanes_of(i):
    return slice(i * 2 * P_SIZE, (i + 1) * 2 * P_SIZE)


def put_states(out_ref, states, first, pairs):
    chunks = pairs * 2 * P_SIZE // OWN
    rows = states.astype(BF).reshape(chunks, OWN, N)
    out_ref[pl.ds(first * 2 * P_SIZE // OWN, chunks), :OWN, :] = rows


def put_note(out_ref, pieces):
    at = iota((16, N), 0)
    note = jnp.zeros((16, N), F32)
    for i, piece in enumerate(pieces):
        note = jnp.where(at == i, piece, note)
    for s in range(N_SEQ):
        out_ref[s, OWN:, :] = note.astype(BF)


def ends_kernel(x_ref, a_ref, b_ref, cum_ref, cum_t_ref, tail_ref, out_ref, pieces):
    step = pl.program_id(0)

    @pl.when(step == 0)
    def _():
        a = a_ref[...]
        upto = (iota((T, T), 0) <= iota((T, T), 1)).astype(F32)
        cum_ref[...] = jnp.dot(a, upto, precision=HIGH, preferred_element_type=F32)
        down = (iota((T, T), 1) <= iota((T, T), 0)).astype(F32)
        cum_t = lax.dot_general(
            down, a, (((1,), (1,)), ((), ())), precision=HIGH, preferred_element_type=F32
        )
        cum_t_ref[...] = cum_t
        total = jnp.concatenate([cum_t[T - 1 :, :], jnp.zeros((1, N - H), F32)], axis=1)
        hi = jnp.floor(total)
        mid = jnp.floor((total - hi) * 256.0) / 256.0
        put_note(out_ref, (hi, mid, total - hi - mid))
        tail = jnp.exp(cum_t[T - 1 :, :] - cum_t)
        high = tail.astype(BF)
        pieces[0] = high
        pieces[1] = (tail - high.astype(F32)).astype(BF)

    width = WIDE * 2 * P_SIZE
    pick = iota((H, width), 0) == step * 2 * WIDE + iota((H, width), 1) // P_SIZE
    pick = pick.astype(BF)
    tail = nn(pieces[0], pick) + nn(pieces[1], pick)
    tail_ref[...] = tail.astype(BF)
    states = tn((x_ref[...] * tail).astype(BF), b_ref[...].astype(BF))
    put_states(out_ref, states, step * WIDE, WIDE)


def local_ends(x, a, b):
    return pl.pallas_call(
        ends_kernel,
        grid=(PAIRS // WIDE,),
        in_specs=[wide(T, WIDE), whole((H, T)), whole((T, N))],
        out_specs=[whole((H, T)), whole((T, H)), wide(T, WIDE), whole((N_SEQ, ROWS, N))],
        out_shape=[
            jax.ShapeDtypeStruct((H, T), F32),
            jax.ShapeDtypeStruct((T, H), F32),
            jax.ShapeDtypeStruct((T, D), BF),
            jax.ShapeDtypeStruct((N_SEQ, ROWS, N), BF),
        ],
        scratch_shapes=[pltpu.VMEM((2, T, H), BF)],
        compiler_params=params(),
        cost_estimate=cost(6),
        name="ends",
    )(x, a, b)


def intra_kernel(x_ref, cum_ref, cum_t_ref, b_ref, c_ref, skip_ref, y_ref, grow_ref, scores):
    step = pl.program_id(0)

    @pl.when(step == 0)
    def _():
        keep = iota((T, T), 0) >= iota((T, T), 1)
        scores[...] = jnp.where(keep, nt(c_ref[...].astype(BF), b_ref[...].astype(BF)), 0.0)

    for i in range(STEP):
        x = x_ref[:, lanes_of(i)]
        xb = x.astype(BF)
        low = low_half(x.shape)
        head = 2 * (step * STEP + i)
        parts = []
        sides = []
        for k in range(2):
            sides.append(column(cum_t_ref[...], head + k))
            diff = sides[k] - cum_ref[pl.ds(head + k, 1), :]
            mixed = (jnp.exp(jnp.minimum(diff, 0.0)) * scores[...]).astype(BF)
            parts.append(nn(mixed, xb))
        skip = jnp.where(low, skip_ref[head], skip_ref[head + 1])
        y_ref[:, lanes_of(i)] = jnp.where(low, parts[0], parts[1]) + skip * x
        grow = jnp.exp(jnp.where(low, sides[0], sides[1]))
        grow_ref[:, lanes_of(i)] = grow.astype(BF)


def intra(x, cum, cum_t, b, c, skip):
    return pl.pallas_call(
        intra_kernel,
        grid=(PAIRS // STEP,),
        in_specs=[
            wide(T, STEP), whole((H, T)), whole((T, H)), whole((T, N)), whole((T, N)), smem(),
        ],
        out_specs=[wide(T, STEP)] * 2,
        out_shape=[jax.ShapeDtypeStruct((T, D), F32), jax.ShapeDtypeStruct((T, D), BF)],
        scratch_shapes=[pltpu.VMEM((T, T), F32)],
        compiler_params=params(),
        cost_estimate=cost(9),
        name="intra",
    )(x, cum, cum_t, b, c, skip)


def inter_kernel(part_ref, grow_ref, c_ref, start_ref, y_ref):
    read = nt(c_ref[...].astype(BF), start_ref[...])
    y_ref[...] = (part_ref[...] + grow_ref[...].astype(F32) * read).astype(BF)


def inter(part, grow, c, start):
    return pl.pallas_call(
        inter_kernel,
        grid=(PAIRS // WIDE,),
        in_specs=[wide(T, WIDE), wide(T, WIDE), whole((T, N)), state_block(WIDE)],
        out_specs=wide(T, WIDE),
        out_shape=jax.ShapeDtypeStruct((T, D), BF),
        compiler_params=params(),
        cost_estimate=cost(5),
        name="inter",
    )(part, grow, c, start)


def chain_kernel(reverse, mine_ref, parts_ref, totals_ref, out_ref):
    owner = (mine_ref[0] * OWN + iota((OWN, N), 0)) // P_SIZE == iota((OWN, N), 1)
    carry = jnp.zeros((OWN, N), F32)
    for s in range(N_SEQ - 1, -1, -1) if reverse else range(N_SEQ):
        out_ref[s] = carry.astype(BF)
        pieces = totals_ref[s, OWN:, :].astype(F32)
        total = pieces[0:1, :] + pieces[1:2, :] + pieces[2:3, :]
        decay = jnp.sum(jnp.where(owner, total, 0.0), axis=1, keepdims=True)
        carry = jnp.exp(decay) * carry + parts_ref[s, :OWN, :].astype(F32)


def chain(parts, totals, mine, reverse):
    return pl.pallas_call(
        functools.partial(chain_kernel, reverse),
        in_specs=[smem(), vmem(), vmem()],
        out_specs=vmem(),
        out_shape=jax.ShapeDtypeStruct((N_SEQ, OWN, N), BF),
        compiler_params=params(),
        cost_estimate=cost(3),
        name="chain",
    )(mine, parts, totals)


def swap(v, axis):
    return lax.all_to_all(v, axis, 0, 0, tiled=True)


def term_kernel(at_ref, yo_ref, yx_ref, g_ref, first_ref, second_ref):
    half = g_ref.shape[1] // 2
    term = tn(jnp.concatenate([yo_ref[...], yx_ref[...]], axis=0), g_ref[...]).astype(BF)
    for k in range(4):
        rows = slice(k * OWN, (k + 1) * OWN)
        first_ref[k, 0] = term[rows, :half]
        second_ref[0, (k + 4 - at_ref[1]) % 4] = term[rows, half:]


def terms(at, y_own, y_other, g):
    rows = pl.BlockSpec((T, 4 * OWN), lambda i, at: (0, (at[0] + i) % 4))
    half = g.shape[1] // 2
    return pl.pallas_call(
        term_kernel,
        grid_spec=pltpu.PrefetchScalarGridSpec(
            num_scalar_prefetch=1,
            grid=(4,),
            in_specs=[rows, rows, whole(g.shape)],
            out_specs=[
                pl.BlockSpec((4, 1, OWN, half), lambda i, at: (0, i, 0, 0)),
                pl.BlockSpec((1, 4, OWN, half), lambda i, at: (i, 0, 0, 0)),
            ],
        ),
        out_shape=[jax.ShapeDtypeStruct((4, 4, OWN, half), BF)] * 2,
        compiler_params=params(),
        cost_estimate=cost(8),
        name="terms",
    )(at, y_own, y_other, g)


def gy_kernel(g_ref, w_ref, own_ref, other_ref):
    got = nt(g_ref[...], w_ref[...])
    own_ref[...] = got[:T]
    other_ref[...] = got[T:].astype(BF)


def gy_parts(g, w):
    rows = 4 * OWN
    return pl.pallas_call(
        gy_kernel,
        grid=(4,),
        in_specs=[whole(g.shape), pl.BlockSpec((rows, w.shape[1]), lambda i: (i, 0))],
        out_specs=[pl.BlockSpec((T, rows), lambda i: (0, i))] * 2,
        out_shape=[jax.ShapeDtypeStruct((T, D), F32), jax.ShapeDtypeStruct((T, D), BF)],
        compiler_params=params(),
        cost_estimate=cost(8),
        name="gy_parts",
    )(g, w)


def entry_kernel(own_ref, other_ref, x_ref, grow_ref, c_ref, gy_ref, out_ref, sums):
    step = pl.program_id(0)
    c = c_ref[...].astype(BF)
    found = []
    for i in range(WIDE):
        at = lanes_of(i)
        gy = own_ref[:, at] + other_ref[:, at].astype(F32)
        gy_ref[:, at] = gy.astype(BF)
        sums[pl.ds(step * WIDE + i, 1), :] = jnp.sum(gy * x_ref[:, at], axis=0, keepdims=True)
        found.append(tn((gy * grow_ref[:, at].astype(F32)).astype(BF), c))
    put_states(out_ref, jnp.concatenate(found, axis=0), step * WIDE, WIDE)

    @pl.when(step == PAIRS // WIDE - 1)
    def _():
        total = sums[...]
        low = low_half(total.shape)
        head = 2 * iota(total.shape, 0)
        lane = iota(total.shape, 1)
        even = jnp.sum(jnp.where(low, total, 0.0), axis=1, keepdims=True)
        odd = jnp.sum(jnp.where(low, 0.0, total), axis=1, keepdims=True)
        each = jnp.where(lane == head, even, 0.0) + jnp.where(lane == head + 1, odd, 0.0)
        gd = jnp.sum(each, axis=0, keepdims=True)
        hi = gd.astype(BF).astype(F32)
        mid = (gd - hi).astype(BF).astype(F32)
        put_note(out_ref, (hi, mid, gd - hi - mid))


def entries(own, other, x, grow, c):
    return pl.pallas_call(
        entry_kernel,
        grid=(PAIRS // WIDE,),
        in_specs=[wide(T, WIDE)] * 4 + [whole((T, N))],
        out_specs=[wide(T, WIDE), whole((N_SEQ, ROWS, N))],
        out_shape=[
            jax.ShapeDtypeStruct((T, D), BF),
            jax.ShapeDtypeStruct((N_SEQ, ROWS, N), BF),
        ],
        scratch_shapes=[pltpu.VMEM((PAIRS, 2 * P_SIZE), F32)],
        compiler_params=params(),
        cost_estimate=cost(6),
        name="entries",
    )(own, other, x, grow, c)


def within_kernel(
    first, steps, x_ref, gy_ref, cum_ref, cum_t_ref, b_ref, c_ref, skip_ref, *rest
):
    before = rest[:-8]
    gx_ref, ga_ref, gb_ref, gc_ref, scores, d_scores, rows, cols = rest[-8:]
    step = pl.program_id(0)

    @pl.when(step == 0)
    def _():
        keep = iota((T, T), 1) >= iota((T, T), 0)
        scores[...] = jnp.where(keep, nt(b_ref[...].astype(BF), c_ref[...].astype(BF)), 0.0)
        d_scores[...] = jnp.zeros_like(d_scores)
        rows[...] = jnp.zeros_like(rows)
        cols[...] = jnp.zeros_like(cols)

    lanes = iota((T, N), 1)
    low = low_half((T, 2 * P_SIZE))
    for i in range(STEP):
        pair = (first + step) * STEP + i
        at = lanes_of(i)
        x = x_ref[:, at]
        gyb = gy_ref[:, at]
        parts = []
        for k in range(2):
            head = 2 * pair + k
            diff = cum_ref[pl.ds(head, 1), :] - column(cum_t_ref[...], head)
            weights = jnp.exp(jnp.minimum(diff, 0.0))
            mine = jnp.where(low if k == 0 else ~low, x, 0.0).astype(BF)
            d_mixed = weights * nt(mine, gyb)
            d_scores[...] += d_mixed
            parts.append(nn((weights * scores[...]).astype(BF), gyb))
            change = d_mixed * scores[...]
            rows[pl.ds(head, 1), :] = jnp.sum(change, axis=0, keepdims=True)
            down = jnp.sum(change, axis=1, keepdims=True)
            cols[...] -= jnp.where(lanes == head, down, 0.0)
        skip = jnp.where(low, skip_ref[2 * pair], skip_ref[2 * pair + 1])
        gx_ref[:, at] = jnp.where(low, parts[0], parts[1]) + skip * gyb.astype(F32)

    @pl.when(step == steps - 1)
    def _():
        keep = iota((T, T), 1) >= iota((T, T), 0)
        ds = jnp.where(keep, d_scores[...], 0.0).astype(BF)
        gb = nn(ds, c_ref[...].astype(BF))
        gc = tn(ds, b_ref[...].astype(BF))
        after = (iota((T, T), 0) >= iota((T, T), 1)).astype(F32)
        dims = (((0,), (0,)), ((), ()))
        ga = jnp.dot(rows[...], after, precision=HIGH, preferred_element_type=F32)
        up = lax.dot_general(cols[...], after, dims, precision=HIGH, preferred_element_type=F32)
        for out, add, ref in zip((ga_ref, gb_ref, gc_ref), (ga + up[:H], gb, gc), before or (None,) * 3):
            out[...] = add if ref is None else add + ref[...]


def within(first, steps, x, gy, cum, cum_t, b, c, skip, before=()):
    here = pl.BlockSpec((T, STEP * 2 * P_SIZE), lambda p: (0, first + p))
    return pl.pallas_call(
        functools.partial(within_kernel, first, steps),
        grid=(steps,),
        in_specs=[
            here, here, whole((H, T)), whole((T, H)), whole((T, N)), whole((T, N)), smem(),
        ]
        + [whole(v.shape) for v in before],
        out_specs=[wide(T, STEP), whole((H, T)), whole((T, N)), whole((T, N))],
        out_shape=[
            jax.ShapeDtypeStruct((T, steps * STEP * 2 * P_SIZE), F32),
            jax.ShapeDtypeStruct((H, T), F32),
            jax.ShapeDtypeStruct((T, N), F32),
            jax.ShapeDtypeStruct((T, N), F32),
        ],
        scratch_shapes=[
            pltpu.VMEM((T, T), F32),
            pltpu.VMEM((T, T), F32),
            pltpu.VMEM((H, T), F32),
            pltpu.VMEM((T, N), F32),
        ],
        compiler_params=params(),
        cost_estimate=cost(7),
        name="within",
    )(x, gy, cum, cum_t, b, c, skip, *before)


def across_kernel(
    x_ref, gy_ref, grow_ref, tail_ref, part_ref, part2_ref, cum_ref, b_ref, c_ref, start_ref, last_ref,
    ga_in, gb_in, gc_in,
    gx_ref, ga_ref, gb_ref, gc_ref,
    cols, tails, totals,
):
    step = pl.program_id(0)
    bb = b_ref[...].astype(BF)
    cb = c_ref[...].astype(BF)

    @pl.when(step == 0)
    def _():
        cols[...] = jnp.zeros_like(cols)
        tails[...] = jnp.zeros_like(tails)
        gb_ref[...] = gb_in[...]
        gc_ref[...] = gc_in[...]

    width = WIDE * 2 * P_SIZE
    start = start_ref[...]
    last = last_ref[...]
    tail = tail_ref[...].astype(F32)
    pick = iota((width, N), 1) == step * 2 * WIDE + iota((width, N), 0) // P_SIZE
    grown = gy_ref[...].astype(F32) * grow_ref[...].astype(F32)
    cols[...] += nn((grown * nt(cb, start)).astype(BF), pick.astype(BF))
    gc_ref[...] += nn(grown.astype(BF), start)
    faded = x_ref[...] * tail
    back = nt(bb, last)
    tails[...] += nn((faded * back).astype(BF), pick.astype(BF))
    gb_ref[...] += nn(faded.astype(BF), last)
    part = jnp.where(step < PAIRS // WIDE // 2, part_ref[...], part2_ref[...])
    gx_ref[...] = part + tail * back
    both = jnp.sum(start.astype(F32) * last.astype(F32), axis=1, keepdims=True)
    totals[pl.ds(step, 1), :] = jnp.sum(jnp.where(pick, both, 0.0), axis=0, keepdims=True)

    @pl.when(step == PAIRS // WIDE - 1)
    def _():
        after = (iota((T, T), 0) >= iota((T, T), 1)).astype(F32)
        before = (iota((T, T), 0) < iota((T, T), 1)).astype(F32)
        dims = (((0,), (0,)), ((), ()))
        up = lax.dot_general(cols[...], after, dims, precision=HIGH, preferred_element_type=F32)
        up += lax.dot_general(tails[...], before, dims, precision=HIGH, preferred_element_type=F32)
        total = jnp.sum(totals[...], axis=0, keepdims=True)
        total = jnp.sum(jnp.where(iota((H, N), 0) == iota((H, N), 1), total, 0.0), axis=1, keepdims=True)
        ga_ref[...] = ga_in[...] + up[:H] + jnp.exp(cum_ref[:, T - 1 : T]) * total


def across(x, gy, grow, tail, part, part2, cum, b, c, start, last, ga, gb, gc):
    width = WIDE * 2 * P_SIZE
    last_part = PAIRS // WIDE // 2 - 1
    return pl.pallas_call(
        across_kernel,
        grid=(PAIRS // WIDE,),
        in_specs=[wide(T, WIDE)] * 4
        + [
            pl.BlockSpec((T, width), lambda p: (0, jnp.minimum(p, last_part))),
            pl.BlockSpec((T, width), lambda p: (0, jnp.maximum(p - last_part - 1, 0))),
        ]
        + [whole((H, T)), whole((T, N)), whole((T, N))]
        + [state_block(WIDE), state_block(WIDE), whole((H, T)), whole((T, N)), whole((T, N))],
        out_specs=[wide(T, WIDE), whole((H, T)), whole((T, N)), whole((T, N))],
        out_shape=[
            jax.ShapeDtypeStruct((T, D), F32),
            jax.ShapeDtypeStruct((H, T), F32),
            jax.ShapeDtypeStruct((T, N), F32),
            jax.ShapeDtypeStruct((T, N), F32),
        ],
        scratch_shapes=[
            pltpu.VMEM((T, N), F32),
            pltpu.VMEM((T, N), F32),
            pltpu.VMEM((PAIRS // WIDE, N), F32),
        ],
        compiler_params=params(),
        cost_estimate=cost(8),
        name="across",
    )(x, gy, grow, tail, part, part2, cum, b, c, start, last, ga, gb, gc)


def fold_kernel(a0, a1, a2, a3, b0, b1, b2, b3, out_ref):
    sums = []
    for parts in ((a0, a1, a2, a3), (b0, b1, b2, b3)):
        total = parts[0][...].astype(F32)
        for part in parts[1:]:
            total += part[...].astype(F32)
        sums.append(total.astype(BF))
    for q in range(8 * TILES):
        r, c = divmod(q, 10)
        if r < 10:
            tile = sums[c // 5][16 * r : 16 * r + 16, 128 * (c % 5) : 128 * (c % 5) + 128]
        else:
            tile = jnp.zeros((16, 128), BF)
        out_ref[q // TILES, q % TILES] = tile


def fold(parts):
    return pl.pallas_call(
        fold_kernel,
        in_specs=[vmem()] * 8,
        out_specs=vmem(),
        out_shape=jax.ShapeDtypeStruct((8, TILES, 16, 128), BF),
        compiler_params=params(),
        cost_estimate=cost(3),
        name="fold",
    )(*parts)


def groups_of(row0, count, ids_ref):
    heads = (row0 + iota((count, N), 0)) // P_SIZE == iota((count, N), 1)
    return jnp.sum(jnp.where(heads, ids_ref[...], 0.0), axis=1, keepdims=True)


def zsum_kernel(row0_ref, z_ref, ids_ref, got_ref, parts_ref, out_ref, note_ref):
    total = parts_ref[0].astype(F32)
    for z in range(1, 8):
        total += parts_ref[z].astype(F32)
    out_ref[...] = total.astype(BF)
    found = jnp.zeros((16, N), F32)
    for i in range(TILES):
        row = row0_ref[0] + 16 * ((z_ref[0] * TILES + i) // 10)
        place = iota((16, N), 1) - H == groups_of(row, 16, ids_ref).astype(jnp.int32)
        tile = total[i]
        found += jnp.where(place, jnp.sum(tile * tile, axis=1, keepdims=True), 0.0)
    d_sum = jnp.zeros((1, N), F32)
    for s in range(N_SEQ):
        pieces = got_ref[s, OWN:, :].astype(F32)
        d_sum += pieces[0:1, :] + pieces[1:2, :] + pieces[2:3, :]
    note_ref[...] = jnp.sum(found, axis=0, keepdims=True) + d_sum / N_SEQ


def zsum(row0, z, ids, parts, got):
    return pl.pallas_call(
        zsum_kernel,
        in_specs=[smem(), smem()] + [vmem()] * 3,
        out_specs=[vmem(), vmem()],
        out_shape=[
            jax.ShapeDtypeStruct((TILES, 16, 128), BF),
            jax.ShapeDtypeStruct((1, N), F32),
        ],
        compiler_params=params(),
        cost_estimate=cost(2),
        name="zsum",
    )(row0, z, ids, got, parts)


def pack_kernel(tiles_ref, note_ref, out_ref):
    note = note_ref[...]
    hi = note.astype(BF).astype(F32)
    mid = (note - hi).astype(BF).astype(F32)
    at = iota((16, N), 0)
    rows = jnp.where(at == 0, hi, jnp.where(at == 1, mid, jnp.where(at == 2, note - hi - mid, 0.0)))
    for z in range(8):
        out_ref[z, :TILES] = tiles_ref[...]
        out_ref[z, TILES] = rows.astype(BF)


def pack(tiles, note):
    return pl.pallas_call(
        pack_kernel,
        in_specs=[vmem(), vmem()],
        out_specs=vmem(),
        out_shape=jax.ShapeDtypeStruct((8, TILES + 1, 16, 128), BF),
        compiler_params=params(),
        cost_estimate=cost(2),
        name="pack",
    )(tiles, note)


def note_of(ref):
    total = jnp.zeros((1, N), F32)
    for z in range(8):
        rows = ref[z, TILES].astype(F32)
        total += rows[0:1, :] + rows[1:2, :] + rows[2:3, :]
    return total


def tile_of(ref, r, c):
    z, i = divmod(10 * r + c, TILES)
    return ref[z, i].astype(F32)


def clip_kernel(tokens_all, row0_ref, core_ref, ids_ref, own_ref, other_ref, w_ref, d_ref):
    ids = ids_ref[...]
    lane = iota((1, N), 1)
    note = note_of(own_ref) + note_of(other_ref)
    grad_d = jnp.where(lane < H, note, 0.0)
    groups = groups_of(row0_ref[0], OWN, ids_ref)
    w_factor = jnp.zeros((OWN, 1), F32)
    d_factor = jnp.zeros((1, N), F32)
    for g in range(GROUPS):
        here = (ids == float(g)) & (lane < H)
        count = jnp.sum(jnp.where(here, 1.0, 0.0), axis=1, keepdims=True)
        sumsq = jnp.sum(jnp.where(lane == H + g, note, 0.0), axis=1, keepdims=True)
        sumsq += jnp.sum(jnp.where(here, grad_d * grad_d, 0.0), axis=1, keepdims=True)
        bound = 7.0 * jnp.sqrt(count * (P_SIZE * D + 1.0) * tokens_all)
        factor = jnp.minimum(1.0, bound / jnp.sqrt(sumsq + 1e-06))
        w_factor += jnp.where(groups == float(g), factor, 0.0)
        d_factor += jnp.where(here, factor, 0.0)
    d_ref[...] = (grad_d * d_factor)[:, :H]
    for r in range(10):
        scale = w_factor[16 * r : 16 * r + 16, :]
        for ref, core in ((own_ref, core_ref[0]), (other_ref, 1 - core_ref[0])):
            for c in range(10):
                col = pl.multiple_of(core * (D // 2) + 128 * c, 128)
                w_ref[16 * r : 16 * r + 16, pl.ds(col, 128)] = tile_of(ref, r, c) * scale


def clip(tokens_all, row0, core, ids, own, other):
    return pl.pallas_call(
        functools.partial(clip_kernel, tokens_all),
        in_specs=[smem(), smem()] + [vmem()] * 3,
        out_specs=[vmem(), vmem()],
        out_shape=[jax.ShapeDtypeStruct((OWN, D), F32), jax.ShapeDtypeStruct((1, H), F32)],
        compiler_params=params(),
        cost_estimate=cost(3),
        name="clip",
    )(row0, core, ids, own, other)


def shifted(v, axis, d):
    return lax.ppermute(v, axis, [(i, (i + d) % 4) for i in range(4)])


def plus(a, b):
    return (a.astype(F32) + b.astype(F32)).astype(BF)


def far(t, axis):
    m = t.shape[1] // 2
    return shifted(t[2, :m], axis, 1), shifted(t[2, m:], axis, -1)


def passed(t, ra, rb):
    m = t.shape[1] // 2
    up = jnp.concatenate([plus(t[1, :m], ra), t[1, m:]], axis=0)
    down = jnp.concatenate([t[3, :m], plus(t[3, m:], rb)], axis=0)
    return up, down


def near(t, up, down, axis):
    total = t[0].astype(F32) + shifted(up, axis, 1).astype(F32)
    return (total + shifted(down, axis, -1).astype(F32)).astype(BF)


def direct(t, axis):
    return (t[0],) + tuple(shifted(t[d], axis, d) for d in (1, 3, 2))


def other_core(v):
    return lax.ppermute(v, "core", [(0, 1), (1, 0)])


def sum_over(v, axes):
    for unit in (1, 4):
        got = [
            lax.ppermute(v, axes, [(i, i ^ (unit * k)) for i in range(16)]) for k in (1, 2, 3)
        ]
        v = (v + got[0]) + (got[1] + got[2])
    return v


def tie(*values):
    return lax.optimization_barrier(values)


def per_device(x_in, a_log, b_in, c_in, g_out, w_out, d_skip, group_ids):
    x, a, b, c, g = (x_in[0], a_log[0], b_in[0], c_in[0], g_out[0])
    core = lax.axis_index("core")
    half = D // 2
    at = jnp.stack([lax.axis_index("y"), lax.axis_index("x")]).astype(jnp.int32)
    mine = (2 * lax.axis_index("z") + core).reshape(1).astype(jnp.int32)
    at_z = lax.axis_index("z").reshape(1).astype(jnp.int32)
    row0 = ((4 * at[0] + at[1]) * OWN).reshape(1)
    ids = jnp.pad(group_ids.astype(F32), (0, N - H), constant_values=-1.0)[None]
    tokens_all = float(T * N_SEQ * 16)

    g_mine = lax.dynamic_slice_in_dim(g, core * half, half, axis=1)
    g_other = other_core(lax.dynamic_slice_in_dim(g, (1 - core) * half, half, axis=1))

    g_both = jnp.concatenate([g_mine, g_other], axis=0)

    cum, cum_t, tail, sent = local_ends(x, a, b)
    w_out, sent = tie(w_out, sent)
    w_mine = lax.dynamic_slice_in_dim(w_out, core * half, half, axis=1)
    w_half = lax.all_gather(w_mine, ("y", "x"), axis=0, tiled=True)
    got = swap(sent, SEQ)
    y_part, grow = intra(x, cum, cum_t, b, c, d_skip)
    y_part, g_both, at = tie(y_part, g_both, at)
    start = swap(chain(got, got, mine, False), SEQ).reshape(H * P_SIZE, N)
    y_own = inter(y_part, grow, c, start)
    y_other = other_core(y_own)
    first, second = terms(at, y_own, y_other, g_both)

    first = lax.psum_scatter(first.reshape(-1, half // 2), "x", scatter_dimension=0, tiled=True)
    far_y = far(second, "y")
    w_half, _ = tie(w_half, second)
    gy_own, gy_other = gy_parts(g_both, w_half)
    *far_y, gy_own, gy_other = tie(*far_y, gy_own, gy_other)
    gy_other = other_core(gy_other)
    up, down = passed(second, *far_y)
    up, down, gy_own, gy_other = tie(up, down, gy_own, gy_other)
    second = near(second, up, down, "y")
    gy, sent_back = entries(gy_own, gy_other, x, grow, c)
    got_back = swap(sent_back, SEQ)
    steps = PAIRS // STEP // 2
    gx1, *sums = within(0, steps, x, gy, cum, cum_t, b, c, d_skip)
    first, second, gx1 = tie(first, second, gx1)
    first = direct(first.reshape(4, OWN, half // 2), "y")
    second = direct(second, "x")
    tiles = fold(first + second)
    gy, mine, tiles = tie(gy, mine, tiles)
    tiles = swap(tiles, "z")
    states = chain(got_back, got, mine, True)
    gx2, *sums = within(steps, steps, x, gy, cum, cum_t, b, c, d_skip, sums)
    tiles, gx2, states = tie(tiles, gx2, states)
    tiles, note = zsum(row0, at_z, ids, tiles, got_back)
    note, states = tie(note, states)
    last = swap(states, SEQ).reshape(H * P_SIZE, N)
    note = sum_over(note, ("y", "x"))
    tiles, note, last = tie(tiles, note, last)
    tiles = pack(tiles, note)
    tiles, last = tie(tiles, last)
    tiles = swap(tiles, "z")
    gx, ga, gb, gc = across(x, gy, grow, tail, gx1, gx2, cum, b, c, start, last, *sums)
    tiles, ga = tie(tiles, ga)
    tiles_other = other_core(tiles)
    core = core.reshape(1).astype(jnp.int32)
    clipped_w, clipped_d = clip(tokens_all, row0, core, ids, tiles, tiles_other)
    return (gx[None], ga[None], gb[None], gc[None], clipped_w, clipped_d[0])


def solution(mesh):
    fine = Mesh(mesh.devices.reshape(4, 4, 8, 2), ("y", "x", "z", "core"))
    rows = ("y", "x")
    tokens = P(rows, SEQ, None)
    return jax.shard_map(
        per_device,
        mesh=fine,
        in_specs=(
            tokens, P(rows, None, SEQ), tokens, tokens, tokens, P(rows, None), P(), P(),
        ),
        out_specs=(tokens, P(rows, None, SEQ), tokens, tokens, P(rows, None), P()),
        check_vma=False,
    )
```
